32 devices in a mesh: section: 2 (over y), dp: 16 (over z, x, core).
Axes of the slice: x: 2, y: 2, z: 4, core: 2. Of those that a mesh axis runs over, the one named last changes fastest.
Arguments:
- prev_act: bfloat16 [2, 16, 192, 1024], P('section', 'dp'), may hold values from -6 to 6
- memory: bfloat16 [16, 192, 1024], P('dp', None, 'section'), may hold values from -6 to 6
- out_cot: bfloat16 [2, 16, 192, 1024], P('section', 'dp'), may hold values from -6 to 6
- tgt_len: int32 [16], P('dp'), may hold values from 12 to 192, as said below
- src_len: int32 [16], P('dp'), may hold values from 12 to 192, as said below
- norm_gain: bfloat16 [2, 3, 1024], P('section', None, 'dp'), may hold values from 0.25 to 1.75
- norm_bias: bfloat16 [2, 3, 1024], P('section', None, 'dp'), may hold values from -2 to 2
- self_qkv: bfloat16 [2, 1024, 3072], P('section', 'dp'), may hold values from -0.1875 to 0.1875
- self_qv_bias: bfloat16 [2, 2048], P('section', 'dp'), may hold values from -2 to 2
- self_out: bfloat16 [2, 1024, 1024], P('section', 'dp'), may hold values from -0.75 to 0.75
- cross_q: bfloat16 [2, 1024, 1024], P('section', 'dp'), may hold values from -0.1875 to 0.1875
- cross_kv: bfloat16 [2, 1024, 2048], P('section', 'dp'), may hold values from -0.1875 to 0.1875
- cross_qv_bias: bfloat16 [2, 2048], P('section', 'dp'), may hold values from -2 to 2
- cross_out: bfloat16 [2, 1024, 1024], P('section', 'dp'), may hold values from -0.75 to 0.75
- out_bias: bfloat16 [2, 3, 1024], P('section', None, 'dp'), may hold values from -2 to 2
- fc1: bfloat16 [2, 1024, 4096], P('section', 'dp'), may hold values from -0.1875 to 0.1875
- fc1_bias: bfloat16 [2, 4096], P('section', 'dp'), may hold values from -2 to 2
- fc2: bfloat16 [2, 4096, 1024], P('section', 'dp'), may hold values from -0.09375 to 0.09375
Outputs:
- output: bfloat16 [2, 16, 192, 1024], P('section', 'dp')
- input_grad: bfloat16 [2, 16, 192, 1024], P('section', 'dp')
- memory_grad: bfloat16 [16, 192, 1024], P('dp', None, 'section')
- grad_norm_gain: float32 [2, 3, 1024], P('section', None, 'dp')
- grad_norm_bias: float32 [2, 3, 1024], P('section', None, 'dp')
- grad_self_qkv: float32 [2, 1024, 3072], P('section', 'dp')
- grad_self_qv_bias: float32 [2, 2048], P('section', 'dp')
- grad_self_out: float32 [2, 1024, 1024], P('section', 'dp')
- grad_cross_q: float32 [2, 1024, 1024], P('section', 'dp')
- grad_cross_kv: float32 [2, 1024, 2048], P('section', 'dp')
- grad_cross_qv_bias: float32 [2, 2048], P('section', 'dp')
- grad_cross_out: float32 [2, 1024, 1024], P('section', 'dp')
- grad_out_bias: float32 [2, 3, 1024], P('section', None, 'dp')
- grad_fc1: float32 [2, 1024, 4096], P('section', 'dp')
- grad_fc1_bias: float32 [2, 4096], P('section', 'dp')
- grad_fc2: float32 [2, 4096, 1024], P('section', 'dp')
The draws below stay inside these ranges and needn't reach their ends.
Inputs may be any that keep to these rules, and one draw needn't show every extreme that they name: `tgt_len`: A row's target length; in every draw some row has exactly 192. `src_len`: A row's source length; in every draw some row has exactly 192.
All inputs are finite; a program needn't handle non-finite values.
Results may differ from the reference program's by a relative error of at most 0.019.
Values may be sent and summed in bfloat16 or wider, within the bound.
A program may use at most 192 MiB of HBM per device.

```python
import jax
import jax.numpy as jnp
from jax import lax

D = 1024
FF = 4096
H = 16
HD = 64
SEQ_LEN = 192
BATCH = 16
N_SECTION = 2


def ragged_lengths(key):
    level_key, trim_key, full_key = jax.random.split(key, 3)
    level = jax.random.randint(level_key, (BATCH,), 0, 4)
    longest = SEQ_LEN // jnp.power(2, level)
    trim = jax.random.randint(trim_key, (BATCH,), 0, longest // 2 + 1)
    lengths = longest - trim
    full_row = jax.random.randint(full_key, (), 0, BATCH)
    return jnp.where(jnp.arange(BATCH) == full_row, SEQ_LEN, lengths).astype(jnp.int32)


def draw_tgt_len(key, part):
    key = jax.random.fold_in(key, 11)
    return ragged_lengths(key)


def draw_src_len(key, part):
    key = jax.random.fold_in(key, 23)
    return ragged_lengths(key)


def levels(own_key, dims, pieces, low, largest):
    def one(axis_at, blocks):
        heights = jax.random.uniform(jax.random.fold_in(jax.random.fold_in(own_key, 6), axis_at), (blocks,), jnp.float32, low / len(pieces), largest / len(pieces))
        return jnp.repeat(jnp.exp(heights), dims[axis_at] // blocks).reshape((-1,) + (1,) * (len(dims) - axis_at - 1))

    factor_of = one(*pieces[0])
    for cut in pieces[1:]:
        factor_of = factor_of * one(*cut)
    return factor_of


def gaussian(own_key, shape, spread, bound, pieces=(), dtype=jnp.bfloat16):
    array = jax.random.normal(own_key, shape, jnp.float32) * spread
    if len(pieces) > 0:
        array = levels(own_key, shape, pieces, -0.22, 0.18) * array
    return jnp.clip(array, min=-bound, max=bound).astype(dtype)


def setup_inputs(seed: int = 0) -> dict:
    seeds = jax.random.split(jax.random.key(seed), 19)
    return {
        "prev_act": gaussian(seeds[0], (N_SECTION, BATCH, SEQ_LEN, D), 1.0, 6.0, ((0, 2), (1, 16))),
        "memory": gaussian(seeds[1], (BATCH, SEQ_LEN, D), 1.0, 6.0, ((0, 16), (2, 2))),
        "out_cot": gaussian(seeds[2], (N_SECTION, BATCH, SEQ_LEN, D), 1.0, 6.0, ((0, 2), (1, 16))),
        "tgt_len": draw_tgt_len(jax.random.fold_in(seeds[18], 71), 0),
        "src_len": draw_src_len(jax.random.fold_in(seeds[18], 71), 0),
        "norm_gain": jnp.clip(1.0 + 0.15 * jax.random.normal(seeds[5], (N_SECTION, 3, D), jnp.float32), 0.25, 1.75).astype(jnp.bfloat16),
        "norm_bias": gaussian(seeds[6], (N_SECTION, 3, D), 0.3, 2.0, ((0, 2), (2, 16))),
        "self_qkv": gaussian(seeds[7], (N_SECTION, D, 3 * D), D ** -0.5, 0.1875, ((0, 2), (1, 16))),
        "self_qv_bias": gaussian(seeds[8], (N_SECTION, 2 * D), 0.3, 2.0, ((0, 2), (1, 16))),
        "self_out": gaussian(seeds[9], (N_SECTION, D, D), (D // 16) ** -0.5, 0.75, ((0, 2), (1, 16))),
        "cross_q": gaussian(seeds[10], (N_SECTION, D, D), D ** -0.5, 0.1875, ((0, 2), (1, 16))),
        "cross_kv": gaussian(seeds[11], (N_SECTION, D, 2 * D), D ** -0.5, 0.1875, ((0, 2), (1, 16))),
        "cross_qv_bias": gaussian(seeds[12], (N_SECTION, 2 * D), 0.3, 2.0, ((0, 2), (1, 16))),
        "cross_out": gaussian(seeds[13], (N_SECTION, D, D), (D // 16) ** -0.5, 0.75, ((0, 2), (1, 16))),
        "out_bias": gaussian(seeds[14], (N_SECTION, 3, D), 0.3, 2.0, ((0, 2), (2, 16))),
        "fc1": gaussian(seeds[15], (N_SECTION, D, FF), D ** -0.5, 0.1875, ((0, 2), (1, 16))),
        "fc1_bias": gaussian(seeds[16], (N_SECTION, FF), 0.3, 2.0, ((0, 2), (1, 16))),
        "fc2": gaussian(seeds[17], (N_SECTION, FF, D), FF ** -0.5, 0.09375, ((0, 2), (1, 16))),
    }


@jax.custom_vjp
def low(v):
    return lax.optimization_barrier(v.astype(jnp.bfloat16)).astype(jnp.float32)

@jax.custom_vjp
def low_back(v):
    return v

def low_keep(v):
    return (low(v), None)

def low_pass(kept, grad):
    return (grad,)

def back_keep(v):
    return (v, None)

def back_low(kept, grad):
    return (low(grad),)
low.defvjp(low_keep, low_pass)
low_back.defvjp(back_keep, back_low)
HIGHEST = lax.Precision.HIGHEST
EPSILON = 1e-05
MASKED = -1000000000.0

def layer_norm(rows, gain, shift_term):
    center = rows - lax.optimization_barrier(jnp.mean(rows, -1, keepdims=True))
    scale = lax.rsqrt(lax.optimization_barrier(jnp.mean(center * center, -1, keepdims=True)) + EPSILON)
    return center * scale * gain + shift_term

def gelu_exact(values):
    return jax.nn.gelu(values, approximate=False)

def matmul(left, right):
    return jnp.dot(left, right, precision=HIGHEST)

def rounded(values):
    return low(low_back(values))

def attend(query, key_rows, value_rows, allowed):
    query_heads = query.reshape(query.shape[0], H, HD)
    key_heads = key_rows.reshape(key_rows.shape[0], H, HD)
    value_heads = value_rows.reshape(value_rows.shape[0], H, HD)
    scores = low_back(jnp.einsum('thd,shd->hts', query_heads, key_heads, precision=HIGHEST) * HD ** (-0.5))
    scores = jnp.where(allowed[None], scores, MASKED)
    weights = jnp.exp(scores - lax.optimization_barrier(jnp.max(scores, -1, keepdims=True)))
    probs = weights / lax.optimization_barrier(jnp.sum(weights, -1, keepdims=True))
    mixed = jnp.einsum('hts,shd->thd', low(probs), value_heads, precision=HIGHEST)
    return rounded(mixed.reshape(query.shape[0], H * HD))

def layer(hidden, encoded, params, tgt_count, src_count):
    gains, shifts, w_sqkv, b_sqv, w_sout, w_cq, w_ckv, b_cqv, w_cout, b_out, w_one, b_one, w_two = params
    places = jnp.arange(hidden.shape[0])
    sources = jnp.arange(encoded.shape[0])
    self_ok = (places[None, :] <= places[:, None]) & (places[None, :] < tgt_count)
    cross_ok = jnp.broadcast_to(sources[None, :] < src_count, (hidden.shape[0], encoded.shape[0]))
    first_in = low(layer_norm(hidden, gains[0], shifts[0]))
    joint = matmul(first_in, w_sqkv)
    query_self = rounded(joint[:, :D] + b_sqv[:D])
    keys_self = rounded(joint[:, D:2 * D])
    values_self = rounded(joint[:, 2 * D:] + b_sqv[D:])
    self_mixed = attend(query_self, keys_self, values_self, self_ok)
    after_self = hidden + low_back(matmul(self_mixed, w_sout) + b_out[0])
    second_in = low(layer_norm(after_self, gains[1], shifts[1]))
    query_cross = rounded(matmul(second_in, w_cq) + b_cqv[:D])
    memory_proj = matmul(encoded, w_ckv)
    keys_cross = rounded(memory_proj[:, :D])
    values_cross = rounded(memory_proj[:, D:] + b_cqv[D:])
    cross_mixed = attend(query_cross, keys_cross, values_cross, cross_ok)
    after_cross = after_self + low_back(matmul(cross_mixed, w_cout) + b_out[1])
    third_in = low(layer_norm(after_cross, gains[2], shifts[2]))
    pre_act = low_back(matmul(third_in, w_one) + b_one)
    activ = low(gelu_exact(pre_act))
    return after_cross + low_back(matmul(activ, w_two) + b_out[2])

def reference(prev_act, memory, out_cot, tgt_len, src_len, norm_gain, norm_bias, self_qkv, self_qv_bias, self_out, cross_q, cross_kv, cross_qv_bias, cross_out, out_bias, fc1, fc1_bias, fc2):
    weight_list = (norm_gain, norm_bias, self_qkv, self_qv_bias, self_out, cross_q, cross_kv, cross_qv_bias, cross_out, out_bias, fc1, fc1_bias, fc2)
    encoded = memory.astype(jnp.float32)
    memory_total = jnp.zeros(memory.shape, jnp.float32)
    outputs = []
    returned = []
    totals_all = []
    for section in range(N_SECTION):
        params = tuple((weight[section].astype(jnp.float32) for weight in weight_list))
        source = prev_act[(section - 1) % N_SECTION].astype(jnp.float32)
        cotangent = out_cot[(section + 1) % N_SECTION].astype(jnp.float32)

        def one_row(totals, row, params=params):
            hidden, enc_row, cot_row, tgt_count, src_count = row

            def forward(hidden_in, enc_in, weights):
                return layer(hidden_in, enc_in, weights, tgt_count, src_count)
            result, pullback = jax.vjp(forward, hidden, enc_row, params)
            grad_hidden, grad_enc, grad_weights = pullback(cot_row)
            totals = jax.tree.map(jnp.add, totals, grad_weights)
            return (totals, (result, grad_hidden, grad_enc))
        start = jax.tree.map(jnp.zeros_like, params)
        totals, (result, grad_hidden, grad_enc) = lax.scan(one_row, start, (source, encoded, cotangent, tgt_len, src_len))
        outputs.append(result)
        returned.append(grad_hidden)
        totals_all.append(totals)
        memory_total = memory_total + grad_enc
    output = jnp.stack(outputs).astype(jnp.bfloat16)
    input_grad = jnp.stack([returned[(section + 1) % N_SECTION] for section in range(N_SECTION)]).astype(jnp.bfloat16)
    stacked = [jnp.stack([totals_all[section][index] for section in range(N_SECTION)]) for index in range(13)]
    return (output, input_grad, memory_total.astype(jnp.bfloat16), stacked[0], stacked[1], stacked[2], stacked[3], stacked[4], stacked[5], stacked[6], stacked[7], stacked[8], stacked[9], stacked[10], stacked[11], stacked[12])
```

```python
import functools
from types import SimpleNamespace

import jax
import jax.numpy as jnp
from jax import lax
from jax.experimental import pallas as pl
from jax.experimental.pallas import tpu as pltpu
from jax.sharding import PartitionSpec as P

H = 16
HD = 64


EPSILON = 1e-05
MASKED = -1000000000.0


def passed_along(value, axis, by):
    length = lax.axis_size(axis)
    return lax.ppermute(value, axis, [(i, (i + by) % length) for i in range(length)])


def norm_fwd(rows, gain, shift_term):
    center = rows - jnp.mean(rows, -1, keepdims=True)
    scale = lax.rsqrt(jnp.mean(center * center, -1, keepdims=True) + EPSILON)
    return center * scale * gain + shift_term


def gelu_exact(values):
    return jax.nn.gelu(values, approximate=False)


def product(left, right):
    return jnp.dot(left, right, preferred_element_type=jnp.float32)


def product_right_t(left, right):
    return lax.dot_general(
        left, right, (((1,), (1,)), ((), ())), preferred_element_type=jnp.float32
    )


def product_left_t(left, right):
    return lax.dot_general(
        left, right, (((0,), (0,)), ((), ())), preferred_element_type=jnp.float32
    )


def split_heads(flat, batch_rows):
    return flat.reshape(batch_rows, -1, H, HD)


def softmax_probs(query, key_rows, allowed):
    scores = jnp.einsum(
        "rthd,rshd->rhts", query, key_rows, preferred_element_type=jnp.float32
    ) * HD ** (-0.5)
    scores = jnp.where(allowed[:, None], scores, MASKED)
    weights = jnp.exp(scores - jnp.max(scores, -1, keepdims=True))
    return weights / jnp.sum(weights, -1, keepdims=True)


def attend_fwd(query, key_rows, value_rows, allowed):
    probs = softmax_probs(query, key_rows, allowed)
    mixed = jnp.einsum(
        "rhts,rshd->rthd",
        probs.astype(jnp.bfloat16),
        value_rows,
        preferred_element_type=jnp.float32,
    )
    return mixed.reshape(mixed.shape[0] * mixed.shape[1], -1).astype(jnp.bfloat16)


def attend_back(query, key_rows, value_rows, allowed, grad_mixed):
    probs = softmax_probs(query, key_rows, allowed)
    grad_heads = grad_mixed.reshape(query.shape)
    grad_probs = jnp.einsum(
        "rthd,rshd->rhts", grad_heads, value_rows, preferred_element_type=jnp.float32
    )
    delta = jnp.sum(probs * grad_probs, -1, keepdims=True)
    grad_scores = (probs * (grad_probs - delta)).astype(jnp.bfloat16)
    scale = HD ** (-0.5)
    grad_query = (
        jnp.einsum("rhts,rshd->rthd", grad_scores, key_rows, preferred_element_type=jnp.float32)
        * scale
    )
    grad_keys = (
        jnp.einsum("rhts,rthd->rshd", grad_scores, query, preferred_element_type=jnp.float32)
        * scale
    )
    grad_values = jnp.einsum(
        "rhts,rthd->rshd",
        probs.astype(jnp.bfloat16),
        grad_heads,
        preferred_element_type=jnp.float32,
    )
    width = query.shape[2] * query.shape[3]
    return (
        grad_query.reshape(-1, width).astype(jnp.bfloat16),
        grad_keys.reshape(-1, width).astype(jnp.bfloat16),
        grad_values.reshape(-1, width).astype(jnp.bfloat16),
    )


def unpack(pieces):
    return tuple((piece[0] for piece in pieces))


def on_device(
    prev_act,
    memory,
    out_cot,
    tgt_len,
    src_len,
    norm_gain,
    norm_bias,
    self_qkv,
    self_qv_bias,
    self_out,
    cross_q,
    cross_kv,
    cross_qv_bias,
    cross_out,
    out_bias,
    fc1,
    fc1_bias,
    fc2,
):
    fetched = unpack(
        (
            lax.all_gather(norm_gain, "dp", axis=2, tiled=True),
            lax.all_gather(norm_bias, "dp", axis=2, tiled=True),
            lax.all_gather(self_qkv, "dp", axis=1, tiled=True),
            lax.all_gather(self_qv_bias, "dp", axis=1, tiled=True),
            lax.all_gather(self_out, "dp", axis=1, tiled=True),
            lax.all_gather(cross_q, "dp", axis=1, tiled=True),
            lax.all_gather(cross_kv, "dp", axis=1, tiled=True),
            lax.all_gather(cross_qv_bias, "dp", axis=1, tiled=True),
            lax.all_gather(cross_out, "dp", axis=1, tiled=True),
            lax.all_gather(out_bias, "dp", axis=2, tiled=True),
            lax.all_gather(fc1, "dp", axis=1, tiled=True),
            lax.all_gather(fc1_bias, "dp", axis=1, tiled=True),
            lax.all_gather(fc2, "dp", axis=1, tiled=True),
        )
    )
    gains, shifts, w_sqkv, b_sqv, w_sout, w_cq, w_ckv, b_cqv, w_cout, b_out, w_one, b_one, w_two = (
        fetched
    )
    gain_f = gains.astype(jnp.float32)
    shift_f = shifts.astype(jnp.float32)
    sqv_f = b_sqv.astype(jnp.float32)
    cqv_f = b_cqv.astype(jnp.float32)
    out_f = b_out.astype(jnp.float32)
    one_f = b_one.astype(jnp.float32)
    source = passed_along(prev_act, "section", 1)[0]
    batch_rows, length, width = source.shape
    encoded = lax.all_gather(memory, "section", axis=2, tiled=True)
    mem_flat = encoded.reshape(-1, width)
    places = jnp.arange(length)
    self_ok = (places[None, None, :] <= places[None, :, None]) & (
        places[None, None, :] < tgt_len[:, None, None]
    )
    cross_ok = jnp.arange(encoded.shape[1])[None, None, :] < src_len[:, None, None]
    resid = source.astype(jnp.float32).reshape(-1, width)
    normed_one, pull_one = jax.vjp(norm_fwd, resid, gain_f[0], shift_f[0])
    first_in = normed_one.astype(jnp.bfloat16)
    joint = product(first_in, w_sqkv)
    query_self = (joint[:, :width] + sqv_f[:width]).astype(jnp.bfloat16)
    keys_self = joint[:, width : 2 * width].astype(jnp.bfloat16)
    values_self = (joint[:, 2 * width :] + sqv_f[width:]).astype(jnp.bfloat16)
    self_mixed = attend_fwd(
        split_heads(query_self, batch_rows),
        split_heads(keys_self, batch_rows),
        split_heads(values_self, batch_rows),
        self_ok,
    )
    after_self = resid + (product(self_mixed, w_sout) + out_f[0])
    normed_two, pull_two = jax.vjp(norm_fwd, after_self, gain_f[1], shift_f[1])
    second_in = normed_two.astype(jnp.bfloat16)
    query_cross = (product(second_in, w_cq) + cqv_f[:width]).astype(jnp.bfloat16)
    memory_proj = product(mem_flat, w_ckv)
    keys_cross = memory_proj[:, :width].astype(jnp.bfloat16)
    values_cross = (memory_proj[:, width:] + cqv_f[width:]).astype(jnp.bfloat16)
    cross_mixed = attend_fwd(
        split_heads(query_cross, batch_rows),
        split_heads(keys_cross, batch_rows),
        split_heads(values_cross, batch_rows),
        cross_ok,
    )
    after_cross = after_self + (product(cross_mixed, w_cout) + out_f[1])
    normed_three, pull_three = jax.vjp(norm_fwd, after_cross, gain_f[2], shift_f[2])
    third_in = normed_three.astype(jnp.bfloat16)
    pre_act = product(third_in, w_one) + one_f
    activ, pull_gelu = jax.vjp(gelu_exact, pre_act)
    act_low = activ.astype(jnp.bfloat16)
    result = after_cross + (product(act_low, w_two) + out_f[2])
    output = result.astype(jnp.bfloat16).reshape(1, batch_rows, length, width)
    (
        unused_gains,
        unused_shifts,
        w_sqkv,
        unused_sqv,
        w_sout,
        w_cq,
        w_ckv,
        unused_cqv,
        w_cout,
        unused_out,
        w_one,
        unused_one,
        w_two,
    ) = fetched
    grad_out = passed_along(out_cot, "section", -1)[0].astype(jnp.float32).reshape(-1, width)
    ffn_grad = grad_out.astype(jnp.bfloat16)
    grad_fc2 = product_left_t(act_low, ffn_grad)
    grad_b2 = jnp.sum(ffn_grad, 0, dtype=jnp.float32)
    grad_act = product_right_t(ffn_grad, w_two)
    (grad_pre,) = pull_gelu(grad_act)
    pre_low = grad_pre.astype(jnp.bfloat16)
    grad_fc1 = product_left_t(third_in, pre_low)
    grad_b1 = jnp.sum(pre_low, 0, dtype=jnp.float32)
    grad_mid, grad_gain3, grad_shift3 = pull_three(product_right_t(pre_low, w_one))
    grad_mid = grad_mid + grad_out
    cross_grad = grad_mid.astype(jnp.bfloat16)
    grad_cout = product_left_t(cross_mixed, cross_grad)
    grad_bco = jnp.sum(cross_grad, 0, dtype=jnp.float32)
    grad_cmix = product_right_t(cross_grad, w_cout).astype(jnp.bfloat16)
    grad_qc, grad_kc, grad_vc = attend_back(
        split_heads(query_cross, batch_rows),
        split_heads(keys_cross, batch_rows),
        split_heads(values_cross, batch_rows),
        cross_ok,
        grad_cmix,
    )
    grad_cq = product_left_t(second_in, grad_qc)
    grad_kv = jnp.concatenate([grad_kc, grad_vc], -1)
    grad_ckv = product_left_t(mem_flat, grad_kv)
    grad_cqv = jnp.concatenate(
        [jnp.sum(grad_qc, 0, dtype=jnp.float32), jnp.sum(grad_vc, 0, dtype=jnp.float32)]
    )
    grad_memory = product_right_t(grad_kv, w_ckv).reshape(encoded.shape)
    memory_grad = lax.psum_scatter(
        grad_memory.astype(jnp.bfloat16), "section", scatter_dimension=2, tiled=True
    )
    grad_after, grad_gain2, grad_shift2 = pull_two(product_right_t(grad_qc, w_cq))
    grad_after = grad_after + grad_mid
    self_grad = grad_after.astype(jnp.bfloat16)
    grad_sout = product_left_t(self_mixed, self_grad)
    grad_bso = jnp.sum(self_grad, 0, dtype=jnp.float32)
    grad_smix = product_right_t(self_grad, w_sout).astype(jnp.bfloat16)
    grad_qs, grad_ks, grad_vs = attend_back(
        split_heads(query_self, batch_rows),
        split_heads(keys_self, batch_rows),
        split_heads(values_self, batch_rows),
        self_ok,
        grad_smix,
    )
    grad_qkv = jnp.concatenate([grad_qs, grad_ks, grad_vs], -1)
    grad_sqkv = product_left_t(first_in, grad_qkv)
    grad_sqv = jnp.concatenate(
        [jnp.sum(grad_qs, 0, dtype=jnp.float32), jnp.sum(grad_vs, 0, dtype=jnp.float32)]
    )
    grad_in, grad_gain1, grad_shift1 = pull_one(product_right_t(grad_qkv, w_sqkv))
    grad_in = grad_in + grad_after
    input_grad = passed_along(
        grad_in.astype(jnp.bfloat16).reshape(1, batch_rows, length, width), "section", -1
    )
    grad_gain = jnp.stack([grad_gain1, grad_gain2, grad_gain3])
    grad_shift = jnp.stack([grad_shift1, grad_shift2, grad_shift3])
    grad_obias = jnp.stack([grad_bso, grad_bco, grad_b2])
    sums = (
        lax.psum_scatter(
            grad_gain.astype(jnp.bfloat16), "dp", scatter_dimension=1, tiled=True
        ).astype(jnp.float32),
        lax.psum_scatter(
            grad_shift.astype(jnp.bfloat16), "dp", scatter_dimension=1, tiled=True
        ).astype(jnp.float32),
        lax.psum_scatter(
            grad_sqkv.astype(jnp.bfloat16), "dp", scatter_dimension=0, tiled=True
        ).astype(jnp.float32),
        lax.psum_scatter(
            grad_sqv.astype(jnp.bfloat16), "dp", scatter_dimension=0, tiled=True
        ).astype(jnp.float32),
        lax.psum_scatter(
            grad_sout.astype(jnp.bfloat16), "dp", scatter_dimension=0, tiled=True
        ).astype(jnp.float32),
        lax.psum_scatter(
            grad_cq.astype(jnp.bfloat16), "dp", scatter_dimension=0, tiled=True
        ).astype(jnp.float32),
        lax.psum_scatter(
            grad_ckv.astype(jnp.bfloat16), "dp", scatter_dimension=0, tiled=True
        ).astype(jnp.float32),
        lax.psum_scatter(
            grad_cqv.astype(jnp.bfloat16), "dp", scatter_dimension=0, tiled=True
        ).astype(jnp.float32),
        lax.psum_scatter(
            grad_cout.astype(jnp.bfloat16), "dp", scatter_dimension=0, tiled=True
        ).astype(jnp.float32),
        lax.psum_scatter(
            grad_obias.astype(jnp.bfloat16), "dp", scatter_dimension=1, tiled=True
        ).astype(jnp.float32),
        lax.psum_scatter(
            grad_fc1.astype(jnp.bfloat16), "dp", scatter_dimension=0, tiled=True
        ).astype(jnp.float32),
        lax.psum_scatter(
            grad_b1.astype(jnp.bfloat16), "dp", scatter_dimension=0, tiled=True
        ).astype(jnp.float32),
        lax.psum_scatter(
            grad_fc2.astype(jnp.bfloat16), "dp", scatter_dimension=0, tiled=True
        ).astype(jnp.float32),
    )
    return (
        output,
        input_grad,
        memory_grad,
        sums[0][None],
        sums[1][None],
        sums[2][None],
        sums[3][None],
        sums[4][None],
        sums[5][None],
        sums[6][None],
        sums[7][None],
        sums[8][None],
        sums[9][None],
        sums[10][None],
        sums[11][None],
        sums[12][None],
    )


Z = 4
P_IN = 4
L = 192
D = 1024
T = P_IN * L
FL = 1024
TILE = 32
MESH = pl.DeviceIdType.MESH
F32 = jnp.float32
BF16 = jnp.bfloat16

WEIGHTS = dict(
    qkv=(256, 768, True),
    so=(64, 1024, False),
    ckv=(256, 512, True),
    cq=(256, 256, True),
    co=(64, 1024, False),
    f1=(256, 1024, True),
    f2=(256, 1024, False),
)
SEMS = 200


def run_if(cond, fn):
    if cond is None:
        fn()
    else:
        pl.when(cond)(fn)


def part(index, size, step=None):
    return pl.ds(pl.multiple_of(index * size, size), size if step is None else step)


def nn(left, right):
    return jnp.dot(left, right, preferred_element_type=F32)


def nt(left, right):
    return lax.dot_general(left, right, (((1,), (1,)), ((), ())), preferred_element_type=F32)


def tn(left, right):
    return lax.dot_general(left, right, (((0,), (0,)), ((), ())), preferred_element_type=F32)


def loop(count, body):
    def step(index, carry):
        body(index)
        return carry

    lax.fori_loop(0, count, step, 0)


def gelu_pair(values):
    bell = jnp.exp(-0.5 * values * values)
    step = 1.0 / (1.0 + 0.3275911 * 0.7071067811865476 * jnp.abs(values))
    series = step * (
        0.254829592
        + step
        * (-0.284496736 + step * (1.421413741 + step * (-1.453152027 + step * 1.061405429)))
    )
    above = 0.5 * series * bell
    below = jnp.where(values < 0, above, 1.0 - above)
    return values * below, below + values * bell * 0.3989422804014327


def whiten(rows):
    center = rows - jnp.mean(rows, -1, keepdims=True)
    scale = lax.rsqrt(jnp.mean(center * center, -1, keepdims=True) + EPSILON)
    return center * scale, scale


def whole_kernel(n_sec, mem_cols, *refs):
    given = iter(refs)

    def take(names):
        return SimpleNamespace(**{name: next(given) for name in names})

    def take_weights(**fields):
        for name in WEIGHTS:
            for field in fields:
                setattr(getattr(wt, name), field, next(given))

    wt = SimpleNamespace(**{name: SimpleNamespace() for name in WEIGHTS})
    io = take(dict(prev=0, mem=0, cot=0, small=0))
    take_weights(source=0)
    vars(io).update(vars(take(dict(output=0, input_grad=0, memory_grad=0))))
    take_weights(result=0)
    vars(io).update(vars(take(dict(sums_out=0))))
    buf = take(buffer_shapes(n_sec, mem_cols))
    set_a, set_b, set_c = (take(REDUCE_SHAPES) for _ in range(3))
    take_weights(weight=0, grad=0, to_diag=0, to_opp=0, near=0, far=0)
    send_sems, recv_sems, local_sems = given

    s = lax.axis_index("section")
    d = lax.axis_index("dp")
    z, q = d // P_IN, d % P_IN
    x, c = q // 2, q % 2
    end = (z % 3) == 0
    mid = (z % 3) != 0
    q_core = q + 1 - 2 * c
    q_x = q + 2 - 4 * x
    q_xc = q_x + 1 - 2 * c
    z_adj = z + 1 - 2 * (z % 2)
    z_opp = 3 - z
    z_diag = (z + 2) % 4
    dev_core, dev_x, dev_xc = (s, z * P_IN + q_core), (s, z * P_IN + q_x), (s, z * P_IN + q_xc)
    dev_adj, dev_opp, dev_diag = (s, z_adj * P_IN + q), (s, z_opp * P_IN + q), (s, z_diag * P_IN + q)
    in_plane = ((q_core, dev_core), (q_x, dev_x), (q_xc, dev_xc))

    counter = [0]
    started = []
    local_counter = [0]

    def slot(count=1):
        counter[0] += count
        return counter[0] - count

    def remote(src, dst, k, device):
        return pltpu.make_async_remote_copy(
            src_ref=src, dst_ref=dst, send_sem=send_sems.at[k], recv_sem=recv_sems.at[k],
            device_id=device, device_id_type=MESH,
        )

    def send(src, dst, k, device, cond=None):
        copy = remote(src, dst, k, device)
        run_if(cond, copy.start)
        record = [copy, cond]
        started.append(record)
        return record

    def sent(record):
        run_if(record[1], record[0].wait_send)
        started[:] = [other for other in started if other is not record]

    def arrived(dst, k, cond=None):
        run_if(cond, remote(dst, dst, k, dev_core).wait_recv)

    def local(src, dst):
        copy = pltpu.make_async_copy(src, dst, local_sems.at[local_counter[0]])
        local_counter[0] += 1
        copy.start()
        return copy

    def rows(rows_of, index):
        return rows_of.at[part(index, L)]

    for name, (count, _, by_column) in WEIGHTS.items():
        weight = getattr(wt, name)
        weight.count, weight.by_column = count, by_column
        weight.to_use, weight.swap, weight.to_sum, weight.last = slot(5), slot(3), slot(5), slot(3)

    def block(name, index):
        return name.weight.at[part(index, name.count)]

    def weight_send(name, src):
        k = name.to_use
        send(src, block(name, z), k, dev_adj)
        send(src, block(name, z), k + 1, dev_opp, mid)
        send(src, block(name, z), k + 2, dev_diag, end)

    def weight_relay(name):
        k = name.to_use
        arrived(block(name, z_opp), k + 1, mid)
        send(block(name, z_opp), block(name, z_opp), k + 3, dev_adj, mid)
        arrived(block(name, z_diag), k + 2, mid)
        send(block(name, z_diag), block(name, z_diag), k + 4, dev_adj, mid)

    def weight_ready(name):
        k = name.to_use
        arrived(block(name, z_adj), k)
        arrived(block(name, z_diag), k + 3, end)
        arrived(block(name, z_opp), k + 4, end)


    def swap_start(name):
        size = name.count // P_IN
        place = name.weight.at[part(z * P_IN + q, size)]
        for j, (q_to, device) in enumerate(in_plane):
            send(name.source.at[q_to], place, name.swap + j, device)
        name.own_copy = local(name.source.at[q], place)

    def swap_wait(name):
        size = name.count // P_IN
        for j, (q_from, _) in enumerate(in_plane):
            arrived(name.weight.at[part(z * P_IN + q_from, size)], name.swap + j)
        name.own_copy.wait()

    def grad_block(name, index):
        return name.grad.at[part(index, name.count)]

    def grad_send(name):
        k = name.to_sum
        send(grad_block(name, z_opp), name.to_diag, k, dev_adj, end)
        send(grad_block(name, z_diag), name.to_opp, k + 1, dev_adj, end)
        send(grad_block(name, z_adj), name.near, k + 2, dev_adj)

    def add_rows(count, body):
        size = min(count, 64)
        loop(count // size, lambda i: body(part(i, size)))

    def grad_combine(name):
        k = name.to_sum
        count = name.count

        def add(landed, index):
            def one(place):
                own = grad_block(name, index)[place, :].astype(F32)
                landed[place, :] = (own + landed[place, :].astype(F32)).astype(BF16)

            add_rows(count, one)

        def work():
            arrived(name.to_diag, k)
            add(name.to_diag, z_diag)

        run_if(mid, work)
        send(name.to_diag, name.far, k + 3, dev_diag, mid)

        def more():
            arrived(name.to_opp, k + 1)
            add(name.to_opp, z_opp)

        run_if(mid, more)
        send(name.to_opp, name.far, k + 4, dev_opp, mid)

    result_copies = []

    def grad_final(name):
        k = name.to_sum
        count = name.count
        arrived(name.near, k + 2)
        arrived(name.far, k + 3, end)
        arrived(name.far, k + 4, mid)

        def one(place):
            total = grad_block(name, z)[place, :].astype(F32)
            total = total + name.near[place, :].astype(F32)
            total = total + name.far[place, :].astype(F32)
            name.near[place, :] = total.astype(BF16)

        add_rows(count, one)
        if name.by_column:
            size = count // P_IN
            for j, (q_to, device) in enumerate(in_plane):
                src = name.near.at[part(q_to, size)]
                send(src, name.result.at[q], name.last + j, device)
            src = name.near.at[part(q, size)]
            result_copies.append(local(src, name.result.at[q]))
        else:
            result_copies.append(local(name.near, name.result))

    def last_wait(name):
        for j, (q_from, _) in enumerate(in_plane):
            arrived(name.result.at[q_from], name.last + j)

    def gather_start(name):
        k = slot(3)
        send(rows(name, q), rows(name, q), k, dev_x)
        send(rows(name, q), rows(name, q), k + 1, dev_core)
        return name, k

    def gather_relay(ticket):
        name, k = ticket
        arrived(rows(name, q_x), k)
        send(rows(name, q_x), rows(name, q_x), k + 2, dev_core)

    def gather_ready(ticket):
        name, k = ticket
        arrived(rows(name, q_core), k + 1)
        arrived(rows(name, q_xc), k + 2)

    def gather_finish(ticket):
        gather_relay(ticket)
        gather_ready(ticket)

    def reduce_start(which):
        k = slot(3)
        out = which.parts
        first = send(rows(out, q_xc), rows(which.core, 1), k, dev_core)
        second = send(rows(out, q_core), rows(which.core, 0), k + 1, dev_core)
        return which, k, [first, second]

    def reduce_relay(ticket):
        which, k, records = ticket
        out = which.parts
        arrived(rows(which.core, 1), k)

        def one(i):
            mine = rows(out, q_x)
            place = part(i, TILE)
            total = mine[place, :].astype(F32) + rows(which.core, 1)[place, :].astype(F32)
            mine[place, :] = total.astype(BF16)

        loop(L // TILE, one)
        records.append(send(rows(out, q_x), which.across, k + 2, dev_x))

    def reduce_ready(ticket):
        which, k, records = ticket
        arrived(rows(which.core, 0), k + 1)
        arrived(which.across, k + 2)

    def reduced(ticket, place):
        which = ticket[0]
        total = rows(which.parts, q)[place, :].astype(F32)
        total = total + rows(which.core, 0)[place, :].astype(F32)
        return total + which.across[place, :].astype(F32)

    def reduce_done(ticket):
        for record in ticket[2]:
            sent(record)

    def spread_start(name, src):
        k = slot(8)
        place = name.at[q, z]
        copy = None
        if src is not None:
            copy = local(src, place)
        else:
            src = place
        send(src, place, k, dev_adj)
        send(src, place, k + 1, dev_opp, mid)
        send(src, place, k + 2, dev_diag, end)
        return name, k, copy

    def spread_relay(ticket):
        name, k, copy = ticket
        arrived(name.at[q, z_opp], k + 1, mid)
        send(name.at[q, z_opp], name.at[q, z_opp], k + 3, dev_adj, mid)
        arrived(name.at[q, z_diag], k + 2, mid)
        send(name.at[q, z_diag], name.at[q, z_diag], k + 4, dev_adj, mid)
        arrived(name.at[q, z_adj], k)
        arrived(name.at[q, z_diag], k + 3, end)
        arrived(name.at[q, z_opp], k + 4, end)
        if copy is not None:
            copy.wait()
        for j, (_, device) in enumerate(in_plane):
            send(name.at[q], name.at[q], k + 5 + j, device)

    def spread_ready(ticket):
        name, k, _ = ticket
        for j, (q_from, _) in enumerate(in_plane):
            arrived(name.at[q_from], k + 5 + j)

    def lanes(j, size=256):
        return part(j, size)

    def matmul(left, right, dst, bias=None, bias_row=0, bias_at=0):
        count = right.shape[1] // 256

        def one(j):
            tile = nn(left[...], right[:, lanes(j)])
            if bias is not None:
                tile = tile + bias[bias_row:bias_row + 1, part(j + bias_at, 256)]
            dst[:, lanes(j)] = tile.astype(BF16)

        loop(count, one)

    def matmul_back(left, right, dst):
        def one(j):
            dst[:, lanes(j)] = nt(left[...], right[lanes(j), :]).astype(BF16)

        loop(right.shape[0] // 256, one)

    def weight_grad(left, right, name):
        def one(j):
            name.grad[lanes(j), :] = tn(left[:, lanes(j)], right[...]).astype(BF16)

        loop(left.shape[1] // 256, one)

    low_half = lax.broadcasted_iota(jnp.int32, (L, 128), 1) < 64
    keep_low = low_half.astype(F32).astype(BF16)
    keep_high = (1.0 - low_half.astype(F32)).astype(BF16)

    def both(pair):
        return jnp.concatenate([pair * keep_low, pair * keep_high], axis=0)

    def merge(stacked):
        return jnp.where(low_half, stacked[:L], stacked[L:])

    def attention(qref, q_at, kref, k_at, v_at, causal, length_row, probs, dst):
        def one(i):
            r, pair = i // 2, i % 2
            place = part(r, L)
            query = both(qref[place, part(pair + q_at, 128)])
            scores = nt(query, kref[place, part(pair + k_at, 128)]) * HD ** (-0.5)
            key = lax.broadcasted_iota(jnp.int32, scores.shape, 1)
            limit = buf.sva[r, z][length_row:length_row + 1, 0:1].astype(F32)
            allowed = key.astype(F32) < limit
            if causal:
                at = lax.broadcasted_iota(jnp.int32, scores.shape, 0)
                at = jnp.where(at < L, at, at - L)
                allowed = allowed & (key <= at)
            scores = jnp.where(allowed, scores, MASKED)
            raised = jnp.exp(scores - jnp.max(scores, -1, keepdims=True))
            weights = (raised * (1.0 / jnp.sum(raised, -1, keepdims=True))).astype(BF16)
            probs[i] = weights
            mixed = nn(weights, kref[place, part(pair + v_at, 128)])
            dst[place, part(pair, 128)] = merge(mixed).astype(BF16)

        loop(2 * P_IN, one)

    def attention_back(qref, q_at, kref, k_at, v_at, probs, grad):
        def one(i):
            r, pair = i // 2, i % 2
            place = part(r, L)
            query = both(qref[place, part(pair + q_at, 128)])
            key = kref[place, part(pair + k_at, 128)]
            value = kref[place, part(pair + v_at, 128)]
            mixed_grad = both(grad[place, part(pair, 128)])
            weights = probs[i]
            soft = weights.astype(F32)
            grad_probs = nt(mixed_grad, value)
            delta = jnp.sum(soft * grad_probs, -1, keepdims=True)
            grad_scores = (soft * (grad_probs - delta)).astype(BF16)
            scale = HD ** (-0.5)
            grad_query = merge(nn(grad_scores, key)) * scale
            grad_key = tn(grad_scores, query) * scale
            grad_value = tn(weights, mixed_grad)
            qref[place, part(pair + q_at, 128)] = grad_query.astype(BF16)
            kref[place, part(pair + k_at, 128)] = grad_key.astype(BF16)
            kref[place, part(pair + v_at, 128)] = grad_value.astype(BF16)

        loop(2 * P_IN, one)

    def column_sums(source, first, count, row, at):
        def one(j):
            values = source[:, part(j + first, 256)].astype(F32)
            buf.sg[row:row + 1, part(j + at, 256)] = jnp.sum(values, 0, keepdims=True)

        loop(count, one)

    def norm(load, index, dst):
        def one(i):
            place = part(i, TILE)
            normed, _ = whiten(load(place))
            gain, shift = buf.vec[index:index + 1, :], buf.vec[index + 3:index + 4, :]
            rows(dst, q)[place, :] = (normed * gain + shift).astype(BF16)

        loop(L // TILE, one)

    def norm_back(load, ticket, index, base, dst, low):
        zero = jnp.zeros((1, D), F32)

        def one(i, carry):
            gain_sum, shift_sum, out_sum = carry
            place = part(i, TILE)
            normed, scale = whiten(load(place))
            grad = reduced(ticket, place)
            gained = grad * buf.vec[index:index + 1, :]
            back = gained - jnp.mean(gained, -1, keepdims=True)
            back = back - normed * jnp.mean(gained * normed, -1, keepdims=True)
            total = base(place) + scale * back
            if dst is not None:
                dst[place, :] = total
            rounded = total.astype(BF16)
            low(place, rounded)
            return (
                gain_sum + jnp.sum(grad * normed, 0, keepdims=True),
                shift_sum + jnp.sum(grad, 0, keepdims=True),
                out_sum + jnp.sum(rounded.astype(F32), 0, keepdims=True),
            )

        gain_sum, shift_sum, out_sum = lax.fori_loop(0, L // TILE, one, (zero, zero, zero))
        buf.sg[index:index + 1, :] = gain_sum
        buf.sg[index + 3:index + 4, :] = shift_sum
        return out_sum

    gate = pltpu.get_barrier_semaphore()
    partners = [device for _, device in in_plane] + [dev_adj, dev_opp, dev_diag]
    partners += [((s + j) % n_sec, d) for j in range(1, n_sec)]
    for device in partners:
        pl.semaphore_signal(gate, inc=1, device_id=device, device_id_type=MESH)
    pl.semaphore_wait(gate, len(partners))

    sv = spread_start(buf.sva, io.small)
    k_prev, k_cot, k_mem = slot(), slot(), slot(n_sec)
    send(io.prev, buf.hb, k_prev, ((s + 1) % n_sec, d))
    swap_start(wt.qkv)
    mem_slot = rows(buf.m, q)
    for j in range(1, n_sec):
        send(io.mem, mem_slot.at[:, part(s, mem_cols)], k_mem + j, ((s + j) % n_sec, d))
    mem_copy = local(io.mem, mem_slot.at[:, part(s, mem_cols)])
    send(io.cot, rows(buf.e3, q), k_cot, ((s + n_sec - 1) % n_sec, d))
    for weight in (wt.so, wt.co, wt.f2):
        weight.own_copy = local(weight.source, block(weight, z))
    swap_start(wt.ckv)
    swap_start(wt.cq)

    spread_relay(sv)
    swap_wait(wt.qkv)
    weight_send(wt.qkv, block(wt.qkv, z))
    weight_send(wt.so, wt.so.source)
    spread_ready(sv)

    for tile in range(D // 128):
        pair = buf.sva[2 * (tile % 2), tile // 2].astype(F32)
        pair = pair + buf.sva[2 * (tile % 2) + 1, tile // 2].astype(F32)
        buf.vec[:, tile * 128:(tile + 1) * 128] = pair
    half = lax.broadcasted_iota(jnp.int32, (16, 128), 1) < 64
    even = (jnp.zeros((16, 128), jnp.int32) + c) == 0
    buf.bias[...] = jnp.zeros((8, D), F32)
    for kind in range(2):
        for tile in range(2):
            first = buf.sva[x, tile + 2 * kind].astype(F32)
            second = buf.sva[2 + x, tile + 2 * kind].astype(F32)
            lower = jnp.where(even, first, pltpu.roll(first, 64, 1))
            upper = jnp.where(even, pltpu.roll(second, 64, 1), second)
            both_heads = jnp.where(half, lower, upper)
            for which in range(2):
                at = 512 * kind + 128 * tile
                buf.bias[which:which + 1, at:at + 128] = both_heads[9 + which:10 + which]
    for tile in range(Z):
        unit = buf.sva[q, tile].astype(F32)
        buf.bias[2:3, 256 * tile:256 * tile + 128] = unit[11:12]
        buf.bias[2:3, 256 * tile + 128:256 * tile + 256] = unit[12:13]
    buf.sg[...] = jnp.zeros((16, D), F32)

    arrived(buf.hb, k_prev)

    def hidden(place):
        return buf.hb[place, :].astype(F32)

    norm(hidden, 0, buf.a1)
    a1 = gather_start(buf.a1)
    swap_wait(wt.ckv)
    swap_wait(wt.cq)
    weight_send(wt.ckv, block(wt.ckv, z))
    weight_send(wt.cq, block(wt.cq, z))
    weight_send(wt.co, wt.co.source)
    for j in range(1, n_sec):
        origin = (s + n_sec - j) % n_sec
        arrived(mem_slot.at[:, part(origin, mem_cols)], k_mem + j)
    mem_copy.wait()
    gather_relay(a1)
    memory = gather_start(buf.m)
    swap_start(wt.f1)
    gather_ready(a1)
    weight_relay(wt.qkv)
    weight_ready(wt.qkv)
    matmul(buf.a1, wt.qkv.weight, buf.qkv, buf.bias, 0)
    weight_relay(wt.so)
    gather_finish(memory)
    attention(buf.qkv, 0, buf.qkv, 2, 4, True, 13, buf.p1, buf.o1)
    wt.so.own_copy.wait()
    weight_ready(wt.so)
    matmul(buf.o1, wt.so.weight, set_a.parts)
    step = reduce_start(set_a)
    swap_wait(wt.f1)
    weight_send(wt.f1, block(wt.f1, z))
    weight_relay(wt.ckv)
    reduce_relay(step)
    weight_ready(wt.ckv)
    matmul(buf.m, wt.ckv.weight, buf.kv, buf.bias, 1, 1)
    reduce_ready(step)

    def after_self(i):
        place = part(i, TILE)
        buf.h1[place, :] = hidden(place) + (reduced(step, place) + buf.vec[6:7, :])

    loop(L // TILE, after_self)
    norm(lambda place: buf.h1[place, :], 1, buf.a2)
    a2 = gather_start(buf.a2)
    reduce_done(step)

    weight_send(wt.f2, wt.f2.source)
    weight_relay(wt.cq)
    weight_relay(wt.co)
    arrived(rows(buf.e3, q), k_cot)
    gather_finish(a2)
    e3 = gather_start(buf.e3)
    weight_ready(wt.cq)
    matmul(buf.a2, wt.cq.weight, buf.q2, buf.bias, 1)
    attention(buf.q2, 0, buf.kv, 0, 2, False, 14, buf.p2, buf.o2)
    wt.co.own_copy.wait()
    weight_ready(wt.co)
    matmul(buf.o2, wt.co.weight, set_b.parts)
    step = reduce_start(set_b)
    gather_finish(e3)
    reduce_relay(step)
    reduce_ready(step)

    def after_cross(i):
        place = part(i, TILE)
        buf.h2[place, :] = buf.h1[place, :] + (reduced(step, place) + buf.vec[7:8, :])

    loop(L // TILE, after_cross)
    norm(lambda place: buf.h2[place, :], 2, buf.a3)
    a3 = gather_start(buf.a3)
    reduce_done(step)

    weight_relay(wt.f1)
    gather_finish(a3)
    weight_ready(wt.f1)

    def units(j):
        value = nn(buf.a3[...], wt.f1.weight[:, lanes(j)]) + buf.bias[2:3, lanes(j)]
        activ, slope = gelu_pair(value)
        buf.g[:, lanes(j)] = activ.astype(BF16)
        buf.gp[:, lanes(j)] = slope.astype(BF16)

    loop(FL // 256, units)
    weight_grad(buf.g, buf.e3, wt.f2)
    grad_send(wt.f2)
    weight_relay(wt.f2)
    wt.f2.own_copy.wait()
    weight_ready(wt.f2)

    def units_back(j):
        value = nt(buf.e3[...], wt.f2.weight[lanes(j), :])
        low = (value * buf.gp[:, lanes(j)].astype(F32)).astype(BF16)
        buf.gp[:, lanes(j)] = low
        buf.sg[10:11, lanes(j)] = jnp.sum(low.astype(F32), 0, keepdims=True)

    loop(FL // 256, units_back)
    matmul_back(buf.gp, wt.f1.weight, set_a.parts)
    step = reduce_start(set_a)
    weight_grad(buf.a3, buf.gp, wt.f1)
    grad_send(wt.f1)
    reduce_relay(step)
    matmul(buf.g, wt.f2.weight, set_c.parts)
    final = reduce_start(set_c)
    reduce_ready(step)
    zero = jnp.zeros((1, D), F32)

    def cot_sum(i, carry):
        return carry + jnp.sum(rows(buf.e3, q)[part(i, TILE), :].astype(F32), 0, keepdims=True)

    buf.sg[8:9, :] = lax.fori_loop(0, L // TILE, cot_sum, zero)

    def store(name):
        def low(place, value):
            rows(name, q)[place, :] = value

        return low

    buf.sg[7:8, :] = norm_back(
        lambda place: buf.h2[place, :], step, 2,
        lambda place: rows(buf.e3, q)[place, :].astype(F32), buf.dh, store(buf.e2),
    )
    e2 = gather_start(buf.e2)
    reduce_done(step)
    reduce_relay(final)
    grad_combine(wt.f2)
    gather_finish(e2)

    matmul_back(buf.e2, wt.co.weight, buf.do)
    attention_back(buf.q2, 0, buf.kv, 0, 2, buf.p2, buf.do)
    matmul_back(buf.q2, wt.cq.weight, set_b.parts)
    step = reduce_start(set_b)
    weight_grad(buf.o2, buf.e2, wt.co)
    grad_send(wt.co)
    weight_grad(buf.a2, buf.q2, wt.cq)
    grad_send(wt.cq)
    reduce_relay(step)
    weight_grad(buf.m, buf.kv, wt.ckv)
    grad_send(wt.ckv)
    matmul_back(buf.kv, wt.ckv.weight, set_a.parts)
    mem_step = reduce_start(set_a)
    reduce_ready(final)

    def finish(i):
        place = part(i, TILE)
        total = buf.h2[place, :] + (reduced(final, place) + buf.vec[8:9, :])
        buf.stage[place, :] = total.astype(BF16)

    loop(L // TILE, finish)
    result_copies.append(local(buf.stage, io.output))
    reduce_done(final)
    column_sums(buf.q2, 0, 1, 9, 2)
    column_sums(buf.kv, 1, 1, 9, 3)
    reduce_ready(step)
    buf.sg[6:7, :] = norm_back(
        lambda place: buf.h1[place, :], step, 1,
        lambda place: buf.dh[place, :], buf.dh, store(buf.e1),
    )
    e1 = gather_start(buf.e1)
    reduce_done(step)
    reduce_relay(mem_step)
    grad_combine(wt.f1)
    gather_finish(e1)

    matmul_back(buf.e1, wt.so.weight, buf.do)
    attention_back(buf.qkv, 0, buf.qkv, 2, 4, buf.p1, buf.do)
    matmul_back(buf.qkv, wt.qkv.weight, set_b.parts)
    step = reduce_start(set_b)
    weight_grad(buf.o1, buf.e1, wt.so)
    grad_send(wt.so)
    weight_grad(buf.a1, buf.qkv, wt.qkv)
    grad_send(wt.qkv)
    reduce_relay(step)
    column_sums(buf.qkv, 0, 1, 9, 0)
    column_sums(buf.qkv, 2, 1, 9, 1)

    reduce_ready(mem_step)

    def memory_row(i):
        place = part(i, TILE)
        buf.mb[place, :] = reduced(mem_step, place).astype(BF16)

    loop(L // TILE, memory_row)
    k_back = slot(n_sec)
    for j in range(1, n_sec):
        to = (s + j) % n_sec
        send(buf.mb.at[:, part(to, mem_cols)], buf.ml.at[j], k_back + j, (to, d))
    grad_combine(wt.co)
    grad_combine(wt.cq)
    reduce_ready(step)

    def store_stage(place, value):
        buf.ig[place, :] = value

    norm_back(
        hidden, step, 0, lambda place: buf.dh[place, :], None, store_stage,
    )
    k_in = slot()
    send(buf.ig, io.input_grad, k_in, ((s + n_sec - 1) % n_sec, d))
    buf.sga[q, z] = buf.sg[...].astype(BF16)
    sums = spread_start(buf.sga, None)
    grad_combine(wt.ckv)
    grad_final(wt.f2)
    grad_final(wt.f1)
    spread_relay(sums)
    for j in range(1, n_sec):
        arrived(buf.ml.at[j], k_back + j)

    def memory_total(i):
        place = part(i, TILE)
        total = buf.mb[place, part(s, mem_cols)].astype(F32)
        for j in range(1, n_sec):
            total = total + buf.ml[j, place, :].astype(F32)
        buf.mo[place, :] = total.astype(BF16)

    loop(L // TILE, memory_total)
    result_copies.append(local(buf.mo, io.memory_grad))
    grad_combine(wt.so)
    grad_combine(wt.qkv)
    for weight in (wt.co, wt.cq, wt.ckv, wt.so, wt.qkv):
        grad_final(weight)
    spread_ready(sums)
    result_copies.append(local(buf.sga, io.sums_out))
    for weight in (wt.qkv, wt.ckv, wt.cq, wt.f1):
        last_wait(weight)
    arrived(io.input_grad, k_in)
    for copy in result_copies:
        copy.wait()
    for record in list(started):
        sent(record)
    assert counter[0] <= SEMS


def buffer_shapes(n_sec, mem_cols):
    tokens, row = (T, D), (L, D)
    shapes = dict(
        sva=(P_IN, Z, 16, 128),
        sga=(P_IN, Z, 16, D),
        hb=row, ig=row, stage=row, mb=row,
        ml=(n_sec, L, mem_cols),
        mo=(L, mem_cols),
        qkv=(T, 768), q2=(T, 256), kv=(T, 512), o1=(T, 256), o2=(T, 256), do=(T, 256),
        p1=(2 * P_IN, 2 * L, L), p2=(2 * P_IN, 2 * L, L),
        g=(T, FL), gp=(T, FL),
        a1=tokens, a2=tokens, a3=tokens, m=tokens, e3=tokens, e2=tokens, e1=tokens,
    )
    exact = dict(vec=(16, D), bias=(8, D), sg=(16, D), h1=row, h2=row, dh=row)
    kinds = {name: pltpu.VMEM(shape, BF16) for name, shape in shapes.items()}
    kinds.update({name: pltpu.VMEM(shape, F32) for name, shape in exact.items()})
    return kinds


REDUCE_SHAPES = dict(
    parts=pltpu.VMEM((T, D), BF16),
    core=pltpu.VMEM((2 * L, D), BF16),
    across=pltpu.VMEM((L, D), BF16),
)


def scratch_of(n_sec, mem_cols):
    scratch = list(buffer_shapes(n_sec, mem_cols).values())
    scratch += 3 * list(REDUCE_SHAPES.values())
    for count, columns, _ in WEIGHTS.values():
        scratch += 2 * [pltpu.VMEM((Z * count, columns), BF16)]
        scratch += 4 * [pltpu.VMEM((count, columns), BF16)]
    return scratch + [
        pltpu.SemaphoreType.DMA((SEMS,)),
        pltpu.SemaphoreType.DMA((SEMS,)),
        pltpu.SemaphoreType.DMA((32,)),
    ]


def on_device_planes(
    prev_act, memory, out_cot, tgt_len, src_len, norm_gain, norm_bias, self_qkv, self_qv_bias,
    self_out, cross_q, cross_kv, cross_qv_bias, cross_out, out_bias, fc1, fc1_bias, fc2,
):
    n_sec = lax.axis_size("section")
    d = lax.axis_index("dp")
    mem_cols = memory.shape[2]
    pieces = jnp.concatenate([norm_gain[0], norm_bias[0], out_bias[0]], 0)
    odd = (d % 2).astype(BF16)
    spaced = jnp.concatenate([pieces * (1 - odd), pieces * odd], 1)
    ones = jnp.ones((1, 128), BF16)
    small = jnp.concatenate(
        [
            spaced,
            self_qv_bias,
            cross_qv_bias,
            fc1_bias.reshape(2, 128),
            ones * tgt_len.astype(BF16)[:, None],
            ones * src_len.astype(BF16)[:, None],
            ones,
        ],
        0,
    )

    def to_columns(weight, groups, unit):
        split = weight[0].reshape(-1, groups, Z, P_IN, unit)
        return split.transpose(3, 0, 1, 2, 4).reshape(P_IN, -1, groups * Z * unit)

    def from_columns(grad, groups, unit):
        split = grad.reshape(P_IN, -1, groups, Z, unit)
        return split.transpose(1, 2, 3, 0, 4).reshape(1, -1, groups * Z * P_IN * unit).astype(F32)

    operands = (
        prev_act[0, 0], memory[0], out_cot[0, 0], small,
        to_columns(self_qkv, 3, HD), self_out[0], to_columns(cross_kv, 2, HD),
        to_columns(cross_q, 1, HD), cross_out[0], to_columns(fc1, 1, FL // Z), fc2[0],
    )
    out_shapes = [(L, D), (L, D), (L, mem_cols)]
    for count, columns, by_column in WEIGHTS.values():
        out_shapes.append((P_IN, count // P_IN, columns) if by_column else (count, columns))
    out_shapes.append((P_IN, Z, 16, D))
    results = pl.pallas_call(
        functools.partial(whole_kernel, n_sec, mem_cols),
        out_shape=[jax.ShapeDtypeStruct(shape, BF16) for shape in out_shapes],
        in_specs=[pl.BlockSpec(memory_space=pl.ANY)] * len(operands),
        out_specs=[pl.BlockSpec(memory_space=pl.ANY)] * len(out_shapes),
        scratch_shapes=scratch_of(n_sec, mem_cols),
        compiler_params=pltpu.CompilerParams(
            collective_id=0, has_side_effects=True, vmem_limit_bytes=63 * 2**20
        ),
        cost_estimate=pl.CostEstimate(
            flops=21 * 10**9, bytes_accessed=20 * 2**20, transcendentals=3 * 10**6
        ),
    )(*operands)
    output, input_grad, memory_grad, g_qkv, g_so, g_ckv, g_cq, g_co, g_f1, g_f2, sums = results
    sums = sums.astype(F32)
    by_feature = jnp.sum(sums[:, :, :9], (0, 1))
    own = lax.dynamic_slice_in_dim(by_feature, d * 64, 64, 1)
    by_head = jnp.sum(sums[:, :, 9], 1).reshape(P_IN, 4, Z, 64).transpose(1, 2, 0, 3)
    by_head = by_head.reshape(2, 2048)
    by_unit = jnp.sum(sums[:, :, 10], 1).reshape(P_IN, Z, 256).transpose(1, 0, 2).reshape(1, 4096)
    own_head = lax.dynamic_slice_in_dim(by_head, d * 128, 128, 1)
    own_unit = lax.dynamic_slice_in_dim(by_unit, d * 256, 256, 1)
    return (
        output[None, None],
        input_grad[None, None],
        memory_grad[None],
        own[None, 0:3],
        own[None, 3:6],
        from_columns(g_qkv, 3, HD),
        own_head[0:1],
        g_so[None].astype(F32),
        from_columns(g_cq, 1, HD),
        from_columns(g_ckv, 2, HD),
        own_head[1:2],
        g_co[None].astype(F32),
        own[None, 6:9],
        from_columns(g_f1, 1, FL // Z),
        own_unit,
        g_f2[None].astype(F32),
    )


def solution(mesh):
    in_specs = (
        P("section", "dp", None, None),
        P("dp", None, "section"),
        P("section", "dp", None, None),
        P("dp"),
        P("dp"),
        P("section", None, "dp"),
        P("section", None, "dp"),
        P("section", "dp", None),
        P("section", "dp"),
        P("section", "dp", None),
        P("section", "dp", None),
        P("section", "dp", None),
        P("section", "dp"),
        P("section", "dp", None),
        P("section", None, "dp"),
        P("section", "dp", None),
        P("section", "dp"),
        P("section", "dp", None),
    )
    out_specs = (
        P("section", "dp", None, None),
        P("section", "dp", None, None),
        P("dp", None, "section"),
        P("section", None, "dp"),
        P("section", None, "dp"),
        P("section", "dp", None),
        P("section", "dp"),
        P("section", "dp", None),
        P("section", "dp", None),
        P("section", "dp", None),
        P("section", "dp"),
        P("section", "dp", None),
        P("section", None, "dp"),
        P("section", "dp", None),
        P("section", "dp"),
        P("section", "dp", None),
    )
    planes = Z * P_IN
    fits = mesh.shape["dp"] == planes
    return jax.shard_map(
        on_device_planes if fits else on_device, mesh=mesh, in_specs=in_specs, out_specs=out_specs, check_vma=False
    )
```

```python
import functools
from types import SimpleNamespace

import jax
import jax.numpy as jnp
from jax import lax
from jax.experimental import pallas as pl
from jax.experimental.pallas import tpu as pltpu
from jax.sharding import PartitionSpec as P

H = 16
HD = 64


EPSILON = 1e-05
MASKED = -1000000000.0


def passed_along(value, axis, by):
    length = lax.axis_size(axis)
    return lax.ppermute(value, axis, [(i, (i + by) % length) for i in range(length)])


def norm_fwd(rows, gain, shift_term):
    center = rows - jnp.mean(rows, -1, keepdims=True)
    scale = lax.rsqrt(jnp.mean(center * center, -1, keepdims=True) + EPSILON)
    return center * scale * gain + shift_term


def gelu_exact(values):
    return jax.nn.gelu(values, approximate=False)


def product(left, right):
    return jnp.dot(left, right, preferred_element_type=jnp.float32)


def product_right_t(left, right):
    return lax.dot_general(
        left, right, (((1,), (1,)), ((), ())), preferred_element_type=jnp.float32
    )


def product_left_t(left, right):
    return lax.dot_general(
        left, right, (((0,), (0,)), ((), ())), preferred_element_type=jnp.float32
    )


def split_heads(flat, batch_rows):
    return flat.reshape(batch_rows, -1, H, HD)


def softmax_probs(query, key_rows, allowed):
    scores = jnp.einsum(
        "rthd,rshd->rhts", query, key_rows, preferred_element_type=jnp.float32
    ) * HD ** (-0.5)
    scores = jnp.where(allowed[:, None], scores, MASKED)
    weights = jnp.exp(scores - jnp.max(scores, -1, keepdims=True))
    return weights / jnp.sum(weights, -1, keepdims=True)


def attend_fwd(query, key_rows, value_rows, allowed):
    probs = softmax_probs(query, key_rows, allowed)
    mixed = jnp.einsum(
        "rhts,rshd->rthd",
        probs.astype(jnp.bfloat16),
        value_rows,
        preferred_element_type=jnp.float32,
    )
    return mixed.reshape(mixed.shape[0] * mixed.shape[1], -1).astype(jnp.bfloat16)


def attend_back(query, key_rows, value_rows, allowed, grad_mixed):
    probs = softmax_probs(query, key_rows, allowed)
    grad_heads = grad_mixed.reshape(query.shape)
    grad_probs = jnp.einsum(
        "rthd,rshd->rhts", grad_heads, value_rows, preferred_element_type=jnp.float32
    )
    delta = jnp.sum(probs * grad_probs, -1, keepdims=True)
    grad_scores = (probs * (grad_probs - delta)).astype(jnp.bfloat16)
    scale = HD ** (-0.5)
    grad_query = (
        jnp.einsum("rhts,rshd->rthd", grad_scores, key_rows, preferred_element_type=jnp.float32)
        * scale
    )
    grad_keys = (
        jnp.einsum("rhts,rthd->rshd", grad_scores, query, preferred_element_type=jnp.float32)
        * scale
    )
    grad_values = jnp.einsum(
        "rhts,rthd->rshd",
        probs.astype(jnp.bfloat16),
        grad_heads,
        preferred_element_type=jnp.float32,
    )
    width = query.shape[2] * query.shape[3]
    return (
        grad_query.reshape(-1, width).astype(jnp.bfloat16),
        grad_keys.reshape(-1, width).astype(jnp.bfloat16),
        grad_values.reshape(-1, width).astype(jnp.bfloat16),
    )


def unpack(pieces):
    return tuple((piece[0] for piece in pieces))


def on_device(
    prev_act,
    memory,
    out_cot,
    tgt_len,
    src_len,
    norm_gain,
    norm_bias,
    self_qkv,
    self_qv_bias,
    self_out,
    cross_q,
    cross_kv,
    cross_qv_bias,
    cross_out,
    out_bias,
    fc1,
    fc1_bias,
    fc2,
):
    fetched = unpack(
        (
            lax.all_gather(norm_gain, "dp", axis=2, tiled=True),
            lax.all_gather(norm_bias, "dp", axis=2, tiled=True),
            lax.all_gather(self_qkv, "dp", axis=1, tiled=True),
            lax.all_gather(self_qv_bias, "dp", axis=1, tiled=True),
            lax.all_gather(self_out, "dp", axis=1, tiled=True),
            lax.all_gather(cross_q, "dp", axis=1, tiled=True),
            lax.all_gather(cross_kv, "dp", axis=1, tiled=True),
            lax.all_gather(cross_qv_bias, "dp", axis=1, tiled=True),
            lax.all_gather(cross_out, "dp", axis=1, tiled=True),
            lax.all_gather(out_bias, "dp", axis=2, tiled=True),
            lax.all_gather(fc1, "dp", axis=1, tiled=True),
            lax.all_gather(fc1_bias, "dp", axis=1, tiled=True),
            lax.all_gather(fc2, "dp", axis=1, tiled=True),
        )
    )
    gains, shifts, w_sqkv, b_sqv, w_sout, w_cq, w_ckv, b_cqv, w_cout, b_out, w_one, b_one, w_two = (
        fetched
    )
    gain_f = gains.astype(jnp.float32)
    shift_f = shifts.astype(jnp.float32)
    sqv_f = b_sqv.astype(jnp.float32)
    cqv_f = b_cqv.astype(jnp.float32)
    out_f = b_out.astype(jnp.float32)
    one_f = b_one.astype(jnp.float32)
    source = passed_along(prev_act, "section", 1)[0]
    batch_rows, length, width = source.shape
    encoded = lax.all_gather(memory, "section", axis=2, tiled=True)
    mem_flat = encoded.reshape(-1, width)
    places = jnp.arange(length)
    self_ok = (places[None, None, :] <= places[None, :, None]) & (
        places[None, None, :] < tgt_len[:, None, None]
    )
    cross_ok = jnp.arange(encoded.shape[1])[None, None, :] < src_len[:, None, None]
    resid = source.astype(jnp.float32).reshape(-1, width)
    normed_one, pull_one = jax.vjp(norm_fwd, resid, gain_f[0], shift_f[0])
    first_in = normed_one.astype(jnp.bfloat16)
    joint = product(first_in, w_sqkv)
    query_self = (joint[:, :width] + sqv_f[:width]).astype(jnp.bfloat16)
    keys_self = joint[:, width : 2 * width].astype(jnp.bfloat16)
    values_self = (joint[:, 2 * width :] + sqv_f[width:]).astype(jnp.bfloat16)
    self_mixed = attend_fwd(
        split_heads(query_self, batch_rows),
        split_heads(keys_self, batch_rows),
        split_heads(values_self, batch_rows),
        self_ok,
    )
    after_self = resid + (product(self_mixed, w_sout) + out_f[0])
    normed_two, pull_two = jax.vjp(norm_fwd, after_self, gain_f[1], shift_f[1])
    second_in = normed_two.astype(jnp.bfloat16)
    query_cross = (product(second_in, w_cq) + cqv_f[:width]).astype(jnp.bfloat16)
    memory_proj = product(mem_flat, w_ckv)
    keys_cross = memory_proj[:, :width].astype(jnp.bfloat16)
    values_cross = (memory_proj[:, width:] + cqv_f[width:]).astype(jnp.bfloat16)
    cross_mixed = attend_fwd(
        split_heads(query_cross, batch_rows),
        split_heads(keys_cross, batch_rows),
        split_heads(values_cross, batch_rows),
        cross_ok,
    )
    after_cross = after_self + (product(cross_mixed, w_cout) + out_f[1])
    normed_three, pull_three = jax.vjp(norm_fwd, after_cross, gain_f[2], shift_f[2])
    third_in = normed_three.astype(jnp.bfloat16)
    pre_act = product(third_in, w_one) + one_f
    activ, pull_gelu = jax.vjp(gelu_exact, pre_act)
    act_low = activ.astype(jnp.bfloat16)
    result = after_cross + (product(act_low, w_two) + out_f[2])
    output = result.astype(jnp.bfloat16).reshape(1, batch_rows, length, width)
    (
        unused_gains,
        unused_shifts,
        w_sqkv,
        unused_sqv,
        w_sout,
        w_cq,
        w_ckv,
        unused_cqv,
        w_cout,
        unused_out,
        w_one,
        unused_one,
        w_two,
    ) = fetched
    grad_out = passed_along(out_cot, "section", -1)[0].astype(jnp.float32).reshape(-1, width)
    ffn_grad = grad_out.astype(jnp.bfloat16)
    grad_fc2 = product_left_t(act_low, ffn_grad)
    grad_b2 = jnp.sum(ffn_grad, 0, dtype=jnp.float32)
    grad_act = product_right_t(ffn_grad, w_two)
    (grad_pre,) = pull_gelu(grad_act)
    pre_low = grad_pre.astype(jnp.bfloat16)
    grad_fc1 = product_left_t(third_in, pre_low)
    grad_b1 = jnp.sum(pre_low, 0, dtype=jnp.float32)
    grad_mid, grad_gain3, grad_shift3 = pull_three(product_right_t(pre_low, w_one))
    grad_mid = grad_mid + grad_out
    cross_grad = grad_mid.astype(jnp.bfloat16)
    grad_cout = product_left_t(cross_mixed, cross_grad)
    grad_bco = jnp.sum(cross_grad, 0, dtype=jnp.float32)
    grad_cmix = product_right_t(cross_grad, w_cout).astype(jnp.bfloat16)
    grad_qc, grad_kc, grad_vc = attend_back(
        split_heads(query_cross, batch_rows),
        split_heads(keys_cross, batch_rows),
        split_heads(values_cross, batch_rows),
        cross_ok,
        grad_cmix,
    )
    grad_cq = product_left_t(second_in, grad_qc)
    grad_kv = jnp.concatenate([grad_kc, grad_vc], -1)
    grad_ckv = product_left_t(mem_flat, grad_kv)
    grad_cqv = jnp.concatenate(
        [jnp.sum(grad_qc, 0, dtype=jnp.float32), jnp.sum(grad_vc, 0, dtype=jnp.float32)]
    )
    grad_memory = product_right_t(grad_kv, w_ckv).reshape(encoded.shape)
    memory_grad = lax.psum_scatter(
        grad_memory.astype(jnp.bfloat16), "section", scatter_dimension=2, tiled=True
    )
    grad_after, grad_gain2, grad_shift2 = pull_two(product_right_t(grad_qc, w_cq))
    grad_after = grad_after + grad_mid
    self_grad = grad_after.astype(jnp.bfloat16)
    grad_sout = product_left_t(self_mixed, self_grad)
    grad_bso = jnp.sum(self_grad, 0, dtype=jnp.float32)
    grad_smix = product_right_t(self_grad, w_sout).astype(jnp.bfloat16)
    grad_qs, grad_ks, grad_vs = attend_back(
        split_heads(query_self, batch_rows),
        split_heads(keys_self, batch_rows),
        split_heads(values_self, batch_rows),
        self_ok,
        grad_smix,
    )
    grad_qkv = jnp.concatenate([grad_qs, grad_ks, grad_vs], -1)
    grad_sqkv = product_left_t(first_in, grad_qkv)
    grad_sqv = jnp.concatenate(
        [jnp.sum(grad_qs, 0, dtype=jnp.float32), jnp.sum(grad_vs, 0, dtype=jnp.float32)]
    )
    grad_in, grad_gain1, grad_shift1 = pull_one(product_right_t(grad_qkv, w_sqkv))
    grad_in = grad_in + grad_after
    input_grad = passed_along(
        grad_in.astype(jnp.bfloat16).reshape(1, batch_rows, length, width), "section", -1
    )
    grad_gain = jnp.stack([grad_gain1, grad_gain2, grad_gain3])
    grad_shift = jnp.stack([grad_shift1, grad_shift2, grad_shift3])
    grad_obias = jnp.stack([grad_bso, grad_bco, grad_b2])
    sums = (
        lax.psum_scatter(
            grad_gain.astype(jnp.bfloat16), "dp", scatter_dimension=1, tiled=True
        ).astype(jnp.float32),
        lax.psum_scatter(
            grad_shift.astype(jnp.bfloat16), "dp", scatter_dimension=1, tiled=True
        ).astype(jnp.float32),
        lax.psum_scatter(
            grad_sqkv.astype(jnp.bfloat16), "dp", scatter_dimension=0, tiled=True
        ).astype(jnp.float32),
        lax.psum_scatter(
            grad_sqv.astype(jnp.bfloat16), "dp", scatter_dimension=0, tiled=True
        ).astype(jnp.float32),
        lax.psum_scatter(
            grad_sout.astype(jnp.bfloat16), "dp", scatter_dimension=0, tiled=True
        ).astype(jnp.float32),
        lax.psum_scatter(
            grad_cq.astype(jnp.bfloat16), "dp", scatter_dimension=0, tiled=True
        ).astype(jnp.float32),
        lax.psum_scatter(
            grad_ckv.astype(jnp.bfloat16), "dp", scatter_dimension=0, tiled=True
        ).astype(jnp.float32),
        lax.psum_scatter(
            grad_cqv.astype(jnp.bfloat16), "dp", scatter_dimension=0, tiled=True
        ).astype(jnp.float32),
        lax.psum_scatter(
            grad_cout.astype(jnp.bfloat16), "dp", scatter_dimension=0, tiled=True
        ).astype(jnp.float32),
        lax.psum_scatter(
            grad_obias.astype(jnp.bfloat16), "dp", scatter_dimension=1, tiled=True
        ).astype(jnp.float32),
        lax.psum_scatter(
            grad_fc1.astype(jnp.bfloat16), "dp", scatter_dimension=0, tiled=True
        ).astype(jnp.float32),
        lax.psum_scatter(
            grad_b1.astype(jnp.bfloat16), "dp", scatter_dimension=0, tiled=True
        ).astype(jnp.float32),
        lax.psum_scatter(
            grad_fc2.astype(jnp.bfloat16), "dp", scatter_dimension=0, tiled=True
        ).astype(jnp.float32),
    )
    return (
        output,
        input_grad,
        memory_grad,
        sums[0][None],
        sums[1][None],
        sums[2][None],
        sums[3][None],
        sums[4][None],
        sums[5][None],
        sums[6][None],
        sums[7][None],
        sums[8][None],
        sums[9][None],
        sums[10][None],
        sums[11][None],
        sums[12][None],
    )


Z = 4
P_IN = 4
L = 192
D = 1024
T = P_IN * L
FL = 1024
TILE = 32
MESH = pl.DeviceIdType.MESH
F32 = jnp.float32
BF16 = jnp.bfloat16

WEIGHTS = dict(
    qkv=(256, 768, True),
    so=(64, 1024, False),
    ckv=(256, 512, True),
    cq=(256, 256, True),
    co=(64, 1024, False),
    f1=(256, 1024, True),
    f2=(256, 1024, False),
)
SEMS = 240


def run_if(cond, fn):
    if cond is None:
        fn()
    else:
        pl.when(cond)(fn)


def part(index, size, step=None):
    return pl.ds(pl.multiple_of(index * size, size), size if step is None else step)


def nn(left, right):
    return jnp.dot(left, right, preferred_element_type=F32)


def nt(left, right):
    return lax.dot_general(left, right, (((1,), (1,)), ((), ())), preferred_element_type=F32)


def tn(left, right):
    return lax.dot_general(left, right, (((0,), (0,)), ((), ())), preferred_element_type=F32)


def loop(count, body):
    def step(index, carry):
        body(index)
        return carry

    lax.fori_loop(0, count, step, 0)


def gelu_pair(values):
    bell = jnp.exp(-0.5 * values * values)
    step = 1.0 / (1.0 + 0.3275911 * 0.7071067811865476 * jnp.abs(values))
    series = step * (
        0.254829592
        + step
        * (-0.284496736 + step * (1.421413741 + step * (-1.453152027 + step * 1.061405429)))
    )
    above = 0.5 * series * bell
    below = jnp.where(values < 0, above, 1.0 - above)
    return values * below, below + values * bell * 0.3989422804014327


def whiten(rows):
    center = rows - jnp.mean(rows, -1, keepdims=True)
    scale = lax.rsqrt(jnp.mean(center * center, -1, keepdims=True) + EPSILON)
    return center * scale, scale


def whole_kernel(n_sec, mem_cols, *refs):
    given = iter(refs)

    def take(names):
        return SimpleNamespace(**{name: next(given) for name in names})

    def take_weights(**fields):
        for name in WEIGHTS:
            for field in fields:
                setattr(getattr(wt, name), field, next(given))

    wt = SimpleNamespace(**{name: SimpleNamespace() for name in WEIGHTS})
    io = take(
        dict(
            prev=0, mem=0, cot=0, tgt=0, src=0, gain=0, shift=0, out_bias=0,
            self_bias=0, cross_bias=0, unit_bias=0,
        )
    )
    take_weights(source=0)
    vars(io).update(vars(take(dict(output=0, input_grad=0, memory_grad=0))))
    take_weights(result=0)
    vars(io).update(vars(take(dict(sums_out=0))))
    buf = take(buffer_shapes(n_sec, mem_cols))
    set_a, set_b, set_c = (take(REDUCE_SHAPES) for _ in range(3))
    take_weights(weight=0, grad=0, to_diag=0, to_opp=0, near=0, far=0)
    for weight in (wt.qkv, wt.ckv, wt.cq):
        weight.raw, weight.sorted = next(given), next(given)
    send_sems, recv_sems, local_sems = given

    s = lax.axis_index("section")
    d = lax.axis_index("dp")
    z, q = d // P_IN, d % P_IN
    x, c = q // 2, q % 2
    end = (z % 3) == 0
    mid = (z % 3) != 0
    q_core = q + 1 - 2 * c
    q_x = q + 2 - 4 * x
    q_xc = q_x + 1 - 2 * c
    z_adj = z + 1 - 2 * (z % 2)
    z_opp = 3 - z
    z_diag = (z + 2) % 4
    dev_core, dev_x, dev_xc = (s, z * P_IN + q_core), (s, z * P_IN + q_x), (s, z * P_IN + q_xc)
    dev_adj, dev_opp, dev_diag = (s, z_adj * P_IN + q), (s, z_opp * P_IN + q), (s, z_diag * P_IN + q)
    in_plane = ((q_core, dev_core), (q_x, dev_x), (q_xc, dev_xc))

    counter = [0]
    started = []
    local_counter = [0]

    def slot(count=1):
        counter[0] += count
        return counter[0] - count

    def remote(src, dst, k, device):
        return pltpu.make_async_remote_copy(
            src_ref=src, dst_ref=dst, send_sem=send_sems.at[k], recv_sem=recv_sems.at[k],
            device_id=device, device_id_type=MESH,
        )

    def send(src, dst, k, device, cond=None):
        copy = remote(src, dst, k, device)
        run_if(cond, copy.start)
        record = [copy, cond]
        started.append(record)
        return record

    def sent(record):
        run_if(record[1], record[0].wait_send)
        started[:] = [other for other in started if other is not record]

    def arrived(dst, k, cond=None):
        run_if(cond, remote(dst, dst, k, dev_core).wait_recv)

    def local(src, dst):
        copy = pltpu.make_async_copy(src, dst, local_sems.at[local_counter[0]])
        local_counter[0] += 1
        copy.start()
        return copy

    def rows(rows_of, index):
        return rows_of.at[part(index, L)]

    for name, (count, _, by_column) in WEIGHTS.items():
        weight = getattr(wt, name)
        weight.count, weight.by_column = count, by_column
        weight.to_use, weight.swap, weight.to_sum, weight.last = slot(5), slot(3), slot(5), slot(3)

    def block(name, index):
        return name.weight.at[part(index, name.count)]

    def weight_send(name, src):
        k = name.to_use
        send(src, block(name, z), k, dev_adj)
        send(src, block(name, z), k + 1, dev_opp, mid)
        send(src, block(name, z), k + 2, dev_diag, end)

    def weight_relay(name):
        k = name.to_use
        arrived(block(name, z_opp), k + 1, mid)
        send(block(name, z_opp), block(name, z_opp), k + 3, dev_adj, mid)
        arrived(block(name, z_diag), k + 2, mid)
        send(block(name, z_diag), block(name, z_diag), k + 4, dev_adj, mid)

    def weight_ready(name):
        k = name.to_use
        arrived(block(name, z_adj), k)
        arrived(block(name, z_diag), k + 3, end)
        arrived(block(name, z_opp), k + 4, end)


    def swap_start(name):
        size = name.count // P_IN
        place = name.weight.at[part(z * P_IN + q, size)]
        name.swapped = [
            send(name.sorted.at[q_to], place, name.swap + j, device)
            for j, (q_to, device) in enumerate(in_plane)
        ]
        name.own_copy = [local(name.sorted.at[q], place)]

    def swap_wait(name):
        size = name.count // P_IN
        for j, (q_from, _) in enumerate(in_plane):
            arrived(name.weight.at[part(z * P_IN + q_from, size)], name.swap + j)
        for copy in name.own_copy:
            copy.wait()
        for record in name.swapped:
            sent(record)

    def halves(first, second, odd):
        if odd:
            first = pltpu.roll(first, 64, 1)
        else:
            second = pltpu.roll(second, 64, 1)
        lane = lax.broadcasted_iota(jnp.int32, first.shape, 1)
        return jnp.where(lane < 64, first, second)

    def tile_of(index):
        return slice(index * 128, index * 128 + 128)

    def sort_columns(name):
        for q_to in range(P_IN):
            for tile in range(name.sorted.shape[2] // 128):
                at = 4 * tile + q_to // 2
                first = name.raw[:, tile_of(at)].astype(F32)
                second = name.raw[:, tile_of(at + 2)].astype(F32)
                name.sorted[q_to, :, tile_of(tile)] = halves(first, second, q_to % 2).astype(BF16)

    def unsort_columns(name):
        for tile in range(name.raw.shape[1] // 128):
            group, u = tile // 8, tile % 8
            at = 2 * group + u // 4
            first = name.sorted[2 * (u % 2), :, tile_of(at)].astype(F32)
            second = name.sorted[2 * (u % 2) + 1, :, tile_of(at)].astype(F32)
            name.raw[:, tile_of(tile)] = halves(first, second, (u // 2) % 2).astype(BF16)

    unit_swap, unit_last = slot(3 * Z), slot(3 * Z)

    def unit_columns(rows_of, tile, q_at):
        return rows_of.at[:, part(tile * P_IN + q_at, 256)]

    def unit_swap_start():
        size = wt.f1.count // P_IN
        place = wt.f1.weight.at[part(z * P_IN + q, size)]
        wt.f1.own_copy = []
        for tile in range(Z):
            at = place.at[:, part(tile, 256)]
            for j, (q_to, device) in enumerate(in_plane):
                send(unit_columns(wt.f1.source, tile, q_to), at, unit_swap + 3 * tile + j, device)
            wt.f1.own_copy.append(local(unit_columns(wt.f1.source, tile, q), at))

    def unit_swap_wait():
        size = wt.f1.count // P_IN
        for tile in range(Z):
            for j, (q_from, _) in enumerate(in_plane):
                place = wt.f1.weight.at[part(z * P_IN + q_from, size)]
                arrived(place.at[:, part(tile, 256)], unit_swap + 3 * tile + j)
        for copy in wt.f1.own_copy:
            copy.wait()

    def grad_block(name, index):
        return name.grad.at[part(index, name.count)]

    def grad_send(name):
        k = name.to_sum
        send(grad_block(name, z_opp), name.to_diag, k, dev_adj, end)
        send(grad_block(name, z_diag), name.to_opp, k + 1, dev_adj, end)
        send(grad_block(name, z_adj), name.near, k + 2, dev_adj)

    def add_rows(count, body):
        size = min(count, 64)
        loop(count // size, lambda i: body(part(i, size)))

    def grad_combine(name):
        k = name.to_sum
        count = name.count

        def add(landed, index):
            def one(place):
                own = grad_block(name, index)[place, :].astype(F32)
                landed[place, :] = (own + landed[place, :].astype(F32)).astype(BF16)

            add_rows(count, one)

        def work():
            arrived(name.to_diag, k)
            add(name.to_diag, z_diag)

        run_if(mid, work)
        send(name.to_diag, name.far, k + 3, dev_diag, mid)

        def more():
            arrived(name.to_opp, k + 1)
            add(name.to_opp, z_opp)

        run_if(mid, more)
        send(name.to_opp, name.far, k + 4, dev_opp, mid)

    result_copies = []

    def grad_final(name):
        k = name.to_sum
        count = name.count
        arrived(name.near, k + 2)
        arrived(name.far, k + 3, end)
        arrived(name.far, k + 4, mid)

        def one(place):
            total = grad_block(name, z)[place, :].astype(F32)
            total = total + name.near[place, :].astype(F32)
            total = total + name.far[place, :].astype(F32)
            name.near[place, :] = total.astype(BF16)

        add_rows(count, one)
        size = count // P_IN
        if name is wt.f1:
            for tile in range(Z):
                for j, (q_to, device) in enumerate(in_plane):
                    src = name.near.at[part(q_to, size), part(tile, 256)]
                    dst = unit_columns(name.result, tile, q)
                    send(src, dst, unit_last + 3 * tile + j, device)
                src = name.near.at[part(q, size), part(tile, 256)]
                result_copies.append(local(src, unit_columns(name.result, tile, q)))
        elif name.by_column:
            for j, (q_to, device) in enumerate(in_plane):
                src = name.near.at[part(q_to, size)]
                send(src, name.sorted.at[q], name.last + j, device)
            src = name.near.at[part(q, size)]
            name.own_copy = [local(src, name.sorted.at[q])]
        else:
            result_copies.append(local(name.near, name.result))

    def last_wait(name):
        for j, (q_from, _) in enumerate(in_plane):
            arrived(name.sorted.at[q_from], name.last + j)
        for copy in name.own_copy:
            copy.wait()
        unsort_columns(name)
        result_copies.append(local(name.raw, name.result))

    def unit_last_wait():
        for tile in range(Z):
            for j, (q_from, _) in enumerate(in_plane):
                place = unit_columns(wt.f1.result, tile, q_from)
                arrived(place, unit_last + 3 * tile + j)

    def gather_start(name):
        k = slot(3)
        send(rows(name, q), rows(name, q), k, dev_x)
        send(rows(name, q), rows(name, q), k + 1, dev_core)
        return name, k

    def gather_relay(ticket):
        name, k = ticket
        arrived(rows(name, q_x), k)
        send(rows(name, q_x), rows(name, q_x), k + 2, dev_core)

    def gather_ready(ticket):
        name, k = ticket
        arrived(rows(name, q_core), k + 1)
        arrived(rows(name, q_xc), k + 2)

    def gather_finish(ticket):
        gather_relay(ticket)
        gather_ready(ticket)

    def reduce_start(which):
        k = slot(3)
        out = which.parts
        first = send(rows(out, q_xc), rows(which.core, 1), k, dev_core)
        second = send(rows(out, q_core), rows(which.core, 0), k + 1, dev_core)
        return which, k, [first, second]

    def reduce_relay(ticket):
        which, k, records = ticket
        out = which.parts
        arrived(rows(which.core, 1), k)

        def one(i):
            mine = rows(out, q_x)
            place = part(i, TILE)
            total = mine[place, :].astype(F32) + rows(which.core, 1)[place, :].astype(F32)
            mine[place, :] = total.astype(BF16)

        loop(L // TILE, one)
        records.append(send(rows(out, q_x), which.across, k + 2, dev_x))

    def reduce_ready(ticket):
        which, k, records = ticket
        arrived(rows(which.core, 0), k + 1)
        arrived(which.across, k + 2)

    def reduced(ticket, place):
        which = ticket[0]
        total = rows(which.parts, q)[place, :].astype(F32)
        total = total + rows(which.core, 0)[place, :].astype(F32)
        return total + which.across[place, :].astype(F32)

    def reduce_done(ticket):
        for record in ticket[2]:
            sent(record)

    def spread_start(name, src):
        k = slot(8)
        place = name.at[q, z]
        copy = None
        if src is not None:
            copy = local(src, place)
        else:
            src = place
        send(src, place, k, dev_adj)
        send(src, place, k + 1, dev_opp, mid)
        send(src, place, k + 2, dev_diag, end)
        return name, k, copy

    def spread_relay(ticket):
        name, k, copy = ticket
        arrived(name.at[q, z_opp], k + 1, mid)
        send(name.at[q, z_opp], name.at[q, z_opp], k + 3, dev_adj, mid)
        arrived(name.at[q, z_diag], k + 2, mid)
        send(name.at[q, z_diag], name.at[q, z_diag], k + 4, dev_adj, mid)
        arrived(name.at[q, z_adj], k)
        arrived(name.at[q, z_diag], k + 3, end)
        arrived(name.at[q, z_opp], k + 4, end)
        if copy is not None:
            copy.wait()
        for j, (_, device) in enumerate(in_plane):
            send(name.at[q], name.at[q], k + 5 + j, device)

    def spread_ready(ticket):
        name, k, _ = ticket
        for j, (q_from, _) in enumerate(in_plane):
            arrived(name.at[q_from], k + 5 + j)

    def lanes(j, size=256):
        return part(j, size)

    def matmul(left, right, dst, bias=None, bias_row=0, bias_at=0):
        count = right.shape[1] // 256

        def one(j):
            tile = nn(left[...], right[:, lanes(j)])
            if bias is not None:
                tile = tile + bias[bias_row:bias_row + 1, part(j + bias_at, 256)]
            dst[:, lanes(j)] = tile.astype(BF16)

        loop(count, one)

    def matmul_back(left, right, dst):
        def one(j):
            dst[:, lanes(j)] = nt(left[...], right[lanes(j), :]).astype(BF16)

        loop(right.shape[0] // 256, one)

    def weight_grad(left, right, name):
        def one(j):
            name.grad[lanes(j), :] = tn(left[:, lanes(j)], right[...]).astype(BF16)

        loop(left.shape[1] // 256, one)

    low_half = lax.broadcasted_iota(jnp.int32, (L, 128), 1) < 64
    keep_low = low_half.astype(F32).astype(BF16)
    keep_high = (1.0 - low_half.astype(F32)).astype(BF16)

    def both(pair):
        return jnp.concatenate([pair * keep_low, pair * keep_high], axis=0)

    def merge(stacked):
        return jnp.where(low_half, stacked[:L], stacked[L:])

    def attention(qref, q_at, kref, k_at, v_at, causal, length_row, probs, dst):
        def one(i):
            r, pair = i // 2, i % 2
            place = part(r, L)
            query = both(qref[place, part(pair + q_at, 128)])
            scores = nt(query, kref[place, part(pair + k_at, 128)]) * HD ** (-0.5)
            key = lax.broadcasted_iota(jnp.int32, scores.shape, 1)
            limit = buf.sva[r, z][length_row:length_row + 1, 0:1].astype(F32)
            allowed = key.astype(F32) < limit
            if causal:
                at = lax.broadcasted_iota(jnp.int32, scores.shape, 0)
                at = jnp.where(at < L, at, at - L)
                allowed = allowed & (key <= at)
            scores = jnp.where(allowed, scores, MASKED)
            raised = jnp.exp(scores - jnp.max(scores, -1, keepdims=True))
            weights = (raised * (1.0 / jnp.sum(raised, -1, keepdims=True))).astype(BF16)
            probs[i] = weights
            mixed = nn(weights, kref[place, part(pair + v_at, 128)])
            dst[place, part(pair, 128)] = merge(mixed).astype(BF16)

        loop(2 * P_IN, one)

    def attention_back(qref, q_at, kref, k_at, v_at, probs, grad):
        def one(i):
            r, pair = i // 2, i % 2
            place = part(r, L)
            query = both(qref[place, part(pair + q_at, 128)])
            key = kref[place, part(pair + k_at, 128)]
            value = kref[place, part(pair + v_at, 128)]
            mixed_grad = both(grad[place, part(pair, 128)])
            weights = probs[i]
            soft = weights.astype(F32)
            grad_probs = nt(mixed_grad, value)
            delta = jnp.sum(soft * grad_probs, -1, keepdims=True)
            grad_scores = (soft * (grad_probs - delta)).astype(BF16)
            scale = HD ** (-0.5)
            grad_query = merge(nn(grad_scores, key)) * scale
            grad_key = tn(grad_scores, query) * scale
            grad_value = tn(weights, mixed_grad)
            qref[place, part(pair + q_at, 128)] = grad_query.astype(BF16)
            kref[place, part(pair + k_at, 128)] = grad_key.astype(BF16)
            kref[place, part(pair + v_at, 128)] = grad_value.astype(BF16)

        loop(2 * P_IN, one)

    def column_sums(source, first, count, row, at):
        def one(j):
            values = source[:, part(j + first, 256)].astype(F32)
            buf.sg[row:row + 1, part(j + at, 256)] = jnp.sum(values, 0, keepdims=True)

        loop(count, one)

    def norm(load, index, dst):
        def one(i):
            place = part(i, TILE)
            normed, _ = whiten(load(place))
            gain, shift = buf.vec[index:index + 1, :], buf.vec[index + 3:index + 4, :]
            rows(dst, q)[place, :] = (normed * gain + shift).astype(BF16)

        loop(L // TILE, one)

    def norm_back(load, ticket, index, base, dst, low):
        zero = jnp.zeros((1, D), F32)

        def one(i, carry):
            gain_sum, shift_sum, out_sum = carry
            place = part(i, TILE)
            normed, scale = whiten(load(place))
            grad = reduced(ticket, place)
            gained = grad * buf.vec[index:index + 1, :]
            back = gained - jnp.mean(gained, -1, keepdims=True)
            back = back - normed * jnp.mean(gained * normed, -1, keepdims=True)
            total = base(place) + scale * back
            if dst is not None:
                dst[place, :] = total
            rounded = total.astype(BF16)
            low(place, rounded)
            return (
                gain_sum + jnp.sum(grad * normed, 0, keepdims=True),
                shift_sum + jnp.sum(grad, 0, keepdims=True),
                out_sum + jnp.sum(rounded.astype(F32), 0, keepdims=True),
            )

        gain_sum, shift_sum, out_sum = lax.fori_loop(0, L // TILE, one, (zero, zero, zero))
        buf.sg[index:index + 1, :] = gain_sum
        buf.sg[index + 3:index + 4, :] = shift_sum
        return out_sum

    raw_copies = [local(weight.source, weight.raw) for weight in (wt.qkv, wt.ckv, wt.cq)]
    low_lanes = lax.broadcasted_iota(jnp.int32, (3, 128), 1) < 64
    even_lanes = (jnp.zeros((3, 128), jnp.int32) + c) == 0
    for row, pieces in ((0, io.gain), (3, io.shift), (6, io.out_bias)):
        value = pieces[...].astype(F32)
        twice = jnp.concatenate([value, value], 1)
        buf.sg[row:row + 3, 0:128] = jnp.where(low_lanes == even_lanes, twice, 0.0)
    buf.sg[9:10, 0:128] = io.self_bias[...].astype(F32)
    buf.sg[10:11, 0:128] = io.cross_bias[...].astype(F32)
    buf.sg[11:12, 0:128] = io.unit_bias[:, 0:128].astype(F32)
    buf.sg[12:13, 0:128] = io.unit_bias[:, 128:256].astype(F32)
    buf.sg[13:14, 0:128] = jnp.zeros((1, 128), F32) + io.tgt[0].astype(F32)
    buf.sg[14:15, 0:128] = jnp.zeros((1, 128), F32) + io.src[0].astype(F32)
    buf.sg[15:16, 0:128] = jnp.zeros((1, 128), F32)
    buf.sva[q, z] = buf.sg[:, 0:128].astype(BF16)

    gate = pltpu.get_barrier_semaphore()
    partners = [device for _, device in in_plane] + [dev_adj, dev_opp, dev_diag]
    partners += [((s + j) % n_sec, d) for j in range(1, n_sec)]
    for device in partners:
        pl.semaphore_signal(gate, inc=1, device_id=device, device_id_type=MESH)
    raw_copies[0].wait()
    sort_columns(wt.qkv)
    pl.semaphore_wait(gate, len(partners))

    sv = spread_start(buf.sva, None)
    swap_start(wt.qkv)
    k_prev, k_cot, k_mem = slot(), slot(), slot(n_sec)
    send(io.prev, buf.hb, k_prev, ((s + 1) % n_sec, d))
    mem_slot = rows(buf.m, q)
    for j in range(1, n_sec):
        send(io.mem, mem_slot.at[:, part(s, mem_cols)], k_mem + j, ((s + j) % n_sec, d))
    mem_copy = local(io.mem, mem_slot.at[:, part(s, mem_cols)])
    send(io.cot, rows(buf.e3, q), k_cot, ((s + n_sec - 1) % n_sec, d))
    for weight in (wt.so, wt.co, wt.f2):
        weight.own_copy = [local(weight.source, block(weight, z))]
    for weight, copy in ((wt.ckv, raw_copies[1]), (wt.cq, raw_copies[2])):
        copy.wait()
        sort_columns(weight)
        swap_start(weight)

    spread_relay(sv)
    swap_wait(wt.qkv)
    weight_send(wt.qkv, block(wt.qkv, z))
    weight_send(wt.so, wt.so.source)
    spread_ready(sv)

    for tile in range(D // 128):
        pair = buf.sva[2 * (tile % 2), tile // 2].astype(F32)
        pair = pair + buf.sva[2 * (tile % 2) + 1, tile // 2].astype(F32)
        buf.vec[:, tile * 128:(tile + 1) * 128] = pair
    half = lax.broadcasted_iota(jnp.int32, (16, 128), 1) < 64
    even = (jnp.zeros((16, 128), jnp.int32) + c) == 0
    buf.bias[...] = jnp.zeros((8, D), F32)
    for kind in range(2):
        for tile in range(2):
            first = buf.sva[x, tile + 2 * kind].astype(F32)
            second = buf.sva[2 + x, tile + 2 * kind].astype(F32)
            lower = jnp.where(even, first, pltpu.roll(first, 64, 1))
            upper = jnp.where(even, pltpu.roll(second, 64, 1), second)
            both_heads = jnp.where(half, lower, upper)
            for which in range(2):
                at = 512 * kind + 128 * tile
                buf.bias[which:which + 1, at:at + 128] = both_heads[9 + which:10 + which]
    for tile in range(Z):
        unit = buf.sva[q, tile].astype(F32)
        buf.bias[2:3, 256 * tile:256 * tile + 128] = unit[11:12]
        buf.bias[2:3, 256 * tile + 128:256 * tile + 256] = unit[12:13]
    buf.sg[...] = jnp.zeros((16, D), F32)

    arrived(buf.hb, k_prev)

    def hidden(place):
        return buf.hb[place, :].astype(F32)

    norm(hidden, 0, buf.a1)
    a1 = gather_start(buf.a1)
    swap_wait(wt.ckv)
    swap_wait(wt.cq)
    weight_send(wt.ckv, block(wt.ckv, z))
    weight_send(wt.cq, block(wt.cq, z))
    weight_send(wt.co, wt.co.source)
    for j in range(1, n_sec):
        origin = (s + n_sec - j) % n_sec
        arrived(mem_slot.at[:, part(origin, mem_cols)], k_mem + j)
    mem_copy.wait()
    gather_relay(a1)
    memory = gather_start(buf.m)
    unit_swap_start()
    gather_ready(a1)
    weight_relay(wt.qkv)
    weight_ready(wt.qkv)
    matmul(buf.a1, wt.qkv.weight, buf.qkv, buf.bias, 0)
    weight_relay(wt.so)
    gather_finish(memory)
    attention(buf.qkv, 0, buf.qkv, 2, 4, True, 13, buf.p1, buf.o1)
    wt.so.own_copy[0].wait()
    weight_ready(wt.so)
    matmul(buf.o1, wt.so.weight, set_a.parts)
    step = reduce_start(set_a)
    unit_swap_wait()
    weight_send(wt.f1, block(wt.f1, z))
    weight_relay(wt.ckv)
    reduce_relay(step)
    weight_ready(wt.ckv)
    matmul(buf.m, wt.ckv.weight, buf.kv, buf.bias, 1, 1)
    reduce_ready(step)

    def after_self(i):
        place = part(i, TILE)
        buf.h1[place, :] = hidden(place) + (reduced(step, place) + buf.vec[6:7, :])

    loop(L // TILE, after_self)
    norm(lambda place: buf.h1[place, :], 1, buf.a2)
    a2 = gather_start(buf.a2)
    reduce_done(step)

    weight_send(wt.f2, wt.f2.source)
    weight_relay(wt.cq)
    weight_relay(wt.co)
    arrived(rows(buf.e3, q), k_cot)
    gather_finish(a2)
    e3 = gather_start(buf.e3)
    weight_ready(wt.cq)
    matmul(buf.a2, wt.cq.weight, buf.q2, buf.bias, 1)
    attention(buf.q2, 0, buf.kv, 0, 2, False, 14, buf.p2, buf.o2)
    wt.co.own_copy[0].wait()
    weight_ready(wt.co)
    matmul(buf.o2, wt.co.weight, set_b.parts)
    step = reduce_start(set_b)
    gather_finish(e3)
    reduce_relay(step)
    reduce_ready(step)

    def after_cross(i):
        place = part(i, TILE)
        buf.h2[place, :] = buf.h1[place, :] + (reduced(step, place) + buf.vec[7:8, :])

    loop(L // TILE, after_cross)
    norm(lambda place: buf.h2[place, :], 2, buf.a3)
    a3 = gather_start(buf.a3)
    reduce_done(step)

    weight_relay(wt.f1)
    gather_finish(a3)
    weight_ready(wt.f1)

    def units(j):
        value = nn(buf.a3[...], wt.f1.weight[:, lanes(j)]) + buf.bias[2:3, lanes(j)]
        activ, slope = gelu_pair(value)
        buf.g[:, lanes(j)] = activ.astype(BF16)
        buf.gp[:, lanes(j)] = slope.astype(BF16)

    loop(FL // 256, units)
    weight_grad(buf.g, buf.e3, wt.f2)
    grad_send(wt.f2)
    weight_relay(wt.f2)
    wt.f2.own_copy[0].wait()
    weight_ready(wt.f2)

    def units_back(j):
        value = nt(buf.e3[...], wt.f2.weight[lanes(j), :])
        low = (value * buf.gp[:, lanes(j)].astype(F32)).astype(BF16)
        buf.gp[:, lanes(j)] = low
        buf.sg[10:11, lanes(j)] = jnp.sum(low.astype(F32), 0, keepdims=True)

    loop(FL // 256, units_back)
    matmul_back(buf.gp, wt.f1.weight, set_a.parts)
    step = reduce_start(set_a)
    weight_grad(buf.a3, buf.gp, wt.f1)
    grad_send(wt.f1)
    reduce_relay(step)
    matmul(buf.g, wt.f2.weight, set_c.parts)
    final = reduce_start(set_c)
    reduce_ready(step)
    zero = jnp.zeros((1, D), F32)

    def cot_sum(i, carry):
        return carry + jnp.sum(rows(buf.e3, q)[part(i, TILE), :].astype(F32), 0, keepdims=True)

    buf.sg[8:9, :] = lax.fori_loop(0, L // TILE, cot_sum, zero)

    def store(name):
        def low(place, value):
            rows(name, q)[place, :] = value

        return low

    buf.sg[7:8, :] = norm_back(
        lambda place: buf.h2[place, :], step, 2,
        lambda place: rows(buf.e3, q)[place, :].astype(F32), buf.dh, store(buf.e2),
    )
    e2 = gather_start(buf.e2)
    reduce_done(step)
    reduce_relay(final)
    grad_combine(wt.f2)
    gather_finish(e2)

    matmul_back(buf.e2, wt.co.weight, buf.do)
    attention_back(buf.q2, 0, buf.kv, 0, 2, buf.p2, buf.do)
    matmul_back(buf.q2, wt.cq.weight, set_b.parts)
    step = reduce_start(set_b)
    weight_grad(buf.o2, buf.e2, wt.co)
    grad_send(wt.co)
    weight_grad(buf.a2, buf.q2, wt.cq)
    grad_send(wt.cq)
    reduce_relay(step)
    weight_grad(buf.m, buf.kv, wt.ckv)
    grad_send(wt.ckv)
    matmul_back(buf.kv, wt.ckv.weight, set_a.parts)
    mem_step = reduce_start(set_a)
    reduce_ready(final)

    def finish(i):
        place = part(i, TILE)
        total = buf.h2[place, :] + (reduced(final, place) + buf.vec[8:9, :])
        buf.stage[place, :] = total.astype(BF16)

    loop(L // TILE, finish)
    result_copies.append(local(buf.stage, io.output))
    reduce_done(final)
    column_sums(buf.q2, 0, 1, 9, 2)
    column_sums(buf.kv, 1, 1, 9, 3)
    reduce_ready(step)
    buf.sg[6:7, :] = norm_back(
        lambda place: buf.h1[place, :], step, 1,
        lambda place: buf.dh[place, :], buf.dh, store(buf.e1),
    )
    e1 = gather_start(buf.e1)
    reduce_done(step)
    reduce_relay(mem_step)
    grad_combine(wt.f1)
    gather_finish(e1)

    matmul_back(buf.e1, wt.so.weight, buf.do)
    attention_back(buf.qkv, 0, buf.qkv, 2, 4, buf.p1, buf.do)
    matmul_back(buf.qkv, wt.qkv.weight, set_b.parts)
    step = reduce_start(set_b)
    weight_grad(buf.o1, buf.e1, wt.so)
    grad_send(wt.so)
    weight_grad(buf.a1, buf.qkv, wt.qkv)
    grad_send(wt.qkv)
    reduce_relay(step)
    column_sums(buf.qkv, 0, 1, 9, 0)
    column_sums(buf.qkv, 2, 1, 9, 1)

    reduce_ready(mem_step)

    def memory_row(i):
        place = part(i, TILE)
        buf.mb[place, :] = reduced(mem_step, place).astype(BF16)

    loop(L // TILE, memory_row)
    k_back = slot(n_sec)
    for j in range(1, n_sec):
        to = (s + j) % n_sec
        send(buf.mb.at[:, part(to, mem_cols)], buf.ml.at[j], k_back + j, (to, d))
    grad_combine(wt.co)
    grad_combine(wt.cq)
    reduce_ready(step)

    def store_stage(place, value):
        buf.ig[place, :] = value

    norm_back(
        hidden, step, 0, lambda place: buf.dh[place, :], None, store_stage,
    )
    k_in = slot()
    send(buf.ig, io.input_grad, k_in, ((s + n_sec - 1) % n_sec, d))
    buf.sga[q, z] = buf.sg[...].astype(BF16)
    sums = spread_start(buf.sga, None)
    for j in range(1, n_sec):
        arrived(buf.ml.at[j], k_back + j)

    def memory_total(i):
        place = part(i, TILE)
        total = buf.mb[place, part(s, mem_cols)].astype(F32)
        for j in range(1, n_sec):
            total = total + buf.ml[j, place, :].astype(F32)
        buf.mo[place, :] = total.astype(BF16)

    loop(L // TILE, memory_total)
    result_copies.append(local(buf.mo, io.memory_grad))
    grad_final(wt.f2)
    grad_final(wt.f1)
    grad_combine(wt.ckv)
    for weight in (wt.co, wt.cq, wt.ckv):
        grad_final(weight)
    grad_combine(wt.so)
    grad_combine(wt.qkv)
    unit_last_wait()
    last_wait(wt.ckv)
    last_wait(wt.cq)
    spread_relay(sums)
    for weight in (wt.so, wt.qkv):
        grad_final(weight)
    spread_ready(sums)

    def per_unit(q_at, at):
        total = buf.sga[q_at, 0, :, at].astype(F32)
        for plane in range(1, Z):
            total = total + buf.sga[q_at, plane, :, at].astype(F32)
        return total

    at = part(d // 2, 128)
    feature = per_unit(0, at)
    for q_at in range(1, P_IN):
        feature = feature + per_unit(q_at, at)
    swapped = pltpu.roll(feature, 64, 1)
    buf.sums[...] = jnp.where((jnp.zeros((16, 128), jnp.int32) + c) == 0, feature, swapped)
    head = d % 8
    at = part(2 * (d // 8) + head // 4, 128)
    low_head, high_head = per_unit(2 * c, at), per_unit(2 * c + 1, at)
    first_half = (jnp.zeros((16, 128), jnp.int32) + (head // 2) % 2) == 0
    low_head = jnp.where(first_half, low_head, pltpu.roll(low_head, 64, 1))
    high_head = jnp.where(first_half, pltpu.roll(high_head, 64, 1), high_head)
    buf.sums[9:10, :] = jnp.where(half, low_head, high_head)[9:10]
    at = part(2 * (d // 8) + 4 + head // 4, 128)
    low_head, high_head = per_unit(2 * c, at), per_unit(2 * c + 1, at)
    low_head = jnp.where(first_half, low_head, pltpu.roll(low_head, 64, 1))
    high_head = jnp.where(first_half, pltpu.roll(high_head, 64, 1), high_head)
    buf.sums[10:11, :] = jnp.where(half, low_head, high_head)[9:10]
    buf.sums[11:12, :] = per_unit(q, part(2 * z, 128))[10:11]
    buf.sums[12:13, :] = per_unit(q, part(2 * z + 1, 128))[10:11]
    result_copies.append(local(buf.sums, io.sums_out))
    last_wait(wt.qkv)
    arrived(io.input_grad, k_in)
    for copy in result_copies:
        copy.wait()
    for record in list(started):
        sent(record)
    assert counter[0] <= SEMS


def buffer_shapes(n_sec, mem_cols):
    tokens, row = (T, D), (L, D)
    shapes = dict(
        sva=(P_IN, Z, 16, 128),
        sga=(P_IN, Z, 16, D),
        hb=row, ig=row, stage=row, mb=row,
        ml=(n_sec, L, mem_cols),
        mo=(L, mem_cols),
        qkv=(T, 768), q2=(T, 256), kv=(T, 512), o1=(T, 256), o2=(T, 256), do=(T, 256),
        p1=(2 * P_IN, 2 * L, L), p2=(2 * P_IN, 2 * L, L),
        g=(T, FL), gp=(T, FL),
        a1=tokens, a2=tokens, a3=tokens, m=tokens, e3=tokens, e2=tokens, e1=tokens,
    )
    exact = dict(vec=(16, D), bias=(8, D), sg=(16, D), sums=(16, 128), h1=row, h2=row, dh=row)
    kinds = {name: pltpu.VMEM(shape, BF16) for name, shape in shapes.items()}
    kinds.update({name: pltpu.VMEM(shape, F32) for name, shape in exact.items()})
    return kinds


REDUCE_SHAPES = dict(
    parts=pltpu.VMEM((T, D), BF16),
    core=pltpu.VMEM((2 * L, D), BF16),
    across=pltpu.VMEM((L, D), BF16),
)


def scratch_of(n_sec, mem_cols):
    scratch = list(buffer_shapes(n_sec, mem_cols).values())
    scratch += 3 * list(REDUCE_SHAPES.values())
    for count, columns, _ in WEIGHTS.values():
        scratch += 2 * [pltpu.VMEM((Z * count, columns), BF16)]
        scratch += 4 * [pltpu.VMEM((count, columns), BF16)]
    for columns in (768, 512, 256):
        scratch.append(pltpu.VMEM((64, P_IN * columns), BF16))
        scratch.append(pltpu.VMEM((P_IN, 64, columns), BF16))
    return scratch + [
        pltpu.SemaphoreType.DMA((SEMS,)),
        pltpu.SemaphoreType.DMA((SEMS,)),
        pltpu.SemaphoreType.DMA((48,)),
    ]


def on_device_planes(
    prev_act, memory, out_cot, tgt_len, src_len, norm_gain, norm_bias, self_qkv, self_qv_bias,
    self_out, cross_q, cross_kv, cross_qv_bias, cross_out, out_bias, fc1, fc1_bias, fc2,
):
    n_sec = lax.axis_size("section")
    mem_cols = memory.shape[2]
    operands = (
        prev_act[0, 0], memory[0], out_cot[0, 0], tgt_len, src_len,
        norm_gain[0], norm_bias[0], out_bias[0], self_qv_bias, cross_qv_bias, fc1_bias,
        self_qkv[0], self_out[0], cross_kv[0], cross_q[0], cross_out[0], fc1[0], fc2[0],
    )
    anywhere = pl.BlockSpec(memory_space=pl.ANY)
    in_specs = 3 * [anywhere] + 2 * [pl.BlockSpec(memory_space=pltpu.SMEM)]
    in_specs += 6 * [pl.BlockSpec(memory_space=pltpu.VMEM)] + 7 * [anywhere]
    out_shapes = [(L, D), (L, D), (L, mem_cols)]
    for count, columns, by_column in WEIGHTS.values():
        out_shapes.append((count // P_IN, P_IN * columns) if by_column else (count, columns))
    sums_shape = jax.ShapeDtypeStruct((16, 128), F32)
    results = pl.pallas_call(
        functools.partial(whole_kernel, n_sec, mem_cols),
        out_shape=[jax.ShapeDtypeStruct(shape, BF16) for shape in out_shapes] + [sums_shape],
        in_specs=in_specs,
        out_specs=[anywhere] * (len(out_shapes) + 1),
        scratch_shapes=scratch_of(n_sec, mem_cols),
        compiler_params=pltpu.CompilerParams(
            collective_id=0, has_side_effects=True, vmem_limit_bytes=63 * 2**20
        ),
        cost_estimate=pl.CostEstimate(
            flops=21 * 10**9, bytes_accessed=20 * 2**20, transcendentals=3 * 10**6
        ),
    )(*operands)
    output, input_grad, memory_grad, g_qkv, g_so, g_ckv, g_cq, g_co, g_f1, g_f2, sums = results
    return (
        output[None, None],
        input_grad[None, None],
        memory_grad[None],
        sums[None, 0:3, 0:64],
        sums[None, 3:6, 0:64],
        g_qkv[None].astype(F32),
        sums[9:10],
        g_so[None].astype(F32),
        g_cq[None].astype(F32),
        g_ckv[None].astype(F32),
        sums[10:11],
        g_co[None].astype(F32),
        sums[None, 6:9, 0:64],
        g_f1[None].astype(F32),
        sums[11:13].reshape(1, 256),
        g_f2[None].astype(F32),
    )


def solution(mesh):
    in_specs = (
        P("section", "dp", None, None),
        P("dp", None, "section"),
        P("section", "dp", None, None),
        P("dp"),
        P("dp"),
        P("section", None, "dp"),
        P("section", None, "dp"),
        P("section", "dp", None),
        P("section", "dp"),
        P("section", "dp", None),
        P("section", "dp", None),
        P("section", "dp", None),
        P("section", "dp"),
        P("section", "dp", None),
        P("section", None, "dp"),
        P("section", "dp", None),
        P("section", "dp"),
        P("section", "dp", None),
    )
    out_specs = (
        P("section", "dp", None, None),
        P("section", "dp", None, None),
        P("dp", None, "section"),
        P("section", None, "dp"),
        P("section", None, "dp"),
        P("section", "dp", None),
        P("section", "dp"),
        P("section", "dp", None),
        P("section", "dp", None),
        P("section", "dp", None),
        P("section", "dp"),
        P("section", "dp", None),
        P("section", None, "dp"),
        P("section", "dp", None),
        P("section", "dp"),
        P("section", "dp", None),
    )
    planes = Z * P_IN
    fits = mesh.shape["dp"] == planes
    return jax.shard_map(
        on_device_planes if fits else on_device, mesh=mesh, in_specs=in_specs, out_specs=out_specs, check_vma=False
    )
```

```python
import functools
from types import SimpleNamespace

import jax
import jax.numpy as jnp
from jax import lax
from jax.experimental import pallas as pl
from jax.experimental.pallas import tpu as pltpu
from jax.sharding import PartitionSpec as P

H = 16
HD = 64


EPSILON = 1e-05
MASKED = -1000000000.0


def passed_along(value, axis, by):
    length = lax.axis_size(axis)
    return lax.ppermute(value, axis, [(i, (i + by) % length) for i in range(length)])


def norm_fwd(rows, gain, shift_term):
    center = rows - jnp.mean(rows, -1, keepdims=True)
    scale = lax.rsqrt(jnp.mean(center * center, -1, keepdims=True) + EPSILON)
    return center * scale * gain + shift_term


def gelu_exact(values):
    return jax.nn.gelu(values, approximate=False)


def product(left, right):
    return jnp.dot(left, right, preferred_element_type=jnp.float32)


def product_right_t(left, right):
    return lax.dot_general(
        left, right, (((1,), (1,)), ((), ())), preferred_element_type=jnp.float32
    )


def product_left_t(left, right):
    return lax.dot_general(
        left, right, (((0,), (0,)), ((), ())), preferred_element_type=jnp.float32
    )


def split_heads(flat, batch_rows):
    return flat.reshape(batch_rows, -1, H, HD)


def softmax_probs(query, key_rows, allowed):
    scores = jnp.einsum(
        "rthd,rshd->rhts", query, key_rows, preferred_element_type=jnp.float32
    ) * HD ** (-0.5)
    scores = jnp.where(allowed[:, None], scores, MASKED)
    weights = jnp.exp(scores - jnp.max(scores, -1, keepdims=True))
    return weights / jnp.sum(weights, -1, keepdims=True)


def attend_fwd(query, key_rows, value_rows, allowed):
    probs = softmax_probs(query, key_rows, allowed)
    mixed = jnp.einsum(
        "rhts,rshd->rthd",
        probs.astype(jnp.bfloat16),
        value_rows,
        preferred_element_type=jnp.float32,
    )
    return mixed.reshape(mixed.shape[0] * mixed.shape[1], -1).astype(jnp.bfloat16)


def attend_back(query, key_rows, value_rows, allowed, grad_mixed):
    probs = softmax_probs(query, key_rows, allowed)
    grad_heads = grad_mixed.reshape(query.shape)
    grad_probs = jnp.einsum(
        "rthd,rshd->rhts", grad_heads, value_rows, preferred_element_type=jnp.float32
    )
    delta = jnp.sum(probs * grad_probs, -1, keepdims=True)
    grad_scores = (probs * (grad_probs - delta)).astype(jnp.bfloat16)
    scale = HD ** (-0.5)
    grad_query = (
        jnp.einsum("rhts,rshd->rthd", grad_scores, key_rows, preferred_element_type=jnp.float32)
        * scale
    )
    grad_keys = (
        jnp.einsum("rhts,rthd->rshd", grad_scores, query, preferred_element_type=jnp.float32)
        * scale
    )
    grad_values = jnp.einsum(
        "rhts,rthd->rshd",
        probs.astype(jnp.bfloat16),
        grad_heads,
        preferred_element_type=jnp.float32,
    )
    width = query.shape[2] * query.shape[3]
    return (
        grad_query.reshape(-1, width).astype(jnp.bfloat16),
        grad_keys.reshape(-1, width).astype(jnp.bfloat16),
        grad_values.reshape(-1, width).astype(jnp.bfloat16),
    )


def unpack(pieces):
    return tuple((piece[0] for piece in pieces))


def on_device(
    prev_act,
    memory,
    out_cot,
    tgt_len,
    src_len,
    norm_gain,
    norm_bias,
    self_qkv,
    self_qv_bias,
    self_out,
    cross_q,
    cross_kv,
    cross_qv_bias,
    cross_out,
    out_bias,
    fc1,
    fc1_bias,
    fc2,
):
    fetched = unpack(
        (
            lax.all_gather(norm_gain, "dp", axis=2, tiled=True),
            lax.all_gather(norm_bias, "dp", axis=2, tiled=True),
            lax.all_gather(self_qkv, "dp", axis=1, tiled=True),
            lax.all_gather(self_qv_bias, "dp", axis=1, tiled=True),
            lax.all_gather(self_out, "dp", axis=1, tiled=True),
            lax.all_gather(cross_q, "dp", axis=1, tiled=True),
            lax.all_gather(cross_kv, "dp", axis=1, tiled=True),
            lax.all_gather(cross_qv_bias, "dp", axis=1, tiled=True),
            lax.all_gather(cross_out, "dp", axis=1, tiled=True),
            lax.all_gather(out_bias, "dp", axis=2, tiled=True),
            lax.all_gather(fc1, "dp", axis=1, tiled=True),
            lax.all_gather(fc1_bias, "dp", axis=1, tiled=True),
            lax.all_gather(fc2, "dp", axis=1, tiled=True),
        )
    )
    gains, shifts, w_sqkv, b_sqv, w_sout, w_cq, w_ckv, b_cqv, w_cout, b_out, w_one, b_one, w_two = (
        fetched
    )
    gain_f = gains.astype(jnp.float32)
    shift_f = shifts.astype(jnp.float32)
    sqv_f = b_sqv.astype(jnp.float32)
    cqv_f = b_cqv.astype(jnp.float32)
    out_f = b_out.astype(jnp.float32)
    one_f = b_one.astype(jnp.float32)
    source = passed_along(prev_act, "section", 1)[0]
    batch_rows, length, width = source.shape
    encoded = lax.all_gather(memory, "section", axis=2, tiled=True)
    mem_flat = encoded.reshape(-1, width)
    places = jnp.arange(length)
    self_ok = (places[None, None, :] <= places[None, :, None]) & (
        places[None, None, :] < tgt_len[:, None, None]
    )
    cross_ok = jnp.arange(encoded.shape[1])[None, None, :] < src_len[:, None, None]
    resid = source.astype(jnp.float32).reshape(-1, width)
    normed_one, pull_one = jax.vjp(norm_fwd, resid, gain_f[0], shift_f[0])
    first_in = normed_one.astype(jnp.bfloat16)
    joint = product(first_in, w_sqkv)
    query_self = (joint[:, :width] + sqv_f[:width]).astype(jnp.bfloat16)
    keys_self = joint[:, width : 2 * width].astype(jnp.bfloat16)
    values_self = (joint[:, 2 * width :] + sqv_f[width:]).astype(jnp.bfloat16)
    self_mixed = attend_fwd(
        split_heads(query_self, batch_rows),
        split_heads(keys_self, batch_rows),
        split_heads(values_self, batch_rows),
        self_ok,
    )
    after_self = resid + (product(self_mixed, w_sout) + out_f[0])
    normed_two, pull_two = jax.vjp(norm_fwd, after_self, gain_f[1], shift_f[1])
    second_in = normed_two.astype(jnp.bfloat16)
    query_cross = (product(second_in, w_cq) + cqv_f[:width]).astype(jnp.bfloat16)
    memory_proj = product(mem_flat, w_ckv)
    keys_cross = memory_proj[:, :width].astype(jnp.bfloat16)
    values_cross = (memory_proj[:, width:] + cqv_f[width:]).astype(jnp.bfloat16)
    cross_mixed = attend_fwd(
        split_heads(query_cross, batch_rows),
        split_heads(keys_cross, batch_rows),
        split_heads(values_cross, batch_rows),
        cross_ok,
    )
    after_cross = after_self + (product(cross_mixed, w_cout) + out_f[1])
    normed_three, pull_three = jax.vjp(norm_fwd, after_cross, gain_f[2], shift_f[2])
    third_in = normed_three.astype(jnp.bfloat16)
    pre_act = product(third_in, w_one) + one_f
    activ, pull_gelu = jax.vjp(gelu_exact, pre_act)
    act_low = activ.astype(jnp.bfloat16)
    result = after_cross + (product(act_low, w_two) + out_f[2])
    output = result.astype(jnp.bfloat16).reshape(1, batch_rows, length, width)
    (
        unused_gains,
        unused_shifts,
        w_sqkv,
        unused_sqv,
        w_sout,
        w_cq,
        w_ckv,
        unused_cqv,
        w_cout,
        unused_out,
        w_one,
        unused_one,
        w_two,
    ) = fetched
    grad_out = passed_along(out_cot, "section", -1)[0].astype(jnp.float32).reshape(-1, width)
    ffn_grad = grad_out.astype(jnp.bfloat16)
    grad_fc2 = product_left_t(act_low, ffn_grad)
    grad_b2 = jnp.sum(ffn_grad, 0, dtype=jnp.float32)
    grad_act = product_right_t(ffn_grad, w_two)
    (grad_pre,) = pull_gelu(grad_act)
    pre_low = grad_pre.astype(jnp.bfloat16)
    grad_fc1 = product_left_t(third_in, pre_low)
    grad_b1 = jnp.sum(pre_low, 0, dtype=jnp.float32)
    grad_mid, grad_gain3, grad_shift3 = pull_three(product_right_t(pre_low, w_one))
    grad_mid = grad_mid + grad_out
    cross_grad = grad_mid.astype(jnp.bfloat16)
    grad_cout = product_left_t(cross_mixed, cross_grad)
    grad_bco = jnp.sum(cross_grad, 0, dtype=jnp.float32)
    grad_cmix = product_right_t(cross_grad, w_cout).astype(jnp.bfloat16)
    grad_qc, grad_kc, grad_vc = attend_back(
        split_heads(query_cross, batch_rows),
        split_heads(keys_cross, batch_rows),
        split_heads(values_cross, batch_rows),
        cross_ok,
        grad_cmix,
    )
    grad_cq = product_left_t(second_in, grad_qc)
    grad_kv = jnp.concatenate([grad_kc, grad_vc], -1)
    grad_ckv = product_left_t(mem_flat, grad_kv)
    grad_cqv = jnp.concatenate(
        [jnp.sum(grad_qc, 0, dtype=jnp.float32), jnp.sum(grad_vc, 0, dtype=jnp.float32)]
    )
    grad_memory = product_right_t(grad_kv, w_ckv).reshape(encoded.shape)
    memory_grad = lax.psum_scatter(
        grad_memory.astype(jnp.bfloat16), "section", scatter_dimension=2, tiled=True
    )
    grad_after, grad_gain2, grad_shift2 = pull_two(product_right_t(grad_qc, w_cq))
    grad_after = grad_after + grad_mid
    self_grad = grad_after.astype(jnp.bfloat16)
    grad_sout = product_left_t(self_mixed, self_grad)
    grad_bso = jnp.sum(self_grad, 0, dtype=jnp.float32)
    grad_smix = product_right_t(self_grad, w_sout).astype(jnp.bfloat16)
    grad_qs, grad_ks, grad_vs = attend_back(
        split_heads(query_self, batch_rows),
        split_heads(keys_self, batch_rows),
        split_heads(values_self, batch_rows),
        self_ok,
        grad_smix,
    )
    grad_qkv = jnp.concatenate([grad_qs, grad_ks, grad_vs], -1)
    grad_sqkv = product_left_t(first_in, grad_qkv)
    grad_sqv = jnp.concatenate(
        [jnp.sum(grad_qs, 0, dtype=jnp.float32), jnp.sum(grad_vs, 0, dtype=jnp.float32)]
    )
    grad_in, grad_gain1, grad_shift1 = pull_one(product_right_t(grad_qkv, w_sqkv))
    grad_in = grad_in + grad_after
    input_grad = passed_along(
        grad_in.astype(jnp.bfloat16).reshape(1, batch_rows, length, width), "section", -1
    )
    grad_gain = jnp.stack([grad_gain1, grad_gain2, grad_gain3])
    grad_shift = jnp.stack([grad_shift1, grad_shift2, grad_shift3])
    grad_obias = jnp.stack([grad_bso, grad_bco, grad_b2])
    sums = (
        lax.psum_scatter(
            grad_gain.astype(jnp.bfloat16), "dp", scatter_dimension=1, tiled=True
        ).astype(jnp.float32),
        lax.psum_scatter(
            grad_shift.astype(jnp.bfloat16), "dp", scatter_dimension=1, tiled=True
        ).astype(jnp.float32),
        lax.psum_scatter(
            grad_sqkv.astype(jnp.bfloat16), "dp", scatter_dimension=0, tiled=True
        ).astype(jnp.float32),
        lax.psum_scatter(
            grad_sqv.astype(jnp.bfloat16), "dp", scatter_dimension=0, tiled=True
        ).astype(jnp.float32),
        lax.psum_scatter(
            grad_sout.astype(jnp.bfloat16), "dp", scatter_dimension=0, tiled=True
        ).astype(jnp.float32),
        lax.psum_scatter(
            grad_cq.astype(jnp.bfloat16), "dp", scatter_dimension=0, tiled=True
        ).astype(jnp.float32),
        lax.psum_scatter(
            grad_ckv.astype(jnp.bfloat16), "dp", scatter_dimension=0, tiled=True
        ).astype(jnp.float32),
        lax.psum_scatter(
            grad_cqv.astype(jnp.bfloat16), "dp", scatter_dimension=0, tiled=True
        ).astype(jnp.float32),
        lax.psum_scatter(
            grad_cout.astype(jnp.bfloat16), "dp", scatter_dimension=0, tiled=True
        ).astype(jnp.float32),
        lax.psum_scatter(
            grad_obias.astype(jnp.bfloat16), "dp", scatter_dimension=1, tiled=True
        ).astype(jnp.float32),
        lax.psum_scatter(
            grad_fc1.astype(jnp.bfloat16), "dp", scatter_dimension=0, tiled=True
        ).astype(jnp.float32),
        lax.psum_scatter(
            grad_b1.astype(jnp.bfloat16), "dp", scatter_dimension=0, tiled=True
        ).astype(jnp.float32),
        lax.psum_scatter(
            grad_fc2.astype(jnp.bfloat16), "dp", scatter_dimension=0, tiled=True
        ).astype(jnp.float32),
    )
    return (
        output,
        input_grad,
        memory_grad,
        sums[0][None],
        sums[1][None],
        sums[2][None],
        sums[3][None],
        sums[4][None],
        sums[5][None],
        sums[6][None],
        sums[7][None],
        sums[8][None],
        sums[9][None],
        sums[10][None],
        sums[11][None],
        sums[12][None],
    )


Z = 4
P_IN = 4
L = 192
D = 1024
T = P_IN * L
FL = 1024
TILE = 32
MESH = pl.DeviceIdType.MESH
F32 = jnp.float32
BF16 = jnp.bfloat16

WEIGHTS = dict(
    qkv=(256, 768, True),
    so=(64, 1024, False),
    ckv=(256, 512, True),
    cq=(256, 256, True),
    co=(64, 1024, False),
    f1=(256, 1024, True),
    f2=(256, 1024, False),
)
SEMS = 240


def run_if(cond, fn):
    if cond is None:
        fn()
    else:
        pl.when(cond)(fn)


def part(index, size, step=None):
    return pl.ds(pl.multiple_of(index * size, size), size if step is None else step)


def nn(left, right):
    return jnp.dot(left, right, preferred_element_type=F32)


def nt(left, right):
    return lax.dot_general(left, right, (((1,), (1,)), ((), ())), preferred_element_type=F32)


def tn(left, right):
    return lax.dot_general(left, right, (((0,), (0,)), ((), ())), preferred_element_type=F32)


def loop(count, body, unroll=1):
    def step(index, carry):
        body(index)
        return carry

    lax.fori_loop(0, count, step, 0, unroll=unroll)


def gelu_pair(values):
    bell = jnp.exp(-0.5 * values * values)
    step = 1.0 / (1.0 + 0.3275911 * 0.7071067811865476 * jnp.abs(values))
    series = step * (
        0.254829592
        + step
        * (-0.284496736 + step * (1.421413741 + step * (-1.453152027 + step * 1.061405429)))
    )
    above = 0.5 * series * bell
    below = jnp.where(values < 0, above, 1.0 - above)
    return values * below, below + values * bell * 0.3989422804014327


def whiten(rows):
    center = rows - jnp.mean(rows, -1, keepdims=True)
    scale = lax.rsqrt(jnp.mean(center * center, -1, keepdims=True) + EPSILON)
    return center * scale, scale


def whole_kernel(n_sec, mem_cols, *refs):
    given = iter(refs)

    def take(names):
        return SimpleNamespace(**{name: next(given) for name in names})

    def take_weights(**fields):
        for name in WEIGHTS:
            for field in fields:
                setattr(getattr(wt, name), field, next(given))

    wt = SimpleNamespace(**{name: SimpleNamespace() for name in WEIGHTS})
    io = take(
        dict(
            prev=0, mem=0, cot=0, tgt=0, src=0, gain=0, shift=0, out_bias=0,
            self_bias=0, cross_bias=0, unit_bias=0,
        )
    )
    take_weights(source=0)
    vars(io).update(vars(take(dict(output=0, input_grad=0, memory_grad=0))))
    take_weights(result=0)
    vars(io).update(vars(take(dict(sums_out=0))))
    buf = take(buffer_shapes(n_sec, mem_cols))
    set_a, set_b, set_c = (take(REDUCE_SHAPES) for _ in range(3))
    take_weights(weight=0, grad=0, near=0, far=0)
    for weight in (wt.qkv, wt.so, wt.ckv, wt.cq, wt.co):
        weight.to_diag, weight.to_opp, weight.through = next(given), next(given), next(given)
    for weight in (wt.qkv, wt.ckv, wt.cq):
        weight.raw, weight.sorted = next(given), next(given)
    send_sems, recv_sems, local_sems = given

    s = lax.axis_index("section")
    d = lax.axis_index("dp")
    z, q = d // P_IN, d % P_IN
    x, c = q // 2, q % 2
    end = (z % 3) == 0
    mid = (z % 3) != 0
    q_core = q + 1 - 2 * c
    q_x = q + 2 - 4 * x
    q_xc = q_x + 1 - 2 * c
    z_adj = z + 1 - 2 * (z % 2)
    z_opp = 3 - z
    z_diag = (z + 2) % 4
    dev_core, dev_x, dev_xc = (s, z * P_IN + q_core), (s, z * P_IN + q_x), (s, z * P_IN + q_xc)
    dev_adj, dev_opp, dev_diag = (s, z_adj * P_IN + q), (s, z_opp * P_IN + q), (s, z_diag * P_IN + q)
    in_plane = ((q_core, dev_core), (q_x, dev_x), (q_xc, dev_xc))

    counter = [0]
    started = []
    local_counter = [0]

    def slot(count=1):
        counter[0] += count
        return counter[0] - count

    def remote(src, dst, k, device):
        return pltpu.make_async_remote_copy(
            src_ref=src, dst_ref=dst, send_sem=send_sems.at[k], recv_sem=recv_sems.at[k],
            device_id=device, device_id_type=MESH,
        )

    def send(src, dst, k, device, cond=None):
        copy = remote(src, dst, k, device)
        run_if(cond, copy.start)
        record = [copy, cond]
        started.append(record)
        return record

    def sent(record):
        run_if(record[1], record[0].wait_send)
        started[:] = [other for other in started if other is not record]

    def arrived(dst, k, cond=None):
        run_if(cond, remote(dst, dst, k, dev_core).wait_recv)

    def local(src, dst):
        copy = pltpu.make_async_copy(src, dst, local_sems.at[local_counter[0]])
        local_counter[0] += 1
        copy.start()
        return copy

    def rows(rows_of, index):
        return rows_of.at[part(index, L)]

    for name, (count, _, by_column) in WEIGHTS.items():
        weight = getattr(wt, name)
        weight.count, weight.by_column = count, by_column
        weight.to_use, weight.swap, weight.to_sum, weight.last = slot(5), slot(3), slot(6), slot(3)

    def block(name, index):
        return name.weight.at[part(index, name.count)]

    def send_inward(name, src):
        send(src, block(name, z), name.to_use, dev_adj, end)

    def send_across(name, src):
        send(src, block(name, z), name.to_use + 1, dev_opp, mid)

    def weight_outward(name, src):
        send(src, block(name, z), name.to_use, dev_adj, mid)

    def relay_inward(name):
        k = name.to_use
        arrived(block(name, z_adj), k, mid)
        send(block(name, z_adj), block(name, z_adj), k + 2, dev_opp, mid)

    def relay_near(name):
        k = name.to_use
        arrived(block(name, z_opp), k + 1, mid)
        send(block(name, z_opp), block(name, z_opp), k + 3, dev_adj, mid)

    def relay_far(name):
        k = name.to_use
        arrived(block(name, z_diag), k + 2, mid)
        send(block(name, z_diag), block(name, z_diag), k + 4, dev_adj, mid)

    def weight_ready(name):
        k = name.to_use
        arrived(block(name, z_adj), k, end)
        arrived(block(name, z_diag), k + 3, end)
        arrived(block(name, z_opp), k + 4, end)

    def inner_ready(name):
        k = name.to_use
        arrived(block(name, z_opp), k + 1, mid)
        arrived(block(name, z_diag), k + 2, mid)


    def swap_start(name):
        size = name.count // P_IN
        place = name.weight.at[part(z * P_IN + q, size)]
        name.swapped = [
            send(name.sorted.at[q_to], place, name.swap + j, device)
            for j, (q_to, device) in enumerate(in_plane)
        ]
        name.own_copy = [local(name.sorted.at[q], place)]

    def swap_wait(name):
        size = name.count // P_IN
        for j, (q_from, _) in enumerate(in_plane):
            arrived(name.weight.at[part(z * P_IN + q_from, size)], name.swap + j)
        for copy in name.own_copy:
            copy.wait()
        for record in name.swapped:
            sent(record)

    def halves(first, second, odd):
        if odd:
            first = pltpu.roll(first, 64, 1)
        else:
            second = pltpu.roll(second, 64, 1)
        lane = lax.broadcasted_iota(jnp.int32, first.shape, 1)
        return jnp.where(lane < 64, first, second)

    def tile_of(index):
        return slice(index * 128, index * 128 + 128)

    def sort_columns(name):
        for q_to in range(P_IN):
            for tile in range(name.sorted.shape[2] // 128):
                at = 4 * tile + q_to // 2
                first = name.raw[:, tile_of(at)].astype(F32)
                second = name.raw[:, tile_of(at + 2)].astype(F32)
                name.sorted[q_to, :, tile_of(tile)] = halves(first, second, q_to % 2).astype(BF16)

    def unsort_columns(name):
        for tile in range(name.raw.shape[1] // 128):
            group, u = tile // 8, tile % 8
            at = 2 * group + u // 4
            first = name.sorted[2 * (u % 2), :, tile_of(at)].astype(F32)
            second = name.sorted[2 * (u % 2) + 1, :, tile_of(at)].astype(F32)
            name.raw[:, tile_of(tile)] = halves(first, second, (u // 2) % 2).astype(BF16)

    unit_swap, unit_last = slot(3 * Z), slot(3 * Z)

    def unit_columns(rows_of, tile, q_at):
        return rows_of.at[:, part(tile * P_IN + q_at, 256)]

    def unit_swap_start():
        size = wt.f1.count // P_IN
        place = wt.f1.weight.at[part(z * P_IN + q, size)]
        wt.f1.own_copy = []
        for tile in range(Z):
            at = place.at[:, part(tile, 256)]
            for j, (q_to, device) in enumerate(in_plane):
                send(unit_columns(wt.f1.source, tile, q_to), at, unit_swap + 3 * tile + j, device)
            wt.f1.own_copy.append(local(unit_columns(wt.f1.source, tile, q), at))

    def unit_swap_wait(cond):
        size = wt.f1.count // P_IN
        for tile in range(Z):
            for j, (q_from, _) in enumerate(in_plane):
                place = wt.f1.weight.at[part(z * P_IN + q_from, size)]
                arrived(place.at[:, part(tile, 256)], unit_swap + 3 * tile + j, cond)
        for copy in wt.f1.own_copy:
            run_if(cond, copy.wait)

    def grad_block(name, index):
        return name.grad.at[part(index, name.count)]

    def grad_send_far(name):
        return send(grad_block(name, z_opp), name.to_diag, name.to_sum, dev_adj, end)

    def grad_send_middle(name):
        return send(grad_block(name, z_diag), name.to_opp, name.to_sum + 1, dev_adj, end)

    def grad_send_near(name):
        return send(grad_block(name, z_adj), name.near, name.to_sum + 2, dev_adj, end)

    def grad_send(name):
        grad_send_far(name)
        grad_send_middle(name)
        grad_send_near(name)

    def add_rows(count, body):
        size = min(count, 64)
        loop(count // size, lambda i: body(part(i, size)))

    def grad_add(name, landed, index):
        def one(place):
            own = grad_block(name, index)[place, :].astype(F32)
            landed[place, :] = (own + landed[place, :].astype(F32)).astype(BF16)

        add_rows(name.count, one)

    def grad_combine_far(name):
        k = name.to_sum
        arrived(name.to_diag, k, mid)
        run_if(mid, lambda: grad_add(name, name.to_diag, z_diag))
        send(name.to_diag, name.through, k + 3, dev_opp, mid)

    def grad_combine_middle(name):
        k = name.to_sum
        arrived(name.to_opp, k + 1, mid)
        run_if(mid, lambda: grad_add(name, name.to_opp, z_opp))
        send(name.to_opp, name.far, k + 4, dev_opp, mid)

    def grad_combine(name):
        grad_combine_far(name)
        grad_combine_middle(name)

    def grad_outward(name):
        k = name.to_sum
        arrived(name.through, k + 3, mid)
        run_if(mid, lambda: grad_add(name, name.through, z_adj))
        send(name.through, name.near, k + 5, dev_adj, mid)

    result_copies = []

    def inner_grad_far(name):
        send(grad_block(name, z_diag), name.far, name.to_sum, dev_opp, mid)

    def inner_grad_near(name):
        send(grad_block(name, z_opp), name.near, name.to_sum + 1, dev_opp, mid)

    def inner_grad_combine(name):
        k = name.to_sum

        def add():
            arrived(name.far, k)

            def one(place):
                own = grad_block(name, z_adj)[place, :].astype(F32)
                name.far[place, :] = (own + name.far[place, :].astype(F32)).astype(BF16)

            add_rows(name.count, one)

        run_if(mid, add)
        send(name.far, name.near, k + 2, dev_adj, mid)

    def inner_grad_total(name):
        k = name.to_sum
        arrived(name.near, k + 2, end)

        def add():
            arrived(name.near, k + 1)

            def one(place):
                own = grad_block(name, z)[place, :].astype(F32)
                name.near[place, :] = (own + name.near[place, :].astype(F32)).astype(BF16)

            add_rows(name.count, one)

        run_if(mid, add)

    def grad_total(name):
        k = name.to_sum
        arrived(name.near, k + 5, end)
        arrived(name.near, k + 2, mid)
        arrived(name.far, k + 4, mid)

        def add_far():
            def one(place):
                total = name.near[place, :].astype(F32) + name.far[place, :].astype(F32)
                name.near[place, :] = (total + grad_block(name, z)[place, :].astype(F32)).astype(BF16)

            add_rows(name.count, one)

        run_if(mid, add_far)
        run_if(end, lambda: grad_add(name, name.near, z))

    def grad_final(name):
        count = name.count
        if name is wt.f1 or name is wt.f2:
            inner_grad_total(name)
        else:
            grad_total(name)
        size = count // P_IN
        if name is wt.f1:
            for tile in range(Z):
                for j, (q_to, device) in enumerate(in_plane):
                    src = name.near.at[part(q_to, size), part(tile, 256)]
                    dst = unit_columns(name.result, tile, q)
                    send(src, dst, unit_last + 3 * tile + j, device)
                src = name.near.at[part(q, size), part(tile, 256)]
                result_copies.append(local(src, unit_columns(name.result, tile, q)))
        elif name.by_column:
            for j, (q_to, device) in enumerate(in_plane):
                src = name.near.at[part(q_to, size)]
                send(src, name.sorted.at[q], name.last + j, device)
            src = name.near.at[part(q, size)]
            name.own_copy = [local(src, name.sorted.at[q])]
        else:
            result_copies.append(local(name.near, name.result))

    def last_wait(name):
        for j, (q_from, _) in enumerate(in_plane):
            arrived(name.sorted.at[q_from], name.last + j)
        for copy in name.own_copy:
            copy.wait()
        unsort_columns(name)
        result_copies.append(local(name.raw, name.result))

    def unit_last_wait():
        for tile in range(Z):
            for j, (q_from, _) in enumerate(in_plane):
                place = unit_columns(wt.f1.result, tile, q_from)
                arrived(place, unit_last + 3 * tile + j)

    def gather_start(name, cond=None):
        k = slot(3)
        first = send(rows(name, q), rows(name, q), k, dev_x, cond)
        second = send(rows(name, q), rows(name, q), k + 1, dev_core, cond)
        return name, k, [first, second], cond

    def gather_relay(ticket):
        name, k, records, cond = ticket
        arrived(rows(name, q_x), k, cond)
        records.append(send(rows(name, q_x), rows(name, q_x), k + 2, dev_core, cond))

    def gather_ready(ticket):
        name, k, _, cond = ticket
        arrived(rows(name, q_core), k + 1, cond)
        arrived(rows(name, q_xc), k + 2, cond)

    def gather_finish(ticket):
        gather_relay(ticket)
        gather_ready(ticket)

    def reduce_start(which, cond=None):
        k = slot(3)
        out = which.parts
        first = send(rows(out, q_xc), rows(which.core, 1), k, dev_core, cond)
        second = send(rows(out, q_core), rows(which.core, 0), k + 1, dev_core, cond)
        return which, k, [first, second], cond

    def reduce_relay(ticket):
        which, k, records, cond = ticket
        out = which.parts
        arrived(rows(which.core, 1), k, cond)

        def add():
            def one(i):
                mine = rows(out, q_x)
                place = part(i, TILE)
                total = mine[place, :].astype(F32) + rows(which.core, 1)[place, :].astype(F32)
                mine[place, :] = total.astype(BF16)

            loop(L // TILE, one)

        run_if(cond, add)
        records.append(send(rows(out, q_x), which.across, k + 2, dev_x, cond))

    def reduce_ready(ticket):
        which, k, _, cond = ticket
        arrived(rows(which.core, 0), k + 1, cond)
        arrived(which.across, k + 2, cond)

    def reduced(ticket, place):
        which = ticket[0]
        total = rows(which.parts, q)[place, :].astype(F32)
        total = total + rows(which.core, 0)[place, :].astype(F32)
        return total + which.across[place, :].astype(F32)

    def reduce_done(ticket):
        for record in ticket[2]:
            sent(record)

    def spread_start(name, src):
        k = slot(8)
        place = name.at[q, z]
        copy = None
        if src is not None:
            copy = local(src, place)
        else:
            src = place
        send(src, place, k, dev_adj)
        send(src, place, k + 1, dev_opp, mid)
        send(src, place, k + 2, dev_diag, end)
        return name, k, copy

    def spread_relay(ticket):
        name, k, copy = ticket
        arrived(name.at[q, z_opp], k + 1, mid)
        send(name.at[q, z_opp], name.at[q, z_opp], k + 3, dev_adj, mid)
        arrived(name.at[q, z_diag], k + 2, mid)
        send(name.at[q, z_diag], name.at[q, z_diag], k + 4, dev_adj, mid)
        arrived(name.at[q, z_adj], k)
        arrived(name.at[q, z_diag], k + 3, end)
        arrived(name.at[q, z_opp], k + 4, end)
        if copy is not None:
            copy.wait()
        for j, (_, device) in enumerate(in_plane):
            send(name.at[q], name.at[q], k + 5 + j, device)

    def spread_ready(ticket):
        name, k, _ = ticket
        for j, (q_from, _) in enumerate(in_plane):
            arrived(name.at[q_from], k + 5 + j)

    def lanes(j, size=256):
        return part(j, size)

    def matmul(left, right, dst, bias=None, bias_row=0, bias_at=0):
        count = right.shape[1] // 256

        def one(j):
            tile = nn(left[...], right[:, lanes(j)])
            if bias is not None:
                tile = tile + bias[bias_row:bias_row + 1, part(j + bias_at, 256)]
            dst[:, lanes(j)] = tile.astype(BF16)

        loop(count, one)

    def matmul_back(left, right, dst):
        def one(j):
            dst[:, lanes(j)] = nt(left[...], right[lanes(j), :]).astype(BF16)

        loop(right.shape[0] // 256, one)

    def weight_grad(left, right, name):
        def one(j):
            name.grad[lanes(j), :] = tn(left[:, lanes(j)], right[...]).astype(BF16)

        loop(left.shape[1] // 256, one)

    low_half = lax.broadcasted_iota(jnp.int32, (L, 128), 1) < 64
    keep_low = low_half.astype(F32).astype(BF16)
    keep_high = (1.0 - low_half.astype(F32)).astype(BF16)

    def both(pair):
        return jnp.concatenate([pair * keep_low, pair * keep_high], axis=0)

    def merge(stacked):
        return jnp.where(low_half, stacked[:L], stacked[L:])

    def attention(qref, q_at, kref, k_at, v_at, causal, length_row, probs, dst):
        def one(i):
            r, pair = i // 2, i % 2
            place = part(r, L)
            query = both(qref[place, part(pair + q_at, 128)])
            scores = nt(query, kref[place, part(pair + k_at, 128)]) * HD ** (-0.5)
            key = lax.broadcasted_iota(jnp.int32, scores.shape, 1)
            limit = buf.sva[r, z][length_row:length_row + 1, 0:1].astype(F32)
            allowed = key.astype(F32) < limit
            if causal:
                at = lax.broadcasted_iota(jnp.int32, scores.shape, 0)
                at = jnp.where(at < L, at, at - L)
                allowed = allowed & (key <= at)
            scores = jnp.where(allowed, scores, MASKED)
            raised = jnp.exp(scores - jnp.max(scores, -1, keepdims=True))
            weights = (raised * (1.0 / jnp.sum(raised, -1, keepdims=True))).astype(BF16)
            probs[i] = weights
            mixed = nn(weights, kref[place, part(pair + v_at, 128)])
            dst[place, part(pair, 128)] = merge(mixed).astype(BF16)

        loop(2 * P_IN, one, 2)

    def attention_back(qref, q_at, kref, k_at, v_at, probs, grad):
        def one(i):
            r, pair = i // 2, i % 2
            place = part(r, L)
            query = both(qref[place, part(pair + q_at, 128)])
            key = kref[place, part(pair + k_at, 128)]
            value = kref[place, part(pair + v_at, 128)]
            mixed_grad = both(grad[place, part(pair, 128)])
            weights = probs[i]
            soft = weights.astype(F32)
            grad_probs = nt(mixed_grad, value)
            delta = jnp.sum(soft * grad_probs, -1, keepdims=True)
            grad_scores = (soft * (grad_probs - delta)).astype(BF16)
            scale = HD ** (-0.5)
            grad_query = merge(nn(grad_scores, key)) * scale
            grad_key = tn(grad_scores, query) * scale
            grad_value = tn(weights, mixed_grad)
            qref[place, part(pair + q_at, 128)] = grad_query.astype(BF16)
            kref[place, part(pair + k_at, 128)] = grad_key.astype(BF16)
            kref[place, part(pair + v_at, 128)] = grad_value.astype(BF16)

        loop(2 * P_IN, one, 2)

    def column_sums(source, first, count, row, at):
        def one(j):
            values = source[:, part(j + first, 256)].astype(F32)
            buf.sg[row:row + 1, part(j + at, 256)] = jnp.sum(values, 0, keepdims=True)

        loop(count, one)

    def norm(load, index, dst):
        def one(i):
            place = part(i, TILE)
            normed, _ = whiten(load(place))
            gain, shift = buf.vec[index:index + 1, :], buf.vec[index + 3:index + 4, :]
            rows(dst, q)[place, :] = (normed * gain + shift).astype(BF16)

        loop(L // TILE, one)

    def norm_back(load, incoming, index, base, dst, low, out_row=None):
        zero = jnp.zeros((1, D), F32)

        def one(i, carry):
            gain_sum, shift_sum, out_sum = carry
            place = part(i, TILE)
            normed, scale = whiten(load(place))
            grad = incoming(place)
            gained = grad * buf.vec[index:index + 1, :]
            back = gained - jnp.mean(gained, -1, keepdims=True)
            back = back - normed * jnp.mean(gained * normed, -1, keepdims=True)
            total = base(place) + scale * back
            if dst is not None:
                dst[place, :] = total
            rounded = total.astype(BF16)
            low(place, rounded)
            return (
                gain_sum + jnp.sum(grad * normed, 0, keepdims=True),
                shift_sum + jnp.sum(grad, 0, keepdims=True),
                out_sum + jnp.sum(rounded.astype(F32), 0, keepdims=True),
            )

        gain_sum, shift_sum, out_sum = lax.fori_loop(0, L // TILE, one, (zero, zero, zero))
        buf.sg[index:index + 1, :] = gain_sum
        buf.sg[index + 3:index + 4, :] = shift_sum
        if out_row is not None:
            buf.sg[out_row:out_row + 1, :] = out_sum

    gate = pltpu.get_barrier_semaphore()
    partners = [device for _, device in in_plane] + [dev_adj, dev_opp, dev_diag]
    partners += [((s + j) % n_sec, d) for j in range(1, n_sec)]
    for device in partners:
        pl.semaphore_signal(gate, inc=1, device_id=device, device_id_type=MESH)
    raw_copies = [local(weight.source, weight.raw) for weight in (wt.qkv, wt.ckv, wt.cq)]
    low_lanes = lax.broadcasted_iota(jnp.int32, (3, 128), 1) < 64
    even_lanes = (jnp.zeros((3, 128), jnp.int32) + c) == 0
    for row, pieces in ((0, io.gain), (3, io.shift), (6, io.out_bias)):
        value = pieces[...].astype(F32)
        twice = jnp.concatenate([value, value], 1)
        buf.sg[row:row + 3, 0:128] = jnp.where(low_lanes == even_lanes, twice, 0.0)
    buf.sg[9:10, 0:128] = io.self_bias[...].astype(F32)
    buf.sg[10:11, 0:128] = io.cross_bias[...].astype(F32)
    buf.sg[11:12, 0:128] = io.unit_bias[:, 0:128].astype(F32)
    buf.sg[12:13, 0:128] = io.unit_bias[:, 128:256].astype(F32)
    buf.sg[13:14, 0:128] = jnp.zeros((1, 128), F32) + io.tgt[0].astype(F32)
    buf.sg[14:15, 0:128] = jnp.zeros((1, 128), F32) + io.src[0].astype(F32)
    buf.sg[15:16, 0:128] = jnp.zeros((1, 128), F32)
    buf.sva[q, z] = buf.sg[:, 0:128].astype(BF16)

    raw_copies[0].wait()
    sort_columns(wt.qkv)
    pl.semaphore_wait(gate, len(partners))

    sv = spread_start(buf.sva, None)
    swap_start(wt.qkv)
    k_prev, k_cot, k_mem = slot(), slot(), slot(n_sec)
    send(io.prev, buf.hb, k_prev, ((s + 1) % n_sec, d))
    mem_slot = rows(buf.m, q)
    for j in range(1, n_sec):
        send(io.mem, mem_slot.at[:, part(s, mem_cols)], k_mem + j, ((s + j) % n_sec, d))
    mem_copy = local(io.mem, mem_slot.at[:, part(s, mem_cols)])
    send(io.cot, rows(buf.e3, q), k_cot, ((s + n_sec - 1) % n_sec, d))
    for weight in (wt.so, wt.co, wt.f2):
        weight.own_copy = [local(weight.source, block(weight, z))]
    for weight, copy in ((wt.ckv, raw_copies[1]), (wt.cq, raw_copies[2])):
        copy.wait()
        sort_columns(weight)
        swap_start(weight)

    spread_relay(sv)
    swap_wait(wt.qkv)
    send_inward(wt.qkv, block(wt.qkv, z))
    send_across(wt.qkv, block(wt.qkv, z))
    weight_outward(wt.qkv, block(wt.qkv, z))
    spread_ready(sv)

    for tile in range(D // 128):
        pair = buf.sva[2 * (tile % 2), tile // 2].astype(F32)
        pair = pair + buf.sva[2 * (tile % 2) + 1, tile // 2].astype(F32)
        buf.vec[:, tile * 128:(tile + 1) * 128] = pair
    half = lax.broadcasted_iota(jnp.int32, (16, 128), 1) < 64
    even = (jnp.zeros((16, 128), jnp.int32) + c) == 0
    buf.bias[...] = jnp.zeros((8, D), F32)
    for kind in range(2):
        for tile in range(2):
            first = buf.sva[x, tile + 2 * kind].astype(F32)
            second = buf.sva[2 + x, tile + 2 * kind].astype(F32)
            lower = jnp.where(even, first, pltpu.roll(first, 64, 1))
            upper = jnp.where(even, pltpu.roll(second, 64, 1), second)
            both_heads = jnp.where(half, lower, upper)
            for which in range(2):
                at = 512 * kind + 128 * tile
                buf.bias[which:which + 1, at:at + 128] = both_heads[9 + which:10 + which]
    for tile in range(Z):
        unit = buf.sva[q, tile].astype(F32)
        buf.bias[2:3, 256 * tile:256 * tile + 128] = unit[11:12]
        buf.bias[2:3, 256 * tile + 128:256 * tile + 256] = unit[12:13]
    buf.sg[...] = jnp.zeros((16, D), F32)

    arrived(buf.hb, k_prev)

    def hidden(place):
        return buf.hb[place, :].astype(F32)

    norm(hidden, 0, buf.a1)
    a1 = gather_start(buf.a1)
    relay_inward(wt.qkv)
    relay_near(wt.qkv)
    weight_outward(wt.so, wt.so.source)
    send_inward(wt.so, wt.so.source)
    swap_wait(wt.ckv)
    send_inward(wt.ckv, block(wt.ckv, z))
    for j in range(1, n_sec):
        origin = (s + n_sec - j) % n_sec
        arrived(mem_slot.at[:, part(origin, mem_cols)], k_mem + j)
    mem_copy.wait()
    gather_relay(a1)
    memory = gather_start(buf.m)
    unit_swap_start()
    send_across(wt.so, wt.so.source)
    relay_inward(wt.so)
    swap_wait(wt.cq)
    send_inward(wt.cq, block(wt.cq, z))
    send_inward(wt.co, wt.co.source)
    relay_far(wt.qkv)
    arrived(rows(buf.e3, q), k_cot)
    k_units = slot(4)
    to_middle = send(rows(buf.e3, q), rows(buf.e3b, q), k_units, dev_adj, end)
    gather_ready(a1)
    weight_ready(wt.qkv)
    matmul(buf.a1, wt.qkv.weight, buf.qkv, buf.bias, 0)
    send_across(wt.ckv, block(wt.ckv, z))
    unit_swap_wait(end)
    send_inward(wt.f1, block(wt.f1, z))
    attention(buf.qkv, 0, buf.qkv, 2, 4, True, 13, buf.p1, buf.o1)
    relay_inward(wt.ckv)
    relay_near(wt.so)
    relay_far(wt.so)
    weight_outward(wt.ckv, block(wt.ckv, z))
    send_across(wt.cq, block(wt.cq, z))
    wt.so.own_copy[0].wait()
    weight_ready(wt.so)
    matmul(buf.o1, wt.so.weight, set_a.parts)
    step = reduce_start(set_a)
    send_inward(wt.f2, wt.f2.source)
    relay_inward(wt.cq)
    weight_outward(wt.cq, block(wt.cq, z))
    reduce_relay(step)
    relay_near(wt.ckv)
    gather_finish(memory)
    relay_far(wt.ckv)
    send_across(wt.co, wt.co.source)
    relay_inward(wt.co)
    unit_swap_wait(mid)
    send_across(wt.f1, block(wt.f1, z))
    reduce_ready(step)

    def after_self(i):
        place = part(i, TILE)
        buf.h1[place, :] = hidden(place) + (reduced(step, place) + buf.vec[6:7, :])

    loop(L // TILE, after_self)
    norm(lambda place: buf.h1[place, :], 1, buf.a2)
    a2 = gather_start(buf.a2)
    reduce_done(step)
    relay_near(wt.cq)
    weight_outward(wt.co, wt.co.source)
    relay_far(wt.cq)
    weight_ready(wt.ckv)
    matmul(buf.m, wt.ckv.weight, buf.kv, buf.bias, 1, 1)
    relay_near(wt.co)
    send_across(wt.f2, wt.f2.source)
    relay_far(wt.co)
    relay_inward(wt.f1)

    gather_finish(a2)
    e3 = gather_start(buf.e3, mid)
    weight_ready(wt.cq)
    matmul(buf.a2, wt.cq.weight, buf.q2, buf.bias, 1)
    attention(buf.q2, 0, buf.kv, 0, 2, False, 14, buf.p2, buf.o2)
    wt.co.own_copy[0].wait()
    weight_ready(wt.co)
    matmul(buf.o2, wt.co.weight, set_b.parts)
    step = reduce_start(set_b)
    relay_inward(wt.f2)
    gather_finish(e3)
    reduce_relay(step)
    reduce_ready(step)

    def after_cross(i):
        place = part(i, TILE)
        buf.h2[place, :] = buf.h1[place, :] + (reduced(step, place) + buf.vec[7:8, :])

    loop(L // TILE, after_cross)
    norm(lambda place: buf.h2[place, :], 2, buf.a3)
    send(rows(buf.a3, q), rows(buf.a3b, q), k_units + 1, dev_adj, end)
    a3 = gather_start(buf.a3, mid)
    reduce_done(step)

    def units(normed, activs, slopes):
        def one(j):
            value = nn(normed[...], wt.f1.weight[:, lanes(j)]) + buf.bias[2:3, lanes(j)]
            activ, slope = gelu_pair(value)
            activs[:, lanes(j)] = activ.astype(BF16)
            slopes[:, lanes(j)] = slope.astype(BF16)

        loop(FL // 256, one)

    def units_back(grad, slopes):
        def one(j):
            value = nt(grad[...], wt.f2.weight[lanes(j), :])
            low = (value * slopes[:, lanes(j)].astype(F32)).astype(BF16)
            slopes[:, lanes(j)] = low
            total = jnp.sum(low.astype(F32), 0, keepdims=True)
            buf.sg[10:11, lanes(j)] = buf.sg[10:11, lanes(j)] + total

        loop(FL // 256, one)

    def weight_grads(left, right, left_b, right_b, name):
        def one(j):
            total = tn(left[:, lanes(j)], right[...]) + tn(left_b[:, lanes(j)], right_b[...])
            name.grad[lanes(j), :] = total.astype(BF16)

        loop(left.shape[1] // 256, one)

    def fold(ticket, dst):
        def one(i):
            place = part(i, TILE)
            dst[place, :] = reduced(ticket, place).astype(BF16)

        loop(L // TILE, one)

    def on_mid(fn, *args):
        run_if(mid, lambda: fn(*args))

    def cot_sum(i, carry):
        return carry + jnp.sum(rows(buf.e3, q)[part(i, TILE), :].astype(F32), 0, keepdims=True)

    buf.sg[8:9, :] = lax.fori_loop(0, L // TILE, cot_sum, jnp.zeros((1, D), F32))

    gather_relay(a3)
    arrived(rows(buf.e3b, q), k_units, mid)
    e3b = gather_start(buf.e3b, mid)
    gather_ready(a3)
    inner_ready(wt.f1)
    on_mid(units, buf.a3, buf.g, buf.gp)
    wt.f2.own_copy[0].wait()
    inner_ready(wt.f2)
    on_mid(units_back, buf.e3, buf.gp)
    arrived(rows(buf.a3b, q), k_units + 1, mid)
    a3b = gather_start(buf.a3b, mid)
    gather_relay(e3b)
    on_mid(matmul_back, buf.gp, wt.f1.weight, set_a.parts)
    step = reduce_start(set_a, mid)
    gather_ready(e3b)
    gather_finish(a3b)
    reduce_relay(step)
    on_mid(units, buf.a3b, buf.gb, buf.gpb)
    on_mid(units_back, buf.e3b, buf.gpb)
    on_mid(matmul_back, buf.gpb, wt.f1.weight, set_b.parts)
    step_b = reduce_start(set_b, mid)
    on_mid(matmul, buf.gb, wt.f2.weight, set_c.parts)
    reduce_relay(step_b)
    final = reduce_start(set_c, mid)
    on_mid(weight_grads, buf.g, buf.e3, buf.gb, buf.e3b, wt.f2)
    inner_grad_far(wt.f2)
    on_mid(weight_grads, buf.a3, buf.gp, buf.a3b, buf.gpb, wt.f1)
    inner_grad_far(wt.f1)
    inner_grad_near(wt.f2)
    inner_grad_near(wt.f1)
    reduce_ready(step_b)
    on_mid(fold, step_b, buf.back)
    send(buf.back, buf.back, k_units + 2, dev_adj, mid)

    def store(name):
        def low(place, value):
            rows(name, q)[place, :] = value

        return low

    def units_norm_back(incoming):
        norm_back(
            lambda place: buf.h2[place, :], incoming, 2,
            lambda place: rows(buf.e3, q)[place, :].astype(F32), buf.dh, store(buf.e2), 7,
        )

    reduce_done(e3)
    sent(to_middle)
    reduce_ready(step)
    on_mid(units_norm_back, lambda place: reduced(step, place))
    arrived(buf.back, k_units + 2, end)
    run_if(end, lambda: units_norm_back(lambda place: buf.back[place, :].astype(F32)))
    e2 = gather_start(buf.e2)
    reduce_done(step)
    reduce_done(step_b)
    gather_finish(e2)
    reduce_relay(final)

    weight_grad(buf.o2, buf.e2, wt.co)
    grad_send(wt.co)
    matmul_back(buf.e2, wt.co.weight, buf.do)
    attention_back(buf.q2, 0, buf.kv, 0, 2, buf.p2, buf.do)
    matmul_back(buf.q2, wt.cq.weight, set_b.parts)
    step = reduce_start(set_b)
    weight_grad(buf.a2, buf.q2, wt.cq)
    grad_send(wt.cq)
    reduce_relay(step)
    weight_grad(buf.m, buf.kv, wt.ckv)
    grad_send(wt.ckv)
    matmul_back(buf.kv, wt.ckv.weight, set_a.parts)
    mem_step = reduce_start(set_a)
    column_sums(buf.q2, 0, 1, 9, 2)
    column_sums(buf.kv, 1, 1, 9, 3)
    reduce_ready(final)
    on_mid(fold, final, buf.tail)
    send(buf.tail, buf.tail, k_units + 3, dev_adj, mid)
    reduce_done(final)
    grad_combine(wt.co)
    reduce_ready(step)
    norm_back(
        lambda place: buf.h1[place, :], lambda place: reduced(step, place), 1,
        lambda place: buf.dh[place, :], buf.dh, store(buf.e3), 6,
    )
    e1 = gather_start(buf.e3)
    reduce_done(step)
    grad_combine(wt.cq)
    grad_outward(wt.co)
    gather_finish(e1)
    reduce_relay(mem_step)

    weight_grad(buf.o1, buf.e3, wt.so)
    grad_send(wt.so)
    matmul_back(buf.e3, wt.so.weight, buf.do)
    attention_back(buf.qkv, 0, buf.qkv, 2, 4, buf.p1, buf.do)
    weight_grad(buf.a1, buf.qkv, wt.qkv)
    far_part = grad_send_far(wt.qkv)
    matmul_back(buf.qkv, wt.qkv.weight, set_b.parts)
    step = reduce_start(set_b)
    column_sums(buf.qkv, 0, 1, 9, 0)
    column_sums(buf.qkv, 2, 1, 9, 1)
    inner_grad_combine(wt.f2)
    inner_grad_combine(wt.f1)
    reduce_relay(step)
    grad_combine(wt.ckv)
    grad_outward(wt.cq)
    on_mid(matmul, buf.g, wt.f2.weight, set_c.parts)
    final = reduce_start(set_c, mid)

    reduce_ready(mem_step)
    fold(mem_step, buf.mb)
    k_back = slot(n_sec)
    for j in range(1, n_sec):
        to = (s + j) % n_sec
        send(buf.mb.at[:, part(to, mem_cols)], buf.ml.at[j], k_back + j, (to, d))
    sent(far_part)
    middle_part = grad_send_middle(wt.qkv)
    grad_outward(wt.ckv)
    reduce_ready(step)

    def store_stage(place, value):
        buf.ig[place, :] = value

    norm_back(
        hidden, lambda place: reduced(step, place), 0,
        lambda place: buf.dh[place, :], None, store_stage,
    )
    k_in = slot()
    send(buf.ig, io.input_grad, k_in, ((s + n_sec - 1) % n_sec, d))
    buf.sga[q, z] = buf.sg[...].astype(BF16)
    sums = spread_start(buf.sga, None)
    reduce_relay(final)
    grad_combine(wt.so)
    sent(middle_part)
    grad_send_near(wt.qkv)

    def finish(incoming):
        def one(i):
            place = part(i, TILE)
            total = buf.h2[place, :] + (incoming(place) + buf.vec[8:9, :])
            buf.stage[place, :] = total.astype(BF16)

        loop(L // TILE, one)

    arrived(buf.tail, k_units + 3, end)
    run_if(end, lambda: finish(lambda place: buf.tail[place, :].astype(F32)))
    for j in range(1, n_sec):
        arrived(buf.ml.at[j], k_back + j)

    def memory_total(i):
        place = part(i, TILE)
        total = buf.mb[place, part(s, mem_cols)].astype(F32)
        for j in range(1, n_sec):
            total = total + buf.ml[j, place, :].astype(F32)
        buf.mo[place, :] = total.astype(BF16)

    loop(L // TILE, memory_total)
    result_copies.append(local(buf.mo, io.memory_grad))
    grad_outward(wt.so)
    grad_combine_far(wt.qkv)
    for weight in (wt.co, wt.cq, wt.ckv, wt.f2, wt.f1):
        grad_final(weight)
    spread_relay(sums)
    grad_combine_middle(wt.qkv)
    reduce_ready(final)
    on_mid(finish, lambda place: reduced(final, place))
    result_copies.append(local(buf.stage, io.output))
    grad_outward(wt.qkv)
    grad_final(wt.so)
    last_wait(wt.ckv)
    last_wait(wt.cq)
    unit_last_wait()
    grad_final(wt.qkv)
    spread_ready(sums)

    def per_unit(q_at, at):
        total = buf.sga[q_at, 0, :, at].astype(F32)
        for plane in range(1, Z):
            total = total + buf.sga[q_at, plane, :, at].astype(F32)
        return total

    at = part(d // 2, 128)
    feature = per_unit(0, at)
    for q_at in range(1, P_IN):
        feature = feature + per_unit(q_at, at)
    swapped = pltpu.roll(feature, 64, 1)
    buf.sums[...] = jnp.where((jnp.zeros((16, 128), jnp.int32) + c) == 0, feature, swapped)
    head = d % 8
    at = part(2 * (d // 8) + head // 4, 128)
    low_head, high_head = per_unit(2 * c, at), per_unit(2 * c + 1, at)
    first_half = (jnp.zeros((16, 128), jnp.int32) + (head // 2) % 2) == 0
    low_head = jnp.where(first_half, low_head, pltpu.roll(low_head, 64, 1))
    high_head = jnp.where(first_half, pltpu.roll(high_head, 64, 1), high_head)
    buf.sums[9:10, :] = jnp.where(half, low_head, high_head)[9:10]
    at = part(2 * (d // 8) + 4 + head // 4, 128)
    low_head, high_head = per_unit(2 * c, at), per_unit(2 * c + 1, at)
    low_head = jnp.where(first_half, low_head, pltpu.roll(low_head, 64, 1))
    high_head = jnp.where(first_half, pltpu.roll(high_head, 64, 1), high_head)
    buf.sums[10:11, :] = jnp.where(half, low_head, high_head)[9:10]
    buf.sums[11:12, :] = per_unit(q, part(2 * z, 128))[10:11]
    buf.sums[12:13, :] = per_unit(q, part(2 * z + 1, 128))[10:11]
    result_copies.append(local(buf.sums, io.sums_out))
    last_wait(wt.qkv)
    arrived(io.input_grad, k_in)
    for copy in result_copies:
        copy.wait()
    for record in list(started):
        sent(record)
    assert counter[0] <= SEMS


def buffer_shapes(n_sec, mem_cols):
    tokens, row = (T, D), (L, D)
    shapes = dict(
        sva=(P_IN, Z, 16, 128),
        sga=(P_IN, Z, 16, D),
        hb=row, ig=row, stage=row, mb=row,
        ml=(n_sec, L, mem_cols),
        mo=(L, mem_cols),
        qkv=(T, 768), q2=(T, 256), kv=(T, 512), o1=(T, 256), o2=(T, 256), do=(T, 256),
        p1=(2 * P_IN, 2 * L, L), p2=(2 * P_IN, 2 * L, L),
        g=(T, FL), gp=(T, FL),
        a1=tokens, a2=tokens, a3=tokens, m=tokens, e3=tokens, e2=tokens,
        a3b=tokens, e3b=tokens, gb=(T, FL), gpb=(T, FL), back=row, tail=row,
    )
    exact = dict(vec=(16, D), bias=(8, D), sg=(16, D), sums=(16, 128), h1=row, h2=row, dh=row)
    kinds = {name: pltpu.VMEM(shape, BF16) for name, shape in shapes.items()}
    kinds.update({name: pltpu.VMEM(shape, F32) for name, shape in exact.items()})
    return kinds


REDUCE_SHAPES = dict(
    parts=pltpu.VMEM((T, D), BF16),
    core=pltpu.VMEM((2 * L, D), BF16),
    across=pltpu.VMEM((L, D), BF16),
)


def scratch_of(n_sec, mem_cols):
    scratch = list(buffer_shapes(n_sec, mem_cols).values())
    scratch += 3 * list(REDUCE_SHAPES.values())
    for count, columns, _ in WEIGHTS.values():
        scratch += 2 * [pltpu.VMEM((Z * count, columns), BF16)]
        scratch += 2 * [pltpu.VMEM((count, columns), BF16)]
    for count, columns, _ in list(WEIGHTS.values())[:5]:
        scratch += 3 * [pltpu.VMEM((count, columns), BF16)]
    for columns in (768, 512, 256):
        scratch.append(pltpu.VMEM((64, P_IN * columns), BF16))
        scratch.append(pltpu.VMEM((P_IN, 64, columns), BF16))
    return scratch + [
        pltpu.SemaphoreType.DMA((SEMS,)),
        pltpu.SemaphoreType.DMA((SEMS,)),
        pltpu.SemaphoreType.DMA((48,)),
    ]


def finish_kernel(*refs):
    moved, low, sums = refs[:3], refs[3:10], refs[10]
    moved_out, high, small = refs[11:14], refs[14:21], refs[21:27]
    low_buf, high_buf, moved_buf, sems = refs[27:34], refs[34:41], refs[41:44], refs[44]
    inward = [
        pltpu.make_async_copy(src, dst, sems.at[i])
        for i, (src, dst) in enumerate(zip(low + moved, low_buf + moved_buf))
    ]
    for copy in inward:
        copy.start()
    outward = []
    gain, shift, out_bias, self_bias, cross_bias, unit_bias = small
    gain[0] = sums[0:3, 0:64]
    shift[0] = sums[3:6, 0:64]
    out_bias[0] = sums[6:9, 0:64]
    self_bias[...] = sums[9:10, :]
    cross_bias[...] = sums[10:11, :]
    unit_bias[:, 0:128] = sums[11:12, :]
    unit_bias[:, 128:256] = sums[12:13, :]
    for i, copy in enumerate(inward[:7]):
        copy.wait()
        rows_in = low_buf[i].shape[0]

        def one(j, i=i):
            place = part(j, 16)
            high_buf[i][place, :] = low_buf[i][place, :].astype(F32)

        loop(rows_in // 16, one)
        back = pltpu.make_async_copy(high_buf[i], high[i], sems.at[10 + i])
        back.start()
        outward.append(back)
    for i, copy in enumerate(inward[7:]):
        copy.wait()
        back = pltpu.make_async_copy(moved_buf[i], moved_out[i], sems.at[17 + i])
        back.start()
        outward.append(back)
    for copy in outward:
        copy.wait()


def on_device_planes(
    prev_act, memory, out_cot, tgt_len, src_len, norm_gain, norm_bias, self_qkv, self_qv_bias,
    self_out, cross_q, cross_kv, cross_qv_bias, cross_out, out_bias, fc1, fc1_bias, fc2,
):
    n_sec = lax.axis_size("section")
    mem_cols = memory.shape[2]
    operands = (
        prev_act[0, 0], memory[0], out_cot[0, 0], tgt_len, src_len,
        norm_gain[0], norm_bias[0], out_bias[0], self_qv_bias, cross_qv_bias, fc1_bias,
        self_qkv[0], self_out[0], cross_kv[0], cross_q[0], cross_out[0], fc1[0], fc2[0],
    )
    anywhere = pl.BlockSpec(memory_space=pl.ANY)
    in_specs = 3 * [anywhere] + 2 * [pl.BlockSpec(memory_space=pltpu.SMEM)]
    in_specs += 6 * [pl.BlockSpec(memory_space=pltpu.VMEM)] + 7 * [anywhere]
    out_shapes = [(L, D), (L, D), (L, mem_cols)]
    for count, columns, by_column in WEIGHTS.values():
        out_shapes.append((count // P_IN, P_IN * columns) if by_column else (count, columns))
    sums_shape = jax.ShapeDtypeStruct((16, 128), F32)
    results = pl.pallas_call(
        functools.partial(whole_kernel, n_sec, mem_cols),
        out_shape=[jax.ShapeDtypeStruct(shape, BF16) for shape in out_shapes] + [sums_shape],
        in_specs=in_specs,
        out_specs=[anywhere] * (len(out_shapes) + 1),
        scratch_shapes=scratch_of(n_sec, mem_cols),
        compiler_params=pltpu.CompilerParams(
            collective_id=0, has_side_effects=True, vmem_limit_bytes=64 * 2**20 - 2**16
        ),
        cost_estimate=pl.CostEstimate(
            flops=21 * 10**9, bytes_accessed=20 * 2**20, transcendentals=3 * 10**6
        ),
    )(*operands)
    shapes = [result.shape for result in results]
    vmem = pl.BlockSpec(memory_space=pltpu.VMEM)
    finished = pl.pallas_call(
        finish_kernel,
        out_shape=[jax.ShapeDtypeStruct(shape, BF16) for shape in shapes[:3]]
        + [jax.ShapeDtypeStruct(shape, F32) for shape in shapes[3:10]]
        + [jax.ShapeDtypeStruct(shape, F32) for shape in [(1, 3, 64)] * 3 + [(1, 128), (1, 128), (1, 256)]],
        in_specs=10 * [anywhere] + [vmem],
        out_specs=10 * [anywhere] + 6 * [vmem],
        scratch_shapes=[pltpu.VMEM(shape, BF16) for shape in shapes[3:10]]
        + [pltpu.VMEM(shape, F32) for shape in shapes[3:10]]
        + [pltpu.VMEM(shape, BF16) for shape in shapes[:3]]
        + [pltpu.SemaphoreType.DMA((20,))],
        compiler_params=pltpu.CompilerParams(vmem_limit_bytes=63 * 2**20),
        cost_estimate=pl.CostEstimate(flops=0, bytes_accessed=9 * 2**20, transcendentals=0),
    )(*results)
    (
        output, input_grad, memory_grad, g_qkv, g_so, g_ckv, g_cq, g_co, g_f1, g_f2,
        gain, shift, biases, self_biases, cross_biases, units,
    ) = finished
    return (
        output[None, None],
        input_grad[None, None],
        memory_grad[None],
        gain,
        shift,
        g_qkv[None],
        self_biases,
        g_so[None],
        g_cq[None],
        g_ckv[None],
        cross_biases,
        g_co[None],
        biases,
        g_f1[None],
        units,
        g_f2[None],
    )


def solution(mesh):
    in_specs = (
        P("section", "dp", None, None),
        P("dp", None, "section"),
        P("section", "dp", None, None),
        P("dp"),
        P("dp"),
        P("section", None, "dp"),
        P("section", None, "dp"),
        P("section", "dp", None),
        P("section", "dp"),
        P("section", "dp", None),
        P("section", "dp", None),
        P("section", "dp", None),
        P("section", "dp"),
        P("section", "dp", None),
        P("section", None, "dp"),
        P("section", "dp", None),
        P("section", "dp"),
        P("section", "dp", None),
    )
    out_specs = (
        P("section", "dp", None, None),
        P("section", "dp", None, None),
        P("dp", None, "section"),
        P("section", None, "dp"),
        P("section", None, "dp"),
        P("section", "dp", None),
        P("section", "dp"),
        P("section", "dp", None),
        P("section", "dp", None),
        P("section", "dp", None),
        P("section", "dp"),
        P("section", "dp", None),
        P("section", None, "dp"),
        P("section", "dp", None),
        P("section", "dp"),
        P("section", "dp", None),
    )
    planes = Z * P_IN
    fits = mesh.shape["dp"] == planes
    return jax.shard_map(
        on_device_planes if fits else on_device, mesh=mesh, in_specs=in_specs, out_specs=out_specs, check_vma=False
    )
```

```python
import functools
from types import SimpleNamespace

import jax
import jax.numpy as jnp
from jax import lax
from jax.experimental import pallas as pl
from jax.experimental.pallas import tpu as pltpu
from jax.sharding import PartitionSpec as P

H = 16
HD = 64


EPSILON = 1e-05
MASKED = -1000000000.0


def passed_along(value, axis, by):
    length = lax.axis_size(axis)
    return lax.ppermute(value, axis, [(i, (i + by) % length) for i in range(length)])


def norm_fwd(rows, gain, shift_term):
    center = rows - jnp.mean(rows, -1, keepdims=True)
    scale = lax.rsqrt(jnp.mean(center * center, -1, keepdims=True) + EPSILON)
    return center * scale * gain + shift_term


def gelu_exact(values):
    return jax.nn.gelu(values, approximate=False)


def product(left, right):
    return jnp.dot(left, right, preferred_element_type=jnp.float32)


def product_right_t(left, right):
    return lax.dot_general(
        left, right, (((1,), (1,)), ((), ())), preferred_element_type=jnp.float32
    )


def product_left_t(left, right):
    return lax.dot_general(
        left, right, (((0,), (0,)), ((), ())), preferred_element_type=jnp.float32
    )


def split_heads(flat, batch_rows):
    return flat.reshape(batch_rows, -1, H, HD)


def softmax_probs(query, key_rows, allowed):
    scores = jnp.einsum(
        "rthd,rshd->rhts", query, key_rows, preferred_element_type=jnp.float32
    ) * HD ** (-0.5)
    scores = jnp.where(allowed[:, None], scores, MASKED)
    weights = jnp.exp(scores - jnp.max(scores, -1, keepdims=True))
    return weights / jnp.sum(weights, -1, keepdims=True)


def attend_fwd(query, key_rows, value_rows, allowed):
    probs = softmax_probs(query, key_rows, allowed)
    mixed = jnp.einsum(
        "rhts,rshd->rthd",
        probs.astype(jnp.bfloat16),
        value_rows,
        preferred_element_type=jnp.float32,
    )
    return mixed.reshape(mixed.shape[0] * mixed.shape[1], -1).astype(jnp.bfloat16)


def attend_back(query, key_rows, value_rows, allowed, grad_mixed):
    probs = softmax_probs(query, key_rows, allowed)
    grad_heads = grad_mixed.reshape(query.shape)
    grad_probs = jnp.einsum(
        "rthd,rshd->rhts", grad_heads, value_rows, preferred_element_type=jnp.float32
    )
    delta = jnp.sum(probs * grad_probs, -1, keepdims=True)
    grad_scores = (probs * (grad_probs - delta)).astype(jnp.bfloat16)
    scale = HD ** (-0.5)
    grad_query = (
        jnp.einsum("rhts,rshd->rthd", grad_scores, key_rows, preferred_element_type=jnp.float32)
        * scale
    )
    grad_keys = (
        jnp.einsum("rhts,rthd->rshd", grad_scores, query, preferred_element_type=jnp.float32)
        * scale
    )
    grad_values = jnp.einsum(
        "rhts,rthd->rshd",
        probs.astype(jnp.bfloat16),
        grad_heads,
        preferred_element_type=jnp.float32,
    )
    width = query.shape[2] * query.shape[3]
    return (
        grad_query.reshape(-1, width).astype(jnp.bfloat16),
        grad_keys.reshape(-1, width).astype(jnp.bfloat16),
        grad_values.reshape(-1, width).astype(jnp.bfloat16),
    )


def unpack(pieces):
    return tuple((piece[0] for piece in pieces))


def on_device(
    prev_act,
    memory,
    out_cot,
    tgt_len,
    src_len,
    norm_gain,
    norm_bias,
    self_qkv,
    self_qv_bias,
    self_out,
    cross_q,
    cross_kv,
    cross_qv_bias,
    cross_out,
    out_bias,
    fc1,
    fc1_bias,
    fc2,
):
    fetched = unpack(
        (
            lax.all_gather(norm_gain, "dp", axis=2, tiled=True),
            lax.all_gather(norm_bias, "dp", axis=2, tiled=True),
            lax.all_gather(self_qkv, "dp", axis=1, tiled=True),
            lax.all_gather(self_qv_bias, "dp", axis=1, tiled=True),
            lax.all_gather(self_out, "dp", axis=1, tiled=True),
            lax.all_gather(cross_q, "dp", axis=1, tiled=True),
            lax.all_gather(cross_kv, "dp", axis=1, tiled=True),
            lax.all_gather(cross_qv_bias, "dp", axis=1, tiled=True),
            lax.all_gather(cross_out, "dp", axis=1, tiled=True),
            lax.all_gather(out_bias, "dp", axis=2, tiled=True),
            lax.all_gather(fc1, "dp", axis=1, tiled=True),
            lax.all_gather(fc1_bias, "dp", axis=1, tiled=True),
            lax.all_gather(fc2, "dp", axis=1, tiled=True),
        )
    )
    gains, shifts, w_sqkv, b_sqv, w_sout, w_cq, w_ckv, b_cqv, w_cout, b_out, w_one, b_one, w_two = (
        fetched
    )
    gain_f = gains.astype(jnp.float32)
    shift_f = shifts.astype(jnp.float32)
    sqv_f = b_sqv.astype(jnp.float32)
    cqv_f = b_cqv.astype(jnp.float32)
    out_f = b_out.astype(jnp.float32)
    one_f = b_one.astype(jnp.float32)
    source = passed_along(prev_act, "section", 1)[0]
    batch_rows, length, width = source.shape
    encoded = lax.all_gather(memory, "section", axis=2, tiled=True)
    mem_flat = encoded.reshape(-1, width)
    places = jnp.arange(length)
    self_ok = (places[None, None, :] <= places[None, :, None]) & (
        places[None, None, :] < tgt_len[:, None, None]
    )
    cross_ok = jnp.arange(encoded.shape[1])[None, None, :] < src_len[:, None, None]
    resid = source.astype(jnp.float32).reshape(-1, width)
    normed_one, pull_one = jax.vjp(norm_fwd, resid, gain_f[0], shift_f[0])
    first_in = normed_one.astype(jnp.bfloat16)
    joint = product(first_in, w_sqkv)
    query_self = (joint[:, :width] + sqv_f[:width]).astype(jnp.bfloat16)
    keys_self = joint[:, width : 2 * width].astype(jnp.bfloat16)
    values_self = (joint[:, 2 * width :] + sqv_f[width:]).astype(jnp.bfloat16)
    self_mixed = attend_fwd(
        split_heads(query_self, batch_rows),
        split_heads(keys_self, batch_rows),
        split_heads(values_self, batch_rows),
        self_ok,
    )
    after_self = resid + (product(self_mixed, w_sout) + out_f[0])
    normed_two, pull_two = jax.vjp(norm_fwd, after_self, gain_f[1], shift_f[1])
    second_in = normed_two.astype(jnp.bfloat16)
    query_cross = (product(second_in, w_cq) + cqv_f[:width]).astype(jnp.bfloat16)
    memory_proj = product(mem_flat, w_ckv)
    keys_cross = memory_proj[:, :width].astype(jnp.bfloat16)
    values_cross = (memory_proj[:, width:] + cqv_f[width:]).astype(jnp.bfloat16)
    cross_mixed = attend_fwd(
        split_heads(query_cross, batch_rows),
        split_heads(keys_cross, batch_rows),
        split_heads(values_cross, batch_rows),
        cross_ok,
    )
    after_cross = after_self + (product(cross_mixed, w_cout) + out_f[1])
    normed_three, pull_three = jax.vjp(norm_fwd, after_cross, gain_f[2], shift_f[2])
    third_in = normed_three.astype(jnp.bfloat16)
    pre_act = product(third_in, w_one) + one_f
    activ, pull_gelu = jax.vjp(gelu_exact, pre_act)
    act_low = activ.astype(jnp.bfloat16)
    result = after_cross + (product(act_low, w_two) + out_f[2])
    output = result.astype(jnp.bfloat16).reshape(1, batch_rows, length, width)
    (
        unused_gains,
        unused_shifts,
        w_sqkv,
        unused_sqv,
        w_sout,
        w_cq,
        w_ckv,
        unused_cqv,
        w_cout,
        unused_out,
        w_one,
        unused_one,
        w_two,
    ) = fetched
    grad_out = passed_along(out_cot, "section", -1)[0].astype(jnp.float32).reshape(-1, width)
    ffn_grad = grad_out.astype(jnp.bfloat16)
    grad_fc2 = product_left_t(act_low, ffn_grad)
    grad_b2 = jnp.sum(ffn_grad, 0, dtype=jnp.float32)
    grad_act = product_right_t(ffn_grad, w_two)
    (grad_pre,) = pull_gelu(grad_act)
    pre_low = grad_pre.astype(jnp.bfloat16)
    grad_fc1 = product_left_t(third_in, pre_low)
    grad_b1 = jnp.sum(pre_low, 0, dtype=jnp.float32)
    grad_mid, grad_gain3, grad_shift3 = pull_three(product_right_t(pre_low, w_one))
    grad_mid = grad_mid + grad_out
    cross_grad = grad_mid.astype(jnp.bfloat16)
    grad_cout = product_left_t(cross_mixed, cross_grad)
    grad_bco = jnp.sum(cross_grad, 0, dtype=jnp.float32)
    grad_cmix = product_right_t(cross_grad, w_cout).astype(jnp.bfloat16)
    grad_qc, grad_kc, grad_vc = attend_back(
        split_heads(query_cross, batch_rows),
        split_heads(keys_cross, batch_rows),
        split_heads(values_cross, batch_rows),
        cross_ok,
        grad_cmix,
    )
    grad_cq = product_left_t(second_in, grad_qc)
    grad_kv = jnp.concatenate([grad_kc, grad_vc], -1)
    grad_ckv = product_left_t(mem_flat, grad_kv)
    grad_cqv = jnp.concatenate(
        [jnp.sum(grad_qc, 0, dtype=jnp.float32), jnp.sum(grad_vc, 0, dtype=jnp.float32)]
    )
    grad_memory = product_right_t(grad_kv, w_ckv).reshape(encoded.shape)
    memory_grad = lax.psum_scatter(
        grad_memory.astype(jnp.bfloat16), "section", scatter_dimension=2, tiled=True
    )
    grad_after, grad_gain2, grad_shift2 = pull_two(product_right_t(grad_qc, w_cq))
    grad_after = grad_after + grad_mid
    self_grad = grad_after.astype(jnp.bfloat16)
    grad_sout = product_left_t(self_mixed, self_grad)
    grad_bso = jnp.sum(self_grad, 0, dtype=jnp.float32)
    grad_smix = product_right_t(self_grad, w_sout).astype(jnp.bfloat16)
    grad_qs, grad_ks, grad_vs = attend_back(
        split_heads(query_self, batch_rows),
        split_heads(keys_self, batch_rows),
        split_heads(values_self, batch_rows),
        self_ok,
        grad_smix,
    )
    grad_qkv = jnp.concatenate([grad_qs, grad_ks, grad_vs], -1)
    grad_sqkv = product_left_t(first_in, grad_qkv)
    grad_sqv = jnp.concatenate(
        [jnp.sum(grad_qs, 0, dtype=jnp.float32), jnp.sum(grad_vs, 0, dtype=jnp.float32)]
    )
    grad_in, grad_gain1, grad_shift1 = pull_one(product_right_t(grad_qkv, w_sqkv))
    grad_in = grad_in + grad_after
    input_grad = passed_along(
        grad_in.astype(jnp.bfloat16).reshape(1, batch_rows, length, width), "section", -1
    )
    grad_gain = jnp.stack([grad_gain1, grad_gain2, grad_gain3])
    grad_shift = jnp.stack([grad_shift1, grad_shift2, grad_shift3])
    grad_obias = jnp.stack([grad_bso, grad_bco, grad_b2])
    sums = (
        lax.psum_scatter(
            grad_gain.astype(jnp.bfloat16), "dp", scatter_dimension=1, tiled=True
        ).astype(jnp.float32),
        lax.psum_scatter(
            grad_shift.astype(jnp.bfloat16), "dp", scatter_dimension=1, tiled=True
        ).astype(jnp.float32),
        lax.psum_scatter(
            grad_sqkv.astype(jnp.bfloat16), "dp", scatter_dimension=0, tiled=True
        ).astype(jnp.float32),
        lax.psum_scatter(
            grad_sqv.astype(jnp.bfloat16), "dp", scatter_dimension=0, tiled=True
        ).astype(jnp.float32),
        lax.psum_scatter(
            grad_sout.astype(jnp.bfloat16), "dp", scatter_dimension=0, tiled=True
        ).astype(jnp.float32),
        lax.psum_scatter(
            grad_cq.astype(jnp.bfloat16), "dp", scatter_dimension=0, tiled=True
        ).astype(jnp.float32),
        lax.psum_scatter(
            grad_ckv.astype(jnp.bfloat16), "dp", scatter_dimension=0, tiled=True
        ).astype(jnp.float32),
        lax.psum_scatter(
            grad_cqv.astype(jnp.bfloat16), "dp", scatter_dimension=0, tiled=True
        ).astype(jnp.float32),
        lax.psum_scatter(
            grad_cout.astype(jnp.bfloat16), "dp", scatter_dimension=0, tiled=True
        ).astype(jnp.float32),
        lax.psum_scatter(
            grad_obias.astype(jnp.bfloat16), "dp", scatter_dimension=1, tiled=True
        ).astype(jnp.float32),
        lax.psum_scatter(
            grad_fc1.astype(jnp.bfloat16), "dp", scatter_dimension=0, tiled=True
        ).astype(jnp.float32),
        lax.psum_scatter(
            grad_b1.astype(jnp.bfloat16), "dp", scatter_dimension=0, tiled=True
        ).astype(jnp.float32),
        lax.psum_scatter(
            grad_fc2.astype(jnp.bfloat16), "dp", scatter_dimension=0, tiled=True
        ).astype(jnp.float32),
    )
    return (
        output,
        input_grad,
        memory_grad,
        sums[0][None],
        sums[1][None],
        sums[2][None],
        sums[3][None],
        sums[4][None],
        sums[5][None],
        sums[6][None],
        sums[7][None],
        sums[8][None],
        sums[9][None],
        sums[10][None],
        sums[11][None],
        sums[12][None],
    )


Z = 4
P_IN = 4
L = 192
D = 1024
T = P_IN * L
FL = 1024
TILE = 32
MESH = pl.DeviceIdType.MESH
F32 = jnp.float32
BF16 = jnp.bfloat16

WEIGHTS = dict(
    qkv=(256, 768, True),
    so=(64, 1024, False),
    ckv=(256, 512, True),
    cq=(256, 256, True),
    co=(64, 1024, False),
    f1=(256, 1024, True),
    f2=(256, 1024, False),
)
SEMS = 320


def run_if(cond, fn):
    if cond is None:
        fn()
    else:
        pl.when(cond)(fn)


def part(index, size, step=None):
    return pl.ds(pl.multiple_of(index * size, size), size if step is None else step)


def nn(left, right):
    return jnp.dot(left, right, preferred_element_type=F32)


def nt(left, right):
    return lax.dot_general(left, right, (((1,), (1,)), ((), ())), preferred_element_type=F32)


def tn(left, right):
    return lax.dot_general(left, right, (((0,), (0,)), ((), ())), preferred_element_type=F32)


def loop(count, body, unroll=1, first=0):
    def step(index, carry):
        body(index)
        return carry

    lax.fori_loop(first, first + count, step, 0, unroll=unroll)


HALF = L // 2
TILES = HALF // TILE


def gelu_pair(values):
    bell = jnp.exp(-0.5 * values * values)
    step = 1.0 / (1.0 + 0.3275911 * 0.7071067811865476 * jnp.abs(values))
    series = step * (
        0.254829592
        + step
        * (-0.284496736 + step * (1.421413741 + step * (-1.453152027 + step * 1.061405429)))
    )
    above = 0.5 * series * bell
    below = jnp.where(values < 0, above, 1.0 - above)
    return values * below, below + values * bell * 0.3989422804014327


def whiten(rows):
    center = rows - jnp.mean(rows, -1, keepdims=True)
    scale = lax.rsqrt(jnp.mean(center * center, -1, keepdims=True) + EPSILON)
    return center * scale, scale


def whole_kernel(n_sec, mem_cols, *refs):
    given = iter(refs)

    def take(names):
        return SimpleNamespace(**{name: next(given) for name in names})

    def take_weights(**fields):
        for name in WEIGHTS:
            for field in fields:
                setattr(getattr(wt, name), field, next(given))

    wt = SimpleNamespace(**{name: SimpleNamespace() for name in WEIGHTS})
    io = take(
        dict(
            prev=0, mem=0, cot=0, tgt=0, src=0, gain=0, shift=0, out_bias=0,
            self_bias=0, cross_bias=0, unit_bias=0,
        )
    )
    take_weights(source=0)
    vars(io).update(vars(take(dict(output=0, input_grad=0, memory_grad=0))))
    take_weights(result=0)
    vars(io).update(vars(take(dict(sums_out=0))))
    buf = take(buffer_shapes(n_sec, mem_cols))
    set_a, set_b, set_c = (take(REDUCE_SHAPES) for _ in range(3))
    take_weights(weight=0, grad=0, near=0, far=0)
    for weight in (wt.qkv, wt.so, wt.ckv, wt.cq, wt.co):
        weight.to_diag, weight.to_opp, weight.through = next(given), next(given), next(given)
    for weight in (wt.qkv, wt.ckv, wt.cq):
        weight.raw, weight.sorted = next(given), next(given)
    send_sems, recv_sems, local_sems = given

    s = lax.axis_index("section")
    d = lax.axis_index("dp")
    z, q = d // P_IN, d % P_IN
    x, c = q // 2, q % 2
    end = (z % 3) == 0
    mid = (z % 3) != 0
    q_core = q + 1 - 2 * c
    q_x = q + 2 - 4 * x
    q_xc = q_x + 1 - 2 * c
    z_adj = z + 1 - 2 * (z % 2)
    z_opp = 3 - z
    z_diag = (z + 2) % 4
    dev_core, dev_x, dev_xc = (s, z * P_IN + q_core), (s, z * P_IN + q_x), (s, z * P_IN + q_xc)
    dev_adj, dev_opp, dev_diag = (s, z_adj * P_IN + q), (s, z_opp * P_IN + q), (s, z_diag * P_IN + q)
    in_plane = ((q_core, dev_core), (q_x, dev_x), (q_xc, dev_xc))

    counter = [0]
    started = []
    local_counter = [0]

    def slot(count=1):
        counter[0] += count
        return counter[0] - count

    def remote(src, dst, k, device):
        return pltpu.make_async_remote_copy(
            src_ref=src, dst_ref=dst, send_sem=send_sems.at[k], recv_sem=recv_sems.at[k],
            device_id=device, device_id_type=MESH,
        )

    def send(src, dst, k, device, cond=None):
        copy = remote(src, dst, k, device)
        run_if(cond, copy.start)
        record = [copy, cond]
        started.append(record)
        return record

    def sent(record):
        run_if(record[1], record[0].wait_send)
        started[:] = [other for other in started if other is not record]

    def arrived(dst, k, cond=None):
        run_if(cond, remote(dst, dst, k, dev_core).wait_recv)

    def local(src, dst, cond=None):
        copy = pltpu.make_async_copy(src, dst, local_sems.at[local_counter[0]])
        local_counter[0] += 1
        run_if(cond, copy.start)
        return copy

    def keep(src, dst, cond=None):
        result_copies.append((local(src, dst, cond), cond))

    def rows(rows_of, index):
        return rows_of.at[part(index, L)]

    for name, (count, _, by_column) in WEIGHTS.items():
        weight = getattr(wt, name)
        weight.count, weight.by_column = count, by_column
        weight.to_use, weight.swap, weight.to_sum, weight.last = slot(5), slot(3), slot(6), slot(3)

    def block(name, index):
        return name.weight.at[part(index, name.count)]

    def send_inward(name, src):
        send(src, block(name, z), name.to_use, dev_adj, end)

    def send_across(name, src):
        send(src, block(name, z), name.to_use + 1, dev_opp, mid)

    def weight_outward(name, src):
        send(src, block(name, z), name.to_use, dev_adj, mid)

    def relay_inward(name):
        k = name.to_use
        arrived(block(name, z_adj), k, mid)
        send(block(name, z_adj), block(name, z_adj), k + 2, dev_opp, mid)

    def relay_near(name):
        k = name.to_use
        arrived(block(name, z_opp), k + 1, mid)
        send(block(name, z_opp), block(name, z_opp), k + 3, dev_adj, mid)

    def relay_far(name):
        k = name.to_use
        arrived(block(name, z_diag), k + 2, mid)
        send(block(name, z_diag), block(name, z_diag), k + 4, dev_adj, mid)

    def weight_ready(name):
        k = name.to_use
        arrived(block(name, z_adj), k, end)
        arrived(block(name, z_diag), k + 3, end)
        arrived(block(name, z_opp), k + 4, end)

    def inner_ready(name):
        k = name.to_use
        arrived(block(name, z_opp), k + 1, mid)
        arrived(block(name, z_diag), k + 2, mid)


    def swap_start(name):
        size = name.count // P_IN
        place = name.weight.at[part(z * P_IN + q, size)]
        name.swapped = [
            send(name.sorted.at[q_to], place, name.swap + j, device)
            for j, (q_to, device) in enumerate(in_plane)
        ]
        name.own_copy = [local(name.sorted.at[q], place)]

    def swap_wait(name):
        size = name.count // P_IN
        for j, (q_from, _) in enumerate(in_plane):
            arrived(name.weight.at[part(z * P_IN + q_from, size)], name.swap + j)
        for copy in name.own_copy:
            copy.wait()
        for record in name.swapped:
            sent(record)

    def halves(first, second, odd):
        if odd:
            first = pltpu.roll(first, 64, 1)
        else:
            second = pltpu.roll(second, 64, 1)
        lane = lax.broadcasted_iota(jnp.int32, first.shape, 1)
        return jnp.where(lane < 64, first, second)

    def tile_of(index):
        return slice(index * 128, index * 128 + 128)

    def sort_columns(name):
        for q_to in range(P_IN):
            for tile in range(name.sorted.shape[2] // 128):
                at = 4 * tile + q_to // 2
                first = name.raw[:, tile_of(at)].astype(F32)
                second = name.raw[:, tile_of(at + 2)].astype(F32)
                name.sorted[q_to, :, tile_of(tile)] = halves(first, second, q_to % 2).astype(BF16)

    def unsort_columns(name):
        for tile in range(name.raw.shape[1] // 128):
            group, u = tile // 8, tile % 8
            at = 2 * group + u // 4
            first = name.sorted[2 * (u % 2), :, tile_of(at)].astype(F32)
            second = name.sorted[2 * (u % 2) + 1, :, tile_of(at)].astype(F32)
            name.raw[:, tile_of(tile)] = halves(first, second, (u // 2) % 2).astype(BF16)

    unit_swap, unit_last = slot(3 * Z), slot(3 * Z)

    def unit_columns(rows_of, tile, q_at):
        return rows_of.at[:, part(tile * P_IN + q_at, 256)]

    def unit_swap_start():
        size = wt.f1.count // P_IN
        place = wt.f1.weight.at[part(z * P_IN + q, size)]
        wt.f1.own_copy = []
        for tile in range(Z):
            at = place.at[:, part(tile, 256)]
            for j, (q_to, device) in enumerate(in_plane):
                send(unit_columns(wt.f1.source, tile, q_to), at, unit_swap + 3 * tile + j, device)
            wt.f1.own_copy.append(local(unit_columns(wt.f1.source, tile, q), at))

    def unit_swap_wait(cond):
        size = wt.f1.count // P_IN
        for tile in range(Z):
            for j, (q_from, _) in enumerate(in_plane):
                place = wt.f1.weight.at[part(z * P_IN + q_from, size)]
                arrived(place.at[:, part(tile, 256)], unit_swap + 3 * tile + j, cond)
        for copy in wt.f1.own_copy:
            run_if(cond, copy.wait)

    def grad_block(name, index):
        return name.grad.at[part(index, name.count)]

    def grad_send_far(name):
        return send(grad_block(name, z_opp), name.to_diag, name.to_sum, dev_adj, end)

    def grad_send_middle(name):
        return send(grad_block(name, z_diag), name.to_opp, name.to_sum + 1, dev_adj, end)

    def grad_send_near(name):
        return send(grad_block(name, z_adj), name.near, name.to_sum + 2, dev_adj, end)

    def grad_send(name):
        grad_send_far(name)
        grad_send_middle(name)
        grad_send_near(name)

    def add_rows(count, body):
        size = min(count, 64)
        loop(count // size, lambda i: body(part(i, size)))

    def grad_add(name, landed, index):
        def one(place):
            own = grad_block(name, index)[place, :].astype(F32)
            landed[place, :] = (own + landed[place, :].astype(F32)).astype(BF16)

        add_rows(name.count, one)

    def grad_combine_far(name):
        k = name.to_sum
        arrived(name.to_diag, k, mid)
        run_if(mid, lambda: grad_add(name, name.to_diag, z_diag))
        send(name.to_diag, name.through, k + 3, dev_opp, mid)

    def grad_combine_middle(name):
        k = name.to_sum
        arrived(name.to_opp, k + 1, mid)
        run_if(mid, lambda: grad_add(name, name.to_opp, z_opp))
        send(name.to_opp, name.far, k + 4, dev_opp, mid)

    def grad_combine(name):
        grad_combine_far(name)
        grad_combine_middle(name)

    def grad_outward(name):
        k = name.to_sum
        arrived(name.through, k + 3, mid)
        run_if(mid, lambda: grad_add(name, name.through, z_adj))
        send(name.through, name.near, k + 5, dev_adj, mid)

    result_copies = []

    def inner_grad_far(name):
        send(grad_block(name, z_diag), name.far, name.to_sum, dev_opp, mid)

    def inner_grad_near(name):
        send(grad_block(name, z_opp), name.near, name.to_sum + 1, dev_opp, mid)

    def inner_grad_combine(name):
        k = name.to_sum

        def add():
            arrived(name.far, k)

            def one(place):
                own = grad_block(name, z_adj)[place, :].astype(F32)
                name.far[place, :] = (own + name.far[place, :].astype(F32)).astype(BF16)

            add_rows(name.count, one)

        run_if(mid, add)
        send(name.far, name.near, k + 2, dev_adj, mid)

    def inner_grad_total(name, cond):
        k = name.to_sum
        if cond is end:
            arrived(name.near, k + 2, end)
        else:
            arrived(name.near, k + 1, mid)
            run_if(mid, lambda: grad_add(name, name.near, z))

    def grad_total(name):
        k = name.to_sum
        arrived(name.near, k + 5, end)
        arrived(name.near, k + 2, mid)
        arrived(name.far, k + 4, mid)

        def add_far():
            def one(place):
                total = name.near[place, :].astype(F32) + name.far[place, :].astype(F32)
                name.near[place, :] = (total + grad_block(name, z)[place, :].astype(F32)).astype(BF16)

            add_rows(name.count, one)

        run_if(mid, add_far)
        run_if(end, lambda: grad_add(name, name.near, z))

    def grad_final(name):
        grad_total(name)
        if name.by_column:
            size = name.count // P_IN
            for j, (q_to, device) in enumerate(in_plane):
                src = name.near.at[part(q_to, size)]
                send(src, name.sorted.at[q], name.last + j, device)
            src = name.near.at[part(q, size)]
            name.own_copy = [local(src, name.sorted.at[q])]
        else:
            keep(name.near, name.result)

    def inner_final(cond):
        inner_grad_total(wt.f2, cond)
        keep(wt.f2.near, wt.f2.result, cond)
        inner_grad_total(wt.f1, cond)
        size = wt.f1.count // P_IN
        for tile in range(Z):
            dst = unit_columns(wt.f1.result, tile, q)
            for j, (q_to, device) in enumerate(in_plane):
                src = wt.f1.near.at[part(q_to, size), part(tile, 256)]
                send(src, dst, unit_last + 3 * tile + j, device, cond)
            keep(wt.f1.near.at[part(q, size), part(tile, 256)], dst, cond)

    def last_wait(name):
        for j, (q_from, _) in enumerate(in_plane):
            arrived(name.sorted.at[q_from], name.last + j)
        for copy in name.own_copy:
            copy.wait()
        unsort_columns(name)
        keep(name.raw, name.result)

    def unit_last_wait():
        for tile in range(Z):
            for j, (q_from, _) in enumerate(in_plane):
                place = unit_columns(wt.f1.result, tile, q_from)
                arrived(place, unit_last + 3 * tile + j)

    def piece(name, index, h, parts):
        size = L // parts
        return name.at[part(index * parts + h, size)]

    def half_major(name, index, h, parts=2):
        return name.at[part(h * P_IN + index, HALF)]

    def gather_open(name, cond=None, parts=1, lay=piece):
        return name, slot(3 * parts), [], cond, parts, lay

    def gather_part(ticket, h, cond=None):
        name, k, records, usual, parts, lay = ticket
        cond = usual if cond is None else cond
        own = lay(name, q, h, parts)
        records.append(send(own, own, k + 3 * h, dev_x, cond))
        records.append(send(own, own, k + 3 * h + 1, dev_core, cond))

    def gather_start(name, cond=None):
        ticket = gather_open(name, cond)
        gather_part(ticket, 0)
        return ticket

    def gather_relay_part(ticket, h):
        name, k, records, cond, parts, lay = ticket
        other = lay(name, q_x, h, parts)
        arrived(other, k + 3 * h, cond)
        records.append(send(other, other, k + 3 * h + 2, dev_core, cond))

    def gather_ready_part(ticket, h):
        name, k, _, cond, parts, lay = ticket
        arrived(lay(name, q_core, h, parts), k + 3 * h + 1, cond)
        arrived(lay(name, q_xc, h, parts), k + 3 * h + 2, cond)

    def gather_relay(ticket):
        for h in range(ticket[4]):
            gather_relay_part(ticket, h)

    def gather_ready(ticket):
        for h in range(ticket[4]):
            gather_ready_part(ticket, h)

    def gather_finish(ticket):
        gather_relay(ticket)
        gather_ready(ticket)

    def reduce_start(which, cond=None):
        k = slot(4)
        out = which.parts
        first = send(rows(out, q_xc), rows(which.core, 1), k, dev_core, cond)
        second = send(rows(out, q_core), rows(which.core, 0), k + 1, dev_core, cond)
        return which, k, [first, second], cond, piece

    def reduce_open(which, cond):
        return which, slot(6), [], cond, half_major

    def reduce_start_half(ticket, h):
        which, k, records, cond, lay = ticket
        for j, index in ((1, q_xc), (0, q_core)):
            src, dst = lay(which.parts, index, h), piece(which.core, j, h, 2)
            records.append(send(src, dst, k + 4 * h + 1 - j, dev_core, cond))

    def reduce_relay_half(ticket, h):
        which, k, records, cond, lay = ticket
        landed = piece(which.core, 1, h, 2)
        if lay is half_major:
            arrived(landed, k + 4 * h, cond)
        elif h == 0:
            arrived(rows(which.core, 1), k, cond)
        mine = lay(which.parts, q_x, h, 2)

        def add():
            def one(i):
                place = part(i, TILE)
                total = mine[place, :].astype(F32) + landed[place, :].astype(F32)
                mine[place, :] = total.astype(BF16)

            loop(TILES, one)

        run_if(cond, add)
        dst = which.across.at[part(h, HALF)]
        records.append(send(mine, dst, k + 2 + h, dev_x, cond))
        return records[-1]

    def reduce_relay(ticket):
        reduce_relay_half(ticket, 0)
        reduce_relay_half(ticket, 1)

    def reduce_relay_paced(ticket):
        record = reduce_relay_half(ticket, 0)
        ticket[2][:] = [other for other in ticket[2] if other is not record]
        sent(record)
        reduce_relay_half(ticket, 1)

    def reduce_ready_half(ticket, h):
        which, k, _, cond, lay = ticket
        if lay is half_major:
            arrived(piece(which.core, 0, h, 2), k + 4 * h + 1, cond)
        elif h == 0:
            arrived(rows(which.core, 0), k + 1, cond)
        arrived(which.across.at[part(h, HALF)], k + 2 + h, cond)

    def reduce_ready(ticket):
        reduce_ready_half(ticket, 0)
        reduce_ready_half(ticket, 1)

    def reduced(ticket, place):
        which = ticket[0]
        total = rows(which.parts, q)[place, :].astype(F32)
        total = total + rows(which.core, 0)[place, :].astype(F32)
        return total + which.across[place, :].astype(F32)

    def fold(ticket, dst, halves=(0, 1)):
        which, lay = ticket[0], ticket[4]
        for h in halves:
            mine, landed = lay(which.parts, q, h, 2), piece(which.core, 0, h, 2)

            def one(i, h=h, mine=mine, landed=landed):
                place, here = part(i, TILE), part(i + h * TILES, TILE)
                total = mine[place, :].astype(F32) + landed[place, :].astype(F32)
                dst[here, :] = (total + which.across[here, :].astype(F32)).astype(BF16)

            loop(TILES, one)

    def reduce_done(ticket):
        for record in ticket[2]:
            sent(record)

    def spread_start(place):
        k = slot(8)
        send(place(z), place(z), k, dev_adj)
        send(place(z), place(z), k + 1, dev_opp, mid)
        send(place(z), place(z), k + 2, dev_diag, end)
        return place, k

    def spread_relay(ticket):
        place, k = ticket
        arrived(place(z_opp), k + 1, mid)
        send(place(z_opp), place(z_opp), k + 3, dev_adj, mid)
        arrived(place(z_diag), k + 2, mid)
        send(place(z_diag), place(z_diag), k + 4, dev_adj, mid)
        arrived(place(z_adj), k)
        arrived(place(z_diag), k + 3, end)
        arrived(place(z_opp), k + 4, end)

    def spread_plane(ticket, name):
        k = ticket[1]
        for j, (_, device) in enumerate(in_plane):
            send(name.at[q], name.at[q], k + 5 + j, device)

    def spread_ready(ticket, name):
        k = ticket[1]
        for j, (q_from, _) in enumerate(in_plane):
            arrived(name.at[q_from], k + 5 + j)

    def lanes(j, size=256):
        return part(j, size)

    def matmul(left, right, dst, bias=None, bias_row=0, bias_at=0):
        count = right.shape[1] // 256

        def one(j):
            tile = nn(left[...], right[:, lanes(j)])
            if bias is not None:
                tile = tile + bias[bias_row:bias_row + 1, part(j + bias_at, 256)]
            dst[:, lanes(j)] = tile.astype(BF16)

        loop(count, one)

    def matmul_back(left, right, dst, at=slice(0, T)):
        def one(j):
            dst[at, lanes(j)] = nt(left[at, :], right[lanes(j), :]).astype(BF16)

        loop(right.shape[0] // 256, one)

    def weight_grad(left, right, name, more=False):
        def one(j):
            total = tn(left[:, lanes(j)], right[...])
            if more:
                total = total + name.grad[lanes(j), :].astype(F32)
            name.grad[lanes(j), :] = total.astype(BF16)

        loop(left.shape[1] // 256, one)

    low_half = lax.broadcasted_iota(jnp.int32, (L, 128), 1) < 64
    keep_low = low_half.astype(F32).astype(BF16)
    keep_high = (1.0 - low_half.astype(F32)).astype(BF16)

    def both(pair):
        return jnp.concatenate([pair * keep_low, pair * keep_high], axis=0)

    def merge(stacked):
        return jnp.where(low_half, stacked[:L], stacked[L:])

    def attention(qref, q_at, kref, k_at, v_at, causal, length_row, probs, dst):
        def one(i):
            r, pair = i // 2, i % 2
            place = part(r, L)
            query = both(qref[place, part(pair + q_at, 128)])
            scores = nt(query, kref[place, part(pair + k_at, 128)]) * HD ** (-0.5)
            key = lax.broadcasted_iota(jnp.int32, scores.shape, 1)
            limit = buf.sva[r, z][length_row:length_row + 1, 0:1].astype(F32)
            allowed = key.astype(F32) < limit
            if causal:
                at = lax.broadcasted_iota(jnp.int32, scores.shape, 0)
                at = jnp.where(at < L, at, at - L)
                allowed = allowed & (key <= at)
            scores = jnp.where(allowed, scores, MASKED)
            raised = jnp.exp(scores - jnp.max(scores, -1, keepdims=True))
            weights = (raised * (1.0 / jnp.sum(raised, -1, keepdims=True))).astype(BF16)
            probs[i] = weights
            mixed = nn(weights, kref[place, part(pair + v_at, 128)])
            dst[place, part(pair, 128)] = merge(mixed).astype(BF16)

        loop(2 * P_IN, one, 2)

    def attention_back(qref, q_at, kref, k_at, v_at, probs, grad):
        def one(i):
            r, pair = i // 2, i % 2
            place = part(r, L)
            query = both(qref[place, part(pair + q_at, 128)])
            key = kref[place, part(pair + k_at, 128)]
            value = kref[place, part(pair + v_at, 128)]
            mixed_grad = both(grad[place, part(pair, 128)])
            weights = probs[i]
            soft = weights.astype(F32)
            grad_probs = nt(mixed_grad, value)
            delta = jnp.sum(soft * grad_probs, -1, keepdims=True)
            grad_scores = (soft * (grad_probs - delta)).astype(BF16)
            scale = HD ** (-0.5)
            grad_query = merge(nn(grad_scores, key)) * scale
            grad_key = tn(grad_scores, query) * scale
            grad_value = tn(weights, mixed_grad)
            qref[place, part(pair + q_at, 128)] = grad_query.astype(BF16)
            kref[place, part(pair + k_at, 128)] = grad_key.astype(BF16)
            kref[place, part(pair + v_at, 128)] = grad_value.astype(BF16)

        loop(2 * P_IN, one, 2)

    def column_sums(source, first, count, row, at):
        def one(j):
            values = source[:, part(j + first, 256)].astype(F32)
            buf.sg[row:row + 1, part(j + at, 256)] = jnp.sum(values, 0, keepdims=True)

        loop(count, one)

    def norm(load, index, dst, halves=(0, 1)):
        def one(i):
            place = part(i, TILE)
            normed, _ = whiten(load(place))
            gain, shift = buf.vec[index:index + 1, :], buf.vec[index + 3:index + 4, :]
            rows(dst, q)[place, :] = (normed * gain + shift).astype(BF16)

        loop(TILES * len(halves), one, first=TILES * halves[0])

    def norm_back(load, incoming, index, base, dst, low, out_row=None, halves=(0, 1)):
        zero = jnp.zeros((1, D), F32)

        def one(i, carry):
            gain_sum, shift_sum, out_sum = carry
            place = part(i, TILE)
            normed, scale = whiten(load(place))
            grad = incoming(place)
            gained = grad * buf.vec[index:index + 1, :]
            back = gained - jnp.mean(gained, -1, keepdims=True)
            back = back - normed * jnp.mean(gained * normed, -1, keepdims=True)
            total = base(place) + scale * back
            if dst is not None:
                dst[place, :] = total
            rounded = total.astype(BF16)
            low(place, rounded)
            return (
                gain_sum + jnp.sum(grad * normed, 0, keepdims=True),
                shift_sum + jnp.sum(grad, 0, keepdims=True),
                out_sum + jnp.sum(rounded.astype(F32), 0, keepdims=True),
            )

        first = TILES * halves[0]
        last = first + TILES * len(halves)
        gain_sum, shift_sum, out_sum = lax.fori_loop(first, last, one, (zero, zero, zero))
        buf.sg[index:index + 1, :] = buf.sg[index:index + 1, :] + gain_sum
        buf.sg[index + 3:index + 4, :] = buf.sg[index + 3:index + 4, :] + shift_sum
        if out_row is not None:
            buf.sg[out_row:out_row + 1, :] = buf.sg[out_row:out_row + 1, :] + out_sum

    gate = pltpu.get_barrier_semaphore()
    partners = [device for _, device in in_plane] + [dev_adj, dev_opp, dev_diag]
    partners += [((s + j) % n_sec, d) for j in range(1, n_sec)]
    for device in partners:
        pl.semaphore_signal(gate, inc=1, device_id=device, device_id_type=MESH)
    raw_copies = [local(weight.source, weight.raw) for weight in (wt.qkv, wt.ckv, wt.cq)]
    low_lanes = lax.broadcasted_iota(jnp.int32, (3, 128), 1) < 64
    even_lanes = (jnp.zeros((3, 128), jnp.int32) + c) == 0
    for row, pieces in ((0, io.gain), (3, io.shift), (6, io.out_bias)):
        value = pieces[...].astype(F32)
        twice = jnp.concatenate([value, value], 1)
        buf.sg[row:row + 3, 0:128] = jnp.where(low_lanes == even_lanes, twice, 0.0)
    buf.sg[9:10, 0:128] = io.self_bias[...].astype(F32)
    buf.sg[10:11, 0:128] = io.cross_bias[...].astype(F32)
    buf.sg[11:12, 0:128] = io.unit_bias[:, 0:128].astype(F32)
    buf.sg[12:13, 0:128] = io.unit_bias[:, 128:256].astype(F32)
    buf.sg[13:14, 0:128] = jnp.zeros((1, 128), F32) + io.tgt[0].astype(F32)
    buf.sg[14:15, 0:128] = jnp.zeros((1, 128), F32) + io.src[0].astype(F32)
    buf.sg[15:16, 0:128] = jnp.zeros((1, 128), F32)
    buf.sva[q, z] = buf.sg[:, 0:128].astype(BF16)

    raw_copies[0].wait()
    sort_columns(wt.qkv)
    pl.semaphore_wait(gate, len(partners))

    sv = spread_start(lambda plane: buf.sva.at[q, plane])
    swap_start(wt.qkv)
    k_prev, k_cot, k_mem = slot(), slot(), slot(n_sec)
    send(io.prev, buf.hb, k_prev, ((s + 1) % n_sec, d))
    for weight in (wt.so, wt.co):
        send_inward(weight, weight.source)
        send_across(weight, weight.source)
        weight_outward(weight, weight.source)
    mem_slot = rows(buf.m, q)
    for j in range(1, n_sec):
        send(io.mem, mem_slot.at[:, part(s, mem_cols)], k_mem + j, ((s + j) % n_sec, d))
    mem_copy = local(io.mem, mem_slot.at[:, part(s, mem_cols)])
    send(io.cot, rows(buf.e3, q), k_cot, ((s + n_sec - 1) % n_sec, d))
    for weight in (wt.so, wt.co, wt.f2):
        weight.own_copy = [local(weight.source, block(weight, z))]
    for weight, copy in ((wt.ckv, raw_copies[1]), (wt.cq, raw_copies[2])):
        copy.wait()
        sort_columns(weight)
        swap_start(weight)

    swap_wait(wt.qkv)
    send_inward(wt.qkv, block(wt.qkv, z))
    send_across(wt.qkv, block(wt.qkv, z))
    weight_outward(wt.qkv, block(wt.qkv, z))
    unit_swap_start()
    spread_relay(sv)
    spread_plane(sv, buf.sva)
    spread_ready(sv, buf.sva)

    for tile in range(D // 128):
        pair = buf.sva[2 * (tile % 2), tile // 2].astype(F32)
        pair = pair + buf.sva[2 * (tile % 2) + 1, tile // 2].astype(F32)
        buf.vec[:, tile * 128:(tile + 1) * 128] = pair
    half = lax.broadcasted_iota(jnp.int32, (16, 128), 1) < 64
    even = (jnp.zeros((16, 128), jnp.int32) + c) == 0
    buf.bias[...] = jnp.zeros((8, D), F32)
    for kind in range(2):
        for tile in range(2):
            first = buf.sva[x, tile + 2 * kind].astype(F32)
            second = buf.sva[2 + x, tile + 2 * kind].astype(F32)
            lower = jnp.where(even, first, pltpu.roll(first, 64, 1))
            upper = jnp.where(even, pltpu.roll(second, 64, 1), second)
            both_heads = jnp.where(half, lower, upper)
            for which in range(2):
                at = 512 * kind + 128 * tile
                buf.bias[which:which + 1, at:at + 128] = both_heads[9 + which:10 + which]
    for tile in range(Z):
        unit = buf.sva[q, tile].astype(F32)
        buf.bias[2:3, 256 * tile:256 * tile + 128] = unit[11:12]
        buf.bias[2:3, 256 * tile + 128:256 * tile + 256] = unit[12:13]
    buf.sg[...] = jnp.zeros((16, D), F32)

    arrived(buf.hb, k_prev)

    def hidden(place):
        return buf.hb[place, :].astype(F32)

    norm(hidden, 0, buf.a1)
    a1 = gather_start(buf.a1)
    relay_inward(wt.qkv)
    relay_near(wt.qkv)
    swap_wait(wt.ckv)
    send_inward(wt.ckv, block(wt.ckv, z))
    for j in range(1, n_sec):
        origin = (s + n_sec - j) % n_sec
        arrived(mem_slot.at[:, part(origin, mem_cols)], k_mem + j)
    mem_copy.wait()
    gather_relay(a1)
    memory = gather_start(buf.m)
    relay_inward(wt.so)
    swap_wait(wt.cq)
    send_inward(wt.cq, block(wt.cq, z))
    relay_far(wt.qkv)
    arrived(rows(buf.e3, q), k_cot)
    k_units = slot(16)
    to_middle = [send(rows(buf.e3, q), rows(buf.e3, q), k_units + 9, dev_x, end)]

    def cot_inward(index, k):
        for h in range(2):
            src, dst = piece(buf.e3, index, h, 2), half_major(buf.e3b, index, h)
            to_middle.append(send(src, dst, k + h, dev_adj, end))

    cot_inward(q, k_units)
    gather_ready(a1)
    unit_swap_wait(end)
    send_inward(wt.f1, block(wt.f1, z))
    weight_ready(wt.qkv)
    matmul(buf.a1, wt.qkv.weight, buf.qkv, buf.bias, 0)
    send_across(wt.ckv, block(wt.ckv, z))
    attention(buf.qkv, 0, buf.qkv, 2, 4, True, 13, buf.p1, buf.o1)
    relay_inward(wt.ckv)
    relay_near(wt.so)
    relay_far(wt.so)
    weight_outward(wt.ckv, block(wt.ckv, z))
    send_across(wt.cq, block(wt.cq, z))
    wt.so.own_copy[0].wait()
    weight_ready(wt.so)
    matmul(buf.o1, wt.so.weight, set_a.parts)
    step = reduce_start(set_a)
    send_inward(wt.f2, wt.f2.source)
    relay_inward(wt.cq)
    weight_outward(wt.cq, block(wt.cq, z))
    reduce_relay(step)
    arrived(rows(buf.e3, q_x), k_units + 9, end)
    cot_inward(q_x, k_units + 2)
    relay_near(wt.ckv)
    gather_finish(memory)
    relay_far(wt.ckv)
    relay_inward(wt.co)
    unit_swap_wait(mid)
    send_across(wt.f1, block(wt.f1, z))
    reduce_ready(step)

    def after_self(i):
        place = part(i, TILE)
        buf.h1[place, :] = hidden(place) + (reduced(step, place) + buf.vec[6:7, :])

    loop(L // TILE, after_self)
    norm(lambda place: buf.h1[place, :], 1, buf.a2)
    a2 = gather_start(buf.a2)
    reduce_done(step)
    relay_near(wt.cq)
    relay_far(wt.cq)
    weight_ready(wt.ckv)
    matmul(buf.m, wt.ckv.weight, buf.kv, buf.bias, 1, 1)
    relay_near(wt.co)
    send_across(wt.f2, wt.f2.source)
    relay_far(wt.co)
    relay_inward(wt.f1)

    gather_finish(a2)
    e3 = gather_start(buf.e3, mid)
    weight_ready(wt.cq)
    matmul(buf.a2, wt.cq.weight, buf.q2, buf.bias, 1)
    attention(buf.q2, 0, buf.kv, 0, 2, False, 14, buf.p2, buf.o2)
    wt.co.own_copy[0].wait()
    weight_ready(wt.co)
    matmul(buf.o2, wt.co.weight, set_b.parts)
    step = reduce_start(set_b)
    relay_inward(wt.f2)
    gather_finish(e3)
    reduce_relay_paced(step)

    def after_cross(i):
        place = part(i, TILE)
        buf.h2[place, :] = buf.h1[place, :] + (reduced(step, place) + buf.vec[7:8, :])

    a3 = gather_open(buf.a3, mid, 2)
    for h in range(2):
        reduce_ready_half(step, h)
        loop(TILES, after_cross, first=h * TILES)
        norm(lambda place: buf.h2[place, :], 2, buf.a3, (h,))
        send(piece(buf.a3, q, h, 2), half_major(buf.a3b, q, h), k_units + 10 + h, dev_adj, end)
        gather_part(a3, h)
    reduce_done(step)

    def units(normed, activs, slopes, at=slice(0, T)):
        def one(j):
            value = nn(normed[at, :], wt.f1.weight[:, lanes(j)]) + buf.bias[2:3, lanes(j)]
            activ, slope = gelu_pair(value)
            activs[at, lanes(j)] = activ.astype(BF16)
            slopes[at, lanes(j)] = slope.astype(BF16)

        loop(FL // 256, one, 2)

    def units_back(grad, slopes, at=slice(0, T)):
        def one(j):
            value = nt(grad[at, :], wt.f2.weight[lanes(j), :])
            low = (value * slopes[at, lanes(j)].astype(F32)).astype(BF16)
            slopes[at, lanes(j)] = low
            total = jnp.sum(low.astype(F32), 0, keepdims=True)
            buf.sg[10:11, lanes(j)] = buf.sg[10:11, lanes(j)] + total

        loop(FL // 256, one)

    def weight_grads(left, right, left_b, right_b, name, first, count):
        def one(j):
            total = tn(left[:, lanes(j)], right[...]) + tn(left_b[:, lanes(j)], right_b[...])
            name.grad[lanes(j), :] = total.astype(BF16)

        loop(count, one, first=first)

    def on_mid(fn, *args):
        run_if(mid, lambda: fn(*args))

    def cot_sum(i, carry):
        return carry + jnp.sum(rows(buf.e3, q)[part(i, TILE), :].astype(F32), 0, keepdims=True)

    buf.sg[8:9, :] = lax.fori_loop(0, L // TILE, cot_sum, jnp.zeros((1, D), F32))

    for index, k in ((q, k_units), (q_x, k_units + 2)):
        for h in range(2):
            landed = half_major(buf.e3b, index, h)
            arrived(landed, k + h, mid)
            send(landed, landed, k + 4 + h, dev_core, mid)
    gather_relay(a3)
    a3b = gather_open(buf.a3b, mid, 2, half_major)
    arrived(half_major(buf.a3b, q, 0), k_units + 10, mid)
    gather_part(a3b, 0)
    gather_ready(a3)
    inner_ready(wt.f1)
    on_mid(units, buf.a3, buf.g, buf.gp)
    arrived(half_major(buf.a3b, q, 1), k_units + 11, mid)
    gather_part(a3b, 1)
    on_mid(weight_grad, buf.g, buf.e3, wt.f2)
    wt.f2.own_copy[0].wait()
    inner_ready(wt.f2)
    on_mid(units_back, buf.e3, buf.gp)
    on_mid(matmul_back, buf.gp, wt.f1.weight, set_a.parts)
    step = reduce_start(set_a, mid)
    for index, k in ((q_core, k_units + 4), (q_xc, k_units + 6)):
        for h in range(2):
            arrived(half_major(buf.e3b, index, h), k + h, mid)
    step_b = reduce_open(set_b, mid)
    for h in range(2):
        at = slice(h * T // 2, (h + 1) * T // 2)
        if h == 0:
            gather_relay(a3b)
            gather_ready_part(a3b, 0)
            reduce_relay(step)
        else:
            gather_ready_part(a3b, 1)
            reduce_relay_half(step_b, 0)
        on_mid(units, buf.a3b, buf.gb, buf.gpb, at)
        on_mid(units_back, buf.e3b, buf.gpb, at)
        on_mid(matmul_back, buf.gpb, wt.f1.weight, set_b.parts, at)
        reduce_start_half(step_b, h)

    def back_outward(h):
        reduce_ready_half(step_b, h)
        on_mid(fold, step_b, buf.back, (h,))
        ready = buf.back.at[part(h, HALF)]
        send(ready, ready, k_units + 12 + h, dev_adj, mid)

    def store(name):
        def low(place, value):
            rows(name, q)[place, :] = value

        return low

    def units_norm_back(incoming, halves):
        norm_back(
            lambda place: buf.h2[place, :], incoming, 2,
            lambda place: rows(buf.e3, q)[place, :].astype(F32), buf.dh, store(buf.e2), 7, halves,
        )

    reduce_done(e3)
    for record in to_middle:
        sent(record)
    back_outward(0)
    reduce_relay_half(step_b, 1)
    on_mid(weight_grad, buf.gb, buf.e3b, wt.f2, True)
    inner_grad_far(wt.f2)
    inner_grad_near(wt.f2)
    reduce_ready(step)
    on_mid(units_norm_back, lambda place: reduced(step, place), (0, 1))
    e2 = gather_open(buf.e2, None, 2)
    gather_part(e2, 0, mid)
    back_outward(1)
    gather_part(e2, 1, mid)
    on_mid(weight_grads, buf.a3, buf.gp, buf.a3b, buf.gpb, wt.f1, 0, Z)
    inner_grad_far(wt.f1)
    inner_grad_near(wt.f1)
    on_mid(matmul, buf.gb, wt.f2.weight, set_c.parts)
    final = reduce_open(set_c, mid)
    reduce_start_half(final, 0)
    reduce_start_half(final, 1)
    for h in range(2):
        arrived(buf.back.at[part(h, HALF)], k_units + 12 + h, end)
        run_if(
            end,
            lambda h=h: units_norm_back(lambda place: buf.back[place, :].astype(F32), (h,)),
        )
        gather_part(e2, h, end)
    reduce_done(step)
    reduce_done(step_b)
    gather_finish(e2)
    reduce_relay(final)

    weight_grad(buf.o2, buf.e2, wt.co)
    grad_send(wt.co)
    matmul_back(buf.e2, wt.co.weight, buf.do)
    attention_back(buf.q2, 0, buf.kv, 0, 2, buf.p2, buf.do)
    matmul_back(buf.q2, wt.cq.weight, set_b.parts)
    step = reduce_start(set_b)
    weight_grad(buf.a2, buf.q2, wt.cq)
    grad_send(wt.cq)
    reduce_relay(step)
    weight_grad(buf.m, buf.kv, wt.ckv)
    grad_send(wt.ckv)
    matmul_back(buf.kv, wt.ckv.weight, set_a.parts)
    mem_step = reduce_start(set_a)
    column_sums(buf.q2, 0, 1, 9, 2)
    column_sums(buf.kv, 1, 1, 9, 3)
    reduce_ready(final)
    on_mid(fold, final, buf.tail)
    send(buf.tail, buf.tail, k_units + 14, dev_adj, mid)
    reduce_done(final)
    grad_combine(wt.co)
    inner_grad_combine(wt.f2)
    reduce_ready(step)
    norm_back(
        lambda place: buf.h1[place, :], lambda place: reduced(step, place), 1,
        lambda place: buf.dh[place, :], buf.dh, store(buf.e3), 6,
    )
    e1 = gather_start(buf.e3)
    reduce_done(step)
    grad_combine(wt.cq)
    gather_finish(e1)
    reduce_relay(mem_step)
    grad_combine(wt.ckv)

    weight_grad(buf.o1, buf.e3, wt.so)
    grad_send(wt.so)
    matmul_back(buf.e3, wt.so.weight, buf.do)
    attention_back(buf.qkv, 0, buf.qkv, 2, 4, buf.p1, buf.do)
    inner_grad_combine(wt.f1)
    grad_outward(wt.co)
    inner_final(mid)
    weight_grad(buf.a1, buf.qkv, wt.qkv)
    far_part = grad_send_far(wt.qkv)
    matmul_back(buf.qkv, wt.qkv.weight, set_b.parts)
    step = reduce_start(set_b)
    column_sums(buf.qkv, 0, 1, 9, 0)
    column_sums(buf.qkv, 2, 1, 9, 1)
    grad_outward(wt.cq)
    reduce_relay(step)
    grad_combine(wt.so)
    on_mid(matmul, buf.g, wt.f2.weight, set_c.parts)
    final = reduce_start(set_c, mid)

    reduce_ready(mem_step)
    fold(mem_step, buf.mb)
    k_back = slot(n_sec)
    for j in range(1, n_sec):
        to = (s + j) % n_sec
        send(buf.mb.at[:, part(to, mem_cols)], buf.ml.at[j], k_back + j, (to, d))
    sent(far_part)
    middle_part = grad_send_middle(wt.qkv)
    grad_combine_far(wt.qkv)
    grad_outward(wt.ckv)
    reduce_ready(step)

    def store_stage(place, value):
        buf.ig[place, :] = value

    norm_back(
        hidden, lambda place: reduced(step, place), 0,
        lambda place: buf.dh[place, :], None, store_stage,
    )
    k_in = slot()
    send(buf.ig, io.input_grad, k_in, ((s + n_sec - 1) % n_sec, d))
    buf.sga[z] = buf.sg[...].astype(BF16)
    sums = spread_start(lambda plane: buf.sga.at[plane])
    inner_final(end)
    for weight in (wt.co, wt.cq):
        grad_final(weight)
    reduce_relay(final)
    sent(middle_part)
    grad_send_near(wt.qkv)
    grad_combine_middle(wt.qkv)
    grad_outward(wt.so)
    grad_final(wt.ckv)
    spread_relay(sums)
    planes = buf.sga[0].astype(F32)
    for plane in range(1, Z):
        planes = planes + buf.sga[plane].astype(F32)
    buf.sgp[q] = planes.astype(BF16)
    spread_plane(sums, buf.sgp)

    def finish(incoming):
        def one(i):
            place = part(i, TILE)
            total = buf.h2[place, :] + (incoming(place) + buf.vec[8:9, :])
            buf.stage[place, :] = total.astype(BF16)

        loop(L // TILE, one)

    arrived(buf.tail, k_units + 14, end)
    run_if(end, lambda: finish(lambda place: buf.tail[place, :].astype(F32)))
    for j in range(1, n_sec):
        arrived(buf.ml.at[j], k_back + j)

    def memory_total(i):
        place = part(i, TILE)
        total = buf.mb[place, part(s, mem_cols)].astype(F32)
        for j in range(1, n_sec):
            total = total + buf.ml[j, place, :].astype(F32)
        buf.mo[place, :] = total.astype(BF16)

    loop(L // TILE, memory_total)
    keep(buf.mo, io.memory_grad)
    grad_outward(wt.qkv)
    grad_final(wt.so)
    grad_final(wt.qkv)
    unit_last_wait()
    last_wait(wt.cq)
    last_wait(wt.ckv)
    reduce_ready(final)
    on_mid(finish, lambda place: reduced(final, place))
    keep(buf.stage, io.output)
    spread_ready(sums, buf.sgp)

    def per_unit(q_at, at):
        return buf.sgp[q_at, :, at].astype(F32)

    at = part(d // 2, 128)
    feature = per_unit(0, at)
    for q_at in range(1, P_IN):
        feature = feature + per_unit(q_at, at)
    swapped = pltpu.roll(feature, 64, 1)
    buf.sums[...] = jnp.where((jnp.zeros((16, 128), jnp.int32) + c) == 0, feature, swapped)
    head = d % 8
    at = part(2 * (d // 8) + head // 4, 128)
    low_head, high_head = per_unit(2 * c, at), per_unit(2 * c + 1, at)
    first_half = (jnp.zeros((16, 128), jnp.int32) + (head // 2) % 2) == 0
    low_head = jnp.where(first_half, low_head, pltpu.roll(low_head, 64, 1))
    high_head = jnp.where(first_half, pltpu.roll(high_head, 64, 1), high_head)
    buf.sums[9:10, :] = jnp.where(half, low_head, high_head)[9:10]
    at = part(2 * (d // 8) + 4 + head // 4, 128)
    low_head, high_head = per_unit(2 * c, at), per_unit(2 * c + 1, at)
    low_head = jnp.where(first_half, low_head, pltpu.roll(low_head, 64, 1))
    high_head = jnp.where(first_half, pltpu.roll(high_head, 64, 1), high_head)
    buf.sums[10:11, :] = jnp.where(half, low_head, high_head)[9:10]
    buf.sums[11:12, :] = per_unit(q, part(2 * z, 128))[10:11]
    buf.sums[12:13, :] = per_unit(q, part(2 * z + 1, 128))[10:11]
    keep(buf.sums, io.sums_out)
    last_wait(wt.qkv)
    arrived(io.input_grad, k_in)
    for copy, cond in result_copies:
        run_if(cond, copy.wait)
    for record in list(started):
        sent(record)
    assert counter[0] <= SEMS


def buffer_shapes(n_sec, mem_cols):
    tokens, row = (T, D), (L, D)
    shapes = dict(
        sva=(P_IN, Z, 16, 128),
        sga=(Z, 16, D),
        sgp=(P_IN, 16, D),
        hb=row, ig=row, stage=row, mb=row,
        ml=(n_sec, L, mem_cols),
        mo=(L, mem_cols),
        qkv=(T, 768), q2=(T, 256), kv=(T, 512), o1=(T, 256), o2=(T, 256), do=(T, 256),
        p1=(2 * P_IN, 2 * L, L), p2=(2 * P_IN, 2 * L, L),
        g=(T, FL), gp=(T, FL),
        a1=tokens, a2=tokens, a3=tokens, m=tokens, e3=tokens, e2=tokens,
        a3b=tokens, e3b=tokens, gb=(T, FL), gpb=(T, FL), back=row, tail=row,
    )
    exact = dict(vec=(16, D), bias=(8, D), sg=(16, D), sums=(16, 128), h1=row, h2=row, dh=row)
    kinds = {name: pltpu.VMEM(shape, BF16) for name, shape in shapes.items()}
    kinds.update({name: pltpu.VMEM(shape, F32) for name, shape in exact.items()})
    return kinds


REDUCE_SHAPES = dict(
    parts=pltpu.VMEM((T, D), BF16),
    core=pltpu.VMEM((2 * L, D), BF16),
    across=pltpu.VMEM((L, D), BF16),
)


def scratch_of(n_sec, mem_cols):
    scratch = list(buffer_shapes(n_sec, mem_cols).values())
    scratch += 3 * list(REDUCE_SHAPES.values())
    for count, columns, _ in WEIGHTS.values():
        scratch += 2 * [pltpu.VMEM((Z * count, columns), BF16)]
        scratch += 2 * [pltpu.VMEM((count, columns), BF16)]
    for count, columns, _ in list(WEIGHTS.values())[:5]:
        scratch += 3 * [pltpu.VMEM((count, columns), BF16)]
    for columns in (768, 512, 256):
        scratch.append(pltpu.VMEM((64, P_IN * columns), BF16))
        scratch.append(pltpu.VMEM((P_IN, 64, columns), BF16))
    return scratch + [
        pltpu.SemaphoreType.DMA((SEMS,)),
        pltpu.SemaphoreType.DMA((SEMS,)),
        pltpu.SemaphoreType.DMA((48,)),
    ]


def finish_kernel(*refs):
    moved, low, sums = refs[:3], refs[3:10], refs[10]
    moved_out, high, small = refs[11:14], refs[14:21], refs[21:27]
    low_buf, high_buf, moved_buf, sems = refs[27:34], refs[34:41], refs[41:44], refs[44]
    inward = [
        pltpu.make_async_copy(src, dst, sems.at[i])
        for i, (src, dst) in enumerate(zip(low + moved, low_buf + moved_buf))
    ]
    for copy in inward:
        copy.start()
    outward = []
    gain, shift, out_bias, self_bias, cross_bias, unit_bias = small
    gain[0] = sums[0:3, 0:64]
    shift[0] = sums[3:6, 0:64]
    out_bias[0] = sums[6:9, 0:64]
    self_bias[...] = sums[9:10, :]
    cross_bias[...] = sums[10:11, :]
    unit_bias[:, 0:128] = sums[11:12, :]
    unit_bias[:, 128:256] = sums[12:13, :]
    for i, copy in enumerate(inward[:7]):
        copy.wait()
        rows_in = low_buf[i].shape[0]

        def one(j, i=i):
            place = part(j, 16)
            high_buf[i][place, :] = low_buf[i][place, :].astype(F32)

        loop(rows_in // 16, one)
        back = pltpu.make_async_copy(high_buf[i], high[i], sems.at[10 + i])
        back.start()
        outward.append(back)
    for i, copy in enumerate(inward[7:]):
        copy.wait()
        back = pltpu.make_async_copy(moved_buf[i], moved_out[i], sems.at[17 + i])
        back.start()
        outward.append(back)
    for copy in outward:
        copy.wait()


def on_device_planes(
    prev_act, memory, out_cot, tgt_len, src_len, norm_gain, norm_bias, self_qkv, self_qv_bias,
    self_out, cross_q, cross_kv, cross_qv_bias, cross_out, out_bias, fc1, fc1_bias, fc2,
):
    n_sec = lax.axis_size("section")
    mem_cols = memory.shape[2]
    operands = (
        prev_act[0, 0], memory[0], out_cot[0, 0], tgt_len, src_len,
        norm_gain[0], norm_bias[0], out_bias[0], self_qv_bias, cross_qv_bias, fc1_bias,
        self_qkv[0], self_out[0], cross_kv[0], cross_q[0], cross_out[0], fc1[0], fc2[0],
    )
    anywhere = pl.BlockSpec(memory_space=pl.ANY)
    in_specs = 3 * [anywhere] + 2 * [pl.BlockSpec(memory_space=pltpu.SMEM)]
    in_specs += 6 * [pl.BlockSpec(memory_space=pltpu.VMEM)] + 7 * [anywhere]
    out_shapes = [(L, D), (L, D), (L, mem_cols)]
    for count, columns, by_column in WEIGHTS.values():
        out_shapes.append((count // P_IN, P_IN * columns) if by_column else (count, columns))
    sums_shape = jax.ShapeDtypeStruct((16, 128), F32)
    results = pl.pallas_call(
        functools.partial(whole_kernel, n_sec, mem_cols),
        out_shape=[jax.ShapeDtypeStruct(shape, BF16) for shape in out_shapes] + [sums_shape],
        in_specs=in_specs,
        out_specs=[anywhere] * (len(out_shapes) + 1),
        scratch_shapes=scratch_of(n_sec, mem_cols),
        compiler_params=pltpu.CompilerParams(
            collective_id=0, has_side_effects=True, vmem_limit_bytes=64 * 2**20 - 2**16
        ),
        cost_estimate=pl.CostEstimate(
            flops=21 * 10**9, bytes_accessed=20 * 2**20, transcendentals=3 * 10**6
        ),
    )(*operands)
    shapes = [result.shape for result in results]
    vmem = pl.BlockSpec(memory_space=pltpu.VMEM)
    finished = pl.pallas_call(
        finish_kernel,
        out_shape=[jax.ShapeDtypeStruct(shape, BF16) for shape in shapes[:3]]
        + [jax.ShapeDtypeStruct(shape, F32) for shape in shapes[3:10]]
        + [jax.ShapeDtypeStruct(shape, F32) for shape in [(1, 3, 64)] * 3 + [(1, 128), (1, 128), (1, 256)]],
        in_specs=10 * [anywhere] + [vmem],
        out_specs=10 * [anywhere] + 6 * [vmem],
        scratch_shapes=[pltpu.VMEM(shape, BF16) for shape in shapes[3:10]]
        + [pltpu.VMEM(shape, F32) for shape in shapes[3:10]]
        + [pltpu.VMEM(shape, BF16) for shape in shapes[:3]]
        + [pltpu.SemaphoreType.DMA((20,))],
        compiler_params=pltpu.CompilerParams(vmem_limit_bytes=63 * 2**20),
        cost_estimate=pl.CostEstimate(flops=0, bytes_accessed=9 * 2**20, transcendentals=0),
    )(*results)
    (
        output, input_grad, memory_grad, g_qkv, g_so, g_ckv, g_cq, g_co, g_f1, g_f2,
        gain, shift, biases, self_biases, cross_biases, units,
    ) = finished
    return (
        output[None, None],
        input_grad[None, None],
        memory_grad[None],
        gain,
        shift,
        g_qkv[None],
        self_biases,
        g_so[None],
        g_cq[None],
        g_ckv[None],
        cross_biases,
        g_co[None],
        biases,
        g_f1[None],
        units,
        g_f2[None],
    )


def solution(mesh):
    in_specs = (
        P("section", "dp", None, None),
        P("dp", None, "section"),
        P("section", "dp", None, None),
        P("dp"),
        P("dp"),
        P("section", None, "dp"),
        P("section", None, "dp"),
        P("section", "dp", None),
        P("section", "dp"),
        P("section", "dp", None),
        P("section", "dp", None),
        P("section", "dp", None),
        P("section", "dp"),
        P("section", "dp", None),
        P("section", None, "dp"),
        P("section", "dp", None),
        P("section", "dp"),
        P("section", "dp", None),
    )
    out_specs = (
        P("section", "dp", None, None),
        P("section", "dp", None, None),
        P("dp", None, "section"),
        P("section", None, "dp"),
        P("section", None, "dp"),
        P("section", "dp", None),
        P("section", "dp"),
        P("section", "dp", None),
        P("section", "dp", None),
        P("section", "dp", None),
        P("section", "dp"),
        P("section", "dp", None),
        P("section", None, "dp"),
        P("section", "dp", None),
        P("section", "dp"),
        P("section", "dp", None),
    )
    planes = Z * P_IN
    fits = mesh.shape["dp"] == planes
    return jax.shard_map(
        on_device_planes if fits else on_device, mesh=mesh, in_specs=in_specs, out_specs=out_specs, check_vma=False
    )
```

```python
import functools
from types import SimpleNamespace

import jax
import jax.numpy as jnp
from jax import lax
from jax.experimental import pallas as pl
from jax.experimental.pallas import tpu as pltpu
from jax.sharding import PartitionSpec as P

H = 16
HD = 64


EPSILON = 1e-05
MASKED = -1000000000.0


def passed_along(value, axis, by):
    length = lax.axis_size(axis)
    return lax.ppermute(value, axis, [(i, (i + by) % length) for i in range(length)])


def norm_fwd(rows, gain, shift_term):
    center = rows - jnp.mean(rows, -1, keepdims=True)
    scale = lax.rsqrt(jnp.mean(center * center, -1, keepdims=True) + EPSILON)
    return center * scale * gain + shift_term


def gelu_exact(values):
    return jax.nn.gelu(values, approximate=False)


def product(left, right):
    return jnp.dot(left, right, preferred_element_type=jnp.float32)


def product_right_t(left, right):
    return lax.dot_general(
        left, right, (((1,), (1,)), ((), ())), preferred_element_type=jnp.float32
    )


def product_left_t(left, right):
    return lax.dot_general(
        left, right, (((0,), (0,)), ((), ())), preferred_element_type=jnp.float32
    )


def split_heads(flat, batch_rows):
    return flat.reshape(batch_rows, -1, H, HD)


def softmax_probs(query, key_rows, allowed):
    scores = jnp.einsum(
        "rthd,rshd->rhts", query, key_rows, preferred_element_type=jnp.float32
    ) * HD ** (-0.5)
    scores = jnp.where(allowed[:, None], scores, MASKED)
    weights = jnp.exp(scores - jnp.max(scores, -1, keepdims=True))
    return weights / jnp.sum(weights, -1, keepdims=True)


def attend_fwd(query, key_rows, value_rows, allowed):
    probs = softmax_probs(query, key_rows, allowed)
    mixed = jnp.einsum(
        "rhts,rshd->rthd",
        probs.astype(jnp.bfloat16),
        value_rows,
        preferred_element_type=jnp.float32,
    )
    return mixed.reshape(mixed.shape[0] * mixed.shape[1], -1).astype(jnp.bfloat16)


def attend_back(query, key_rows, value_rows, allowed, grad_mixed):
    probs = softmax_probs(query, key_rows, allowed)
    grad_heads = grad_mixed.reshape(query.shape)
    grad_probs = jnp.einsum(
        "rthd,rshd->rhts", grad_heads, value_rows, preferred_element_type=jnp.float32
    )
    delta = jnp.sum(probs * grad_probs, -1, keepdims=True)
    grad_scores = (probs * (grad_probs - delta)).astype(jnp.bfloat16)
    scale = HD ** (-0.5)
    grad_query = (
        jnp.einsum("rhts,rshd->rthd", grad_scores, key_rows, preferred_element_type=jnp.float32)
        * scale
    )
    grad_keys = (
        jnp.einsum("rhts,rthd->rshd", grad_scores, query, preferred_element_type=jnp.float32)
        * scale
    )
    grad_values = jnp.einsum(
        "rhts,rthd->rshd",
        probs.astype(jnp.bfloat16),
        grad_heads,
        preferred_element_type=jnp.float32,
    )
    width = query.shape[2] * query.shape[3]
    return (
        grad_query.reshape(-1, width).astype(jnp.bfloat16),
        grad_keys.reshape(-1, width).astype(jnp.bfloat16),
        grad_values.reshape(-1, width).astype(jnp.bfloat16),
    )


def unpack(pieces):
    return tuple((piece[0] for piece in pieces))


def on_device(
    prev_act,
    memory,
    out_cot,
    tgt_len,
    src_len,
    norm_gain,
    norm_bias,
    self_qkv,
    self_qv_bias,
    self_out,
    cross_q,
    cross_kv,
    cross_qv_bias,
    cross_out,
    out_bias,
    fc1,
    fc1_bias,
    fc2,
):
    fetched = unpack(
        (
            lax.all_gather(norm_gain, "dp", axis=2, tiled=True),
            lax.all_gather(norm_bias, "dp", axis=2, tiled=True),
            lax.all_gather(self_qkv, "dp", axis=1, tiled=True),
            lax.all_gather(self_qv_bias, "dp", axis=1, tiled=True),
            lax.all_gather(self_out, "dp", axis=1, tiled=True),
            lax.all_gather(cross_q, "dp", axis=1, tiled=True),
            lax.all_gather(cross_kv, "dp", axis=1, tiled=True),
            lax.all_gather(cross_qv_bias, "dp", axis=1, tiled=True),
            lax.all_gather(cross_out, "dp", axis=1, tiled=True),
            lax.all_gather(out_bias, "dp", axis=2, tiled=True),
            lax.all_gather(fc1, "dp", axis=1, tiled=True),
            lax.all_gather(fc1_bias, "dp", axis=1, tiled=True),
            lax.all_gather(fc2, "dp", axis=1, tiled=True),
        )
    )
    gains, shifts, w_sqkv, b_sqv, w_sout, w_cq, w_ckv, b_cqv, w_cout, b_out, w_one, b_one, w_two = (
        fetched
    )
    gain_f = gains.astype(jnp.float32)
    shift_f = shifts.astype(jnp.float32)
    sqv_f = b_sqv.astype(jnp.float32)
    cqv_f = b_cqv.astype(jnp.float32)
    out_f = b_out.astype(jnp.float32)
    one_f = b_one.astype(jnp.float32)
    source = passed_along(prev_act, "section", 1)[0]
    batch_rows, length, width = source.shape
    encoded = lax.all_gather(memory, "section", axis=2, tiled=True)
    mem_flat = encoded.reshape(-1, width)
    places = jnp.arange(length)
    self_ok = (places[None, None, :] <= places[None, :, None]) & (
        places[None, None, :] < tgt_len[:, None, None]
    )
    cross_ok = jnp.arange(encoded.shape[1])[None, None, :] < src_len[:, None, None]
    resid = source.astype(jnp.float32).reshape(-1, width)
    normed_one, pull_one = jax.vjp(norm_fwd, resid, gain_f[0], shift_f[0])
    first_in = normed_one.astype(jnp.bfloat16)
    joint = product(first_in, w_sqkv)
    query_self = (joint[:, :width] + sqv_f[:width]).astype(jnp.bfloat16)
    keys_self = joint[:, width : 2 * width].astype(jnp.bfloat16)
    values_self = (joint[:, 2 * width :] + sqv_f[width:]).astype(jnp.bfloat16)
    self_mixed = attend_fwd(
        split_heads(query_self, batch_rows),
        split_heads(keys_self, batch_rows),
        split_heads(values_self, batch_rows),
        self_ok,
    )
    after_self = resid + (product(self_mixed, w_sout) + out_f[0])
    normed_two, pull_two = jax.vjp(norm_fwd, after_self, gain_f[1], shift_f[1])
    second_in = normed_two.astype(jnp.bfloat16)
    query_cross = (product(second_in, w_cq) + cqv_f[:width]).astype(jnp.bfloat16)
    memory_proj = product(mem_flat, w_ckv)
    keys_cross = memory_proj[:, :width].astype(jnp.bfloat16)
    values_cross = (memory_proj[:, width:] + cqv_f[width:]).astype(jnp.bfloat16)
    cross_mixed = attend_fwd(
        split_heads(query_cross, batch_rows),
        split_heads(keys_cross, batch_rows),
        split_heads(values_cross, batch_rows),
        cross_ok,
    )
    after_cross = after_self + (product(cross_mixed, w_cout) + out_f[1])
    normed_three, pull_three = jax.vjp(norm_fwd, after_cross, gain_f[2], shift_f[2])
    third_in = normed_three.astype(jnp.bfloat16)
    pre_act = product(third_in, w_one) + one_f
    activ, pull_gelu = jax.vjp(gelu_exact, pre_act)
    act_low = activ.astype(jnp.bfloat16)
    result = after_cross + (product(act_low, w_two) + out_f[2])
    output = result.astype(jnp.bfloat16).reshape(1, batch_rows, length, width)
    (
        unused_gains,
        unused_shifts,
        w_sqkv,
        unused_sqv,
        w_sout,
        w_cq,
        w_ckv,
        unused_cqv,
        w_cout,
        unused_out,
        w_one,
        unused_one,
        w_two,
    ) = fetched
    grad_out = passed_along(out_cot, "section", -1)[0].astype(jnp.float32).reshape(-1, width)
    ffn_grad = grad_out.astype(jnp.bfloat16)
    grad_fc2 = product_left_t(act_low, ffn_grad)
    grad_b2 = jnp.sum(ffn_grad, 0, dtype=jnp.float32)
    grad_act = product_right_t(ffn_grad, w_two)
    (grad_pre,) = pull_gelu(grad_act)
    pre_low = grad_pre.astype(jnp.bfloat16)
    grad_fc1 = product_left_t(third_in, pre_low)
    grad_b1 = jnp.sum(pre_low, 0, dtype=jnp.float32)
    grad_mid, grad_gain3, grad_shift3 = pull_three(product_right_t(pre_low, w_one))
    grad_mid = grad_mid + grad_out
    cross_grad = grad_mid.astype(jnp.bfloat16)
    grad_cout = product_left_t(cross_mixed, cross_grad)
    grad_bco = jnp.sum(cross_grad, 0, dtype=jnp.float32)
    grad_cmix = product_right_t(cross_grad, w_cout).astype(jnp.bfloat16)
    grad_qc, grad_kc, grad_vc = attend_back(
        split_heads(query_cross, batch_rows),
        split_heads(keys_cross, batch_rows),
        split_heads(values_cross, batch_rows),
        cross_ok,
        grad_cmix,
    )
    grad_cq = product_left_t(second_in, grad_qc)
    grad_kv = jnp.concatenate([grad_kc, grad_vc], -1)
    grad_ckv = product_left_t(mem_flat, grad_kv)
    grad_cqv = jnp.concatenate(
        [jnp.sum(grad_qc, 0, dtype=jnp.float32), jnp.sum(grad_vc, 0, dtype=jnp.float32)]
    )
    grad_memory = product_right_t(grad_kv, w_ckv).reshape(encoded.shape)
    memory_grad = lax.psum_scatter(
        grad_memory.astype(jnp.bfloat16), "section", scatter_dimension=2, tiled=True
    )
    grad_after, grad_gain2, grad_shift2 = pull_two(product_right_t(grad_qc, w_cq))
    grad_after = grad_after + grad_mid
    self_grad = grad_after.astype(jnp.bfloat16)
    grad_sout = product_left_t(self_mixed, self_grad)
    grad_bso = jnp.sum(self_grad, 0, dtype=jnp.float32)
    grad_smix = product_right_t(self_grad, w_sout).astype(jnp.bfloat16)
    grad_qs, grad_ks, grad_vs = attend_back(
        split_heads(query_self, batch_rows),
        split_heads(keys_self, batch_rows),
        split_heads(values_self, batch_rows),
        self_ok,
        grad_smix,
    )
    grad_qkv = jnp.concatenate([grad_qs, grad_ks, grad_vs], -1)
    grad_sqkv = product_left_t(first_in, grad_qkv)
    grad_sqv = jnp.concatenate(
        [jnp.sum(grad_qs, 0, dtype=jnp.float32), jnp.sum(grad_vs, 0, dtype=jnp.float32)]
    )
    grad_in, grad_gain1, grad_shift1 = pull_one(product_right_t(grad_qkv, w_sqkv))
    grad_in = grad_in + grad_after
    input_grad = passed_along(
        grad_in.astype(jnp.bfloat16).reshape(1, batch_rows, length, width), "section", -1
    )
    grad_gain = jnp.stack([grad_gain1, grad_gain2, grad_gain3])
    grad_shift = jnp.stack([grad_shift1, grad_shift2, grad_shift3])
    grad_obias = jnp.stack([grad_bso, grad_bco, grad_b2])
    sums = (
        lax.psum_scatter(
            grad_gain.astype(jnp.bfloat16), "dp", scatter_dimension=1, tiled=True
        ).astype(jnp.float32),
        lax.psum_scatter(
            grad_shift.astype(jnp.bfloat16), "dp", scatter_dimension=1, tiled=True
        ).astype(jnp.float32),
        lax.psum_scatter(
            grad_sqkv.astype(jnp.bfloat16), "dp", scatter_dimension=0, tiled=True
        ).astype(jnp.float32),
        lax.psum_scatter(
            grad_sqv.astype(jnp.bfloat16), "dp", scatter_dimension=0, tiled=True
        ).astype(jnp.float32),
        lax.psum_scatter(
            grad_sout.astype(jnp.bfloat16), "dp", scatter_dimension=0, tiled=True
        ).astype(jnp.float32),
        lax.psum_scatter(
            grad_cq.astype(jnp.bfloat16), "dp", scatter_dimension=0, tiled=True
        ).astype(jnp.float32),
        lax.psum_scatter(
            grad_ckv.astype(jnp.bfloat16), "dp", scatter_dimension=0, tiled=True
        ).astype(jnp.float32),
        lax.psum_scatter(
            grad_cqv.astype(jnp.bfloat16), "dp", scatter_dimension=0, tiled=True
        ).astype(jnp.float32),
        lax.psum_scatter(
            grad_cout.astype(jnp.bfloat16), "dp", scatter_dimension=0, tiled=True
        ).astype(jnp.float32),
        lax.psum_scatter(
            grad_obias.astype(jnp.bfloat16), "dp", scatter_dimension=1, tiled=True
        ).astype(jnp.float32),
        lax.psum_scatter(
            grad_fc1.astype(jnp.bfloat16), "dp", scatter_dimension=0, tiled=True
        ).astype(jnp.float32),
        lax.psum_scatter(
            grad_b1.astype(jnp.bfloat16), "dp", scatter_dimension=0, tiled=True
        ).astype(jnp.float32),
        lax.psum_scatter(
            grad_fc2.astype(jnp.bfloat16), "dp", scatter_dimension=0, tiled=True
        ).astype(jnp.float32),
    )
    return (
        output,
        input_grad,
        memory_grad,
        sums[0][None],
        sums[1][None],
        sums[2][None],
        sums[3][None],
        sums[4][None],
        sums[5][None],
        sums[6][None],
        sums[7][None],
        sums[8][None],
        sums[9][None],
        sums[10][None],
        sums[11][None],
        sums[12][None],
    )


Z = 4
P_IN = 4
L = 192
D = 1024
T = P_IN * L
FL = 1024
TILE = 32
MESH = pl.DeviceIdType.MESH
F32 = jnp.float32
BF16 = jnp.bfloat16

WEIGHTS = dict(
    qkv=(256, 768, True),
    so=(64, 1024, False),
    ckv=(256, 512, True),
    cq=(256, 256, True),
    co=(64, 1024, False),
    f1=(256, 1024, True),
    f2=(256, 1024, False),
)
SEMS = 320


def run_if(cond, fn):
    if cond is None:
        fn()
    else:
        pl.when(cond)(fn)


def part(index, size, step=None):
    return pl.ds(pl.multiple_of(index * size, size), size if step is None else step)


def nn(left, right):
    return jnp.dot(left, right, preferred_element_type=F32)


def nt(left, right):
    return lax.dot_general(left, right, (((1,), (1,)), ((), ())), preferred_element_type=F32)


def tn(left, right):
    return lax.dot_general(left, right, (((0,), (0,)), ((), ())), preferred_element_type=F32)


def loop(count, body, unroll=1, first=0):
    def step(index, carry):
        body(index)
        return carry

    lax.fori_loop(first, first + count, step, 0, unroll=unroll)


HALF = L // 2
TILES = HALF // TILE


def gelu_pair(values):
    bell = jnp.exp(-0.5 * values * values)
    step = 1.0 / (1.0 + 0.3275911 * 0.7071067811865476 * jnp.abs(values))
    series = step * (
        0.254829592
        + step
        * (-0.284496736 + step * (1.421413741 + step * (-1.453152027 + step * 1.061405429)))
    )
    above = 0.5 * series * bell
    below = jnp.where(values < 0, above, 1.0 - above)
    return values * below, below + values * bell * 0.3989422804014327


def whiten(rows):
    center = rows - jnp.mean(rows, -1, keepdims=True)
    scale = lax.rsqrt(jnp.mean(center * center, -1, keepdims=True) + EPSILON)
    return center * scale, scale


def whole_kernel(n_sec, mem_cols, *refs):
    given = iter(refs)

    def take(names):
        return SimpleNamespace(**{name: next(given) for name in names})

    def take_weights(**fields):
        for name in WEIGHTS:
            for field in fields:
                setattr(getattr(wt, name), field, next(given))

    wt = SimpleNamespace(**{name: SimpleNamespace() for name in WEIGHTS})
    io = take(
        dict(
            prev=0, mem=0, cot=0, tgt=0, src=0, gain=0, shift=0, out_bias=0,
            self_bias=0, cross_bias=0, unit_bias=0,
        )
    )
    take_weights(source=0)
    vars(io).update(vars(take(dict(output=0, input_grad=0, memory_grad=0))))
    take_weights(result=0)
    vars(io).update(vars(take(dict(sums_out=0))))
    buf = take(buffer_shapes(n_sec, mem_cols))
    set_a, set_b, set_c = (take(REDUCE_SHAPES) for _ in range(3))
    take_weights(weight=0, grad=0, near=0, far=0)
    for weight in (wt.qkv, wt.so, wt.ckv, wt.cq, wt.co):
        weight.to_diag, weight.to_opp, weight.through = next(given), next(given), next(given)
    for weight in (wt.qkv, wt.ckv, wt.cq):
        weight.raw, weight.sorted = next(given), next(given)
    send_sems, recv_sems, local_sems = given

    s = lax.axis_index("section")
    d = lax.axis_index("dp")
    z, q = d // P_IN, d % P_IN
    x, c = q // 2, q % 2
    end = (z % 3) == 0
    mid = (z % 3) != 0
    q_core = q + 1 - 2 * c
    q_x = q + 2 - 4 * x
    q_xc = q_x + 1 - 2 * c
    z_adj = z + 1 - 2 * (z % 2)
    z_opp = 3 - z
    z_diag = (z + 2) % 4
    dev_core, dev_x, dev_xc = (s, z * P_IN + q_core), (s, z * P_IN + q_x), (s, z * P_IN + q_xc)
    dev_adj, dev_opp, dev_diag = (s, z_adj * P_IN + q), (s, z_opp * P_IN + q), (s, z_diag * P_IN + q)
    in_plane = ((q_core, dev_core), (q_x, dev_x), (q_xc, dev_xc))

    counter = [0]
    started = []
    local_counter = [0]

    def slot(count=1):
        counter[0] += count
        return counter[0] - count

    def remote(src, dst, k, device):
        return pltpu.make_async_remote_copy(
            src_ref=src, dst_ref=dst, send_sem=send_sems.at[k], recv_sem=recv_sems.at[k],
            device_id=device, device_id_type=MESH,
        )

    def send(src, dst, k, device, cond=None):
        copy = remote(src, dst, k, device)
        run_if(cond, copy.start)
        record = [copy, cond]
        started.append(record)
        return record

    def sent(record):
        run_if(record[1], record[0].wait_send)
        started[:] = [other for other in started if other is not record]

    def arrived(dst, k, cond=None):
        run_if(cond, remote(dst, dst, k, dev_core).wait_recv)

    def local(src, dst, cond=None):
        copy = pltpu.make_async_copy(src, dst, local_sems.at[local_counter[0]])
        local_counter[0] += 1
        run_if(cond, copy.start)
        return copy

    def keep(src, dst, cond=None):
        result_copies.append((local(src, dst, cond), cond))

    def rows(rows_of, index):
        return rows_of.at[part(index, L)]

    for name, (count, _, by_column) in WEIGHTS.items():
        weight = getattr(wt, name)
        weight.count, weight.by_column = count, by_column
        weight.pieces, weight.piece = 1, 0
        weight.to_use, weight.swap, weight.to_sum, weight.last = slot(5), slot(3), slot(6), slot(3)

    def block(name, index):
        return name.weight.at[part(index * name.pieces + name.piece, name.count)]

    first_weights = [
        SimpleNamespace(
            weight=wt.qkv.weight, count=wt.qkv.count // 2, pieces=2, piece=h, to_use=slot(5)
        )
        for h in range(2)
    ]

    def send_inward(name, src):
        send(src, block(name, z), name.to_use, dev_adj, end)

    def send_across(name, src):
        send(src, block(name, z), name.to_use + 1, dev_opp, mid)

    def weight_outward(name, src):
        send(src, block(name, z), name.to_use, dev_adj, mid)

    def relay_inward(name):
        k = name.to_use
        arrived(block(name, z_adj), k, mid)
        send(block(name, z_adj), block(name, z_adj), k + 2, dev_opp, mid)

    def relay_near(name):
        k = name.to_use
        arrived(block(name, z_opp), k + 1, mid)
        send(block(name, z_opp), block(name, z_opp), k + 3, dev_adj, mid)

    def relay_far(name):
        k = name.to_use
        arrived(block(name, z_diag), k + 2, mid)
        send(block(name, z_diag), block(name, z_diag), k + 4, dev_adj, mid)

    def weight_ready(name):
        k = name.to_use
        arrived(block(name, z_adj), k, end)
        arrived(block(name, z_diag), k + 3, end)
        arrived(block(name, z_opp), k + 4, end)

    def inner_ready(name):
        k = name.to_use
        arrived(block(name, z_opp), k + 1, mid)
        arrived(block(name, z_diag), k + 2, mid)


    def swap_start(name):
        size = name.count // P_IN
        place = name.weight.at[part(z * P_IN + q, size)]
        name.swapped = [
            send(name.sorted.at[q_to], place, name.swap + j, device)
            for j, (q_to, device) in enumerate(in_plane)
        ]
        name.own_copy = [local(name.sorted.at[q], place)]

    def swap_wait(name):
        size = name.count // P_IN
        for j, (q_from, _) in enumerate(in_plane):
            arrived(name.weight.at[part(z * P_IN + q_from, size)], name.swap + j)
        for copy in name.own_copy:
            copy.wait()
        for record in name.swapped:
            sent(record)

    def halves(first, second, odd):
        if odd:
            first = pltpu.roll(first, 64, 1)
        else:
            second = pltpu.roll(second, 64, 1)
        lane = lax.broadcasted_iota(jnp.int32, first.shape, 1)
        return jnp.where(lane < 64, first, second)

    def tile_of(index):
        return slice(index * 128, index * 128 + 128)

    def sort_columns(name):
        for q_to in range(P_IN):
            for tile in range(name.sorted.shape[2] // 128):
                at = 4 * tile + q_to // 2
                first = name.raw[:, tile_of(at)].astype(F32)
                second = name.raw[:, tile_of(at + 2)].astype(F32)
                name.sorted[q_to, :, tile_of(tile)] = halves(first, second, q_to % 2).astype(BF16)

    def unsort_columns(name):
        for tile in range(name.raw.shape[1] // 128):
            group, u = tile // 8, tile % 8
            at = 2 * group + u // 4
            first = name.sorted[2 * (u % 2), :, tile_of(at)].astype(F32)
            second = name.sorted[2 * (u % 2) + 1, :, tile_of(at)].astype(F32)
            name.raw[:, tile_of(tile)] = halves(first, second, (u // 2) % 2).astype(BF16)

    unit_swap, unit_last = slot(3 * Z), slot(3 * Z)

    def unit_columns(rows_of, tile, q_at):
        return rows_of.at[:, part(tile * P_IN + q_at, 256)]

    def unit_swap_start():
        size = wt.f1.count // P_IN
        place = wt.f1.weight.at[part(z * P_IN + q, size)]
        wt.f1.own_copy = []
        for tile in range(Z):
            at = place.at[:, part(tile, 256)]
            for j, (q_to, device) in enumerate(in_plane):
                send(unit_columns(wt.f1.source, tile, q_to), at, unit_swap + 3 * tile + j, device)
            wt.f1.own_copy.append(local(unit_columns(wt.f1.source, tile, q), at))

    def unit_swap_wait(cond):
        size = wt.f1.count // P_IN
        for tile in range(Z):
            for j, (q_from, _) in enumerate(in_plane):
                place = wt.f1.weight.at[part(z * P_IN + q_from, size)]
                arrived(place.at[:, part(tile, 256)], unit_swap + 3 * tile + j, cond)
        for copy in wt.f1.own_copy:
            run_if(cond, copy.wait)

    def grad_block(name, index):
        return name.grad.at[part(index, name.count)]

    def grad_send_far(name):
        return send(grad_block(name, z_opp), name.to_diag, name.to_sum, dev_adj, end)

    def grad_send_middle(name):
        return send(grad_block(name, z_diag), name.to_opp, name.to_sum + 1, dev_adj, end)

    def grad_send_near(name):
        return send(grad_block(name, z_adj), name.near, name.to_sum + 2, dev_adj, end)

    def grad_send(name):
        grad_send_far(name)
        grad_send_middle(name)
        grad_send_near(name)

    def add_rows(count, body):
        size = min(count, 64)
        loop(count // size, lambda i: body(part(i, size)))

    def grad_add(name, landed, index):
        def one(place):
            own = grad_block(name, index)[place, :].astype(F32)
            landed[place, :] = (own + landed[place, :].astype(F32)).astype(BF16)

        add_rows(name.count, one)

    def grad_combine_far(name):
        k = name.to_sum
        arrived(name.to_diag, k, mid)
        run_if(mid, lambda: grad_add(name, name.to_diag, z_diag))
        send(name.to_diag, name.through, k + 3, dev_opp, mid)

    def grad_combine_middle(name):
        k = name.to_sum
        arrived(name.to_opp, k + 1, mid)
        run_if(mid, lambda: grad_add(name, name.to_opp, z_opp))
        send(name.to_opp, name.far, k + 4, dev_opp, mid)

    def grad_combine(name):
        grad_combine_far(name)
        grad_combine_middle(name)

    def grad_outward(name):
        k = name.to_sum
        arrived(name.through, k + 3, mid)
        run_if(mid, lambda: grad_add(name, name.through, z_adj))
        send(name.through, name.near, k + 5, dev_adj, mid)

    result_copies = []

    def inner_grad_far(name):
        send(grad_block(name, z_diag), name.far, name.to_sum, dev_opp, mid)

    def inner_grad_near(name):
        send(grad_block(name, z_opp), name.near, name.to_sum + 1, dev_opp, mid)

    def inner_grad_combine(name):
        k = name.to_sum

        def add():
            arrived(name.far, k)

            def one(place):
                own = grad_block(name, z_adj)[place, :].astype(F32)
                name.far[place, :] = (own + name.far[place, :].astype(F32)).astype(BF16)

            add_rows(name.count, one)

        run_if(mid, add)
        send(name.far, name.near, k + 2, dev_adj, mid)

    def inner_grad_total(name, cond):
        k = name.to_sum
        if cond is end:
            arrived(name.near, k + 2, end)
        else:
            arrived(name.near, k + 1, mid)
            run_if(mid, lambda: grad_add(name, name.near, z))

    def grad_total(name):
        k = name.to_sum
        arrived(name.near, k + 5, end)
        arrived(name.near, k + 2, mid)
        arrived(name.far, k + 4, mid)

        def add_far():
            def one(place):
                total = name.near[place, :].astype(F32) + name.far[place, :].astype(F32)
                name.near[place, :] = (total + grad_block(name, z)[place, :].astype(F32)).astype(BF16)

            add_rows(name.count, one)

        run_if(mid, add_far)
        run_if(end, lambda: grad_add(name, name.near, z))

    def grad_final(name):
        grad_total(name)
        if name.by_column:
            size = name.count // P_IN
            for j, (q_to, device) in enumerate(in_plane):
                src = name.near.at[part(q_to, size)]
                send(src, name.sorted.at[q], name.last + j, device)
            src = name.near.at[part(q, size)]
            name.own_copy = [local(src, name.sorted.at[q])]
        else:
            keep(name.near, name.result)

    def inner_final(cond):
        inner_grad_total(wt.f2, cond)
        keep(wt.f2.near, wt.f2.result, cond)
        inner_grad_total(wt.f1, cond)
        size = wt.f1.count // P_IN
        for tile in range(Z):
            dst = unit_columns(wt.f1.result, tile, q)
            for j, (q_to, device) in enumerate(in_plane):
                src = wt.f1.near.at[part(q_to, size), part(tile, 256)]
                send(src, dst, unit_last + 3 * tile + j, device, cond)
            keep(wt.f1.near.at[part(q, size), part(tile, 256)], dst, cond)

    def last_wait(name):
        for j, (q_from, _) in enumerate(in_plane):
            arrived(name.sorted.at[q_from], name.last + j)
        for copy in name.own_copy:
            copy.wait()
        unsort_columns(name)
        keep(name.raw, name.result)

    def unit_last_wait():
        for tile in range(Z):
            for j, (q_from, _) in enumerate(in_plane):
                place = unit_columns(wt.f1.result, tile, q_from)
                arrived(place, unit_last + 3 * tile + j)

    def piece(name, index, h, parts):
        size = L // parts
        return name.at[part(index * parts + h, size)]

    def half_major(name, index, h, parts=2):
        return name.at[part(h * P_IN + index, HALF)]

    def gather_open(name, cond=None, parts=1, lay=piece):
        return name, slot(3 * parts), [], cond, parts, lay

    def gather_part(ticket, h, cond=None):
        name, k, records, usual, parts, lay = ticket
        cond = usual if cond is None else cond
        own = lay(name, q, h, parts)
        records.append(send(own, own, k + 3 * h, dev_x, cond))
        records.append(send(own, own, k + 3 * h + 1, dev_core, cond))

    def gather_start(name, cond=None):
        ticket = gather_open(name, cond)
        gather_part(ticket, 0)
        return ticket

    def gather_relay_part(ticket, h):
        name, k, records, cond, parts, lay = ticket
        other = lay(name, q_x, h, parts)
        arrived(other, k + 3 * h, cond)
        records.append(send(other, other, k + 3 * h + 2, dev_core, cond))

    def gather_ready_part(ticket, h):
        name, k, _, cond, parts, lay = ticket
        arrived(lay(name, q_core, h, parts), k + 3 * h + 1, cond)
        arrived(lay(name, q_xc, h, parts), k + 3 * h + 2, cond)

    def gather_relay(ticket):
        for h in range(ticket[4]):
            gather_relay_part(ticket, h)

    def gather_ready(ticket):
        for h in range(ticket[4]):
            gather_ready_part(ticket, h)

    def gather_finish(ticket):
        gather_relay(ticket)
        gather_ready(ticket)

    def reduce_start(which, cond=None):
        k = slot(4)
        out = which.parts
        first = send(rows(out, q_xc), rows(which.core, 1), k, dev_core, cond)
        second = send(rows(out, q_core), rows(which.core, 0), k + 1, dev_core, cond)
        return which, k, [first, second], cond, piece

    def reduce_open(which, cond):
        return which, slot(6), [], cond, half_major

    def reduce_start_half(ticket, h):
        which, k, records, cond, lay = ticket
        for j, index in ((1, q_xc), (0, q_core)):
            src, dst = lay(which.parts, index, h), piece(which.core, j, h, 2)
            records.append(send(src, dst, k + 4 * h + 1 - j, dev_core, cond))

    def reduce_relay_half(ticket, h):
        which, k, records, cond, lay = ticket
        landed = piece(which.core, 1, h, 2)
        if lay is half_major:
            arrived(landed, k + 4 * h, cond)
        elif h == 0:
            arrived(rows(which.core, 1), k, cond)
        mine = lay(which.parts, q_x, h, 2)

        def add():
            def one(i):
                place = part(i, TILE)
                total = mine[place, :].astype(F32) + landed[place, :].astype(F32)
                mine[place, :] = total.astype(BF16)

            loop(TILES, one)

        run_if(cond, add)
        dst = which.across.at[part(h, HALF)]
        records.append(send(mine, dst, k + 2 + h, dev_x, cond))
        return records[-1]

    def reduce_relay(ticket):
        reduce_relay_half(ticket, 0)
        reduce_relay_half(ticket, 1)

    def reduce_ready_half(ticket, h):
        which, k, _, cond, lay = ticket
        if lay is half_major:
            arrived(piece(which.core, 0, h, 2), k + 4 * h + 1, cond)
        elif h == 0:
            arrived(rows(which.core, 0), k + 1, cond)
        arrived(which.across.at[part(h, HALF)], k + 2 + h, cond)

    def reduce_ready(ticket):
        reduce_ready_half(ticket, 0)
        reduce_ready_half(ticket, 1)

    def reduced(ticket, place):
        which = ticket[0]
        total = rows(which.parts, q)[place, :].astype(F32)
        total = total + rows(which.core, 0)[place, :].astype(F32)
        return total + which.across[place, :].astype(F32)

    def fold(ticket, dst, halves=(0, 1)):
        which, lay = ticket[0], ticket[4]
        for h in halves:
            mine, landed = lay(which.parts, q, h, 2), piece(which.core, 0, h, 2)

            def one(i, h=h, mine=mine, landed=landed):
                place, here = part(i, TILE), part(i + h * TILES, TILE)
                total = mine[place, :].astype(F32) + landed[place, :].astype(F32)
                dst[here, :] = (total + which.across[here, :].astype(F32)).astype(BF16)

            loop(TILES, one)

    def reduce_done(ticket):
        for record in ticket[2]:
            sent(record)

    def spread_start(place):
        k = slot(8)
        for j, device in enumerate((dev_diag, dev_opp, dev_adj)):
            send(place(z), place(z), k + j, device)
        return place, k

    def spread_wait(ticket):
        place, k = ticket
        for j, plane in enumerate((z_diag, z_opp, z_adj)):
            arrived(place(plane), k + j)

    def spread_plane(ticket, name):
        k = ticket[1]
        for j, (_, device) in enumerate(in_plane):
            send(name.at[q], name.at[q], k + 5 + j, device)

    def spread_ready(ticket, name):
        k = ticket[1]
        for j, (q_from, _) in enumerate(in_plane):
            arrived(name.at[q_from], k + 5 + j)

    def lanes(j, size=256):
        return part(j, size)

    def matmul(left, right, dst, bias=None, bias_row=0, bias_at=0):
        count = right.shape[1] // 256

        def one(j):
            tile = nn(left[...], right[:, lanes(j)])
            if bias is not None:
                tile = tile + bias[bias_row:bias_row + 1, part(j + bias_at, 256)]
            dst[:, lanes(j)] = tile.astype(BF16)

        loop(count, one)

    def matmul_back(left, right, dst, at=slice(0, T)):
        def one(j):
            dst[at, lanes(j)] = nt(left[at, :], right[lanes(j), :]).astype(BF16)

        loop(right.shape[0] // 256, one)

    def weight_grad(left, right, name, more=False):
        def one(j):
            total = tn(left[:, lanes(j)], right[...])
            if more:
                total = total + name.grad[lanes(j), :].astype(F32)
            name.grad[lanes(j), :] = total.astype(BF16)

        loop(left.shape[1] // 256, one)

    low_half = lax.broadcasted_iota(jnp.int32, (L, 128), 1) < 64
    keep_low = low_half.astype(F32).astype(BF16)
    keep_high = (1.0 - low_half.astype(F32)).astype(BF16)

    def both(pair):
        return jnp.concatenate([pair * keep_low, pair * keep_high], axis=0)

    def merge(stacked):
        return jnp.where(low_half, stacked[:L], stacked[L:])

    def attention(qref, q_at, kref, k_at, v_at, causal, length_row, probs, dst):
        def one(i):
            r, pair = i // 2, i % 2
            place = part(r, L)
            query = both(qref[place, part(pair + q_at, 128)])
            scores = nt(query, kref[place, part(pair + k_at, 128)]) * HD ** (-0.5)
            key = lax.broadcasted_iota(jnp.int32, scores.shape, 1)
            limit = buf.sva[r, z][length_row:length_row + 1, 0:1].astype(F32)
            allowed = key.astype(F32) < limit
            if causal:
                at = lax.broadcasted_iota(jnp.int32, scores.shape, 0)
                at = jnp.where(at < L, at, at - L)
                allowed = allowed & (key <= at)
            scores = jnp.where(allowed, scores, MASKED)
            raised = jnp.exp(scores - jnp.max(scores, -1, keepdims=True))
            weights = (raised * (1.0 / jnp.sum(raised, -1, keepdims=True))).astype(BF16)
            probs[i] = weights
            mixed = nn(weights, kref[place, part(pair + v_at, 128)])
            dst[place, part(pair, 128)] = merge(mixed).astype(BF16)

        loop(2 * P_IN, one, 2)

    def attention_back(qref, q_at, kref, k_at, v_at, probs, grad):
        def one(i):
            r, pair = i // 2, i % 2
            place = part(r, L)
            query = both(qref[place, part(pair + q_at, 128)])
            key = kref[place, part(pair + k_at, 128)]
            value = kref[place, part(pair + v_at, 128)]
            mixed_grad = both(grad[place, part(pair, 128)])
            weights = probs[i]
            soft = weights.astype(F32)
            grad_probs = nt(mixed_grad, value)
            delta = jnp.sum(soft * grad_probs, -1, keepdims=True)
            grad_scores = (soft * (grad_probs - delta)).astype(BF16)
            scale = HD ** (-0.5)
            grad_query = merge(nn(grad_scores, key)) * scale
            grad_key = tn(grad_scores, query) * scale
            grad_value = tn(weights, mixed_grad)
            qref[place, part(pair + q_at, 128)] = grad_query.astype(BF16)
            kref[place, part(pair + k_at, 128)] = grad_key.astype(BF16)
            kref[place, part(pair + v_at, 128)] = grad_value.astype(BF16)

        loop(2 * P_IN, one, 2)

    def column_sums(source, first, count, row, at):
        def one(j):
            values = source[:, part(j + first, 256)].astype(F32)
            buf.sg[row:row + 1, part(j + at, 256)] = jnp.sum(values, 0, keepdims=True)

        loop(count, one)

    def norm(load, index, dst, halves=(0, 1)):
        def one(i):
            place = part(i, TILE)
            normed, _ = whiten(load(place))
            gain, shift = buf.vec[index:index + 1, :], buf.vec[index + 3:index + 4, :]
            rows(dst, q)[place, :] = (normed * gain + shift).astype(BF16)

        loop(TILES * len(halves), one, first=TILES * halves[0])

    def norm_back(load, incoming, index, base, dst, low, out_row=None, halves=(0, 1)):
        zero = jnp.zeros((1, D), F32)

        def one(i, carry):
            gain_sum, shift_sum, out_sum = carry
            place = part(i, TILE)
            normed, scale = whiten(load(place))
            grad = incoming(place)
            gained = grad * buf.vec[index:index + 1, :]
            back = gained - jnp.mean(gained, -1, keepdims=True)
            back = back - normed * jnp.mean(gained * normed, -1, keepdims=True)
            total = base(place) + scale * back
            if dst is not None:
                dst[place, :] = total
            rounded = total.astype(BF16)
            low(place, rounded)
            return (
                gain_sum + jnp.sum(grad * normed, 0, keepdims=True),
                shift_sum + jnp.sum(grad, 0, keepdims=True),
                out_sum + jnp.sum(rounded.astype(F32), 0, keepdims=True),
            )

        first = TILES * halves[0]
        last = first + TILES * len(halves)
        gain_sum, shift_sum, out_sum = lax.fori_loop(first, last, one, (zero, zero, zero))
        buf.sg[index:index + 1, :] = buf.sg[index:index + 1, :] + gain_sum
        buf.sg[index + 3:index + 4, :] = buf.sg[index + 3:index + 4, :] + shift_sum
        if out_row is not None:
            buf.sg[out_row:out_row + 1, :] = buf.sg[out_row:out_row + 1, :] + out_sum

    gate = pltpu.get_barrier_semaphore()
    partners = [device for _, device in in_plane] + [dev_adj, dev_opp, dev_diag]
    partners += [((s + j) % n_sec, d) for j in range(1, n_sec)]
    for device in partners:
        pl.semaphore_signal(gate, inc=1, device_id=device, device_id_type=MESH)
    raw_copies = [local(weight.source, weight.raw) for weight in (wt.qkv, wt.ckv, wt.cq)]
    low_lanes = lax.broadcasted_iota(jnp.int32, (3, 128), 1) < 64
    even_lanes = (jnp.zeros((3, 128), jnp.int32) + c) == 0
    for row, pieces in ((0, io.gain), (3, io.shift), (6, io.out_bias)):
        value = pieces[...].astype(F32)
        twice = jnp.concatenate([value, value], 1)
        buf.sg[row:row + 3, 0:128] = jnp.where(low_lanes == even_lanes, twice, 0.0)
    buf.sg[9:10, 0:128] = io.self_bias[...].astype(F32)
    buf.sg[10:11, 0:128] = io.cross_bias[...].astype(F32)
    buf.sg[11:12, 0:128] = io.unit_bias[:, 0:128].astype(F32)
    buf.sg[12:13, 0:128] = io.unit_bias[:, 128:256].astype(F32)
    buf.sg[13:14, 0:128] = jnp.zeros((1, 128), F32) + io.tgt[0].astype(F32)
    buf.sg[14:15, 0:128] = jnp.zeros((1, 128), F32) + io.src[0].astype(F32)
    buf.sg[15:16, 0:128] = jnp.zeros((1, 128), F32)
    buf.sva[q, z] = buf.sg[:, 0:128].astype(BF16)

    raw_copies[0].wait()
    sort_columns(wt.qkv)
    pl.semaphore_wait(gate, len(partners))

    sv = spread_start(lambda plane: buf.sva.at[q, plane])
    swap_start(wt.qkv)
    k_prev, k_cot, k_mem = slot(), slot(), slot(n_sec)
    send(io.prev, buf.hb, k_prev, ((s + 1) % n_sec, d))
    mem_slot = rows(buf.m, q)
    for j in range(1, n_sec):
        send(io.mem, mem_slot.at[:, part(s, mem_cols)], k_mem + j, ((s + j) % n_sec, d))
    mem_copy = local(io.mem, mem_slot.at[:, part(s, mem_cols)])
    send(io.cot, rows(buf.e3, q), k_cot, ((s + n_sec - 1) % n_sec, d))
    for weight in (wt.so, wt.co, wt.f2):
        weight.own_copy = [local(weight.source, block(weight, z))]
    send_inward(wt.so, wt.so.source)
    send_across(wt.so, wt.so.source)
    weight_outward(wt.so, wt.so.source)
    swap_wait(wt.qkv)
    for weight in first_weights:
        send_inward(weight, block(weight, z))
        send_across(weight, block(weight, z))
        weight_outward(weight, block(weight, z))
    spread_wait(sv)
    spread_plane(sv, buf.sva)
    for weight, copy in ((wt.ckv, raw_copies[1]), (wt.cq, raw_copies[2])):
        copy.wait()
        sort_columns(weight)
        swap_start(weight)
    spread_ready(sv, buf.sva)

    for tile in range(D // 128):
        pair = buf.sva[2 * (tile % 2), tile // 2].astype(F32)
        pair = pair + buf.sva[2 * (tile % 2) + 1, tile // 2].astype(F32)
        buf.vec[:, tile * 128:(tile + 1) * 128] = pair
    half = lax.broadcasted_iota(jnp.int32, (16, 128), 1) < 64
    even = (jnp.zeros((16, 128), jnp.int32) + c) == 0
    buf.bias[...] = jnp.zeros((8, D), F32)
    for kind in range(2):
        for tile in range(2):
            first = buf.sva[x, tile + 2 * kind].astype(F32)
            second = buf.sva[2 + x, tile + 2 * kind].astype(F32)
            lower = jnp.where(even, first, pltpu.roll(first, 64, 1))
            upper = jnp.where(even, pltpu.roll(second, 64, 1), second)
            both_heads = jnp.where(half, lower, upper)
            for which in range(2):
                at = 512 * kind + 128 * tile
                buf.bias[which:which + 1, at:at + 128] = both_heads[9 + which:10 + which]
    for tile in range(Z):
        unit = buf.sva[q, tile].astype(F32)
        buf.bias[2:3, 256 * tile:256 * tile + 128] = unit[11:12]
        buf.bias[2:3, 256 * tile + 128:256 * tile + 256] = unit[12:13]
    buf.sg[...] = jnp.zeros((16, D), F32)

    relay_inward(first_weights[0])
    relay_near(first_weights[0])
    arrived(buf.hb, k_prev)

    def hidden(place):
        return buf.hb[place, :].astype(F32)

    norm(hidden, 0, buf.a1)
    a1 = gather_start(buf.a1)
    unit_swap_start()
    relay_inward(first_weights[1])
    relay_near(first_weights[1])
    relay_inward(wt.so)
    swap_wait(wt.ckv)
    send_inward(wt.ckv, block(wt.ckv, z))
    swap_wait(wt.cq)
    send_inward(wt.cq, block(wt.cq, z))
    send_inward(wt.co, wt.co.source)
    send_across(wt.ckv, block(wt.ckv, z))
    for j in range(1, n_sec):
        origin = (s + n_sec - j) % n_sec
        arrived(mem_slot.at[:, part(origin, mem_cols)], k_mem + j)
    mem_copy.wait()
    memory = gather_start(buf.m)
    arrived(rows(buf.e3, q), k_cot)
    k_units = slot(16)
    to_middle = [send(rows(buf.e3, q), rows(buf.e3, q), k_units + 9, dev_x, end)]

    def cot_inward(index, k):
        for h in range(2):
            src, dst = piece(buf.e3, index, h, 2), half_major(buf.e3b, index, h)
            to_middle.append(send(src, dst, k + h, dev_adj, end))

    cot_inward(q, k_units)
    relay_far(first_weights[0])
    gather_relay(a1)
    relay_far(first_weights[1])
    relay_near(wt.so)
    relay_inward(wt.ckv)
    gather_ready(a1)
    unit_swap_wait(end)
    send_inward(wt.f1, block(wt.f1, z))
    for weight in first_weights:
        weight_ready(weight)
    matmul(buf.a1, wt.qkv.weight, buf.qkv, buf.bias, 0)
    relay_far(wt.so)
    weight_outward(wt.ckv, block(wt.ckv, z))
    send_across(wt.cq, block(wt.cq, z))
    attention(buf.qkv, 0, buf.qkv, 2, 4, True, 13, buf.p1, buf.o1)
    relay_inward(wt.cq)
    send_across(wt.co, wt.co.source)
    wt.so.own_copy[0].wait()
    weight_ready(wt.so)
    matmul(buf.o1, wt.so.weight, set_a.parts)
    step = reduce_start(set_a)
    send_inward(wt.f2, wt.f2.source)
    relay_inward(wt.co)
    relay_near(wt.ckv)
    weight_outward(wt.cq, block(wt.cq, z))
    reduce_relay(step)
    arrived(rows(buf.e3, q_x), k_units + 9, end)
    cot_inward(q_x, k_units + 2)
    gather_finish(memory)
    relay_far(wt.ckv)
    unit_swap_wait(mid)
    send_across(wt.f1, block(wt.f1, z))

    def after_self(i):
        place = part(i, TILE)
        buf.h1[place, :] = hidden(place) + (reduced(step, place) + buf.vec[6:7, :])

    a2 = gather_open(buf.a2, None, 2)
    for h in range(2):
        reduce_ready_half(step, h)
        loop(TILES, after_self, first=h * TILES)
        norm(lambda place: buf.h1[place, :], 1, buf.a2, (h,))
        gather_part(a2, h)
    reduce_done(step)
    relay_near(wt.cq)
    weight_outward(wt.co, wt.co.source)
    relay_far(wt.cq)
    weight_ready(wt.ckv)
    matmul(buf.m, wt.ckv.weight, buf.kv, buf.bias, 1, 1)
    relay_near(wt.co)
    send_across(wt.f2, wt.f2.source)
    relay_far(wt.co)
    relay_inward(wt.f1)

    gather_finish(a2)
    e3 = gather_start(buf.e3, mid)
    weight_ready(wt.cq)
    matmul(buf.a2, wt.cq.weight, buf.q2, buf.bias, 1)
    attention(buf.q2, 0, buf.kv, 0, 2, False, 14, buf.p2, buf.o2)
    wt.co.own_copy[0].wait()
    weight_ready(wt.co)
    matmul(buf.o2, wt.co.weight, set_b.parts)
    step = reduce_start(set_b)
    relay_inward(wt.f2)
    gather_finish(e3)
    reduce_relay(step)

    def after_cross(i):
        place = part(i, TILE)
        buf.h2[place, :] = buf.h1[place, :] + (reduced(step, place) + buf.vec[7:8, :])

    a3 = gather_open(buf.a3, mid, 2)
    for h in range(2):
        reduce_ready_half(step, h)
        loop(TILES, after_cross, first=h * TILES)
        norm(lambda place: buf.h2[place, :], 2, buf.a3, (h,))
        send(piece(buf.a3, q, h, 2), half_major(buf.a3b, q, h), k_units + 10 + h, dev_adj, end)
        gather_part(a3, h)
    reduce_done(step)

    def units(normed, activs, slopes, at=slice(0, T)):
        def one(j):
            value = nn(normed[at, :], wt.f1.weight[:, lanes(j)]) + buf.bias[2:3, lanes(j)]
            activ, slope = gelu_pair(value)
            activs[at, lanes(j)] = activ.astype(BF16)
            slopes[at, lanes(j)] = slope.astype(BF16)

        loop(FL // 256, one, 2)

    def units_back(grad, slopes, at=slice(0, T)):
        def one(j):
            value = nt(grad[at, :], wt.f2.weight[lanes(j), :])
            low = (value * slopes[at, lanes(j)].astype(F32)).astype(BF16)
            slopes[at, lanes(j)] = low
            total = jnp.sum(low.astype(F32), 0, keepdims=True)
            buf.sg[10:11, lanes(j)] = buf.sg[10:11, lanes(j)] + total

        loop(FL // 256, one)

    def weight_grads(left, right, left_b, right_b, name, first, count):
        def one(j):
            total = tn(left[:, lanes(j)], right[...]) + tn(left_b[:, lanes(j)], right_b[...])
            name.grad[lanes(j), :] = total.astype(BF16)

        loop(count, one, first=first)

    def finish(incoming):
        def one(i):
            place = part(i, TILE)
            total = buf.h2[place, :] + (incoming(place) + buf.vec[8:9, :])
            buf.stage[place, :] = total.astype(BF16)

        loop(L // TILE, one)

    def on_mid(fn, *args):
        run_if(mid, lambda: fn(*args))

    def cot_sum(i, carry):
        return carry + jnp.sum(rows(buf.e3, q)[part(i, TILE), :].astype(F32), 0, keepdims=True)

    buf.sg[8:9, :] = lax.fori_loop(0, L // TILE, cot_sum, jnp.zeros((1, D), F32))

    for index, k in ((q, k_units), (q_x, k_units + 2)):
        for h in range(2):
            landed = half_major(buf.e3b, index, h)
            arrived(landed, k + h, mid)
            send(landed, landed, k + 4 + h, dev_core, mid)
    gather_relay(a3)
    a3b = gather_open(buf.a3b, mid, 2, half_major)
    arrived(half_major(buf.a3b, q, 0), k_units + 10, mid)
    gather_part(a3b, 0)
    gather_ready(a3)
    inner_ready(wt.f1)
    on_mid(units, buf.a3, buf.g, buf.gp)
    arrived(half_major(buf.a3b, q, 1), k_units + 11, mid)
    gather_part(a3b, 1)
    on_mid(weight_grad, buf.g, buf.e3, wt.f2)
    for index, k in ((q_core, k_units + 4), (q_xc, k_units + 6)):
        for h in range(2):
            arrived(half_major(buf.e3b, index, h), k + h, mid)
    gather_relay_part(a3b, 0)
    wt.f2.own_copy[0].wait()
    inner_ready(wt.f2)
    on_mid(matmul, buf.g, wt.f2.weight, set_c.parts)
    final = reduce_start(set_c, mid)
    gather_ready_part(a3b, 0)
    step_b = reduce_open(set_b, mid)
    for h in range(2):
        at = slice(h * T // 2, (h + 1) * T // 2)
        if h == 1:
            gather_ready_part(a3b, 1)
        on_mid(units, buf.a3b, buf.gb, buf.gpb, at)
        if h == 0:
            reduce_relay(final)
        else:
            reduce_relay_half(step_b, 0)
            on_mid(weight_grad, buf.gb, buf.e3b, wt.f2, True)
            inner_grad_far(wt.f2)
            inner_grad_near(wt.f2)
        on_mid(units_back, buf.e3b, buf.gpb, at)
        if h == 0:
            gather_relay_part(a3b, 1)
        on_mid(matmul_back, buf.gpb, wt.f1.weight, set_b.parts, at)
        reduce_start_half(step_b, h)

    def back_outward(h):
        reduce_ready_half(step_b, h)
        on_mid(fold, step_b, buf.back, (h,))
        ready = buf.back.at[part(h, HALF)]
        send(ready, ready, k_units + 12 + h, dev_adj, mid)

    reduce_relay_half(step_b, 1)
    on_mid(units_back, buf.e3, buf.gp)
    back_outward(0)
    on_mid(matmul_back, buf.gp, wt.f1.weight, set_a.parts)
    reduce_ready(final)
    on_mid(finish, lambda place: reduced(final, place))
    reduce_done(final)
    step = reduce_start(set_a, mid)
    back_outward(1)
    reduce_relay(step)
    on_mid(weight_grads, buf.a3, buf.gp, buf.a3b, buf.gpb, wt.f1, 0, Z)
    inner_grad_far(wt.f1)
    inner_grad_near(wt.f1)
    on_mid(matmul, buf.gb, wt.f2.weight, set_c.parts)

    def store(name):
        def low(place, value):
            rows(name, q)[place, :] = value

        return low

    def units_norm_back(incoming, halves):
        norm_back(
            lambda place: buf.h2[place, :], incoming, 2,
            lambda place: rows(buf.e3, q)[place, :].astype(F32), buf.dh, store(buf.e2), 7, halves,
        )

    reduce_done(e3)
    for record in to_middle:
        sent(record)
    reduce_ready(step)
    final_b = reduce_open(set_c, mid)
    reduce_start_half(final_b, 0)
    reduce_start_half(final_b, 1)
    on_mid(units_norm_back, lambda place: reduced(step, place), (0, 1))
    e2 = gather_open(buf.e2, None, 2)
    gather_part(e2, 0, mid)
    gather_part(e2, 1, mid)
    inner_grad_combine(wt.f2)
    for h in range(2):
        arrived(buf.back.at[part(h, HALF)], k_units + 12 + h, end)
        run_if(
            end,
            lambda h=h: units_norm_back(lambda place: buf.back[place, :].astype(F32), (h,)),
        )
        gather_part(e2, h, end)
    reduce_done(step)
    reduce_done(step_b)
    gather_finish(e2)
    reduce_relay(final_b)

    weight_grad(buf.o2, buf.e2, wt.co)
    grad_send(wt.co)
    matmul_back(buf.e2, wt.co.weight, buf.do)
    attention_back(buf.q2, 0, buf.kv, 0, 2, buf.p2, buf.do)
    matmul_back(buf.q2, wt.cq.weight, set_b.parts)
    step = reduce_start(set_b)
    weight_grad(buf.a2, buf.q2, wt.cq)
    grad_send(wt.cq)
    reduce_relay(step)
    weight_grad(buf.m, buf.kv, wt.ckv)
    grad_send(wt.ckv)
    matmul_back(buf.kv, wt.ckv.weight, set_a.parts)
    mem_step = reduce_start(set_a)
    column_sums(buf.q2, 0, 1, 9, 2)
    column_sums(buf.kv, 1, 1, 9, 3)
    reduce_ready(final_b)
    on_mid(fold, final_b, buf.tail)
    send(buf.tail, buf.tail, k_units + 14, dev_adj, mid)
    reduce_done(final_b)
    grad_combine(wt.co)
    inner_grad_combine(wt.f1)
    grad_combine(wt.cq)
    e1 = gather_open(buf.e3, None, 2)
    for h in range(2):
        reduce_ready_half(step, h)
        norm_back(
            lambda place: buf.h1[place, :], lambda place: reduced(step, place), 1,
            lambda place: buf.dh[place, :], buf.dh, store(buf.e3), 6, (h,),
        )
        gather_part(e1, h)
    reduce_done(step)
    grad_combine(wt.ckv)
    gather_finish(e1)
    reduce_relay(mem_step)

    weight_grad(buf.o1, buf.e3, wt.so)
    grad_send(wt.so)
    matmul_back(buf.e3, wt.so.weight, buf.do)
    attention_back(buf.qkv, 0, buf.qkv, 2, 4, buf.p1, buf.do)
    grad_outward(wt.co)
    grad_combine(wt.so)
    run_if(end, lambda: weight_grad(buf.a1, buf.qkv, wt.qkv))
    grad_send_far(wt.qkv)
    grad_send_middle(wt.qkv)
    matmul_back(buf.qkv, wt.qkv.weight, set_b.parts)
    step = reduce_start(set_b)
    on_mid(weight_grad, buf.a1, buf.qkv, wt.qkv)
    column_sums(buf.qkv, 0, 1, 9, 0)
    column_sums(buf.qkv, 2, 1, 9, 1)
    grad_outward(wt.cq)
    reduce_relay(step)
    inner_final(mid)
    grad_combine_far(wt.qkv)

    reduce_ready(mem_step)
    fold(mem_step, buf.mb)
    k_back = slot(n_sec)
    for j in range(1, n_sec):
        to = (s + j) % n_sec
        send(buf.mb.at[:, part(to, mem_cols)], buf.ml.at[j], k_back + j, (to, d))
    grad_outward(wt.ckv)
    reduce_ready(step)

    def store_stage(place, value):
        buf.ig[place, :] = value

    norm_back(
        hidden, lambda place: reduced(step, place), 0,
        lambda place: buf.dh[place, :], None, store_stage,
    )
    k_in = slot()
    send(buf.ig, io.input_grad, k_in, ((s + n_sec - 1) % n_sec, d))
    buf.sga[z] = buf.sg[...].astype(BF16)
    sums = spread_start(lambda plane: buf.sga.at[plane])
    grad_combine_middle(wt.qkv)
    grad_outward(wt.so)
    inner_final(end)
    for weight in (wt.co, wt.cq):
        grad_final(weight)
    grad_send_near(wt.qkv)
    grad_outward(wt.qkv)
    grad_final(wt.ckv)
    spread_wait(sums)
    planes = buf.sga[0].astype(F32)
    for plane in range(1, Z):
        planes = planes + buf.sga[plane].astype(F32)
    buf.sgp[q] = planes.astype(BF16)
    spread_plane(sums, buf.sgp)
    grad_final(wt.so)
    grad_final(wt.qkv)

    arrived(buf.tail, k_units + 14, end)
    run_if(end, lambda: finish(lambda place: buf.tail[place, :].astype(F32)))
    for j in range(1, n_sec):
        arrived(buf.ml.at[j], k_back + j)

    def memory_total(i):
        place = part(i, TILE)
        total = buf.mb[place, part(s, mem_cols)].astype(F32)
        for j in range(1, n_sec):
            total = total + buf.ml[j, place, :].astype(F32)
        buf.mo[place, :] = total.astype(BF16)

    loop(L // TILE, memory_total)
    keep(buf.mo, io.memory_grad)
    unit_last_wait()
    last_wait(wt.cq)
    last_wait(wt.ckv)
    keep(buf.stage, io.output)
    spread_ready(sums, buf.sgp)

    def per_unit(q_at, at):
        return buf.sgp[q_at, :, at].astype(F32)

    at = part(d // 2, 128)
    feature = per_unit(0, at)
    for q_at in range(1, P_IN):
        feature = feature + per_unit(q_at, at)
    swapped = pltpu.roll(feature, 64, 1)
    buf.sums[...] = jnp.where((jnp.zeros((16, 128), jnp.int32) + c) == 0, feature, swapped)
    head = d % 8
    at = part(2 * (d // 8) + head // 4, 128)
    low_head, high_head = per_unit(2 * c, at), per_unit(2 * c + 1, at)
    first_half = (jnp.zeros((16, 128), jnp.int32) + (head // 2) % 2) == 0
    low_head = jnp.where(first_half, low_head, pltpu.roll(low_head, 64, 1))
    high_head = jnp.where(first_half, pltpu.roll(high_head, 64, 1), high_head)
    buf.sums[9:10, :] = jnp.where(half, low_head, high_head)[9:10]
    at = part(2 * (d // 8) + 4 + head // 4, 128)
    low_head, high_head = per_unit(2 * c, at), per_unit(2 * c + 1, at)
    low_head = jnp.where(first_half, low_head, pltpu.roll(low_head, 64, 1))
    high_head = jnp.where(first_half, pltpu.roll(high_head, 64, 1), high_head)
    buf.sums[10:11, :] = jnp.where(half, low_head, high_head)[9:10]
    buf.sums[11:12, :] = per_unit(q, part(2 * z, 128))[10:11]
    buf.sums[12:13, :] = per_unit(q, part(2 * z + 1, 128))[10:11]
    keep(buf.sums, io.sums_out)
    last_wait(wt.qkv)
    arrived(io.input_grad, k_in)
    for copy, cond in result_copies:
        run_if(cond, copy.wait)
    for record in list(started):
        sent(record)
    assert counter[0] <= SEMS


def buffer_shapes(n_sec, mem_cols):
    tokens, row = (T, D), (L, D)
    shapes = dict(
        sva=(P_IN, Z, 16, 128),
        sga=(Z, 16, D),
        sgp=(P_IN, 16, D),
        hb=row, ig=row, stage=row, mb=row,
        ml=(n_sec, L, mem_cols),
        mo=(L, mem_cols),
        qkv=(T, 768), q2=(T, 256), kv=(T, 512), o1=(T, 256), o2=(T, 256), do=(T, 256),
        p1=(2 * P_IN, 2 * L, L), p2=(2 * P_IN, 2 * L, L),
        g=(T, FL), gp=(T, FL),
        a1=tokens, a2=tokens, a3=tokens, m=tokens, e3=tokens, e2=tokens,
        a3b=tokens, e3b=tokens, gb=(T, FL), gpb=(T, FL), back=row, tail=row,
    )
    exact = dict(vec=(16, D), bias=(8, D), sg=(16, D), sums=(16, 128), h1=row, h2=row, dh=row)
    kinds = {name: pltpu.VMEM(shape, BF16) for name, shape in shapes.items()}
    kinds.update({name: pltpu.VMEM(shape, F32) for name, shape in exact.items()})
    return kinds


REDUCE_SHAPES = dict(
    parts=pltpu.VMEM((T, D), BF16),
    core=pltpu.VMEM((2 * L, D), BF16),
    across=pltpu.VMEM((L, D), BF16),
)


def scratch_of(n_sec, mem_cols):
    scratch = list(buffer_shapes(n_sec, mem_cols).values())
    scratch += 3 * list(REDUCE_SHAPES.values())
    for count, columns, _ in WEIGHTS.values():
        scratch += 2 * [pltpu.VMEM((Z * count, columns), BF16)]
        scratch += 2 * [pltpu.VMEM((count, columns), BF16)]
    for count, columns, _ in list(WEIGHTS.values())[:5]:
        scratch += 3 * [pltpu.VMEM((count, columns), BF16)]
    for columns in (768, 512, 256):
        scratch.append(pltpu.VMEM((64, P_IN * columns), BF16))
        scratch.append(pltpu.VMEM((P_IN, 64, columns), BF16))
    return scratch + [
        pltpu.SemaphoreType.DMA((SEMS,)),
        pltpu.SemaphoreType.DMA((SEMS,)),
        pltpu.SemaphoreType.DMA((48,)),
    ]


def finish_kernel(*refs):
    moved, low, sums = refs[:3], refs[3:10], refs[10]
    moved_out, high, small = refs[11:14], refs[14:21], refs[21:27]
    low_buf, high_buf, moved_buf = refs[27:34], refs[34:41], refs[41:44]
    small_buf, sems = refs[44:50], refs[50]
    inward = [
        pltpu.make_async_copy(src, dst, sems.at[i])
        for i, (src, dst) in enumerate(zip(low + moved, low_buf + moved_buf))
    ]
    for copy in inward:
        copy.start()
    outward = []
    gain, shift, out_bias, self_bias, cross_bias, unit_bias = small_buf
    gain[0] = sums[0:3, 0:64]
    shift[0] = sums[3:6, 0:64]
    out_bias[0] = sums[6:9, 0:64]
    self_bias[...] = sums[9:10, :]
    cross_bias[...] = sums[10:11, :]
    unit_bias[:, 0:128] = sums[11:12, :]
    unit_bias[:, 128:256] = sums[12:13, :]
    for i, (src, dst) in enumerate(zip(small_buf, small)):
        back = pltpu.make_async_copy(src, dst, sems.at[20 + i])
        back.start()
        outward.append(back)
    for i, copy in enumerate(inward[:7]):
        copy.wait()
        rows_in = low_buf[i].shape[0]

        def one(j, i=i):
            place = part(j, 16)
            high_buf[i][place, :] = low_buf[i][place, :].astype(F32)

        loop(rows_in // 16, one)
        back = pltpu.make_async_copy(high_buf[i], high[i], sems.at[10 + i])
        back.start()
        outward.append(back)
    for i, copy in enumerate(inward[7:]):
        copy.wait()
        back = pltpu.make_async_copy(moved_buf[i], moved_out[i], sems.at[17 + i])
        back.start()
        outward.append(back)
    for copy in outward:
        copy.wait()


def on_device_planes(
    prev_act, memory, out_cot, tgt_len, src_len, norm_gain, norm_bias, self_qkv, self_qv_bias,
    self_out, cross_q, cross_kv, cross_qv_bias, cross_out, out_bias, fc1, fc1_bias, fc2,
):
    n_sec = lax.axis_size("section")
    mem_cols = memory.shape[2]
    operands = (
        prev_act[0, 0], memory[0], out_cot[0, 0], tgt_len, src_len,
        norm_gain[0], norm_bias[0], out_bias[0], self_qv_bias, cross_qv_bias, fc1_bias,
        self_qkv[0], self_out[0], cross_kv[0], cross_q[0], cross_out[0], fc1[0], fc2[0],
    )
    anywhere = pl.BlockSpec(memory_space=pl.ANY)
    in_specs = 3 * [anywhere] + 2 * [pl.BlockSpec(memory_space=pltpu.SMEM)]
    in_specs += 6 * [pl.BlockSpec(memory_space=pltpu.VMEM)] + 7 * [anywhere]
    out_shapes = [(L, D), (L, D), (L, mem_cols)]
    for count, columns, by_column in WEIGHTS.values():
        out_shapes.append((count // P_IN, P_IN * columns) if by_column else (count, columns))
    sums_shape = jax.ShapeDtypeStruct((16, 128), F32)
    results = pl.pallas_call(
        functools.partial(whole_kernel, n_sec, mem_cols),
        out_shape=[jax.ShapeDtypeStruct(shape, BF16) for shape in out_shapes] + [sums_shape],
        in_specs=in_specs,
        out_specs=[anywhere] * (len(out_shapes) + 1),
        scratch_shapes=scratch_of(n_sec, mem_cols),
        compiler_params=pltpu.CompilerParams(
            collective_id=0, has_side_effects=True, vmem_limit_bytes=64 * 2**20 - 2**16
        ),
        cost_estimate=pl.CostEstimate(
            flops=21 * 10**9, bytes_accessed=20 * 2**20, transcendentals=3 * 10**6
        ),
    )(*operands)
    shapes = [result.shape for result in results]
    small_shapes = [(1, 3, 64)] * 3 + [(1, 128), (1, 128), (1, 256)]
    vmem = pl.BlockSpec(memory_space=pltpu.VMEM)
    finished = pl.pallas_call(
        finish_kernel,
        out_shape=[jax.ShapeDtypeStruct(shape, BF16) for shape in shapes[:3]]
        + [jax.ShapeDtypeStruct(shape, F32) for shape in shapes[3:10]]
        + [jax.ShapeDtypeStruct(shape, F32) for shape in small_shapes],
        in_specs=10 * [anywhere] + [vmem],
        out_specs=16 * [anywhere],
        scratch_shapes=[pltpu.VMEM(shape, BF16) for shape in shapes[3:10]]
        + [pltpu.VMEM(shape, F32) for shape in shapes[3:10]]
        + [pltpu.VMEM(shape, BF16) for shape in shapes[:3]]
        + [pltpu.VMEM(shape, F32) for shape in small_shapes]
        + [pltpu.SemaphoreType.DMA((26,))],
        compiler_params=pltpu.CompilerParams(vmem_limit_bytes=63 * 2**20),
        cost_estimate=pl.CostEstimate(flops=0, bytes_accessed=9 * 2**20, transcendentals=0),
    )(*results)
    (
        output, input_grad, memory_grad, g_qkv, g_so, g_ckv, g_cq, g_co, g_f1, g_f2,
        gain, shift, biases, self_biases, cross_biases, units,
    ) = finished
    return (
        output[None, None],
        input_grad[None, None],
        memory_grad[None],
        gain,
        shift,
        g_qkv[None],
        self_biases,
        g_so[None],
        g_cq[None],
        g_ckv[None],
        cross_biases,
        g_co[None],
        biases,
        g_f1[None],
        units,
        g_f2[None],
    )


def solution(mesh):
    in_specs = (
        P("section", "dp", None, None),
        P("dp", None, "section"),
        P("section", "dp", None, None),
        P("dp"),
        P("dp"),
        P("section", None, "dp"),
        P("section", None, "dp"),
        P("section", "dp", None),
        P("section", "dp"),
        P("section", "dp", None),
        P("section", "dp", None),
        P("section", "dp", None),
        P("section", "dp"),
        P("section", "dp", None),
        P("section", None, "dp"),
        P("section", "dp", None),
        P("section", "dp"),
        P("section", "dp", None),
    )
    out_specs = (
        P("section", "dp", None, None),
        P("section", "dp", None, None),
        P("dp", None, "section"),
        P("section", None, "dp"),
        P("section", None, "dp"),
        P("section", "dp", None),
        P("section", "dp"),
        P("section", "dp", None),
        P("section", "dp", None),
        P("section", "dp", None),
        P("section", "dp"),
        P("section", "dp", None),
        P("section", None, "dp"),
        P("section", "dp", None),
        P("section", "dp"),
        P("section", "dp", None),
    )
    planes = Z * P_IN
    fits = mesh.shape["dp"] == planes
    return jax.shard_map(
        on_device_planes if fits else on_device, mesh=mesh, in_specs=in_specs, out_specs=out_specs, check_vma=False
    )
```

```python
import functools
from types import SimpleNamespace

import jax
import jax.numpy as jnp
from jax import lax
from jax.experimental import pallas as pl
from jax.experimental.pallas import tpu as pltpu
from jax.sharding import PartitionSpec as P

H = 16
HD = 64


EPSILON = 1e-05
MASKED = -1000000000.0


def passed_along(value, axis, by):
    length = lax.axis_size(axis)
    return lax.ppermute(value, axis, [(i, (i + by) % length) for i in range(length)])


def norm_fwd(rows, gain, shift_term):
    center = rows - jnp.mean(rows, -1, keepdims=True)
    scale = lax.rsqrt(jnp.mean(center * center, -1, keepdims=True) + EPSILON)
    return center * scale * gain + shift_term


def gelu_exact(values):
    return jax.nn.gelu(values, approximate=False)


def product(left, right):
    return jnp.dot(left, right, preferred_element_type=jnp.float32)


def product_right_t(left, right):
    return lax.dot_general(
        left, right, (((1,), (1,)), ((), ())), preferred_element_type=jnp.float32
    )


def product_left_t(left, right):
    return lax.dot_general(
        left, right, (((0,), (0,)), ((), ())), preferred_element_type=jnp.float32
    )


def split_heads(flat, batch_rows):
    return flat.reshape(batch_rows, -1, H, HD)


def softmax_probs(query, key_rows, allowed):
    scores = jnp.einsum(
        "rthd,rshd->rhts", query, key_rows, preferred_element_type=jnp.float32
    ) * HD ** (-0.5)
    scores = jnp.where(allowed[:, None], scores, MASKED)
    weights = jnp.exp(scores - jnp.max(scores, -1, keepdims=True))
    return weights / jnp.sum(weights, -1, keepdims=True)


def attend_fwd(query, key_rows, value_rows, allowed):
    probs = softmax_probs(query, key_rows, allowed)
    mixed = jnp.einsum(
        "rhts,rshd->rthd",
        probs.astype(jnp.bfloat16),
        value_rows,
        preferred_element_type=jnp.float32,
    )
    return mixed.reshape(mixed.shape[0] * mixed.shape[1], -1).astype(jnp.bfloat16)


def attend_back(query, key_rows, value_rows, allowed, grad_mixed):
    probs = softmax_probs(query, key_rows, allowed)
    grad_heads = grad_mixed.reshape(query.shape)
    grad_probs = jnp.einsum(
        "rthd,rshd->rhts", grad_heads, value_rows, preferred_element_type=jnp.float32
    )
    delta = jnp.sum(probs * grad_probs, -1, keepdims=True)
    grad_scores = (probs * (grad_probs - delta)).astype(jnp.bfloat16)
    scale = HD ** (-0.5)
    grad_query = (
        jnp.einsum("rhts,rshd->rthd", grad_scores, key_rows, preferred_element_type=jnp.float32)
        * scale
    )
    grad_keys = (
        jnp.einsum("rhts,rthd->rshd", grad_scores, query, preferred_element_type=jnp.float32)
        * scale
    )
    grad_values = jnp.einsum(
        "rhts,rthd->rshd",
        probs.astype(jnp.bfloat16),
        grad_heads,
        preferred_element_type=jnp.float32,
    )
    width = query.shape[2] * query.shape[3]
    return (
        grad_query.reshape(-1, width).astype(jnp.bfloat16),
        grad_keys.reshape(-1, width).astype(jnp.bfloat16),
        grad_values.reshape(-1, width).astype(jnp.bfloat16),
    )


def unpack(pieces):
    return tuple((piece[0] for piece in pieces))


def on_device(
    prev_act,
    memory,
    out_cot,
    tgt_len,
    src_len,
    norm_gain,
    norm_bias,
    self_qkv,
    self_qv_bias,
    self_out,
    cross_q,
    cross_kv,
    cross_qv_bias,
    cross_out,
    out_bias,
    fc1,
    fc1_bias,
    fc2,
):
    fetched = unpack(
        (
            lax.all_gather(norm_gain, "dp", axis=2, tiled=True),
            lax.all_gather(norm_bias, "dp", axis=2, tiled=True),
            lax.all_gather(self_qkv, "dp", axis=1, tiled=True),
            lax.all_gather(self_qv_bias, "dp", axis=1, tiled=True),
            lax.all_gather(self_out, "dp", axis=1, tiled=True),
            lax.all_gather(cross_q, "dp", axis=1, tiled=True),
            lax.all_gather(cross_kv, "dp", axis=1, tiled=True),
            lax.all_gather(cross_qv_bias, "dp", axis=1, tiled=True),
            lax.all_gather(cross_out, "dp", axis=1, tiled=True),
            lax.all_gather(out_bias, "dp", axis=2, tiled=True),
            lax.all_gather(fc1, "dp", axis=1, tiled=True),
            lax.all_gather(fc1_bias, "dp", axis=1, tiled=True),
            lax.all_gather(fc2, "dp", axis=1, tiled=True),
        )
    )
    gains, shifts, w_sqkv, b_sqv, w_sout, w_cq, w_ckv, b_cqv, w_cout, b_out, w_one, b_one, w_two = (
        fetched
    )
    gain_f = gains.astype(jnp.float32)
    shift_f = shifts.astype(jnp.float32)
    sqv_f = b_sqv.astype(jnp.float32)
    cqv_f = b_cqv.astype(jnp.float32)
    out_f = b_out.astype(jnp.float32)
    one_f = b_one.astype(jnp.float32)
    source = passed_along(prev_act, "section", 1)[0]
    batch_rows, length, width = source.shape
    encoded = lax.all_gather(memory, "section", axis=2, tiled=True)
    mem_flat = encoded.reshape(-1, width)
    places = jnp.arange(length)
    self_ok = (places[None, None, :] <= places[None, :, None]) & (
        places[None, None, :] < tgt_len[:, None, None]
    )
    cross_ok = jnp.arange(encoded.shape[1])[None, None, :] < src_len[:, None, None]
    resid = source.astype(jnp.float32).reshape(-1, width)
    normed_one, pull_one = jax.vjp(norm_fwd, resid, gain_f[0], shift_f[0])
    first_in = normed_one.astype(jnp.bfloat16)
    joint = product(first_in, w_sqkv)
    query_self = (joint[:, :width] + sqv_f[:width]).astype(jnp.bfloat16)
    keys_self = joint[:, width : 2 * width].astype(jnp.bfloat16)
    values_self = (joint[:, 2 * width :] + sqv_f[width:]).astype(jnp.bfloat16)
    self_mixed = attend_fwd(
        split_heads(query_self, batch_rows),
        split_heads(keys_self, batch_rows),
        split_heads(values_self, batch_rows),
        self_ok,
    )
    after_self = resid + (product(self_mixed, w_sout) + out_f[0])
    normed_two, pull_two = jax.vjp(norm_fwd, after_self, gain_f[1], shift_f[1])
    second_in = normed_two.astype(jnp.bfloat16)
    query_cross = (product(second_in, w_cq) + cqv_f[:width]).astype(jnp.bfloat16)
    memory_proj = product(mem_flat, w_ckv)
    keys_cross = memory_proj[:, :width].astype(jnp.bfloat16)
    values_cross = (memory_proj[:, width:] + cqv_f[width:]).astype(jnp.bfloat16)
    cross_mixed = attend_fwd(
        split_heads(query_cross, batch_rows),
        split_heads(keys_cross, batch_rows),
        split_heads(values_cross, batch_rows),
        cross_ok,
    )
    after_cross = after_self + (product(cross_mixed, w_cout) + out_f[1])
    normed_three, pull_three = jax.vjp(norm_fwd, after_cross, gain_f[2], shift_f[2])
    third_in = normed_three.astype(jnp.bfloat16)
    pre_act = product(third_in, w_one) + one_f
    activ, pull_gelu = jax.vjp(gelu_exact, pre_act)
    act_low = activ.astype(jnp.bfloat16)
    result = after_cross + (product(act_low, w_two) + out_f[2])
    output = result.astype(jnp.bfloat16).reshape(1, batch_rows, length, width)
    (
        unused_gains,
        unused_shifts,
        w_sqkv,
        unused_sqv,
        w_sout,
        w_cq,
        w_ckv,
        unused_cqv,
        w_cout,
        unused_out,
        w_one,
        unused_one,
        w_two,
    ) = fetched
    grad_out = passed_along(out_cot, "section", -1)[0].astype(jnp.float32).reshape(-1, width)
    ffn_grad = grad_out.astype(jnp.bfloat16)
    grad_fc2 = product_left_t(act_low, ffn_grad)
    grad_b2 = jnp.sum(ffn_grad, 0, dtype=jnp.float32)
    grad_act = product_right_t(ffn_grad, w_two)
    (grad_pre,) = pull_gelu(grad_act)
    pre_low = grad_pre.astype(jnp.bfloat16)
    grad_fc1 = product_left_t(third_in, pre_low)
    grad_b1 = jnp.sum(pre_low, 0, dtype=jnp.float32)
    grad_mid, grad_gain3, grad_shift3 = pull_three(product_right_t(pre_low, w_one))
    grad_mid = grad_mid + grad_out
    cross_grad = grad_mid.astype(jnp.bfloat16)
    grad_cout = product_left_t(cross_mixed, cross_grad)
    grad_bco = jnp.sum(cross_grad, 0, dtype=jnp.float32)
    grad_cmix = product_right_t(cross_grad, w_cout).astype(jnp.bfloat16)
    grad_qc, grad_kc, grad_vc = attend_back(
        split_heads(query_cross, batch_rows),
        split_heads(keys_cross, batch_rows),
        split_heads(values_cross, batch_rows),
        cross_ok,
        grad_cmix,
    )
    grad_cq = product_left_t(second_in, grad_qc)
    grad_kv = jnp.concatenate([grad_kc, grad_vc], -1)
    grad_ckv = product_left_t(mem_flat, grad_kv)
    grad_cqv = jnp.concatenate(
        [jnp.sum(grad_qc, 0, dtype=jnp.float32), jnp.sum(grad_vc, 0, dtype=jnp.float32)]
    )
    grad_memory = product_right_t(grad_kv, w_ckv).reshape(encoded.shape)
    memory_grad = lax.psum_scatter(
        grad_memory.astype(jnp.bfloat16), "section", scatter_dimension=2, tiled=True
    )
    grad_after, grad_gain2, grad_shift2 = pull_two(product_right_t(grad_qc, w_cq))
    grad_after = grad_after + grad_mid
    self_grad = grad_after.astype(jnp.bfloat16)
    grad_sout = product_left_t(self_mixed, self_grad)
    grad_bso = jnp.sum(self_grad, 0, dtype=jnp.float32)
    grad_smix = product_right_t(self_grad, w_sout).astype(jnp.bfloat16)
    grad_qs, grad_ks, grad_vs = attend_back(
        split_heads(query_self, batch_rows),
        split_heads(keys_self, batch_rows),
        split_heads(values_self, batch_rows),
        self_ok,
        grad_smix,
    )
    grad_qkv = jnp.concatenate([grad_qs, grad_ks, grad_vs], -1)
    grad_sqkv = product_left_t(first_in, grad_qkv)
    grad_sqv = jnp.concatenate(
        [jnp.sum(grad_qs, 0, dtype=jnp.float32), jnp.sum(grad_vs, 0, dtype=jnp.float32)]
    )
    grad_in, grad_gain1, grad_shift1 = pull_one(product_right_t(grad_qkv, w_sqkv))
    grad_in = grad_in + grad_after
    input_grad = passed_along(
        grad_in.astype(jnp.bfloat16).reshape(1, batch_rows, length, width), "section", -1
    )
    grad_gain = jnp.stack([grad_gain1, grad_gain2, grad_gain3])
    grad_shift = jnp.stack([grad_shift1, grad_shift2, grad_shift3])
    grad_obias = jnp.stack([grad_bso, grad_bco, grad_b2])
    sums = (
        lax.psum_scatter(
            grad_gain.astype(jnp.bfloat16), "dp", scatter_dimension=1, tiled=True
        ).astype(jnp.float32),
        lax.psum_scatter(
            grad_shift.astype(jnp.bfloat16), "dp", scatter_dimension=1, tiled=True
        ).astype(jnp.float32),
        lax.psum_scatter(
            grad_sqkv.astype(jnp.bfloat16), "dp", scatter_dimension=0, tiled=True
        ).astype(jnp.float32),
        lax.psum_scatter(
            grad_sqv.astype(jnp.bfloat16), "dp", scatter_dimension=0, tiled=True
        ).astype(jnp.float32),
        lax.psum_scatter(
            grad_sout.astype(jnp.bfloat16), "dp", scatter_dimension=0, tiled=True
        ).astype(jnp.float32),
        lax.psum_scatter(
            grad_cq.astype(jnp.bfloat16), "dp", scatter_dimension=0, tiled=True
        ).astype(jnp.float32),
        lax.psum_scatter(
            grad_ckv.astype(jnp.bfloat16), "dp", scatter_dimension=0, tiled=True
        ).astype(jnp.float32),
        lax.psum_scatter(
            grad_cqv.astype(jnp.bfloat16), "dp", scatter_dimension=0, tiled=True
        ).astype(jnp.float32),
        lax.psum_scatter(
            grad_cout.astype(jnp.bfloat16), "dp", scatter_dimension=0, tiled=True
        ).astype(jnp.float32),
        lax.psum_scatter(
            grad_obias.astype(jnp.bfloat16), "dp", scatter_dimension=1, tiled=True
        ).astype(jnp.float32),
        lax.psum_scatter(
            grad_fc1.astype(jnp.bfloat16), "dp", scatter_dimension=0, tiled=True
        ).astype(jnp.float32),
        lax.psum_scatter(
            grad_b1.astype(jnp.bfloat16), "dp", scatter_dimension=0, tiled=True
        ).astype(jnp.float32),
        lax.psum_scatter(
            grad_fc2.astype(jnp.bfloat16), "dp", scatter_dimension=0, tiled=True
        ).astype(jnp.float32),
    )
    return (
        output,
        input_grad,
        memory_grad,
        sums[0][None],
        sums[1][None],
        sums[2][None],
        sums[3][None],
        sums[4][None],
        sums[5][None],
        sums[6][None],
        sums[7][None],
        sums[8][None],
        sums[9][None],
        sums[10][None],
        sums[11][None],
        sums[12][None],
    )


Z = 4
P_IN = 4
L = 192
D = 1024
T = P_IN * L
FL = 1024
TILE = 32
MESH = pl.DeviceIdType.MESH
F32 = jnp.float32
BF16 = jnp.bfloat16

WEIGHTS = dict(
    qkv=(256, 768, True),
    so=(64, 1024, False),
    ckv=(256, 512, True),
    cq=(256, 256, True),
    co=(64, 1024, False),
    f1=(256, 1024, True),
    f2=(256, 1024, False),
)
SEMS = 320


def run_if(cond, fn):
    if cond is None:
        fn()
    else:
        pl.when(cond)(fn)


def part(index, size, step=None):
    return pl.ds(pl.multiple_of(index * size, size), size if step is None else step)


def nn(left, right):
    return jnp.dot(left, right, preferred_element_type=F32)


def nt(left, right):
    return lax.dot_general(left, right, (((1,), (1,)), ((), ())), preferred_element_type=F32)


def tn(left, right):
    return lax.dot_general(left, right, (((0,), (0,)), ((), ())), preferred_element_type=F32)


def loop(count, body, unroll=1, first=0):
    def step(index, carry):
        body(index)
        return carry

    lax.fori_loop(first, first + count, step, 0, unroll=unroll)


HALF = L // 2
TILES = HALF // TILE


def gelu_pair(values):
    bell = jnp.exp(-0.5 * values * values)
    step = 1.0 / (1.0 + 0.3275911 * 0.7071067811865476 * jnp.abs(values))
    series = step * (
        0.254829592
        + step
        * (-0.284496736 + step * (1.421413741 + step * (-1.453152027 + step * 1.061405429)))
    )
    above = 0.5 * series * bell
    below = jnp.where(values < 0, above, 1.0 - above)
    return values * below, below + values * bell * 0.3989422804014327


def whiten(rows):
    center = rows - jnp.mean(rows, -1, keepdims=True)
    scale = lax.rsqrt(jnp.mean(center * center, -1, keepdims=True) + EPSILON)
    return center * scale, scale


def whole_kernel(n_sec, mem_cols, *refs):
    given = iter(refs)

    def take(names):
        return SimpleNamespace(**{name: next(given) for name in names})

    def take_weights(**fields):
        for name in WEIGHTS:
            for field in fields:
                setattr(getattr(wt, name), field, next(given))

    wt = SimpleNamespace(**{name: SimpleNamespace() for name in WEIGHTS})
    io = take(
        dict(
            prev=0, mem=0, cot=0, tgt=0, src=0, gain=0, shift=0, out_bias=0,
            self_bias=0, cross_bias=0, unit_bias=0,
        )
    )
    take_weights(source=0)
    vars(io).update(vars(take(dict(output=0, input_grad=0, memory_grad=0))))
    take_weights(result=0)
    vars(io).update(vars(take(dict(sums_out=0))))
    buf = take(buffer_shapes(n_sec, mem_cols))
    set_a, set_b, set_c = (take(REDUCE_SHAPES) for _ in range(3))
    take_weights(weight=0, grad=0, near=0, far=0)
    for weight in (wt.qkv, wt.so, wt.ckv, wt.cq, wt.co):
        weight.to_diag, weight.to_opp, weight.through = next(given), next(given), next(given)
    for weight in (wt.qkv, wt.ckv, wt.cq):
        weight.raw, weight.sorted = next(given), next(given)
    send_sems, recv_sems, local_sems = given

    s = lax.axis_index("section")
    d = lax.axis_index("dp")
    z, q = d // P_IN, d % P_IN
    x, c = q // 2, q % 2
    end = (z % 3) == 0
    mid = (z % 3) != 0
    q_core = q + 1 - 2 * c
    q_x = q + 2 - 4 * x
    q_xc = q_x + 1 - 2 * c
    z_adj = z + 1 - 2 * (z % 2)
    z_opp = 3 - z
    z_diag = (z + 2) % 4
    dev_core, dev_x, dev_xc = (s, z * P_IN + q_core), (s, z * P_IN + q_x), (s, z * P_IN + q_xc)
    dev_adj, dev_opp, dev_diag = (s, z_adj * P_IN + q), (s, z_opp * P_IN + q), (s, z_diag * P_IN + q)
    in_plane = ((q_core, dev_core), (q_x, dev_x), (q_xc, dev_xc))

    counter = [0]
    started = []
    local_counter = [0]

    def slot(count=1):
        counter[0] += count
        return counter[0] - count

    def remote(src, dst, k, device):
        return pltpu.make_async_remote_copy(
            src_ref=src, dst_ref=dst, send_sem=send_sems.at[k], recv_sem=recv_sems.at[k],
            device_id=device, device_id_type=MESH,
        )

    def send(src, dst, k, device, cond=None):
        copy = remote(src, dst, k, device)
        run_if(cond, copy.start)
        record = [copy, cond]
        started.append(record)
        return record

    def sent(record):
        run_if(record[1], record[0].wait_send)
        started[:] = [other for other in started if other is not record]

    def arrived(dst, k, cond=None):
        run_if(cond, remote(dst, dst, k, dev_core).wait_recv)

    def local(src, dst, cond=None):
        copy = pltpu.make_async_copy(src, dst, local_sems.at[local_counter[0]])
        local_counter[0] += 1
        run_if(cond, copy.start)
        return copy

    def keep(src, dst, cond=None):
        result_copies.append((local(src, dst, cond), cond))

    def rows(rows_of, index):
        return rows_of.at[part(index, L)]

    for name, (count, _, by_column) in WEIGHTS.items():
        weight = getattr(wt, name)
        weight.count, weight.by_column = count, by_column
        weight.pieces, weight.piece = 1, 0
        weight.to_use, weight.swap, weight.to_sum, weight.last = slot(5), slot(3), slot(6), slot(3)

    def block(name, index):
        return name.weight.at[part(index * name.pieces + name.piece, name.count)]

    first_weights = [
        SimpleNamespace(
            weight=wt.qkv.weight, count=wt.qkv.count // 2, pieces=2, piece=h, to_use=slot(5)
        )
        for h in range(2)
    ]

    def send_inward(name, src):
        send(src, block(name, z), name.to_use, dev_adj, end)

    def send_across(name, src):
        send(src, block(name, z), name.to_use + 1, dev_opp, mid)

    def weight_outward(name, src):
        send(src, block(name, z), name.to_use, dev_adj, mid)

    def relay_inward(name):
        k = name.to_use
        arrived(block(name, z_adj), k, mid)
        send(block(name, z_adj), block(name, z_adj), k + 2, dev_opp, mid)

    def relay_near(name):
        k = name.to_use
        arrived(block(name, z_opp), k + 1, mid)
        send(block(name, z_opp), block(name, z_opp), k + 3, dev_adj, mid)

    def relay_far(name):
        k = name.to_use
        arrived(block(name, z_diag), k + 2, mid)
        send(block(name, z_diag), block(name, z_diag), k + 4, dev_adj, mid)

    def weight_ready(name):
        k = name.to_use
        arrived(block(name, z_adj), k, end)
        arrived(block(name, z_diag), k + 3, end)
        arrived(block(name, z_opp), k + 4, end)

    def inner_ready(name):
        k = name.to_use
        arrived(block(name, z_opp), k + 1, mid)
        arrived(block(name, z_diag), k + 2, mid)


    def swap_start(name):
        size = name.count // P_IN
        place = name.weight.at[part(z * P_IN + q, size)]
        name.swapped = [
            send(name.sorted.at[q_to], place, name.swap + j, device)
            for j, (q_to, device) in enumerate(in_plane)
        ]
        name.own_copy = [local(name.sorted.at[q], place)]

    def swap_wait(name):
        size = name.count // P_IN
        for j, (q_from, _) in enumerate(in_plane):
            arrived(name.weight.at[part(z * P_IN + q_from, size)], name.swap + j)
        for copy in name.own_copy:
            copy.wait()
        for record in name.swapped:
            sent(record)

    def halves(first, second, odd):
        if odd:
            first = pltpu.roll(first, 64, 1)
        else:
            second = pltpu.roll(second, 64, 1)
        lane = lax.broadcasted_iota(jnp.int32, first.shape, 1)
        return jnp.where(lane < 64, first, second)

    def tile_of(index):
        return slice(index * 128, index * 128 + 128)

    def sort_columns(name):
        for q_to in range(P_IN):
            for tile in range(name.sorted.shape[2] // 128):
                at = 4 * tile + q_to // 2
                first = name.raw[:, tile_of(at)].astype(F32)
                second = name.raw[:, tile_of(at + 2)].astype(F32)
                name.sorted[q_to, :, tile_of(tile)] = halves(first, second, q_to % 2).astype(BF16)

    def unsort_columns(name):
        for tile in range(name.raw.shape[1] // 128):
            group, u = tile // 8, tile % 8
            at = 2 * group + u // 4
            first = name.sorted[2 * (u % 2), :, tile_of(at)].astype(F32)
            second = name.sorted[2 * (u % 2) + 1, :, tile_of(at)].astype(F32)
            name.raw[:, tile_of(tile)] = halves(first, second, (u // 2) % 2).astype(BF16)

    unit_swap, unit_last = slot(3 * Z), slot(3 * Z)

    def unit_columns(rows_of, tile, q_at):
        return rows_of.at[:, part(tile * P_IN + q_at, 256)]

    def unit_swap_start():
        size = wt.f1.count // P_IN
        place = wt.f1.weight.at[part(z * P_IN + q, size)]
        wt.f1.own_copy = []
        for tile in range(Z):
            at = place.at[:, part(tile, 256)]
            for j, (q_to, device) in enumerate(in_plane):
                send(unit_columns(wt.f1.source, tile, q_to), at, unit_swap + 3 * tile + j, device)
            wt.f1.own_copy.append(local(unit_columns(wt.f1.source, tile, q), at))

    def unit_swap_wait(cond):
        size = wt.f1.count // P_IN
        for tile in range(Z):
            for j, (q_from, _) in enumerate(in_plane):
                place = wt.f1.weight.at[part(z * P_IN + q_from, size)]
                arrived(place.at[:, part(tile, 256)], unit_swap + 3 * tile + j, cond)
        for copy in wt.f1.own_copy:
            run_if(cond, copy.wait)

    def grad_block(name, index):
        return name.grad.at[part(index, name.count)]

    def grad_send_far(name):
        return send(grad_block(name, z_opp), name.to_diag, name.to_sum, dev_adj, end)

    def grad_send_middle(name):
        return send(grad_block(name, z_diag), name.to_opp, name.to_sum + 1, dev_adj, end)

    def grad_send_near(name):
        return send(grad_block(name, z_adj), name.near, name.to_sum + 2, dev_adj, end)

    def grad_send(name):
        grad_send_far(name)
        grad_send_middle(name)

    def add_rows(count, body):
        size = min(count, 64)
        loop(count // size, lambda i: body(part(i, size)))

    def grad_add(name, landed, index):
        def one(place):
            own = grad_block(name, index)[place, :].astype(F32)
            landed[place, :] = (own + landed[place, :].astype(F32)).astype(BF16)

        add_rows(name.count, one)

    def grad_combine_far(name):
        k = name.to_sum
        arrived(name.to_diag, k, mid)
        run_if(mid, lambda: grad_add(name, name.to_diag, z_diag))
        send(name.to_diag, name.through, k + 3, dev_opp, mid)

    def grad_combine_middle(name):
        k = name.to_sum
        arrived(name.to_opp, k + 1, mid)
        run_if(mid, lambda: grad_add(name, name.to_opp, z_opp))
        send(name.to_opp, name.far, k + 4, dev_opp, mid)

    def grad_combine(name):
        grad_combine_far(name)
        grad_combine_middle(name)

    def grad_outward(name):
        k = name.to_sum
        arrived(name.through, k + 3, mid)
        run_if(mid, lambda: grad_add(name, name.through, z_adj))
        send(name.through, name.near, k + 5, dev_adj, mid)

    result_copies = []

    def inner_grad_far(name):
        send(grad_block(name, z_diag), name.far, name.to_sum, dev_opp, mid)

    def inner_grad_near(name):
        send(grad_block(name, z_opp), name.near, name.to_sum + 1, dev_opp, mid)

    def inner_grad_combine(name):
        k = name.to_sum

        def add():
            arrived(name.far, k)

            def one(place):
                own = grad_block(name, z_adj)[place, :].astype(F32)
                name.far[place, :] = (own + name.far[place, :].astype(F32)).astype(BF16)

            add_rows(name.count, one)

        run_if(mid, add)
        send(name.far, name.near, k + 2, dev_adj, mid)

    def inner_grad_total(name, cond):
        k = name.to_sum
        if cond is end:
            arrived(name.near, k + 2, end)
        else:
            arrived(name.near, k + 1, mid)
            run_if(mid, lambda: grad_add(name, name.near, z))

    def grad_total(name):
        k = name.to_sum
        arrived(name.near, k + 5, end)
        arrived(name.near, k + 2, mid)
        arrived(name.far, k + 4, mid)

        def add_far():
            def one(place):
                total = name.near[place, :].astype(F32) + name.far[place, :].astype(F32)
                name.near[place, :] = (total + grad_block(name, z)[place, :].astype(F32)).astype(BF16)

            add_rows(name.count, one)

        run_if(mid, add_far)
        run_if(end, lambda: grad_add(name, name.near, z))

    def grad_final(name):
        grad_total(name)
        if name.by_column:
            size = name.count // P_IN
            for j, (q_to, device) in enumerate(in_plane):
                src = name.near.at[part(q_to, size)]
                send(src, name.sorted.at[q], name.last + j, device)
            src = name.near.at[part(q, size)]
            name.own_copy = [local(src, name.sorted.at[q])]
        else:
            keep(name.near, name.result)

    def inner_final(cond):
        inner_grad_total(wt.f2, cond)
        keep(wt.f2.near, wt.f2.result, cond)
        inner_grad_total(wt.f1, cond)
        size = wt.f1.count // P_IN
        for tile in range(Z):
            dst = unit_columns(wt.f1.result, tile, q)
            for j, (q_to, device) in enumerate(in_plane):
                src = wt.f1.near.at[part(q_to, size), part(tile, 256)]
                send(src, dst, unit_last + 3 * tile + j, device, cond)
            keep(wt.f1.near.at[part(q, size), part(tile, 256)], dst, cond)

    def last_wait(name):
        for j, (q_from, _) in enumerate(in_plane):
            arrived(name.sorted.at[q_from], name.last + j)
        for copy in name.own_copy:
            copy.wait()
        unsort_columns(name)
        keep(name.raw, name.result)

    def unit_last_wait():
        for tile in range(Z):
            for j, (q_from, _) in enumerate(in_plane):
                place = unit_columns(wt.f1.result, tile, q_from)
                arrived(place, unit_last + 3 * tile + j)

    def piece(name, index, h, parts):
        size = L // parts
        return name.at[part(index * parts + h, size)]

    def half_major(name, index, h, parts=2):
        return name.at[part(h * P_IN + index, HALF)]

    def gather_open(name, cond=None, parts=1, lay=piece):
        return name, slot(3 * parts), [], cond, parts, lay

    def gather_part(ticket, h, cond=None):
        name, k, records, usual, parts, lay = ticket
        cond = usual if cond is None else cond
        own = lay(name, q, h, parts)
        records.append(send(own, own, k + 3 * h, dev_x, cond))
        records.append(send(own, own, k + 3 * h + 1, dev_core, cond))

    def gather_start(name, cond=None):
        ticket = gather_open(name, cond)
        gather_part(ticket, 0)
        return ticket

    def gather_relay_part(ticket, h):
        name, k, records, cond, parts, lay = ticket
        other = lay(name, q_x, h, parts)
        arrived(other, k + 3 * h, cond)
        records.append(send(other, other, k + 3 * h + 2, dev_core, cond))

    def gather_ready_part(ticket, h):
        name, k, _, cond, parts, lay = ticket
        arrived(lay(name, q_core, h, parts), k + 3 * h + 1, cond)
        arrived(lay(name, q_xc, h, parts), k + 3 * h + 2, cond)

    def gather_relay(ticket):
        for h in range(ticket[4]):
            gather_relay_part(ticket, h)

    def gather_ready(ticket):
        for h in range(ticket[4]):
            gather_ready_part(ticket, h)

    def gather_finish(ticket):
        gather_relay(ticket)
        gather_ready(ticket)

    def reduce_start(which, cond=None):
        k = slot(4)
        out = which.parts
        first = send(rows(out, q_xc), rows(which.core, 1), k, dev_core, cond)
        second = send(rows(out, q_core), rows(which.core, 0), k + 1, dev_core, cond)
        return which, k, [first, second], cond, piece

    def reduce_open(which, cond):
        return which, slot(6), [], cond, half_major

    def reduce_start_half(ticket, h):
        which, k, records, cond, lay = ticket
        for j, index in ((1, q_xc), (0, q_core)):
            src, dst = lay(which.parts, index, h), piece(which.core, j, h, 2)
            records.append(send(src, dst, k + 4 * h + 1 - j, dev_core, cond))

    def reduce_relay_half(ticket, h):
        which, k, records, cond, lay = ticket
        landed = piece(which.core, 1, h, 2)
        if lay is half_major:
            arrived(landed, k + 4 * h, cond)
        elif h == 0:
            arrived(rows(which.core, 1), k, cond)
        mine = lay(which.parts, q_x, h, 2)

        def add():
            def one(i):
                place = part(i, TILE)
                total = mine[place, :].astype(F32) + landed[place, :].astype(F32)
                mine[place, :] = total.astype(BF16)

            loop(TILES, one)

        run_if(cond, add)
        dst = which.across.at[part(h, HALF)]
        records.append(send(mine, dst, k + 2 + h, dev_x, cond))
        return records[-1]

    def reduce_relay(ticket):
        reduce_relay_half(ticket, 0)
        reduce_relay_half(ticket, 1)

    def reduce_ready_half(ticket, h):
        which, k, _, cond, lay = ticket
        if lay is half_major:
            arrived(piece(which.core, 0, h, 2), k + 4 * h + 1, cond)
        elif h == 0:
            arrived(rows(which.core, 0), k + 1, cond)
        arrived(which.across.at[part(h, HALF)], k + 2 + h, cond)

    def reduce_ready(ticket):
        reduce_ready_half(ticket, 0)
        reduce_ready_half(ticket, 1)

    def reduced(ticket, place):
        which = ticket[0]
        total = rows(which.parts, q)[place, :].astype(F32)
        total = total + rows(which.core, 0)[place, :].astype(F32)
        return total + which.across[place, :].astype(F32)

    def fold(ticket, dst, halves=(0, 1)):
        which, lay = ticket[0], ticket[4]
        for h in halves:
            mine, landed = lay(which.parts, q, h, 2), piece(which.core, 0, h, 2)

            def one(i, h=h, mine=mine, landed=landed):
                place, here = part(i, TILE), part(i + h * TILES, TILE)
                total = mine[place, :].astype(F32) + landed[place, :].astype(F32)
                dst[here, :] = (total + which.across[here, :].astype(F32)).astype(BF16)

            loop(TILES, one)

    def reduce_done(ticket):
        for record in ticket[2]:
            sent(record)

    def spread_start(place):
        k = slot(8)
        for j, device in enumerate((dev_diag, dev_opp, dev_adj)):
            send(place(z), place(z), k + j, device)
        return place, k

    def spread_wait(ticket):
        place, k = ticket
        for j, plane in enumerate((z_diag, z_opp, z_adj)):
            arrived(place(plane), k + j)

    def spread_plane(ticket, name):
        k = ticket[1]
        for j, (_, device) in enumerate(in_plane):
            send(name.at[q], name.at[q], k + 5 + j, device)

    def spread_ready(ticket, name):
        k = ticket[1]
        for j, (q_from, _) in enumerate(in_plane):
            arrived(name.at[q_from], k + 5 + j)

    def lanes(j, size=256):
        return part(j, size)

    def matmul(left, right, dst, bias=None, bias_row=0, bias_at=0):
        count = right.shape[1] // 256

        def one(j):
            tile = nn(left[...], right[:, lanes(j)])
            if bias is not None:
                tile = tile + bias[bias_row:bias_row + 1, part(j + bias_at, 256)]
            dst[:, lanes(j)] = tile.astype(BF16)

        loop(count, one)

    def matmul_back(left, right, dst, at=slice(0, T)):
        def one(j):
            dst[at, lanes(j)] = nt(left[at, :], right[lanes(j), :]).astype(BF16)

        loop(right.shape[0] // 256, one)

    def weight_grad(left, right, name, more=False):
        def one(j):
            total = tn(left[:, lanes(j)], right[...])
            if more:
                total = total + name.grad[lanes(j), :].astype(F32)
            name.grad[lanes(j), :] = total.astype(BF16)

        loop(left.shape[1] // 256, one)

    low_half = lax.broadcasted_iota(jnp.int32, (L, 128), 1) < 64
    keep_low = low_half.astype(F32).astype(BF16)
    keep_high = (1.0 - low_half.astype(F32)).astype(BF16)

    def both(pair):
        return jnp.concatenate([pair * keep_low, pair * keep_high], axis=0)

    def merge(stacked):
        return jnp.where(low_half, stacked[:L], stacked[L:])

    def attention(qref, q_at, kref, k_at, v_at, causal, length_row, probs, dst):
        def one(i):
            r, pair = i // 2, i % 2
            place = part(r, L)
            query = both(qref[place, part(pair + q_at, 128)])
            scores = nt(query, kref[place, part(pair + k_at, 128)]) * HD ** (-0.5)
            key = lax.broadcasted_iota(jnp.int32, scores.shape, 1)
            limit = buf.sva[r, z][length_row:length_row + 1, 0:1].astype(F32)
            allowed = key.astype(F32) < limit
            if causal:
                at = lax.broadcasted_iota(jnp.int32, scores.shape, 0)
                at = jnp.where(at < L, at, at - L)
                allowed = allowed & (key <= at)
            scores = jnp.where(allowed, scores, MASKED)
            raised = jnp.exp(scores - jnp.max(scores, -1, keepdims=True))
            weights = (raised * (1.0 / jnp.sum(raised, -1, keepdims=True))).astype(BF16)
            probs[i] = weights
            mixed = nn(weights, kref[place, part(pair + v_at, 128)])
            dst[place, part(pair, 128)] = merge(mixed).astype(BF16)

        loop(2 * P_IN, one, 2)

    def attention_back(qref, q_at, kref, k_at, v_at, probs, grad):
        def one(i):
            r, pair = i // 2, i % 2
            place = part(r, L)
            query = both(qref[place, part(pair + q_at, 128)])
            key = kref[place, part(pair + k_at, 128)]
            value = kref[place, part(pair + v_at, 128)]
            mixed_grad = both(grad[place, part(pair, 128)])
            weights = probs[i]
            soft = weights.astype(F32)
            grad_probs = nt(mixed_grad, value)
            delta = jnp.sum(soft * grad_probs, -1, keepdims=True)
            grad_scores = (soft * (grad_probs - delta)).astype(BF16)
            scale = HD ** (-0.5)
            grad_query = merge(nn(grad_scores, key)) * scale
            grad_key = tn(grad_scores, query) * scale
            grad_value = tn(weights, mixed_grad)
            qref[place, part(pair + q_at, 128)] = grad_query.astype(BF16)
            kref[place, part(pair + k_at, 128)] = grad_key.astype(BF16)
            kref[place, part(pair + v_at, 128)] = grad_value.astype(BF16)

        loop(2 * P_IN, one, 2)

    def column_sums(source, first, count, row, at):
        def one(j):
            values = source[:, part(j + first, 256)].astype(F32)
            buf.sg[row:row + 1, part(j + at, 256)] = jnp.sum(values, 0, keepdims=True)

        loop(count, one)

    def norm(load, index, dst, halves=(0, 1)):
        def one(i):
            place = part(i, TILE)
            normed, _ = whiten(load(place))
            gain, shift = buf.vec[index:index + 1, :], buf.vec[index + 3:index + 4, :]
            rows(dst, q)[place, :] = (normed * gain + shift).astype(BF16)

        loop(TILES * len(halves), one, first=TILES * halves[0])

    def norm_back(load, incoming, index, base, dst, low, out_row=None, halves=(0, 1)):
        zero = jnp.zeros((1, D), F32)

        def one(i, carry):
            gain_sum, shift_sum, out_sum = carry
            place = part(i, TILE)
            normed, scale = whiten(load(place))
            grad = incoming(place)
            gained = grad * buf.vec[index:index + 1, :]
            back = gained - jnp.mean(gained, -1, keepdims=True)
            back = back - normed * jnp.mean(gained * normed, -1, keepdims=True)
            total = base(place) + scale * back
            if dst is not None:
                dst[place, :] = total
            rounded = total.astype(BF16)
            low(place, rounded)
            return (
                gain_sum + jnp.sum(grad * normed, 0, keepdims=True),
                shift_sum + jnp.sum(grad, 0, keepdims=True),
                out_sum + jnp.sum(rounded.astype(F32), 0, keepdims=True),
            )

        first = TILES * halves[0]
        last = first + TILES * len(halves)
        gain_sum, shift_sum, out_sum = lax.fori_loop(first, last, one, (zero, zero, zero))
        buf.sg[index:index + 1, :] = buf.sg[index:index + 1, :] + gain_sum
        buf.sg[index + 3:index + 4, :] = buf.sg[index + 3:index + 4, :] + shift_sum
        if out_row is not None:
            buf.sg[out_row:out_row + 1, :] = buf.sg[out_row:out_row + 1, :] + out_sum

    gate = pltpu.get_barrier_semaphore()
    partners = [device for _, device in in_plane] + [dev_adj, dev_opp, dev_diag]
    partners += [((s + j) % n_sec, d) for j in range(1, n_sec)]
    for device in partners:
        pl.semaphore_signal(gate, inc=1, device_id=device, device_id_type=MESH)
    raw_copies = [local(weight.source, weight.raw) for weight in (wt.qkv, wt.ckv, wt.cq)]
    low_lanes = lax.broadcasted_iota(jnp.int32, (3, 128), 1) < 64
    even_lanes = (jnp.zeros((3, 128), jnp.int32) + c) == 0
    for row, pieces in ((0, io.gain), (3, io.shift), (6, io.out_bias)):
        value = pieces[...].astype(F32)
        twice = jnp.concatenate([value, value], 1)
        buf.sg[row:row + 3, 0:128] = jnp.where(low_lanes == even_lanes, twice, 0.0)
    buf.sg[9:10, 0:128] = io.self_bias[...].astype(F32)
    buf.sg[10:11, 0:128] = io.cross_bias[...].astype(F32)
    buf.sg[11:12, 0:128] = io.unit_bias[:, 0:128].astype(F32)
    buf.sg[12:13, 0:128] = io.unit_bias[:, 128:256].astype(F32)
    buf.sg[13:14, 0:128] = jnp.zeros((1, 128), F32) + io.tgt[0].astype(F32)
    buf.sg[14:15, 0:128] = jnp.zeros((1, 128), F32) + io.src[0].astype(F32)
    buf.sg[15:16, 0:128] = jnp.zeros((1, 128), F32)
    buf.sva[q, z] = buf.sg[:, 0:128].astype(BF16)

    raw_copies[0].wait()
    sort_columns(wt.qkv)
    pl.semaphore_wait(gate, len(partners))

    sv = spread_start(lambda plane: buf.sva.at[q, plane])
    swap_start(wt.qkv)
    k_prev, k_cot, k_mem = slot(), slot(), slot(n_sec)
    send(io.prev, buf.hb, k_prev, ((s + 1) % n_sec, d))
    mem_slot = rows(buf.m, q)
    for j in range(1, n_sec):
        send(io.mem, mem_slot.at[:, part(s, mem_cols)], k_mem + j, ((s + j) % n_sec, d))
    mem_copy = local(io.mem, mem_slot.at[:, part(s, mem_cols)])
    send(io.cot, rows(buf.e3, q), k_cot, ((s + n_sec - 1) % n_sec, d))
    for weight in (wt.so, wt.co, wt.f2):
        weight.own_copy = [local(weight.source, block(weight, z))]
    send_inward(wt.so, wt.so.source)
    send_across(wt.so, wt.so.source)
    weight_outward(wt.so, wt.so.source)
    swap_wait(wt.qkv)
    for weight in first_weights:
        send_inward(weight, block(weight, z))
        send_across(weight, block(weight, z))
        weight_outward(weight, block(weight, z))
    spread_wait(sv)
    spread_plane(sv, buf.sva)
    for weight, copy in ((wt.ckv, raw_copies[1]), (wt.cq, raw_copies[2])):
        copy.wait()
        sort_columns(weight)
        swap_start(weight)
    spread_ready(sv, buf.sva)

    for tile in range(D // 128):
        pair = buf.sva[2 * (tile % 2), tile // 2].astype(F32)
        pair = pair + buf.sva[2 * (tile % 2) + 1, tile // 2].astype(F32)
        buf.vec[:, tile * 128:(tile + 1) * 128] = pair
    half = lax.broadcasted_iota(jnp.int32, (16, 128), 1) < 64
    even = (jnp.zeros((16, 128), jnp.int32) + c) == 0
    buf.bias[...] = jnp.zeros((8, D), F32)
    for kind in range(2):
        for tile in range(2):
            first = buf.sva[x, tile + 2 * kind].astype(F32)
            second = buf.sva[2 + x, tile + 2 * kind].astype(F32)
            lower = jnp.where(even, first, pltpu.roll(first, 64, 1))
            upper = jnp.where(even, pltpu.roll(second, 64, 1), second)
            both_heads = jnp.where(half, lower, upper)
            for which in range(2):
                at = 512 * kind + 128 * tile
                buf.bias[which:which + 1, at:at + 128] = both_heads[9 + which:10 + which]
    for tile in range(Z):
        unit = buf.sva[q, tile].astype(F32)
        buf.bias[2:3, 256 * tile:256 * tile + 128] = unit[11:12]
        buf.bias[2:3, 256 * tile + 128:256 * tile + 256] = unit[12:13]
    buf.sg[...] = jnp.zeros((16, D), F32)

    relay_inward(first_weights[0])
    relay_near(first_weights[0])
    arrived(buf.hb, k_prev)

    def hidden(place):
        return buf.hb[place, :].astype(F32)

    norm(hidden, 0, buf.a1)
    a1 = gather_start(buf.a1)
    unit_swap_start()
    relay_inward(first_weights[1])
    relay_near(first_weights[1])
    relay_inward(wt.so)
    swap_wait(wt.ckv)
    send_inward(wt.ckv, block(wt.ckv, z))
    swap_wait(wt.cq)
    send_inward(wt.cq, block(wt.cq, z))
    send_inward(wt.co, wt.co.source)
    send_across(wt.ckv, block(wt.ckv, z))
    for j in range(1, n_sec):
        origin = (s + n_sec - j) % n_sec
        arrived(mem_slot.at[:, part(origin, mem_cols)], k_mem + j)
    mem_copy.wait()
    memory = gather_start(buf.m)
    arrived(rows(buf.e3, q), k_cot)
    k_units = slot(16)
    to_middle = [send(rows(buf.e3, q), rows(buf.e3, q), k_units + 9, dev_x, end)]

    def cot_inward(index, k):
        for h in range(2):
            src, dst = piece(buf.e3, index, h, 2), half_major(buf.e3b, index, h)
            to_middle.append(send(src, dst, k + h, dev_adj, end))

    cot_inward(q, k_units)
    relay_far(first_weights[0])
    gather_relay(a1)
    relay_far(first_weights[1])
    relay_near(wt.so)
    relay_inward(wt.ckv)
    gather_ready(a1)
    unit_swap_wait(end)
    send_inward(wt.f1, block(wt.f1, z))
    for weight in first_weights:
        weight_ready(weight)
    matmul(buf.a1, wt.qkv.weight, buf.qkv, buf.bias, 0)
    relay_far(wt.so)
    weight_outward(wt.ckv, block(wt.ckv, z))
    send_across(wt.cq, block(wt.cq, z))
    attention(buf.qkv, 0, buf.qkv, 2, 4, True, 13, buf.p1, buf.o1)
    relay_inward(wt.cq)
    send_across(wt.co, wt.co.source)
    wt.so.own_copy[0].wait()
    weight_ready(wt.so)
    matmul(buf.o1, wt.so.weight, set_a.parts)
    step = reduce_start(set_a)
    send_inward(wt.f2, wt.f2.source)
    relay_inward(wt.co)
    relay_near(wt.ckv)
    weight_outward(wt.cq, block(wt.cq, z))
    reduce_relay(step)
    arrived(rows(buf.e3, q_x), k_units + 9, end)
    cot_inward(q_x, k_units + 2)
    gather_finish(memory)
    relay_far(wt.ckv)
    unit_swap_wait(mid)
    send_across(wt.f1, block(wt.f1, z))

    def after_self(i):
        place = part(i, TILE)
        buf.h1[place, :] = hidden(place) + (reduced(step, place) + buf.vec[6:7, :])

    a2 = gather_open(buf.a2, None, 2)
    for h in range(2):
        reduce_ready_half(step, h)
        loop(TILES, after_self, first=h * TILES)
        norm(lambda place: buf.h1[place, :], 1, buf.a2, (h,))
        gather_part(a2, h)
    reduce_done(step)
    relay_near(wt.cq)
    weight_outward(wt.co, wt.co.source)
    relay_far(wt.cq)
    weight_ready(wt.ckv)
    matmul(buf.m, wt.ckv.weight, buf.kv, buf.bias, 1, 1)
    relay_near(wt.co)
    send_across(wt.f2, wt.f2.source)
    relay_far(wt.co)
    relay_inward(wt.f1)

    gather_finish(a2)
    e3 = gather_start(buf.e3, mid)
    weight_ready(wt.cq)
    matmul(buf.a2, wt.cq.weight, buf.q2, buf.bias, 1)
    attention(buf.q2, 0, buf.kv, 0, 2, False, 14, buf.p2, buf.o2)
    wt.co.own_copy[0].wait()
    weight_ready(wt.co)
    matmul(buf.o2, wt.co.weight, set_b.parts)
    step = reduce_start(set_b)
    relay_inward(wt.f2)
    gather_finish(e3)
    reduce_relay(step)

    def after_cross(i):
        place = part(i, TILE)
        buf.h2[place, :] = buf.h1[place, :] + (reduced(step, place) + buf.vec[7:8, :])

    a3 = gather_open(buf.a3, mid, 2)
    for h in range(2):
        reduce_ready_half(step, h)
        loop(TILES, after_cross, first=h * TILES)
        norm(lambda place: buf.h2[place, :], 2, buf.a3, (h,))
        send(piece(buf.a3, q, h, 2), half_major(buf.a3b, q, h), k_units + 10 + h, dev_adj, end)
        gather_part(a3, h)
    reduce_done(step)

    def units(normed, activs, slopes, at=slice(0, T)):
        def one(j):
            value = nn(normed[at, :], wt.f1.weight[:, lanes(j)]) + buf.bias[2:3, lanes(j)]
            activ, slope = gelu_pair(value)
            activs[at, lanes(j)] = activ.astype(BF16)
            slopes[at, lanes(j)] = slope.astype(BF16)

        loop(FL // 256, one, 2)

    def units_back(grad, slopes, at=slice(0, T)):
        def one(j):
            value = nt(grad[at, :], wt.f2.weight[lanes(j), :])
            low = (value * slopes[at, lanes(j)].astype(F32)).astype(BF16)
            slopes[at, lanes(j)] = low
            total = jnp.sum(low.astype(F32), 0, keepdims=True)
            buf.sg[10:11, lanes(j)] = buf.sg[10:11, lanes(j)] + total

        loop(FL // 256, one)

    def weight_grads(left, right, left_b, right_b, name, first, count):
        def one(j):
            total = tn(left[:, lanes(j)], right[...]) + tn(left_b[:, lanes(j)], right_b[...])
            name.grad[lanes(j), :] = total.astype(BF16)

        loop(count, one, first=first)

    def finish(incoming):
        def one(i):
            place = part(i, TILE)
            total = buf.h2[place, :] + (incoming(place) + buf.vec[8:9, :])
            buf.stage[place, :] = total.astype(BF16)

        loop(L // TILE, one)

    def on_mid(fn, *args):
        run_if(mid, lambda: fn(*args))

    def cot_sum(i, carry):
        return carry + jnp.sum(rows(buf.e3, q)[part(i, TILE), :].astype(F32), 0, keepdims=True)

    buf.sg[8:9, :] = lax.fori_loop(0, L // TILE, cot_sum, jnp.zeros((1, D), F32))

    for index, k in ((q, k_units), (q_x, k_units + 2)):
        for h in range(2):
            landed = half_major(buf.e3b, index, h)
            arrived(landed, k + h, mid)
            send(landed, landed, k + 4 + h, dev_core, mid)
    gather_relay(a3)
    a3b = gather_open(buf.a3b, mid, 2, half_major)
    arrived(half_major(buf.a3b, q, 0), k_units + 10, mid)
    gather_part(a3b, 0)
    gather_ready(a3)
    inner_ready(wt.f1)
    on_mid(units, buf.a3, buf.g, buf.gp)
    arrived(half_major(buf.a3b, q, 1), k_units + 11, mid)
    gather_part(a3b, 1)
    on_mid(weight_grad, buf.g, buf.e3, wt.f2)
    for index, k in ((q_core, k_units + 4), (q_xc, k_units + 6)):
        for h in range(2):
            arrived(half_major(buf.e3b, index, h), k + h, mid)
    gather_relay_part(a3b, 0)
    wt.f2.own_copy[0].wait()
    inner_ready(wt.f2)
    on_mid(matmul, buf.g, wt.f2.weight, set_c.parts)
    final = reduce_start(set_c, mid)
    gather_ready_part(a3b, 0)
    step_b = reduce_open(set_b, mid)
    for h in range(2):
        at = slice(h * T // 2, (h + 1) * T // 2)
        if h == 1:
            gather_ready_part(a3b, 1)
        on_mid(units, buf.a3b, buf.gb, buf.gpb, at)
        if h == 0:
            reduce_relay(final)
        else:
            reduce_relay_half(step_b, 0)
            on_mid(weight_grad, buf.gb, buf.e3b, wt.f2, True)
            inner_grad_far(wt.f2)
            inner_grad_near(wt.f2)
        on_mid(units_back, buf.e3b, buf.gpb, at)
        if h == 0:
            gather_relay_part(a3b, 1)
        on_mid(matmul_back, buf.gpb, wt.f1.weight, set_b.parts, at)
        reduce_start_half(step_b, h)

    def back_outward(h):
        reduce_ready_half(step_b, h)
        on_mid(fold, step_b, buf.back, (h,))
        ready = buf.back.at[part(h, HALF)]
        send(ready, ready, k_units + 12 + h, dev_adj, mid)

    reduce_relay_half(step_b, 1)
    on_mid(units_back, buf.e3, buf.gp)
    back_outward(0)
    on_mid(matmul_back, buf.gp, wt.f1.weight, set_a.parts)
    reduce_ready(final)
    on_mid(finish, lambda place: reduced(final, place))
    reduce_done(final)
    step = reduce_start(set_a, mid)
    back_outward(1)
    reduce_relay(step)
    on_mid(weight_grads, buf.a3, buf.gp, buf.a3b, buf.gpb, wt.f1, 0, Z)
    inner_grad_far(wt.f1)
    inner_grad_near(wt.f1)
    on_mid(matmul, buf.gb, wt.f2.weight, set_c.parts)

    def store(name):
        def low(place, value):
            rows(name, q)[place, :] = value

        return low

    def units_norm_back(incoming, halves):
        norm_back(
            lambda place: buf.h2[place, :], incoming, 2,
            lambda place: rows(buf.e3, q)[place, :].astype(F32), buf.dh, store(buf.e2), 7, halves,
        )

    reduce_done(e3)
    for record in to_middle:
        sent(record)
    reduce_ready(step)
    final_b = reduce_open(set_c, mid)
    reduce_start_half(final_b, 0)
    reduce_start_half(final_b, 1)
    on_mid(units_norm_back, lambda place: reduced(step, place), (0, 1))
    e2 = gather_open(buf.e2, None, 2)
    gather_part(e2, 0, mid)
    gather_part(e2, 1, mid)
    inner_grad_combine(wt.f2)
    for h in range(2):
        arrived(buf.back.at[part(h, HALF)], k_units + 12 + h, end)
        run_if(
            end,
            lambda h=h: units_norm_back(lambda place: buf.back[place, :].astype(F32), (h,)),
        )
        gather_part(e2, h, end)
    reduce_done(step)
    reduce_done(step_b)
    gather_finish(e2)
    reduce_relay(final_b)

    weight_grad(buf.o2, buf.e2, wt.co)
    grad_send(wt.co)
    matmul_back(buf.e2, wt.co.weight, buf.do)
    attention_back(buf.q2, 0, buf.kv, 0, 2, buf.p2, buf.do)
    matmul_back(buf.q2, wt.cq.weight, set_b.parts)
    step = reduce_start(set_b)
    weight_grad(buf.a2, buf.q2, wt.cq)
    grad_send(wt.cq)
    reduce_relay(step)
    grad_combine(wt.co)
    grad_combine(wt.cq)
    weight_grad(buf.m, buf.kv, wt.ckv)
    grad_send(wt.ckv)
    grad_send_near(wt.co)
    grad_send_near(wt.cq)
    matmul_back(buf.kv, wt.ckv.weight, set_a.parts)
    mem_step = reduce_start(set_a)
    column_sums(buf.q2, 0, 1, 9, 2)
    column_sums(buf.kv, 1, 1, 9, 3)
    reduce_ready(final_b)
    on_mid(fold, final_b, buf.tail)
    send(buf.tail, buf.tail, k_units + 14, dev_adj, mid)
    reduce_done(final_b)
    inner_grad_combine(wt.f1)
    e1 = gather_open(buf.e3, None, 2)
    for h in range(2):
        reduce_ready_half(step, h)
        norm_back(
            lambda place: buf.h1[place, :], lambda place: reduced(step, place), 1,
            lambda place: buf.dh[place, :], buf.dh, store(buf.e3), 6, (h,),
        )
        gather_part(e1, h)
    reduce_done(step)
    grad_combine(wt.ckv)
    gather_finish(e1)
    reduce_relay(mem_step)

    weight_grad(buf.o1, buf.e3, wt.so)
    grad_send(wt.so)
    matmul_back(buf.e3, wt.so.weight, buf.do)
    attention_back(buf.qkv, 0, buf.qkv, 2, 4, buf.p1, buf.do)
    grad_outward(wt.co)
    grad_combine(wt.so)
    run_if(end, lambda: weight_grad(buf.a1, buf.qkv, wt.qkv))
    grad_send(wt.qkv)
    grad_send_near(wt.ckv)
    grad_send_near(wt.so)
    matmul_back(buf.qkv, wt.qkv.weight, set_b.parts)
    step = reduce_start(set_b)
    on_mid(weight_grad, buf.a1, buf.qkv, wt.qkv)
    column_sums(buf.qkv, 0, 1, 9, 0)
    column_sums(buf.qkv, 2, 1, 9, 1)
    grad_outward(wt.cq)
    reduce_relay(step)
    inner_final(mid)
    grad_combine_far(wt.qkv)

    reduce_ready(mem_step)
    fold(mem_step, buf.mb)
    k_back = slot(n_sec)
    for j in range(1, n_sec):
        to = (s + j) % n_sec
        send(buf.mb.at[:, part(to, mem_cols)], buf.ml.at[j], k_back + j, (to, d))
    grad_outward(wt.ckv)
    grad_combine_middle(wt.qkv)
    grad_outward(wt.so)
    reduce_ready(step)

    def store_stage(place, value):
        buf.ig[place, :] = value

    norm_back(
        hidden, lambda place: reduced(step, place), 0,
        lambda place: buf.dh[place, :], None, store_stage,
    )
    k_in = slot()
    send(buf.ig, io.input_grad, k_in, ((s + n_sec - 1) % n_sec, d))
    buf.sga[z] = buf.sg[...].astype(BF16)
    sums = spread_start(lambda plane: buf.sga.at[plane])
    inner_final(end)
    for weight in (wt.co, wt.cq):
        grad_final(weight)
    grad_send_near(wt.qkv)
    grad_outward(wt.qkv)
    grad_final(wt.ckv)
    spread_wait(sums)
    planes = buf.sga[0].astype(F32)
    for plane in range(1, Z):
        planes = planes + buf.sga[plane].astype(F32)
    buf.sgp[q] = planes.astype(BF16)
    spread_plane(sums, buf.sgp)
    grad_final(wt.so)
    grad_final(wt.qkv)

    arrived(buf.tail, k_units + 14, end)
    run_if(end, lambda: finish(lambda place: buf.tail[place, :].astype(F32)))
    for j in range(1, n_sec):
        arrived(buf.ml.at[j], k_back + j)

    def memory_total(i):
        place = part(i, TILE)
        total = buf.mb[place, part(s, mem_cols)].astype(F32)
        for j in range(1, n_sec):
            total = total + buf.ml[j, place, :].astype(F32)
        buf.mo[place, :] = total.astype(BF16)

    loop(L // TILE, memory_total)
    keep(buf.mo, io.memory_grad)
    unit_last_wait()
    last_wait(wt.cq)
    last_wait(wt.ckv)
    keep(buf.stage, io.output)
    spread_ready(sums, buf.sgp)

    def per_unit(q_at, at):
        return buf.sgp[q_at, :, at].astype(F32)

    at = part(d // 2, 128)
    feature = per_unit(0, at)
    for q_at in range(1, P_IN):
        feature = feature + per_unit(q_at, at)
    swapped = pltpu.roll(feature, 64, 1)
    buf.sums[...] = jnp.where((jnp.zeros((16, 128), jnp.int32) + c) == 0, feature, swapped)
    head = d % 8
    at = part(2 * (d // 8) + head // 4, 128)
    low_head, high_head = per_unit(2 * c, at), per_unit(2 * c + 1, at)
    first_half = (jnp.zeros((16, 128), jnp.int32) + (head // 2) % 2) == 0
    low_head = jnp.where(first_half, low_head, pltpu.roll(low_head, 64, 1))
    high_head = jnp.where(first_half, pltpu.roll(high_head, 64, 1), high_head)
    buf.sums[9:10, :] = jnp.where(half, low_head, high_head)[9:10]
    at = part(2 * (d // 8) + 4 + head // 4, 128)
    low_head, high_head = per_unit(2 * c, at), per_unit(2 * c + 1, at)
    low_head = jnp.where(first_half, low_head, pltpu.roll(low_head, 64, 1))
    high_head = jnp.where(first_half, pltpu.roll(high_head, 64, 1), high_head)
    buf.sums[10:11, :] = jnp.where(half, low_head, high_head)[9:10]
    buf.sums[11:12, :] = per_unit(q, part(2 * z, 128))[10:11]
    buf.sums[12:13, :] = per_unit(q, part(2 * z + 1, 128))[10:11]
    keep(buf.sums, io.sums_out)
    last_wait(wt.qkv)
    arrived(io.input_grad, k_in)
    for copy, cond in result_copies:
        run_if(cond, copy.wait)
    for record in list(started):
        sent(record)
    assert counter[0] <= SEMS


def buffer_shapes(n_sec, mem_cols):
    tokens, row = (T, D), (L, D)
    shapes = dict(
        sva=(P_IN, Z, 16, 128),
        sga=(Z, 16, D),
        sgp=(P_IN, 16, D),
        hb=row, ig=row, stage=row, mb=row,
        ml=(n_sec, L, mem_cols),
        mo=(L, mem_cols),
        qkv=(T, 768), q2=(T, 256), kv=(T, 512), o1=(T, 256), o2=(T, 256), do=(T, 256),
        p1=(2 * P_IN, 2 * L, L), p2=(2 * P_IN, 2 * L, L),
        g=(T, FL), gp=(T, FL),
        a1=tokens, a2=tokens, a3=tokens, m=tokens, e3=tokens, e2=tokens,
        a3b=tokens, e3b=tokens, gb=(T, FL), gpb=(T, FL), back=row, tail=row,
    )
    exact = dict(vec=(16, D), bias=(8, D), sg=(16, D), sums=(16, 128), h1=row, h2=row, dh=row)
    kinds = {name: pltpu.VMEM(shape, BF16) for name, shape in shapes.items()}
    kinds.update({name: pltpu.VMEM(shape, F32) for name, shape in exact.items()})
    return kinds


REDUCE_SHAPES = dict(
    parts=pltpu.VMEM((T, D), BF16),
    core=pltpu.VMEM((2 * L, D), BF16),
    across=pltpu.VMEM((L, D), BF16),
)


def scratch_of(n_sec, mem_cols):
    scratch = list(buffer_shapes(n_sec, mem_cols).values())
    scratch += 3 * list(REDUCE_SHAPES.values())
    for count, columns, _ in WEIGHTS.values():
        scratch += 2 * [pltpu.VMEM((Z * count, columns), BF16)]
        scratch += 2 * [pltpu.VMEM((count, columns), BF16)]
    for count, columns, _ in list(WEIGHTS.values())[:5]:
        scratch += 3 * [pltpu.VMEM((count, columns), BF16)]
    for columns in (768, 512, 256):
        scratch.append(pltpu.VMEM((64, P_IN * columns), BF16))
        scratch.append(pltpu.VMEM((P_IN, 64, columns), BF16))
    return scratch + [
        pltpu.SemaphoreType.DMA((SEMS,)),
        pltpu.SemaphoreType.DMA((SEMS,)),
        pltpu.SemaphoreType.DMA((48,)),
    ]


def finish_kernel(*refs):
    moved, low, sums = refs[:3], refs[3:10], refs[10]
    moved_out, high, small = refs[11:14], refs[14:21], refs[21:27]
    low_buf, high_buf, moved_buf = refs[27:34], refs[34:41], refs[41:44]
    small_buf, sems = refs[44:50], refs[50]
    inward = [
        pltpu.make_async_copy(src, dst, sems.at[i])
        for i, (src, dst) in enumerate(zip(low + moved, low_buf + moved_buf))
    ]
    for copy in inward:
        copy.start()
    outward = []
    gain, shift, out_bias, self_bias, cross_bias, unit_bias = small_buf
    for row in range(3):
        gain[row] = sums[row:row + 1, 0:64]
        shift[row] = sums[row + 3:row + 4, 0:64]
        out_bias[row] = sums[row + 6:row + 7, 0:64]
    self_bias[...] = sums[9:10, :]
    cross_bias[...] = sums[10:11, :]
    unit_bias[:, 0:128] = sums[11:12, :]
    unit_bias[:, 128:256] = sums[12:13, :]
    for i, (src, dst) in enumerate(zip(small_buf, small)):
        back = pltpu.make_async_copy(src, dst, sems.at[20 + i])
        back.start()
        outward.append(back)
    for i, copy in enumerate(inward[:7]):
        copy.wait()
        rows_in = low_buf[i].shape[0]

        def one(j, i=i):
            place = part(j, 16)
            high_buf[i][place, :] = low_buf[i][place, :].astype(F32)

        loop(rows_in // 16, one)
        back = pltpu.make_async_copy(high_buf[i], high[i], sems.at[10 + i])
        back.start()
        outward.append(back)
    for i, copy in enumerate(inward[7:]):
        copy.wait()
        back = pltpu.make_async_copy(moved_buf[i], moved_out[i], sems.at[17 + i])
        back.start()
        outward.append(back)
    for copy in outward:
        copy.wait()


def on_device_planes(
    prev_act, memory, out_cot, tgt_len, src_len, norm_gain, norm_bias, self_qkv, self_qv_bias,
    self_out, cross_q, cross_kv, cross_qv_bias, cross_out, out_bias, fc1, fc1_bias, fc2,
):
    n_sec = lax.axis_size("section")
    mem_cols = memory.shape[2]
    operands = (
        prev_act[0, 0], memory[0], out_cot[0, 0], tgt_len, src_len,
        norm_gain[0], norm_bias[0], out_bias[0], self_qv_bias, cross_qv_bias, fc1_bias,
        self_qkv[0], self_out[0], cross_kv[0], cross_q[0], cross_out[0], fc1[0], fc2[0],
    )
    anywhere = pl.BlockSpec(memory_space=pl.ANY)
    in_specs = 3 * [anywhere] + 2 * [pl.BlockSpec(memory_space=pltpu.SMEM)]
    in_specs += 6 * [pl.BlockSpec(memory_space=pltpu.VMEM)] + 7 * [anywhere]
    out_shapes = [(L, D), (L, D), (L, mem_cols)]
    for count, columns, by_column in WEIGHTS.values():
        out_shapes.append((count // P_IN, P_IN * columns) if by_column else (count, columns))
    sums_shape = jax.ShapeDtypeStruct((16, 128), F32)
    results = pl.pallas_call(
        functools.partial(whole_kernel, n_sec, mem_cols),
        out_shape=[jax.ShapeDtypeStruct(shape, BF16) for shape in out_shapes] + [sums_shape],
        in_specs=in_specs,
        out_specs=[anywhere] * (len(out_shapes) + 1),
        scratch_shapes=scratch_of(n_sec, mem_cols),
        compiler_params=pltpu.CompilerParams(
            collective_id=0, has_side_effects=True, vmem_limit_bytes=64 * 2**20 - 2**16
        ),
        cost_estimate=pl.CostEstimate(
            flops=21 * 10**9, bytes_accessed=20 * 2**20, transcendentals=3 * 10**6
        ),
    )(*operands)
    shapes = [result.shape for result in results]
    small_shapes = [(3, 1, 64)] * 3 + [(1, 128), (1, 128), (1, 256)]
    vmem = pl.BlockSpec(memory_space=pltpu.VMEM)
    finished = pl.pallas_call(
        finish_kernel,
        out_shape=[jax.ShapeDtypeStruct(shape, BF16) for shape in shapes[:3]]
        + [jax.ShapeDtypeStruct(shape, F32) for shape in shapes[3:10]]
        + [jax.ShapeDtypeStruct(shape, F32) for shape in small_shapes],
        in_specs=10 * [anywhere] + [vmem],
        out_specs=16 * [anywhere],
        scratch_shapes=[pltpu.VMEM(shape, BF16) for shape in shapes[3:10]]
        + [pltpu.VMEM(shape, F32) for shape in shapes[3:10]]
        + [pltpu.VMEM(shape, BF16) for shape in shapes[:3]]
        + [pltpu.VMEM(shape, F32) for shape in small_shapes]
        + [pltpu.SemaphoreType.DMA((26,))],
        compiler_params=pltpu.CompilerParams(vmem_limit_bytes=63 * 2**20),
        cost_estimate=pl.CostEstimate(flops=0, bytes_accessed=9 * 2**20, transcendentals=0),
    )(*results)
    (
        output, input_grad, memory_grad, g_qkv, g_so, g_ckv, g_cq, g_co, g_f1, g_f2,
        gain, shift, biases, self_biases, cross_biases, units,
    ) = finished
    return (
        output[None, None],
        input_grad[None, None],
        memory_grad[None],
        gain.transpose(1, 0, 2),
        shift.transpose(1, 0, 2),
        g_qkv[None],
        self_biases,
        g_so[None],
        g_cq[None],
        g_ckv[None],
        cross_biases,
        g_co[None],
        biases.transpose(1, 0, 2),
        g_f1[None],
        units,
        g_f2[None],
    )


def solution(mesh):
    in_specs = (
        P("section", "dp", None, None),
        P("dp", None, "section"),
        P("section", "dp", None, None),
        P("dp"),
        P("dp"),
        P("section", None, "dp"),
        P("section", None, "dp"),
        P("section", "dp", None),
        P("section", "dp"),
        P("section", "dp", None),
        P("section", "dp", None),
        P("section", "dp", None),
        P("section", "dp"),
        P("section", "dp", None),
        P("section", None, "dp"),
        P("section", "dp", None),
        P("section", "dp"),
        P("section", "dp", None),
    )
    out_specs = (
        P("section", "dp", None, None),
        P("section", "dp", None, None),
        P("dp", None, "section"),
        P("section", None, "dp"),
        P("section", None, "dp"),
        P("section", "dp", None),
        P("section", "dp"),
        P("section", "dp", None),
        P("section", "dp", None),
        P("section", "dp", None),
        P("section", "dp"),
        P("section", "dp", None),
        P("section", None, "dp"),
        P("section", "dp", None),
        P("section", "dp"),
        P("section", "dp", None),
    )
    planes = Z * P_IN
    fits = mesh.shape["dp"] == planes
    return jax.shard_map(
        on_device_planes if fits else on_device, mesh=mesh, in_specs=in_specs, out_specs=out_specs, check_vma=False
    )
```

```python
import functools
from types import SimpleNamespace

import jax
import jax.numpy as jnp
from jax import lax
from jax.experimental import pallas as pl
from jax.experimental.pallas import tpu as pltpu
from jax.sharding import PartitionSpec as P

H = 16
HD = 64


EPSILON = 1e-05
MASKED = -1000000000.0


def passed_along(value, axis, by):
    length = lax.axis_size(axis)
    return lax.ppermute(value, axis, [(i, (i + by) % length) for i in range(length)])


def norm_fwd(rows, gain, shift_term):
    center = rows - jnp.mean(rows, -1, keepdims=True)
    scale = lax.rsqrt(jnp.mean(center * center, -1, keepdims=True) + EPSILON)
    return center * scale * gain + shift_term


def gelu_exact(values):
    return jax.nn.gelu(values, approximate=False)


def product(left, right):
    return jnp.dot(left, right, preferred_element_type=jnp.float32)


def product_right_t(left, right):
    return lax.dot_general(
        left, right, (((1,), (1,)), ((), ())), preferred_element_type=jnp.float32
    )


def product_left_t(left, right):
    return lax.dot_general(
        left, right, (((0,), (0,)), ((), ())), preferred_element_type=jnp.float32
    )


def split_heads(flat, batch_rows):
    return flat.reshape(batch_rows, -1, H, HD)


def softmax_probs(query, key_rows, allowed):
    scores = jnp.einsum(
        "rthd,rshd->rhts", query, key_rows, preferred_element_type=jnp.float32
    ) * HD ** (-0.5)
    scores = jnp.where(allowed[:, None], scores, MASKED)
    weights = jnp.exp(scores - jnp.max(scores, -1, keepdims=True))
    return weights / jnp.sum(weights, -1, keepdims=True)


def attend_fwd(query, key_rows, value_rows, allowed):
    probs = softmax_probs(query, key_rows, allowed)
    mixed = jnp.einsum(
        "rhts,rshd->rthd",
        probs.astype(jnp.bfloat16),
        value_rows,
        preferred_element_type=jnp.float32,
    )
    return mixed.reshape(mixed.shape[0] * mixed.shape[1], -1).astype(jnp.bfloat16)


def attend_back(query, key_rows, value_rows, allowed, grad_mixed):
    probs = softmax_probs(query, key_rows, allowed)
    grad_heads = grad_mixed.reshape(query.shape)
    grad_probs = jnp.einsum(
        "rthd,rshd->rhts", grad_heads, value_rows, preferred_element_type=jnp.float32
    )
    delta = jnp.sum(probs * grad_probs, -1, keepdims=True)
    grad_scores = (probs * (grad_probs - delta)).astype(jnp.bfloat16)
    scale = HD ** (-0.5)
    grad_query = (
        jnp.einsum("rhts,rshd->rthd", grad_scores, key_rows, preferred_element_type=jnp.float32)
        * scale
    )
    grad_keys = (
        jnp.einsum("rhts,rthd->rshd", grad_scores, query, preferred_element_type=jnp.float32)
        * scale
    )
    grad_values = jnp.einsum(
        "rhts,rthd->rshd",
        probs.astype(jnp.bfloat16),
        grad_heads,
        preferred_element_type=jnp.float32,
    )
    width = query.shape[2] * query.shape[3]
    return (
        grad_query.reshape(-1, width).astype(jnp.bfloat16),
        grad_keys.reshape(-1, width).astype(jnp.bfloat16),
        grad_values.reshape(-1, width).astype(jnp.bfloat16),
    )


def unpack(pieces):
    return tuple((piece[0] for piece in pieces))


def on_device(
    prev_act,
    memory,
    out_cot,
    tgt_len,
    src_len,
    norm_gain,
    norm_bias,
    self_qkv,
    self_qv_bias,
    self_out,
    cross_q,
    cross_kv,
    cross_qv_bias,
    cross_out,
    out_bias,
    fc1,
    fc1_bias,
    fc2,
):
    fetched = unpack(
        (
            lax.all_gather(norm_gain, "dp", axis=2, tiled=True),
            lax.all_gather(norm_bias, "dp", axis=2, tiled=True),
            lax.all_gather(self_qkv, "dp", axis=1, tiled=True),
            lax.all_gather(self_qv_bias, "dp", axis=1, tiled=True),
            lax.all_gather(self_out, "dp", axis=1, tiled=True),
            lax.all_gather(cross_q, "dp", axis=1, tiled=True),
            lax.all_gather(cross_kv, "dp", axis=1, tiled=True),
            lax.all_gather(cross_qv_bias, "dp", axis=1, tiled=True),
            lax.all_gather(cross_out, "dp", axis=1, tiled=True),
            lax.all_gather(out_bias, "dp", axis=2, tiled=True),
            lax.all_gather(fc1, "dp", axis=1, tiled=True),
            lax.all_gather(fc1_bias, "dp", axis=1, tiled=True),
            lax.all_gather(fc2, "dp", axis=1, tiled=True),
        )
    )
    gains, shifts, w_sqkv, b_sqv, w_sout, w_cq, w_ckv, b_cqv, w_cout, b_out, w_one, b_one, w_two = (
        fetched
    )
    gain_f = gains.astype(jnp.float32)
    shift_f = shifts.astype(jnp.float32)
    sqv_f = b_sqv.astype(jnp.float32)
    cqv_f = b_cqv.astype(jnp.float32)
    out_f = b_out.astype(jnp.float32)
    one_f = b_one.astype(jnp.float32)
    source = passed_along(prev_act, "section", 1)[0]
    batch_rows, length, width = source.shape
    encoded = lax.all_gather(memory, "section", axis=2, tiled=True)
    mem_flat = encoded.reshape(-1, width)
    places = jnp.arange(length)
    self_ok = (places[None, None, :] <= places[None, :, None]) & (
        places[None, None, :] < tgt_len[:, None, None]
    )
    cross_ok = jnp.arange(encoded.shape[1])[None, None, :] < src_len[:, None, None]
    resid = source.astype(jnp.float32).reshape(-1, width)
    normed_one, pull_one = jax.vjp(norm_fwd, resid, gain_f[0], shift_f[0])
    first_in = normed_one.astype(jnp.bfloat16)
    joint = product(first_in, w_sqkv)
    query_self = (joint[:, :width] + sqv_f[:width]).astype(jnp.bfloat16)
    keys_self = joint[:, width : 2 * width].astype(jnp.bfloat16)
    values_self = (joint[:, 2 * width :] + sqv_f[width:]).astype(jnp.bfloat16)
    self_mixed = attend_fwd(
        split_heads(query_self, batch_rows),
        split_heads(keys_self, batch_rows),
        split_heads(values_self, batch_rows),
        self_ok,
    )
    after_self = resid + (product(self_mixed, w_sout) + out_f[0])
    normed_two, pull_two = jax.vjp(norm_fwd, after_self, gain_f[1], shift_f[1])
    second_in = normed_two.astype(jnp.bfloat16)
    query_cross = (product(second_in, w_cq) + cqv_f[:width]).astype(jnp.bfloat16)
    memory_proj = product(mem_flat, w_ckv)
    keys_cross = memory_proj[:, :width].astype(jnp.bfloat16)
    values_cross = (memory_proj[:, width:] + cqv_f[width:]).astype(jnp.bfloat16)
    cross_mixed = attend_fwd(
        split_heads(query_cross, batch_rows),
        split_heads(keys_cross, batch_rows),
        split_heads(values_cross, batch_rows),
        cross_ok,
    )
    after_cross = after_self + (product(cross_mixed, w_cout) + out_f[1])
    normed_three, pull_three = jax.vjp(norm_fwd, after_cross, gain_f[2], shift_f[2])
    third_in = normed_three.astype(jnp.bfloat16)
    pre_act = product(third_in, w_one) + one_f
    activ, pull_gelu = jax.vjp(gelu_exact, pre_act)
    act_low = activ.astype(jnp.bfloat16)
    result = after_cross + (product(act_low, w_two) + out_f[2])
    output = result.astype(jnp.bfloat16).reshape(1, batch_rows, length, width)
    (
        unused_gains,
        unused_shifts,
        w_sqkv,
        unused_sqv,
        w_sout,
        w_cq,
        w_ckv,
        unused_cqv,
        w_cout,
        unused_out,
        w_one,
        unused_one,
        w_two,
    ) = fetched
    grad_out = passed_along(out_cot, "section", -1)[0].astype(jnp.float32).reshape(-1, width)
    ffn_grad = grad_out.astype(jnp.bfloat16)
    grad_fc2 = product_left_t(act_low, ffn_grad)
    grad_b2 = jnp.sum(ffn_grad, 0, dtype=jnp.float32)
    grad_act = product_right_t(ffn_grad, w_two)
    (grad_pre,) = pull_gelu(grad_act)
    pre_low = grad_pre.astype(jnp.bfloat16)
    grad_fc1 = product_left_t(third_in, pre_low)
    grad_b1 = jnp.sum(pre_low, 0, dtype=jnp.float32)
    grad_mid, grad_gain3, grad_shift3 = pull_three(product_right_t(pre_low, w_one))
    grad_mid = grad_mid + grad_out
    cross_grad = grad_mid.astype(jnp.bfloat16)
    grad_cout = product_left_t(cross_mixed, cross_grad)
    grad_bco = jnp.sum(cross_grad, 0, dtype=jnp.float32)
    grad_cmix = product_right_t(cross_grad, w_cout).astype(jnp.bfloat16)
    grad_qc, grad_kc, grad_vc = attend_back(
        split_heads(query_cross, batch_rows),
        split_heads(keys_cross, batch_rows),
        split_heads(values_cross, batch_rows),
        cross_ok,
        grad_cmix,
    )
    grad_cq = product_left_t(second_in, grad_qc)
    grad_kv = jnp.concatenate([grad_kc, grad_vc], -1)
    grad_ckv = product_left_t(mem_flat, grad_kv)
    grad_cqv = jnp.concatenate(
        [jnp.sum(grad_qc, 0, dtype=jnp.float32), jnp.sum(grad_vc, 0, dtype=jnp.float32)]
    )
    grad_memory = product_right_t(grad_kv, w_ckv).reshape(encoded.shape)
    memory_grad = lax.psum_scatter(
        grad_memory.astype(jnp.bfloat16), "section", scatter_dimension=2, tiled=True
    )
    grad_after, grad_gain2, grad_shift2 = pull_two(product_right_t(grad_qc, w_cq))
    grad_after = grad_after + grad_mid
    self_grad = grad_after.astype(jnp.bfloat16)
    grad_sout = product_left_t(self_mixed, self_grad)
    grad_bso = jnp.sum(self_grad, 0, dtype=jnp.float32)
    grad_smix = product_right_t(self_grad, w_sout).astype(jnp.bfloat16)
    grad_qs, grad_ks, grad_vs = attend_back(
        split_heads(query_self, batch_rows),
        split_heads(keys_self, batch_rows),
        split_heads(values_self, batch_rows),
        self_ok,
        grad_smix,
    )
    grad_qkv = jnp.concatenate([grad_qs, grad_ks, grad_vs], -1)
    grad_sqkv = product_left_t(first_in, grad_qkv)
    grad_sqv = jnp.concatenate(
        [jnp.sum(grad_qs, 0, dtype=jnp.float32), jnp.sum(grad_vs, 0, dtype=jnp.float32)]
    )
    grad_in, grad_gain1, grad_shift1 = pull_one(product_right_t(grad_qkv, w_sqkv))
    grad_in = grad_in + grad_after
    input_grad = passed_along(
        grad_in.astype(jnp.bfloat16).reshape(1, batch_rows, length, width), "section", -1
    )
    grad_gain = jnp.stack([grad_gain1, grad_gain2, grad_gain3])
    grad_shift = jnp.stack([grad_shift1, grad_shift2, grad_shift3])
    grad_obias = jnp.stack([grad_bso, grad_bco, grad_b2])
    sums = (
        lax.psum_scatter(
            grad_gain.astype(jnp.bfloat16), "dp", scatter_dimension=1, tiled=True
        ).astype(jnp.float32),
        lax.psum_scatter(
            grad_shift.astype(jnp.bfloat16), "dp", scatter_dimension=1, tiled=True
        ).astype(jnp.float32),
        lax.psum_scatter(
            grad_sqkv.astype(jnp.bfloat16), "dp", scatter_dimension=0, tiled=True
        ).astype(jnp.float32),
        lax.psum_scatter(
            grad_sqv.astype(jnp.bfloat16), "dp", scatter_dimension=0, tiled=True
        ).astype(jnp.float32),
        lax.psum_scatter(
            grad_sout.astype(jnp.bfloat16), "dp", scatter_dimension=0, tiled=True
        ).astype(jnp.float32),
        lax.psum_scatter(
            grad_cq.astype(jnp.bfloat16), "dp", scatter_dimension=0, tiled=True
        ).astype(jnp.float32),
        lax.psum_scatter(
            grad_ckv.astype(jnp.bfloat16), "dp", scatter_dimension=0, tiled=True
        ).astype(jnp.float32),
        lax.psum_scatter(
            grad_cqv.astype(jnp.bfloat16), "dp", scatter_dimension=0, tiled=True
        ).astype(jnp.float32),
        lax.psum_scatter(
            grad_cout.astype(jnp.bfloat16), "dp", scatter_dimension=0, tiled=True
        ).astype(jnp.float32),
        lax.psum_scatter(
            grad_obias.astype(jnp.bfloat16), "dp", scatter_dimension=1, tiled=True
        ).astype(jnp.float32),
        lax.psum_scatter(
            grad_fc1.astype(jnp.bfloat16), "dp", scatter_dimension=0, tiled=True
        ).astype(jnp.float32),
        lax.psum_scatter(
            grad_b1.astype(jnp.bfloat16), "dp", scatter_dimension=0, tiled=True
        ).astype(jnp.float32),
        lax.psum_scatter(
            grad_fc2.astype(jnp.bfloat16), "dp", scatter_dimension=0, tiled=True
        ).astype(jnp.float32),
    )
    return (
        output,
        input_grad,
        memory_grad,
        sums[0][None],
        sums[1][None],
        sums[2][None],
        sums[3][None],
        sums[4][None],
        sums[5][None],
        sums[6][None],
        sums[7][None],
        sums[8][None],
        sums[9][None],
        sums[10][None],
        sums[11][None],
        sums[12][None],
    )


Z = 4
P_IN = 4
L = 192
D = 1024
T = P_IN * L
FL = 1024
TILE = 32
MESH = pl.DeviceIdType.MESH
F32 = jnp.float32
BF16 = jnp.bfloat16

WEIGHTS = dict(
    qkv=(256, 768, True),
    so=(64, 1024, False),
    ckv=(256, 512, True),
    cq=(256, 256, True),
    co=(64, 1024, False),
    f1=(256, 1024, True),
    f2=(256, 1024, False),
)
SEMS = 320


def run_if(cond, fn):
    if cond is None:
        fn()
    else:
        pl.when(cond)(fn)


def part(index, size, step=None):
    return pl.ds(pl.multiple_of(index * size, size), size if step is None else step)


def nn(left, right):
    return jnp.dot(left, right, preferred_element_type=F32)


def nt(left, right):
    return lax.dot_general(left, right, (((1,), (1,)), ((), ())), preferred_element_type=F32)


def tn(left, right):
    return lax.dot_general(left, right, (((0,), (0,)), ((), ())), preferred_element_type=F32)


def loop(count, body, unroll=1, first=0):
    def step(index, carry):
        body(index)
        return carry

    lax.fori_loop(first, first + count, step, 0, unroll=unroll)


HALF = L // 2
TILES = HALF // TILE


def gelu_pair(values):
    bell = jnp.exp(-0.5 * values * values)
    step = 1.0 / (1.0 + 0.3275911 * 0.7071067811865476 * jnp.abs(values))
    series = step * (
        0.254829592
        + step
        * (-0.284496736 + step * (1.421413741 + step * (-1.453152027 + step * 1.061405429)))
    )
    above = 0.5 * series * bell
    below = jnp.where(values < 0, above, 1.0 - above)
    return values * below, below + values * bell * 0.3989422804014327


def whiten(rows):
    center = rows - jnp.mean(rows, -1, keepdims=True)
    scale = lax.rsqrt(jnp.mean(center * center, -1, keepdims=True) + EPSILON)
    return center * scale, scale


def whole_kernel(n_sec, mem_cols, *refs):
    given = iter(refs)

    def take(names):
        return SimpleNamespace(**{name: next(given) for name in names})

    def take_weights(**fields):
        for name in WEIGHTS:
            for field in fields:
                setattr(getattr(wt, name), field, next(given))

    wt = SimpleNamespace(**{name: SimpleNamespace() for name in WEIGHTS})
    io = take(
        dict(
            prev=0, mem=0, cot=0, tgt=0, src=0, gain=0, shift=0, out_bias=0,
            self_bias=0, cross_bias=0, unit_bias=0,
        )
    )
    take_weights(source=0)
    vars(io).update(vars(take(dict(output=0, input_grad=0, memory_grad=0))))
    take_weights(result=0)
    vars(io).update(vars(take(dict(sums_out=0))))
    buf = take(buffer_shapes(n_sec, mem_cols))
    set_a, set_b, set_c = (take(REDUCE_SHAPES) for _ in range(3))
    take_weights(weight=0, grad=0, near=0, far=0)
    for weight in (wt.qkv, wt.so, wt.ckv, wt.cq, wt.co):
        weight.to_diag, weight.to_opp, weight.through = next(given), next(given), next(given)
    for weight in (wt.qkv, wt.ckv, wt.cq):
        weight.raw, weight.sorted = next(given), next(given)
    send_sems, recv_sems, local_sems = given

    s = lax.axis_index("section")
    d = lax.axis_index("dp")
    z, q = d // P_IN, d % P_IN
    x, c = q // 2, q % 2
    end = (z % 3) == 0
    mid = (z % 3) != 0
    q_core = q + 1 - 2 * c
    q_x = q + 2 - 4 * x
    q_xc = q_x + 1 - 2 * c
    z_adj = z + 1 - 2 * (z % 2)
    z_opp = 3 - z
    z_diag = (z + 2) % 4
    dev_core, dev_x, dev_xc = (s, z * P_IN + q_core), (s, z * P_IN + q_x), (s, z * P_IN + q_xc)
    dev_adj, dev_opp, dev_diag = (s, z_adj * P_IN + q), (s, z_opp * P_IN + q), (s, z_diag * P_IN + q)
    in_plane = ((q_core, dev_core), (q_x, dev_x), (q_xc, dev_xc))

    counter = [0]
    started = []
    local_counter = [0]

    def slot(count=1):
        counter[0] += count
        return counter[0] - count

    def remote(src, dst, k, device):
        return pltpu.make_async_remote_copy(
            src_ref=src, dst_ref=dst, send_sem=send_sems.at[k], recv_sem=recv_sems.at[k],
            device_id=device, device_id_type=MESH,
        )

    def send(src, dst, k, device, cond=None):
        copy = remote(src, dst, k, device)
        run_if(cond, copy.start)
        record = [copy, cond]
        started.append(record)
        return record

    def sent(record):
        run_if(record[1], record[0].wait_send)
        started[:] = [other for other in started if other is not record]

    def arrived(dst, k, cond=None):
        run_if(cond, remote(dst, dst, k, dev_core).wait_recv)

    def local(src, dst, cond=None):
        copy = pltpu.make_async_copy(src, dst, local_sems.at[local_counter[0]])
        local_counter[0] += 1
        run_if(cond, copy.start)
        return copy

    def keep(src, dst, cond=None):
        result_copies.append((local(src, dst, cond), cond))

    def rows(rows_of, index):
        return rows_of.at[part(index, L)]

    for name, (count, _, by_column) in WEIGHTS.items():
        weight = getattr(wt, name)
        weight.count, weight.by_column = count, by_column
        weight.pieces, weight.piece, weight.last_copies = 1, 0, []
        weight.to_use, weight.swap, weight.to_sum, weight.last = slot(5), slot(3), slot(6), slot(3)

    def block(name, index):
        return name.weight.at[part(index * name.pieces + name.piece, name.count)]

    first_weights = [
        SimpleNamespace(
            weight=wt.qkv.weight, count=wt.qkv.count // 2, pieces=2, piece=h, to_use=slot(5)
        )
        for h in range(2)
    ]

    def send_inward(name, src):
        send(src, block(name, z), name.to_use, dev_adj, end)

    def send_across(name, src):
        send(src, block(name, z), name.to_use + 1, dev_opp, mid)

    def weight_outward(name, src):
        send(src, block(name, z), name.to_use, dev_adj, mid)

    def relay_inward(name):
        k = name.to_use
        arrived(block(name, z_adj), k, mid)
        send(block(name, z_adj), block(name, z_adj), k + 2, dev_opp, mid)

    def relay_near(name):
        k = name.to_use
        arrived(block(name, z_opp), k + 1, mid)
        send(block(name, z_opp), block(name, z_opp), k + 3, dev_adj, mid)

    def relay_far(name):
        k = name.to_use
        arrived(block(name, z_diag), k + 2, mid)
        send(block(name, z_diag), block(name, z_diag), k + 4, dev_adj, mid)

    def weight_ready(name):
        k = name.to_use
        arrived(block(name, z_adj), k, end)
        arrived(block(name, z_diag), k + 3, end)
        arrived(block(name, z_opp), k + 4, end)

    def inner_ready(name):
        k = name.to_use
        arrived(block(name, z_opp), k + 1, mid)
        arrived(block(name, z_diag), k + 2, mid)


    def swap_start(name):
        size = name.count // P_IN
        place = name.weight.at[part(z * P_IN + q, size)]
        name.swapped = [
            send(name.sorted.at[q_to], place, name.swap + j, device)
            for j, (q_to, device) in enumerate(in_plane)
        ]
        name.own_copy = [local(name.sorted.at[q], place)]

    def swap_wait(name):
        size = name.count // P_IN
        for j, (q_from, _) in enumerate(in_plane):
            arrived(name.weight.at[part(z * P_IN + q_from, size)], name.swap + j)
        for copy in name.own_copy:
            copy.wait()
        for record in name.swapped:
            sent(record)

    def halves(first, second, odd):
        if odd:
            first = pltpu.roll(first, 64, 1)
        else:
            second = pltpu.roll(second, 64, 1)
        lane = lax.broadcasted_iota(jnp.int32, first.shape, 1)
        return jnp.where(lane < 64, first, second)

    def tile_of(index):
        return slice(index * 128, index * 128 + 128)

    def sort_columns(name):
        for q_to in range(P_IN):
            for tile in range(name.sorted.shape[2] // 128):
                at = 4 * tile + q_to // 2
                first = name.raw[:, tile_of(at)].astype(F32)
                second = name.raw[:, tile_of(at + 2)].astype(F32)
                name.sorted[q_to, :, tile_of(tile)] = halves(first, second, q_to % 2).astype(BF16)

    def unsort_columns(name):
        for tile in range(name.raw.shape[1] // 128):
            group, u = tile // 8, tile % 8
            at = 2 * group + u // 4
            first = name.sorted[2 * (u % 2), :, tile_of(at)].astype(F32)
            second = name.sorted[2 * (u % 2) + 1, :, tile_of(at)].astype(F32)
            name.raw[:, tile_of(tile)] = halves(first, second, (u // 2) % 2).astype(BF16)

    unit_swap, unit_last = slot(3 * Z), slot(3 * Z)

    def unit_columns(rows_of, tile, q_at):
        return rows_of.at[:, part(tile * P_IN + q_at, 256)]

    def unit_swap_start():
        size = wt.f1.count // P_IN
        place = wt.f1.weight.at[part(z * P_IN + q, size)]
        wt.f1.own_copy = []
        for tile in range(Z):
            at = place.at[:, part(tile, 256)]
            for j, (q_to, device) in enumerate(in_plane):
                send(unit_columns(wt.f1.source, tile, q_to), at, unit_swap + 3 * tile + j, device)
            wt.f1.own_copy.append(local(unit_columns(wt.f1.source, tile, q), at))

    def unit_swap_wait(cond):
        size = wt.f1.count // P_IN
        for tile in range(Z):
            for j, (q_from, _) in enumerate(in_plane):
                place = wt.f1.weight.at[part(z * P_IN + q_from, size)]
                arrived(place.at[:, part(tile, 256)], unit_swap + 3 * tile + j, cond)
        for copy in wt.f1.own_copy:
            run_if(cond, copy.wait)

    def grad_block(name, index):
        return name.grad.at[part(index, name.count)]

    def grad_send_far(name):
        return send(grad_block(name, z_opp), name.to_diag, name.to_sum, dev_adj, end)

    def grad_send_middle(name):
        return send(grad_block(name, z_diag), name.to_opp, name.to_sum + 1, dev_adj, end)

    def grad_send_near(name):
        return send(grad_block(name, z_adj), name.near, name.to_sum + 2, dev_adj, end)

    def grad_send(name):
        grad_send_far(name)
        grad_send_middle(name)

    def add_rows(count, body):
        size = min(count, 64)
        loop(count // size, lambda i: body(part(i, size)))

    def grad_add(name, landed, index):
        def one(place):
            own = grad_block(name, index)[place, :].astype(F32)
            landed[place, :] = (own + landed[place, :].astype(F32)).astype(BF16)

        add_rows(name.count, one)

    def grad_combine_far(name):
        k = name.to_sum
        arrived(name.to_diag, k, mid)
        run_if(mid, lambda: grad_add(name, name.to_diag, z_diag))
        send(name.to_diag, name.through, k + 3, dev_opp, mid)

    def grad_combine_middle(name):
        k = name.to_sum
        arrived(name.to_opp, k + 1, mid)
        run_if(mid, lambda: grad_add(name, name.to_opp, z_opp))
        send(name.to_opp, name.far, k + 4, dev_opp, mid)

    def grad_combine(name):
        grad_combine_far(name)
        grad_combine_middle(name)

    def grad_outward(name):
        k = name.to_sum
        arrived(name.through, k + 3, mid)
        run_if(mid, lambda: grad_add(name, name.through, z_adj))
        send(name.through, name.near, k + 5, dev_adj, mid)

    result_copies = []

    def inner_grad_far(name):
        send(grad_block(name, z_diag), name.far, name.to_sum, dev_opp, mid)

    def inner_grad_near(name):
        send(grad_block(name, z_opp), name.near, name.to_sum + 1, dev_opp, mid)

    def f2_half(rows_of, h):
        return rows_of.at[part(h, wt.f2.count // 2)]

    def f2_near(h):
        src = f2_half(grad_block(wt.f2, z_opp), h)
        send(src, f2_half(wt.f2.near, h), wt.f2.to_sum + 1 + 2 * h, dev_opp, mid)

    def inner_grad_combine(name):
        k = name.to_sum

        def add():
            arrived(name.far, k)

            def one(place):
                own = grad_block(name, z_adj)[place, :].astype(F32)
                name.far[place, :] = (own + name.far[place, :].astype(F32)).astype(BF16)

            add_rows(name.count, one)

        run_if(mid, add)
        send(name.far, name.near, k + 2, dev_adj, mid)

    def grad_total(name, cond):
        k = name.to_sum
        arrived(name.near, k + (5 if cond is end else 2), cond)
        if cond is mid:
            arrived(name.far, k + 4, mid)

        def add():
            def one(place):
                total = name.near[place, :].astype(F32)
                if cond is mid:
                    total = total + name.far[place, :].astype(F32)
                name.near[place, :] = (total + grad_block(name, z)[place, :].astype(F32)).astype(BF16)

            add_rows(name.count, one)

        run_if(cond, add)

    def grad_final(name, cond):
        grad_total(name, cond)
        if name.by_column:
            size = name.count // P_IN
            for j, (q_to, device) in enumerate(in_plane):
                src = name.near.at[part(q_to, size)]
                send(src, name.sorted.at[q], name.last + j, device, cond)
            src = name.near.at[part(q, size)]
            name.last_copies.append((local(src, name.sorted.at[q], cond), cond))
        else:
            keep(name.near, name.result, cond)

    def f2_final(cond):
        if cond is end:
            arrived(wt.f2.near, wt.f2.to_sum + 2, end)
        else:
            for h in range(2):
                arrived(f2_half(wt.f2.near, h), wt.f2.to_sum + 1 + 2 * h, mid)
            run_if(mid, lambda: grad_add(wt.f2, wt.f2.near, z))
        keep(wt.f2.near, wt.f2.result, cond)

    def f1_final(cond):
        if cond is end:
            arrived(wt.f1.near, wt.f1.to_sum + 2, end)
        else:
            arrived(wt.f1.near, wt.f1.to_sum + 1, mid)
            run_if(mid, lambda: grad_add(wt.f1, wt.f1.near, z))
        size = wt.f1.count // P_IN
        for tile in range(Z):
            dst = unit_columns(wt.f1.result, tile, q)
            for j, (q_to, device) in enumerate(in_plane):
                src = wt.f1.near.at[part(q_to, size), part(tile, 256)]
                send(src, dst, unit_last + 3 * tile + j, device, cond)
            keep(wt.f1.near.at[part(q, size), part(tile, 256)], dst, cond)

    def last_wait(name):
        for j, (q_from, _) in enumerate(in_plane):
            arrived(name.sorted.at[q_from], name.last + j)
        for copy, cond in name.last_copies:
            run_if(cond, copy.wait)
        unsort_columns(name)
        keep(name.raw, name.result)

    def unit_last_wait():
        for tile in range(Z):
            for j, (q_from, _) in enumerate(in_plane):
                place = unit_columns(wt.f1.result, tile, q_from)
                arrived(place, unit_last + 3 * tile + j)

    def piece(name, index, h, parts):
        size = L // parts
        return name.at[part(index * parts + h, size)]

    def half_major(name, index, h, parts=2):
        return name.at[part(h * P_IN + index, HALF)]

    def gather_open(name, cond=None, parts=1, lay=piece):
        return name, slot(3 * parts), [], cond, parts, lay

    def gather_part(ticket, h, cond=None):
        name, k, records, usual, parts, lay = ticket
        cond = usual if cond is None else cond
        own = lay(name, q, h, parts)
        records.append(send(own, own, k + 3 * h, dev_x, cond))
        records.append(send(own, own, k + 3 * h + 1, dev_core, cond))

    def gather_start(name, cond=None):
        ticket = gather_open(name, cond)
        gather_part(ticket, 0)
        return ticket

    def gather_relay_part(ticket, h):
        name, k, records, cond, parts, lay = ticket
        other = lay(name, q_x, h, parts)
        arrived(other, k + 3 * h, cond)
        records.append(send(other, other, k + 3 * h + 2, dev_core, cond))

    def gather_ready_part(ticket, h):
        name, k, _, cond, parts, lay = ticket
        arrived(lay(name, q_core, h, parts), k + 3 * h + 1, cond)
        arrived(lay(name, q_xc, h, parts), k + 3 * h + 2, cond)

    def gather_relay(ticket):
        for h in range(ticket[4]):
            gather_relay_part(ticket, h)

    def gather_ready(ticket):
        for h in range(ticket[4]):
            gather_ready_part(ticket, h)

    def gather_finish(ticket):
        gather_relay(ticket)
        gather_ready(ticket)

    def reduce_start(which, cond=None):
        k = slot(4)
        out = which.parts
        first = send(rows(out, q_xc), rows(which.core, 1), k, dev_core, cond)
        second = send(rows(out, q_core), rows(which.core, 0), k + 1, dev_core, cond)
        return which, k, [first, second], cond, piece

    def reduce_open(which, cond):
        return which, slot(6), [], cond, half_major

    def reduce_start_half(ticket, h):
        which, k, records, cond, lay = ticket
        for j, index in ((1, q_xc), (0, q_core)):
            src, dst = lay(which.parts, index, h), piece(which.core, j, h, 2)
            records.append(send(src, dst, k + 4 * h + 1 - j, dev_core, cond))

    def reduce_relay_half(ticket, h):
        which, k, records, cond, lay = ticket
        landed = piece(which.core, 1, h, 2)
        if lay is half_major:
            arrived(landed, k + 4 * h, cond)
        elif h == 0:
            arrived(rows(which.core, 1), k, cond)
        mine = lay(which.parts, q_x, h, 2)

        def add():
            def one(i):
                place = part(i, TILE)
                total = mine[place, :].astype(F32) + landed[place, :].astype(F32)
                mine[place, :] = total.astype(BF16)

            loop(TILES, one)

        run_if(cond, add)
        dst = which.across.at[part(h, HALF)]
        records.append(send(mine, dst, k + 2 + h, dev_x, cond))
        return records[-1]

    def reduce_relay(ticket):
        reduce_relay_half(ticket, 0)
        reduce_relay_half(ticket, 1)

    def reduce_ready_half(ticket, h):
        which, k, _, cond, lay = ticket
        if lay is half_major:
            arrived(piece(which.core, 0, h, 2), k + 4 * h + 1, cond)
        elif h == 0:
            arrived(rows(which.core, 0), k + 1, cond)
        arrived(which.across.at[part(h, HALF)], k + 2 + h, cond)

    def reduce_ready(ticket):
        reduce_ready_half(ticket, 0)
        reduce_ready_half(ticket, 1)

    def reduced(ticket, place):
        which = ticket[0]
        total = rows(which.parts, q)[place, :].astype(F32)
        total = total + rows(which.core, 0)[place, :].astype(F32)
        return total + which.across[place, :].astype(F32)

    def fold(ticket, dst, halves=(0, 1)):
        which, lay = ticket[0], ticket[4]
        for h in halves:
            mine, landed = lay(which.parts, q, h, 2), piece(which.core, 0, h, 2)

            def one(i, h=h, mine=mine, landed=landed):
                place, here = part(i, TILE), part(i + h * TILES, TILE)
                total = mine[place, :].astype(F32) + landed[place, :].astype(F32)
                dst[here, :] = (total + which.across[here, :].astype(F32)).astype(BF16)

            loop(TILES, one)

    def reduce_done(ticket):
        for record in ticket[2]:
            sent(record)

    def spread_start(place):
        k = slot(8)
        for j, device in enumerate((dev_diag, dev_opp, dev_adj)):
            send(place(z), place(z), k + j, device)
        return place, k

    def spread_wait(ticket):
        place, k = ticket
        for j, plane in enumerate((z_diag, z_opp, z_adj)):
            arrived(place(plane), k + j)

    def spread_plane(ticket, name):
        k = ticket[1]
        for j, (_, device) in enumerate(in_plane):
            send(name.at[q], name.at[q], k + 5 + j, device)

    def spread_ready(ticket, name):
        k = ticket[1]
        for j, (q_from, _) in enumerate(in_plane):
            arrived(name.at[q_from], k + 5 + j)

    def lanes(j, size=256):
        return part(j, size)

    def matmul(left, right, dst, bias=None, bias_row=0, bias_at=0):
        count = right.shape[1] // 256

        def one(j):
            tile = nn(left[...], right[:, lanes(j)])
            if bias is not None:
                tile = tile + bias[bias_row:bias_row + 1, part(j + bias_at, 256)]
            dst[:, lanes(j)] = tile.astype(BF16)

        loop(count, one)

    def matmul_back(left, right, dst, at=slice(0, T)):
        def one(j):
            dst[at, lanes(j)] = nt(left[at, :], right[lanes(j), :]).astype(BF16)

        loop(right.shape[0] // 256, one)

    def weight_grad(left, right, name, more=False):
        def one(j):
            total = tn(left[:, lanes(j)], right[...])
            if more:
                total = total + name.grad[lanes(j), :].astype(F32)
            name.grad[lanes(j), :] = total.astype(BF16)

        loop(left.shape[1] // 256, one)

    low_half = lax.broadcasted_iota(jnp.int32, (L, 128), 1) < 64
    keep_low = low_half.astype(F32).astype(BF16)
    keep_high = (1.0 - low_half.astype(F32)).astype(BF16)

    def both(pair):
        return jnp.concatenate([pair * keep_low, pair * keep_high], axis=0)

    def merge(stacked):
        return jnp.where(low_half, stacked[:L], stacked[L:])

    def attention(qref, q_at, kref, k_at, v_at, causal, length_row, probs, dst):
        def one(i):
            r, pair = i // 2, i % 2
            place = part(r, L)
            query = both(qref[place, part(pair + q_at, 128)])
            scores = nt(query, kref[place, part(pair + k_at, 128)]) * HD ** (-0.5)
            key = lax.broadcasted_iota(jnp.int32, scores.shape, 1)
            limit = buf.sva[r, z][length_row:length_row + 1, 0:1].astype(F32)
            allowed = key.astype(F32) < limit
            if causal:
                at = lax.broadcasted_iota(jnp.int32, scores.shape, 0)
                at = jnp.where(at < L, at, at - L)
                allowed = allowed & (key <= at)
            scores = jnp.where(allowed, scores, MASKED)
            raised = jnp.exp(scores - jnp.max(scores, -1, keepdims=True))
            weights = (raised * (1.0 / jnp.sum(raised, -1, keepdims=True))).astype(BF16)
            probs[i] = weights
            mixed = nn(weights, kref[place, part(pair + v_at, 128)])
            dst[place, part(pair, 128)] = merge(mixed).astype(BF16)

        loop(2 * P_IN, one, 2)

    def attention_back(qref, q_at, kref, k_at, v_at, probs, grad):
        def one(i):
            r, pair = i // 2, i % 2
            place = part(r, L)
            query = both(qref[place, part(pair + q_at, 128)])
            key = kref[place, part(pair + k_at, 128)]
            value = kref[place, part(pair + v_at, 128)]
            mixed_grad = both(grad[place, part(pair, 128)])
            weights = probs[i]
            soft = weights.astype(F32)
            grad_probs = nt(mixed_grad, value)
            delta = jnp.sum(soft * grad_probs, -1, keepdims=True)
            grad_scores = (soft * (grad_probs - delta)).astype(BF16)
            scale = HD ** (-0.5)
            grad_query = merge(nn(grad_scores, key)) * scale
            grad_key = tn(grad_scores, query) * scale
            grad_value = tn(weights, mixed_grad)
            qref[place, part(pair + q_at, 128)] = grad_query.astype(BF16)
            kref[place, part(pair + k_at, 128)] = grad_key.astype(BF16)
            kref[place, part(pair + v_at, 128)] = grad_value.astype(BF16)

        loop(2 * P_IN, one, 2)

    def column_sums(source, first, count, row, at):
        def one(j):
            values = source[:, part(j + first, 256)].astype(F32)
            buf.sg[row:row + 1, part(j + at, 256)] = jnp.sum(values, 0, keepdims=True)

        loop(count, one)

    def norm(load, index, dst, halves=(0, 1)):
        def one(i):
            place = part(i, TILE)
            normed, _ = whiten(load(place))
            gain, shift = buf.vec[index:index + 1, :], buf.vec[index + 3:index + 4, :]
            rows(dst, q)[place, :] = (normed * gain + shift).astype(BF16)

        loop(TILES * len(halves), one, first=TILES * halves[0])

    def norm_back(load, incoming, index, base, dst, low, out_row=None, halves=(0, 1)):
        zero = jnp.zeros((1, D), F32)

        def one(i, carry):
            gain_sum, shift_sum, out_sum = carry
            place = part(i, TILE)
            normed, scale = whiten(load(place))
            grad = incoming(place)
            gained = grad * buf.vec[index:index + 1, :]
            back = gained - jnp.mean(gained, -1, keepdims=True)
            back = back - normed * jnp.mean(gained * normed, -1, keepdims=True)
            total = base(place) + scale * back
            if dst is not None:
                dst[place, :] = total
            rounded = total.astype(BF16)
            low(place, rounded)
            return (
                gain_sum + jnp.sum(grad * normed, 0, keepdims=True),
                shift_sum + jnp.sum(grad, 0, keepdims=True),
                out_sum + jnp.sum(rounded.astype(F32), 0, keepdims=True),
            )

        first = TILES * halves[0]
        last = first + TILES * len(halves)
        gain_sum, shift_sum, out_sum = lax.fori_loop(first, last, one, (zero, zero, zero))
        buf.sg[index:index + 1, :] = buf.sg[index:index + 1, :] + gain_sum
        buf.sg[index + 3:index + 4, :] = buf.sg[index + 3:index + 4, :] + shift_sum
        if out_row is not None:
            buf.sg[out_row:out_row + 1, :] = buf.sg[out_row:out_row + 1, :] + out_sum

    gate = pltpu.get_barrier_semaphore()
    partners = [device for _, device in in_plane] + [dev_adj, dev_opp, dev_diag]
    partners += [((s + j) % n_sec, d) for j in range(1, n_sec)]
    for device in partners:
        pl.semaphore_signal(gate, inc=1, device_id=device, device_id_type=MESH)
    raw_copies = [local(weight.source, weight.raw) for weight in (wt.qkv, wt.ckv, wt.cq)]
    low_lanes = lax.broadcasted_iota(jnp.int32, (3, 128), 1) < 64
    even_lanes = (jnp.zeros((3, 128), jnp.int32) + c) == 0
    for row, pieces in ((0, io.gain), (3, io.shift), (6, io.out_bias)):
        value = pieces[...].astype(F32)
        twice = jnp.concatenate([value, value], 1)
        buf.sg[row:row + 3, 0:128] = jnp.where(low_lanes == even_lanes, twice, 0.0)
    buf.sg[9:10, 0:128] = io.self_bias[...].astype(F32)
    buf.sg[10:11, 0:128] = io.cross_bias[...].astype(F32)
    buf.sg[11:12, 0:128] = io.unit_bias[:, 0:128].astype(F32)
    buf.sg[12:13, 0:128] = io.unit_bias[:, 128:256].astype(F32)
    buf.sg[13:14, 0:128] = jnp.zeros((1, 128), F32) + io.tgt[0].astype(F32)
    buf.sg[14:15, 0:128] = jnp.zeros((1, 128), F32) + io.src[0].astype(F32)
    buf.sg[15:16, 0:128] = jnp.zeros((1, 128), F32)
    buf.sva[q, z] = buf.sg[:, 0:128].astype(BF16)

    raw_copies[0].wait()
    sort_columns(wt.qkv)
    pl.semaphore_wait(gate, len(partners))

    sv = spread_start(lambda plane: buf.sva.at[q, plane])
    swap_start(wt.qkv)
    k_prev, k_cot, k_mem = slot(), slot(), slot(n_sec)
    send(io.prev, buf.hb, k_prev, ((s + 1) % n_sec, d))
    mem_slot = rows(buf.m, q)
    for j in range(1, n_sec):
        send(io.mem, mem_slot.at[:, part(s, mem_cols)], k_mem + j, ((s + j) % n_sec, d))
    mem_copy = local(io.mem, mem_slot.at[:, part(s, mem_cols)])
    send(io.cot, rows(buf.e3, q), k_cot, ((s + n_sec - 1) % n_sec, d))
    for weight in (wt.so, wt.co, wt.f2):
        weight.own_copy = [local(weight.source, block(weight, z))]
    send_inward(wt.so, wt.so.source)
    send_across(wt.so, wt.so.source)
    weight_outward(wt.so, wt.so.source)
    swap_wait(wt.qkv)
    for weight in first_weights:
        send_inward(weight, block(weight, z))
        send_across(weight, block(weight, z))
        weight_outward(weight, block(weight, z))
    spread_wait(sv)
    spread_plane(sv, buf.sva)
    for weight, copy in ((wt.ckv, raw_copies[1]), (wt.cq, raw_copies[2])):
        copy.wait()
        sort_columns(weight)
        swap_start(weight)
    spread_ready(sv, buf.sva)

    for tile in range(D // 128):
        pair = buf.sva[2 * (tile % 2), tile // 2].astype(F32)
        pair = pair + buf.sva[2 * (tile % 2) + 1, tile // 2].astype(F32)
        buf.vec[:, tile * 128:(tile + 1) * 128] = pair
    half = lax.broadcasted_iota(jnp.int32, (16, 128), 1) < 64
    even = (jnp.zeros((16, 128), jnp.int32) + c) == 0
    buf.bias[...] = jnp.zeros((8, D), F32)
    for kind in range(2):
        for tile in range(2):
            first = buf.sva[x, tile + 2 * kind].astype(F32)
            second = buf.sva[2 + x, tile + 2 * kind].astype(F32)
            lower = jnp.where(even, first, pltpu.roll(first, 64, 1))
            upper = jnp.where(even, pltpu.roll(second, 64, 1), second)
            both_heads = jnp.where(half, lower, upper)
            for which in range(2):
                at = 512 * kind + 128 * tile
                buf.bias[which:which + 1, at:at + 128] = both_heads[9 + which:10 + which]
    for tile in range(Z):
        unit = buf.sva[q, tile].astype(F32)
        buf.bias[2:3, 256 * tile:256 * tile + 128] = unit[11:12]
        buf.bias[2:3, 256 * tile + 128:256 * tile + 256] = unit[12:13]
    buf.sg[...] = jnp.zeros((16, D), F32)

    relay_inward(first_weights[0])
    relay_near(first_weights[0])
    arrived(buf.hb, k_prev)

    def hidden(place):
        return buf.hb[place, :].astype(F32)

    norm(hidden, 0, buf.a1)
    a1 = gather_start(buf.a1)
    unit_swap_start()
    relay_inward(first_weights[1])
    relay_near(first_weights[1])
    relay_inward(wt.so)
    swap_wait(wt.ckv)
    send_inward(wt.ckv, block(wt.ckv, z))
    swap_wait(wt.cq)
    send_inward(wt.cq, block(wt.cq, z))
    send_inward(wt.co, wt.co.source)
    send_across(wt.ckv, block(wt.ckv, z))
    for j in range(1, n_sec):
        origin = (s + n_sec - j) % n_sec
        arrived(mem_slot.at[:, part(origin, mem_cols)], k_mem + j)
    mem_copy.wait()
    memory = gather_start(buf.m)
    arrived(rows(buf.e3, q), k_cot)
    k_units = slot(16)
    to_middle = [send(rows(buf.e3, q), rows(buf.e3, q), k_units + 9, dev_x, end)]

    def cot_inward(index, k):
        for h in range(2):
            src, dst = piece(buf.e3, index, h, 2), half_major(buf.e3b, index, h)
            to_middle.append(send(src, dst, k + h, dev_adj, end))

    cot_inward(q, k_units)
    relay_far(first_weights[0])
    gather_relay(a1)
    relay_far(first_weights[1])
    relay_near(wt.so)
    relay_inward(wt.ckv)
    gather_ready(a1)
    unit_swap_wait(end)
    send_inward(wt.f1, block(wt.f1, z))
    for weight in first_weights:
        weight_ready(weight)
    matmul(buf.a1, wt.qkv.weight, buf.qkv, buf.bias, 0)
    relay_far(wt.so)
    weight_outward(wt.ckv, block(wt.ckv, z))
    send_across(wt.cq, block(wt.cq, z))
    attention(buf.qkv, 0, buf.qkv, 2, 4, True, 13, buf.p1, buf.o1)
    relay_inward(wt.cq)
    send_across(wt.co, wt.co.source)
    wt.so.own_copy[0].wait()
    weight_ready(wt.so)
    matmul(buf.o1, wt.so.weight, set_a.parts)
    step = reduce_start(set_a)
    send_inward(wt.f2, wt.f2.source)
    relay_inward(wt.co)
    relay_near(wt.ckv)
    weight_outward(wt.cq, block(wt.cq, z))
    reduce_relay(step)
    arrived(rows(buf.e3, q_x), k_units + 9, end)
    cot_inward(q_x, k_units + 2)
    gather_finish(memory)
    relay_far(wt.ckv)
    unit_swap_wait(mid)
    send_across(wt.f1, block(wt.f1, z))

    def after_self(i):
        place = part(i, TILE)
        buf.h1[place, :] = hidden(place) + (reduced(step, place) + buf.vec[6:7, :])

    a2 = gather_open(buf.a2, None, 2)
    for h in range(2):
        reduce_ready_half(step, h)
        loop(TILES, after_self, first=h * TILES)
        norm(lambda place: buf.h1[place, :], 1, buf.a2, (h,))
        gather_part(a2, h)
    reduce_done(step)
    relay_near(wt.cq)
    weight_outward(wt.co, wt.co.source)
    relay_far(wt.cq)
    weight_ready(wt.ckv)
    matmul(buf.m, wt.ckv.weight, buf.kv, buf.bias, 1, 1)
    relay_near(wt.co)
    send_across(wt.f2, wt.f2.source)
    relay_far(wt.co)
    relay_inward(wt.f1)

    gather_finish(a2)
    e3 = gather_start(buf.e3, mid)
    weight_ready(wt.cq)
    matmul(buf.a2, wt.cq.weight, buf.q2, buf.bias, 1)
    attention(buf.q2, 0, buf.kv, 0, 2, False, 14, buf.p2, buf.o2)
    wt.co.own_copy[0].wait()
    weight_ready(wt.co)
    matmul(buf.o2, wt.co.weight, set_b.parts)
    step = reduce_start(set_b)
    relay_inward(wt.f2)
    gather_finish(e3)
    reduce_relay(step)

    def after_cross(i):
        place = part(i, TILE)
        buf.h2[place, :] = buf.h1[place, :] + (reduced(step, place) + buf.vec[7:8, :])

    a3 = gather_open(buf.a3, mid, 2)
    for h in range(2):
        reduce_ready_half(step, h)
        loop(TILES, after_cross, first=h * TILES)
        norm(lambda place: buf.h2[place, :], 2, buf.a3, (h,))
        send(piece(buf.a3, q, h, 2), half_major(buf.a3b, q, h), k_units + 10 + h, dev_adj, end)
        gather_part(a3, h)
    reduce_done(step)

    def units(normed, activs, slopes, at=slice(0, T)):
        def one(j):
            value = nn(normed[at, :], wt.f1.weight[:, lanes(j)]) + buf.bias[2:3, lanes(j)]
            activ, slope = gelu_pair(value)
            activs[at, lanes(j)] = activ.astype(BF16)
            slopes[at, lanes(j)] = slope.astype(BF16)

        loop(FL // 256, one, 2)

    def units_back(grad, slopes, at=slice(0, T)):
        def one(j):
            value = nt(grad[at, :], wt.f2.weight[lanes(j), :])
            low = (value * slopes[at, lanes(j)].astype(F32)).astype(BF16)
            slopes[at, lanes(j)] = low
            total = jnp.sum(low.astype(F32), 0, keepdims=True)
            buf.sg[10:11, lanes(j)] = buf.sg[10:11, lanes(j)] + total

        loop(FL // 256, one)

    def weight_grads(left, right, left_b, right_b, name, first, count):
        def one(j):
            total = tn(left[:, lanes(j)], right[...]) + tn(left_b[:, lanes(j)], right_b[...])
            name.grad[lanes(j), :] = total.astype(BF16)

        loop(count, one, first=first)

    def finish(incoming):
        def one(i):
            place = part(i, TILE)
            total = buf.h2[place, :] + (incoming(place) + buf.vec[8:9, :])
            buf.stage[place, :] = total.astype(BF16)

        loop(L // TILE, one)

    def on_mid(fn, *args):
        run_if(mid, lambda: fn(*args))

    def cot_sum(i, carry):
        return carry + jnp.sum(rows(buf.e3, q)[part(i, TILE), :].astype(F32), 0, keepdims=True)

    buf.sg[8:9, :] = lax.fori_loop(0, L // TILE, cot_sum, jnp.zeros((1, D), F32))

    for index, k in ((q, k_units), (q_x, k_units + 2)):
        for h in range(2):
            landed = half_major(buf.e3b, index, h)
            arrived(landed, k + h, mid)
            send(landed, landed, k + 4 + h, dev_core, mid)
    gather_relay(a3)
    a3b = gather_open(buf.a3b, mid, 2, half_major)
    arrived(half_major(buf.a3b, q, 0), k_units + 10, mid)
    gather_part(a3b, 0)
    gather_ready(a3)
    inner_ready(wt.f1)
    on_mid(units, buf.a3, buf.g, buf.gp)
    arrived(half_major(buf.a3b, q, 1), k_units + 11, mid)
    gather_part(a3b, 1)
    on_mid(weight_grad, buf.g, buf.e3, wt.f2)
    for index, k in ((q_core, k_units + 4), (q_xc, k_units + 6)):
        for h in range(2):
            arrived(half_major(buf.e3b, index, h), k + h, mid)
    gather_relay_part(a3b, 0)
    wt.f2.own_copy[0].wait()
    inner_ready(wt.f2)
    on_mid(matmul, buf.g, wt.f2.weight, set_c.parts)
    final = reduce_start(set_c, mid)
    gather_ready_part(a3b, 0)
    step_b = reduce_open(set_b, mid)
    for h in range(2):
        at = slice(h * T // 2, (h + 1) * T // 2)
        if h == 1:
            gather_ready_part(a3b, 1)
        on_mid(units, buf.a3b, buf.gb, buf.gpb, at)
        if h == 0:
            reduce_relay(final)
        else:
            reduce_relay_half(step_b, 0)
            on_mid(weight_grad, buf.gb, buf.e3b, wt.f2, True)
            inner_grad_far(wt.f2)
            f2_near(0)
        on_mid(units_back, buf.e3b, buf.gpb, at)
        if h == 0:
            gather_relay_part(a3b, 1)
        on_mid(matmul_back, buf.gpb, wt.f1.weight, set_b.parts, at)
        reduce_start_half(step_b, h)

    def back_outward(h):
        reduce_ready_half(step_b, h)
        on_mid(fold, step_b, buf.back, (h,))
        ready = buf.back.at[part(h, HALF)]
        send(ready, ready, k_units + 12 + h, dev_adj, mid)

    reduce_relay_half(step_b, 1)
    on_mid(units_back, buf.e3, buf.gp)
    back_outward(0)
    on_mid(matmul_back, buf.gp, wt.f1.weight, set_a.parts)
    reduce_ready(final)
    on_mid(finish, lambda place: reduced(final, place))
    reduce_done(final)
    step = reduce_start(set_a, mid)
    back_outward(1)
    reduce_relay(step)
    on_mid(weight_grads, buf.a3, buf.gp, buf.a3b, buf.gpb, wt.f1, 0, Z)
    inner_grad_far(wt.f1)
    inner_grad_near(wt.f1)
    on_mid(matmul, buf.gb, wt.f2.weight, set_c.parts)

    def store(name):
        def low(place, value):
            rows(name, q)[place, :] = value

        return low

    def units_norm_back(incoming, halves):
        norm_back(
            lambda place: buf.h2[place, :], incoming, 2,
            lambda place: rows(buf.e3, q)[place, :].astype(F32), buf.dh, store(buf.e2), 7, halves,
        )

    reduce_done(e3)
    for record in to_middle:
        sent(record)
    e2 = gather_open(buf.e2, None, 2)
    for h in range(2):
        reduce_ready_half(step, h)
        on_mid(units_norm_back, lambda place: reduced(step, place), (h,))
        gather_part(e2, h, mid)
    final_b = reduce_open(set_c, mid)
    reduce_start_half(final_b, 0)
    reduce_start_half(final_b, 1)
    inner_grad_combine(wt.f2)
    for h in range(2):
        arrived(buf.back.at[part(h, HALF)], k_units + 12 + h, end)
        run_if(
            end,
            lambda h=h: units_norm_back(lambda place: buf.back[place, :].astype(F32), (h,)),
        )
        gather_part(e2, h, end)
    reduce_done(step)
    reduce_done(step_b)
    gather_finish(e2)
    reduce_relay(final_b)

    weight_grad(buf.o2, buf.e2, wt.co)
    grad_send(wt.co)
    matmul_back(buf.e2, wt.co.weight, buf.do)
    attention_back(buf.q2, 0, buf.kv, 0, 2, buf.p2, buf.do)
    matmul_back(buf.q2, wt.cq.weight, set_b.parts)
    step = reduce_start(set_b)
    weight_grad(buf.a2, buf.q2, wt.cq)
    grad_send(wt.cq)
    reduce_relay(step)
    grad_combine(wt.co)
    grad_combine(wt.cq)
    weight_grad(buf.m, buf.kv, wt.ckv)
    grad_send(wt.ckv)
    grad_send_near(wt.ckv)
    matmul_back(buf.kv, wt.ckv.weight, set_a.parts)
    mem_step = reduce_start(set_a)
    column_sums(buf.q2, 0, 1, 9, 2)
    column_sums(buf.kv, 1, 1, 9, 3)
    reduce_ready(final_b)
    on_mid(fold, final_b, buf.tail)
    send(buf.tail, buf.tail, k_units + 14, dev_adj, mid)
    reduce_done(final_b)
    inner_grad_combine(wt.f1)
    e1 = gather_open(buf.e3, None, 2)
    for h in range(2):
        reduce_ready_half(step, h)
        norm_back(
            lambda place: buf.h1[place, :], lambda place: reduced(step, place), 1,
            lambda place: buf.dh[place, :], buf.dh, store(buf.e3), 6, (h,),
        )
        gather_part(e1, h)
    reduce_done(step)
    grad_combine(wt.ckv)
    gather_finish(e1)
    reduce_relay(mem_step)

    weight_grad(buf.o1, buf.e3, wt.so)
    grad_send(wt.so)
    matmul_back(buf.e3, wt.so.weight, buf.do)
    attention_back(buf.qkv, 0, buf.qkv, 2, 4, buf.p1, buf.do)
    grad_outward(wt.co)
    grad_combine(wt.so)
    run_if(end, lambda: weight_grad(buf.a1, buf.qkv, wt.qkv))
    grad_send(wt.qkv)
    matmul_back(buf.qkv, wt.qkv.weight, set_b.parts)
    step = reduce_start(set_b)
    on_mid(weight_grad, buf.a1, buf.qkv, wt.qkv)
    column_sums(buf.qkv, 0, 1, 9, 0)
    column_sums(buf.qkv, 2, 1, 9, 1)
    grad_outward(wt.cq)
    reduce_relay(step)
    f1_final(mid)
    grad_combine_far(wt.qkv)

    reduce_ready(mem_step)
    fold(mem_step, buf.mb)
    k_back = slot(n_sec)
    for j in range(1, n_sec):
        to = (s + j) % n_sec
        send(buf.mb.at[:, part(to, mem_cols)], buf.ml.at[j], k_back + j, (to, d))
    grad_outward(wt.ckv)
    grad_outward(wt.so)
    reduce_ready(step)

    def store_stage(place, value):
        buf.ig[place, :] = value

    norm_back(
        hidden, lambda place: reduced(step, place), 0,
        lambda place: buf.dh[place, :], None, store_stage,
    )
    k_in = slot()
    send(buf.ig, io.input_grad, k_in, ((s + n_sec - 1) % n_sec, d))
    buf.sga[z] = buf.sg[...].astype(BF16)
    sums = spread_start(lambda plane: buf.sga.at[plane])
    grad_combine_middle(wt.qkv)
    f2_near(1)
    for weight in (wt.qkv, wt.cq, wt.co, wt.so):
        grad_send_near(weight)
    f2_final(end)
    f1_final(end)
    for weight in (wt.co, wt.cq):
        grad_final(weight, end)
    grad_outward(wt.qkv)
    grad_final(wt.ckv, end)
    grad_final(wt.so, end)
    grad_final(wt.ckv, mid)
    spread_wait(sums)
    planes = buf.sga[0].astype(F32)
    for plane in range(1, Z):
        planes = planes + buf.sga[plane].astype(F32)
    buf.sgp[q] = planes.astype(BF16)
    spread_plane(sums, buf.sgp)
    grad_final(wt.qkv, mid)

    arrived(buf.tail, k_units + 14, end)
    run_if(end, lambda: finish(lambda place: buf.tail[place, :].astype(F32)))
    for j in range(1, n_sec):
        arrived(buf.ml.at[j], k_back + j)

    def memory_total(i):
        place = part(i, TILE)
        total = buf.mb[place, part(s, mem_cols)].astype(F32)
        for j in range(1, n_sec):
            total = total + buf.ml[j, place, :].astype(F32)
        buf.mo[place, :] = total.astype(BF16)

    loop(L // TILE, memory_total)
    keep(buf.mo, io.memory_grad)
    grad_final(wt.qkv, end)
    for weight in (wt.cq, wt.co, wt.so):
        grad_final(weight, mid)
    f2_final(mid)
    unit_last_wait()
    last_wait(wt.cq)
    last_wait(wt.ckv)
    keep(buf.stage, io.output)
    spread_ready(sums, buf.sgp)

    def per_unit(q_at, at):
        return buf.sgp[q_at, :, at].astype(F32)

    at = part(d // 2, 128)
    feature = per_unit(0, at)
    for q_at in range(1, P_IN):
        feature = feature + per_unit(q_at, at)
    swapped = pltpu.roll(feature, 64, 1)
    buf.sums[...] = jnp.where((jnp.zeros((16, 128), jnp.int32) + c) == 0, feature, swapped)
    head = d % 8
    at = part(2 * (d // 8) + head // 4, 128)
    low_head, high_head = per_unit(2 * c, at), per_unit(2 * c + 1, at)
    first_half = (jnp.zeros((16, 128), jnp.int32) + (head // 2) % 2) == 0
    low_head = jnp.where(first_half, low_head, pltpu.roll(low_head, 64, 1))
    high_head = jnp.where(first_half, pltpu.roll(high_head, 64, 1), high_head)
    buf.sums[9:10, :] = jnp.where(half, low_head, high_head)[9:10]
    at = part(2 * (d // 8) + 4 + head // 4, 128)
    low_head, high_head = per_unit(2 * c, at), per_unit(2 * c + 1, at)
    low_head = jnp.where(first_half, low_head, pltpu.roll(low_head, 64, 1))
    high_head = jnp.where(first_half, pltpu.roll(high_head, 64, 1), high_head)
    buf.sums[10:11, :] = jnp.where(half, low_head, high_head)[9:10]
    buf.sums[11:12, :] = per_unit(q, part(2 * z, 128))[10:11]
    buf.sums[12:13, :] = per_unit(q, part(2 * z + 1, 128))[10:11]
    keep(buf.sums, io.sums_out)
    last_wait(wt.qkv)
    arrived(io.input_grad, k_in)
    for copy, cond in result_copies:
        run_if(cond, copy.wait)
    for record in list(started):
        sent(record)
    assert counter[0] <= SEMS and local_counter[0] <= 64


def buffer_shapes(n_sec, mem_cols):
    tokens, row = (T, D), (L, D)
    shapes = dict(
        sva=(P_IN, Z, 16, 128),
        sga=(Z, 16, D),
        sgp=(P_IN, 16, D),
        hb=row, ig=row, stage=row, mb=row,
        ml=(n_sec, L, mem_cols),
        mo=(L, mem_cols),
        qkv=(T, 768), q2=(T, 256), kv=(T, 512), o1=(T, 256), o2=(T, 256), do=(T, 256),
        p1=(2 * P_IN, 2 * L, L), p2=(2 * P_IN, 2 * L, L),
        g=(T, FL), gp=(T, FL),
        a1=tokens, a2=tokens, a3=tokens, m=tokens, e3=tokens, e2=tokens,
        a3b=tokens, e3b=tokens, gb=(T, FL), gpb=(T, FL), back=row, tail=row,
    )
    exact = dict(vec=(16, D), bias=(8, D), sg=(16, D), sums=(16, 128), h1=row, h2=row, dh=row)
    kinds = {name: pltpu.VMEM(shape, BF16) for name, shape in shapes.items()}
    kinds.update({name: pltpu.VMEM(shape, F32) for name, shape in exact.items()})
    return kinds


REDUCE_SHAPES = dict(
    parts=pltpu.VMEM((T, D), BF16),
    core=pltpu.VMEM((2 * L, D), BF16),
    across=pltpu.VMEM((L, D), BF16),
)


def scratch_of(n_sec, mem_cols):
    scratch = list(buffer_shapes(n_sec, mem_cols).values())
    scratch += 3 * list(REDUCE_SHAPES.values())
    for count, columns, _ in WEIGHTS.values():
        scratch += 2 * [pltpu.VMEM((Z * count, columns), BF16)]
        scratch += 2 * [pltpu.VMEM((count, columns), BF16)]
    for count, columns, _ in list(WEIGHTS.values())[:5]:
        scratch += 3 * [pltpu.VMEM((count, columns), BF16)]
    for columns in (768, 512, 256):
        scratch.append(pltpu.VMEM((64, P_IN * columns), BF16))
        scratch.append(pltpu.VMEM((P_IN, 64, columns), BF16))
    return scratch + [
        pltpu.SemaphoreType.DMA((SEMS,)),
        pltpu.SemaphoreType.DMA((SEMS,)),
        pltpu.SemaphoreType.DMA((64,)),
    ]


def finish_kernel(*refs):
    moved, low, sums = refs[:3], refs[3:10], refs[10]
    moved_out, high, small = refs[11:14], refs[14:21], refs[21:27]
    low_buf, high_buf, moved_buf = refs[27:34], refs[34:41], refs[41:44]
    small_buf, sems = refs[44:50], refs[50]
    inward = [
        pltpu.make_async_copy(src, dst, sems.at[i])
        for i, (src, dst) in enumerate(zip(low + moved, low_buf + moved_buf))
    ]
    for copy in inward:
        copy.start()
    outward = []
    gain, shift, out_bias, self_bias, cross_bias, unit_bias = small_buf
    for row in range(3):
        gain[row] = sums[row:row + 1, 0:64]
        shift[row] = sums[row + 3:row + 4, 0:64]
        out_bias[row] = sums[row + 6:row + 7, 0:64]
    self_bias[...] = sums[9:10, :]
    cross_bias[...] = sums[10:11, :]
    unit_bias[:, 0:128] = sums[11:12, :]
    unit_bias[:, 128:256] = sums[12:13, :]
    for i, (src, dst) in enumerate(zip(small_buf, small)):
        back = pltpu.make_async_copy(src, dst, sems.at[20 + i])
        back.start()
        outward.append(back)
    for i, copy in enumerate(inward[:7]):
        copy.wait()
        rows_in = low_buf[i].shape[0]

        def one(j, i=i):
            place = part(j, 16)
            high_buf[i][place, :] = low_buf[i][place, :].astype(F32)

        loop(rows_in // 16, one)
        back = pltpu.make_async_copy(high_buf[i], high[i], sems.at[10 + i])
        back.start()
        outward.append(back)
    for i, copy in enumerate(inward[7:]):
        copy.wait()
        back = pltpu.make_async_copy(moved_buf[i], moved_out[i], sems.at[17 + i])
        back.start()
        outward.append(back)
    for copy in outward:
        copy.wait()


def on_device_planes(
    prev_act, memory, out_cot, tgt_len, src_len, norm_gain, norm_bias, self_qkv, self_qv_bias,
    self_out, cross_q, cross_kv, cross_qv_bias, cross_out, out_bias, fc1, fc1_bias, fc2,
):
    n_sec = lax.axis_size("section")
    mem_cols = memory.shape[2]
    operands = (
        prev_act[0, 0], memory[0], out_cot[0, 0], tgt_len, src_len,
        norm_gain[0], norm_bias[0], out_bias[0], self_qv_bias, cross_qv_bias, fc1_bias,
        self_qkv[0], self_out[0], cross_kv[0], cross_q[0], cross_out[0], fc1[0], fc2[0],
    )
    anywhere = pl.BlockSpec(memory_space=pl.ANY)
    in_specs = 3 * [anywhere] + 2 * [pl.BlockSpec(memory_space=pltpu.SMEM)]
    in_specs += 6 * [pl.BlockSpec(memory_space=pltpu.VMEM)] + 7 * [anywhere]
    out_shapes = [(L, D), (L, D), (L, mem_cols)]
    for count, columns, by_column in WEIGHTS.values():
        out_shapes.append((count // P_IN, P_IN * columns) if by_column else (count, columns))
    sums_shape = jax.ShapeDtypeStruct((16, 128), F32)
    results = pl.pallas_call(
        functools.partial(whole_kernel, n_sec, mem_cols),
        out_shape=[jax.ShapeDtypeStruct(shape, BF16) for shape in out_shapes] + [sums_shape],
        in_specs=in_specs,
        out_specs=[anywhere] * (len(out_shapes) + 1),
        scratch_shapes=scratch_of(n_sec, mem_cols),
        compiler_params=pltpu.CompilerParams(
            collective_id=0, has_side_effects=True, vmem_limit_bytes=64 * 2**20 - 2**16
        ),
        cost_estimate=pl.CostEstimate(
            flops=21 * 10**9, bytes_accessed=20 * 2**20, transcendentals=3 * 10**6
        ),
    )(*operands)
    shapes = [result.shape for result in results]
    small_shapes = [(3, 1, 64)] * 3 + [(1, 128), (1, 128), (1, 256)]
    vmem = pl.BlockSpec(memory_space=pltpu.VMEM)
    finished = pl.pallas_call(
        finish_kernel,
        out_shape=[jax.ShapeDtypeStruct(shape, BF16) for shape in shapes[:3]]
        + [jax.ShapeDtypeStruct(shape, F32) for shape in shapes[3:10]]
        + [jax.ShapeDtypeStruct(shape, F32) for shape in small_shapes],
        in_specs=10 * [anywhere] + [vmem],
        out_specs=16 * [anywhere],
        scratch_shapes=[pltpu.VMEM(shape, BF16) for shape in shapes[3:10]]
        + [pltpu.VMEM(shape, F32) for shape in shapes[3:10]]
        + [pltpu.VMEM(shape, BF16) for shape in shapes[:3]]
        + [pltpu.VMEM(shape, F32) for shape in small_shapes]
        + [pltpu.SemaphoreType.DMA((26,))],
        compiler_params=pltpu.CompilerParams(vmem_limit_bytes=63 * 2**20),
        cost_estimate=pl.CostEstimate(flops=0, bytes_accessed=9 * 2**20, transcendentals=0),
    )(*results)
    (
        output, input_grad, memory_grad, g_qkv, g_so, g_ckv, g_cq, g_co, g_f1, g_f2,
        gain, shift, biases, self_biases, cross_biases, units,
    ) = finished
    return (
        output[None, None],
        input_grad[None, None],
        memory_grad[None],
        gain.transpose(1, 0, 2),
        shift.transpose(1, 0, 2),
        g_qkv[None],
        self_biases,
        g_so[None],
        g_cq[None],
        g_ckv[None],
        cross_biases,
        g_co[None],
        biases.transpose(1, 0, 2),
        g_f1[None],
        units,
        g_f2[None],
    )


def solution(mesh):
    in_specs = (
        P("section", "dp", None, None),
        P("dp", None, "section"),
        P("section", "dp", None, None),
        P("dp"),
        P("dp"),
        P("section", None, "dp"),
        P("section", None, "dp"),
        P("section", "dp", None),
        P("section", "dp"),
        P("section", "dp", None),
        P("section", "dp", None),
        P("section", "dp", None),
        P("section", "dp"),
        P("section", "dp", None),
        P("section", None, "dp"),
        P("section", "dp", None),
        P("section", "dp"),
        P("section", "dp", None),
    )
    out_specs = (
        P("section", "dp", None, None),
        P("section", "dp", None, None),
        P("dp", None, "section"),
        P("section", None, "dp"),
        P("section", None, "dp"),
        P("section", "dp", None),
        P("section", "dp"),
        P("section", "dp", None),
        P("section", "dp", None),
        P("section", "dp", None),
        P("section", "dp"),
        P("section", "dp", None),
        P("section", None, "dp"),
        P("section", "dp", None),
        P("section", "dp"),
        P("section", "dp", None),
    )
    planes = Z * P_IN
    fits = mesh.shape["dp"] == planes
    return jax.shard_map(
        on_device_planes if fits else on_device, mesh=mesh, in_specs=in_specs, out_specs=out_specs, check_vma=False
    )
```

```python
import functools
from types import SimpleNamespace

import jax
import jax.numpy as jnp
from jax import lax
from jax.experimental import pallas as pl
from jax.experimental.pallas import tpu as pltpu
from jax.sharding import PartitionSpec as P

H = 16
HD = 64


EPSILON = 1e-05
MASKED = -1000000000.0


def passed_along(value, axis, by):
    length = lax.axis_size(axis)
    return lax.ppermute(value, axis, [(i, (i + by) % length) for i in range(length)])


def norm_fwd(rows, gain, shift_term):
    center = rows - jnp.mean(rows, -1, keepdims=True)
    scale = lax.rsqrt(jnp.mean(center * center, -1, keepdims=True) + EPSILON)
    return center * scale * gain + shift_term


def gelu_exact(values):
    return jax.nn.gelu(values, approximate=False)


def product(left, right):
    return jnp.dot(left, right, preferred_element_type=jnp.float32)


def product_right_t(left, right):
    return lax.dot_general(
        left, right, (((1,), (1,)), ((), ())), preferred_element_type=jnp.float32
    )


def product_left_t(left, right):
    return lax.dot_general(
        left, right, (((0,), (0,)), ((), ())), preferred_element_type=jnp.float32
    )


def split_heads(flat, batch_rows):
    return flat.reshape(batch_rows, -1, H, HD)


def softmax_probs(query, key_rows, allowed):
    scores = jnp.einsum(
        "rthd,rshd->rhts", query, key_rows, preferred_element_type=jnp.float32
    ) * HD ** (-0.5)
    scores = jnp.where(allowed[:, None], scores, MASKED)
    weights = jnp.exp(scores - jnp.max(scores, -1, keepdims=True))
    return weights / jnp.sum(weights, -1, keepdims=True)


def attend_fwd(query, key_rows, value_rows, allowed):
    probs = softmax_probs(query, key_rows, allowed)
    mixed = jnp.einsum(
        "rhts,rshd->rthd",
        probs.astype(jnp.bfloat16),
        value_rows,
        preferred_element_type=jnp.float32,
    )
    return mixed.reshape(mixed.shape[0] * mixed.shape[1], -1).astype(jnp.bfloat16)


def attend_back(query, key_rows, value_rows, allowed, grad_mixed):
    probs = softmax_probs(query, key_rows, allowed)
    grad_heads = grad_mixed.reshape(query.shape)
    grad_probs = jnp.einsum(
        "rthd,rshd->rhts", grad_heads, value_rows, preferred_element_type=jnp.float32
    )
    delta = jnp.sum(probs * grad_probs, -1, keepdims=True)
    grad_scores = (probs * (grad_probs - delta)).astype(jnp.bfloat16)
    scale = HD ** (-0.5)
    grad_query = (
        jnp.einsum("rhts,rshd->rthd", grad_scores, key_rows, preferred_element_type=jnp.float32)
        * scale
    )
    grad_keys = (
        jnp.einsum("rhts,rthd->rshd", grad_scores, query, preferred_element_type=jnp.float32)
        * scale
    )
    grad_values = jnp.einsum(
        "rhts,rthd->rshd",
        probs.astype(jnp.bfloat16),
        grad_heads,
        preferred_element_type=jnp.float32,
    )
    width = query.shape[2] * query.shape[3]
    return (
        grad_query.reshape(-1, width).astype(jnp.bfloat16),
        grad_keys.reshape(-1, width).astype(jnp.bfloat16),
        grad_values.reshape(-1, width).astype(jnp.bfloat16),
    )


def unpack(pieces):
    return tuple((piece[0] for piece in pieces))


def on_device(
    prev_act,
    memory,
    out_cot,
    tgt_len,
    src_len,
    norm_gain,
    norm_bias,
    self_qkv,
    self_qv_bias,
    self_out,
    cross_q,
    cross_kv,
    cross_qv_bias,
    cross_out,
    out_bias,
    fc1,
    fc1_bias,
    fc2,
):
    fetched = unpack(
        (
            lax.all_gather(norm_gain, "dp", axis=2, tiled=True),
            lax.all_gather(norm_bias, "dp", axis=2, tiled=True),
            lax.all_gather(self_qkv, "dp", axis=1, tiled=True),
            lax.all_gather(self_qv_bias, "dp", axis=1, tiled=True),
            lax.all_gather(self_out, "dp", axis=1, tiled=True),
            lax.all_gather(cross_q, "dp", axis=1, tiled=True),
            lax.all_gather(cross_kv, "dp", axis=1, tiled=True),
            lax.all_gather(cross_qv_bias, "dp", axis=1, tiled=True),
            lax.all_gather(cross_out, "dp", axis=1, tiled=True),
            lax.all_gather(out_bias, "dp", axis=2, tiled=True),
            lax.all_gather(fc1, "dp", axis=1, tiled=True),
            lax.all_gather(fc1_bias, "dp", axis=1, tiled=True),
            lax.all_gather(fc2, "dp", axis=1, tiled=True),
        )
    )
    gains, shifts, w_sqkv, b_sqv, w_sout, w_cq, w_ckv, b_cqv, w_cout, b_out, w_one, b_one, w_two = (
        fetched
    )
    gain_f = gains.astype(jnp.float32)
    shift_f = shifts.astype(jnp.float32)
    sqv_f = b_sqv.astype(jnp.float32)
    cqv_f = b_cqv.astype(jnp.float32)
    out_f = b_out.astype(jnp.float32)
    one_f = b_one.astype(jnp.float32)
    source = passed_along(prev_act, "section", 1)[0]
    batch_rows, length, width = source.shape
    encoded = lax.all_gather(memory, "section", axis=2, tiled=True)
    mem_flat = encoded.reshape(-1, width)
    places = jnp.arange(length)
    self_ok = (places[None, None, :] <= places[None, :, None]) & (
        places[None, None, :] < tgt_len[:, None, None]
    )
    cross_ok = jnp.arange(encoded.shape[1])[None, None, :] < src_len[:, None, None]
    resid = source.astype(jnp.float32).reshape(-1, width)
    normed_one, pull_one = jax.vjp(norm_fwd, resid, gain_f[0], shift_f[0])
    first_in = normed_one.astype(jnp.bfloat16)
    joint = product(first_in, w_sqkv)
    query_self = (joint[:, :width] + sqv_f[:width]).astype(jnp.bfloat16)
    keys_self = joint[:, width : 2 * width].astype(jnp.bfloat16)
    values_self = (joint[:, 2 * width :] + sqv_f[width:]).astype(jnp.bfloat16)
    self_mixed = attend_fwd(
        split_heads(query_self, batch_rows),
        split_heads(keys_self, batch_rows),
        split_heads(values_self, batch_rows),
        self_ok,
    )
    after_self = resid + (product(self_mixed, w_sout) + out_f[0])
    normed_two, pull_two = jax.vjp(norm_fwd, after_self, gain_f[1], shift_f[1])
    second_in = normed_two.astype(jnp.bfloat16)
    query_cross = (product(second_in, w_cq) + cqv_f[:width]).astype(jnp.bfloat16)
    memory_proj = product(mem_flat, w_ckv)
    keys_cross = memory_proj[:, :width].astype(jnp.bfloat16)
    values_cross = (memory_proj[:, width:] + cqv_f[width:]).astype(jnp.bfloat16)
    cross_mixed = attend_fwd(
        split_heads(query_cross, batch_rows),
        split_heads(keys_cross, batch_rows),
        split_heads(values_cross, batch_rows),
        cross_ok,
    )
    after_cross = after_self + (product(cross_mixed, w_cout) + out_f[1])
    normed_three, pull_three = jax.vjp(norm_fwd, after_cross, gain_f[2], shift_f[2])
    third_in = normed_three.astype(jnp.bfloat16)
    pre_act = product(third_in, w_one) + one_f
    activ, pull_gelu = jax.vjp(gelu_exact, pre_act)
    act_low = activ.astype(jnp.bfloat16)
    result = after_cross + (product(act_low, w_two) + out_f[2])
    output = result.astype(jnp.bfloat16).reshape(1, batch_rows, length, width)
    (
        unused_gains,
        unused_shifts,
        w_sqkv,
        unused_sqv,
        w_sout,
        w_cq,
        w_ckv,
        unused_cqv,
        w_cout,
        unused_out,
        w_one,
        unused_one,
        w_two,
    ) = fetched
    grad_out = passed_along(out_cot, "section", -1)[0].astype(jnp.float32).reshape(-1, width)
    ffn_grad = grad_out.astype(jnp.bfloat16)
    grad_fc2 = product_left_t(act_low, ffn_grad)
    grad_b2 = jnp.sum(ffn_grad, 0, dtype=jnp.float32)
    grad_act = product_right_t(ffn_grad, w_two)
    (grad_pre,) = pull_gelu(grad_act)
    pre_low = grad_pre.astype(jnp.bfloat16)
    grad_fc1 = product_left_t(third_in, pre_low)
    grad_b1 = jnp.sum(pre_low, 0, dtype=jnp.float32)
    grad_mid, grad_gain3, grad_shift3 = pull_three(product_right_t(pre_low, w_one))
    grad_mid = grad_mid + grad_out
    cross_grad = grad_mid.astype(jnp.bfloat16)
    grad_cout = product_left_t(cross_mixed, cross_grad)
    grad_bco = jnp.sum(cross_grad, 0, dtype=jnp.float32)
    grad_cmix = product_right_t(cross_grad, w_cout).astype(jnp.bfloat16)
    grad_qc, grad_kc, grad_vc = attend_back(
        split_heads(query_cross, batch_rows),
        split_heads(keys_cross, batch_rows),
        split_heads(values_cross, batch_rows),
        cross_ok,
        grad_cmix,
    )
    grad_cq = product_left_t(second_in, grad_qc)
    grad_kv = jnp.concatenate([grad_kc, grad_vc], -1)
    grad_ckv = product_left_t(mem_flat, grad_kv)
    grad_cqv = jnp.concatenate(
        [jnp.sum(grad_qc, 0, dtype=jnp.float32), jnp.sum(grad_vc, 0, dtype=jnp.float32)]
    )
    grad_memory = product_right_t(grad_kv, w_ckv).reshape(encoded.shape)
    memory_grad = lax.psum_scatter(
        grad_memory.astype(jnp.bfloat16), "section", scatter_dimension=2, tiled=True
    )
    grad_after, grad_gain2, grad_shift2 = pull_two(product_right_t(grad_qc, w_cq))
    grad_after = grad_after + grad_mid
    self_grad = grad_after.astype(jnp.bfloat16)
    grad_sout = product_left_t(self_mixed, self_grad)
    grad_bso = jnp.sum(self_grad, 0, dtype=jnp.float32)
    grad_smix = product_right_t(self_grad, w_sout).astype(jnp.bfloat16)
    grad_qs, grad_ks, grad_vs = attend_back(
        split_heads(query_self, batch_rows),
        split_heads(keys_self, batch_rows),
        split_heads(values_self, batch_rows),
        self_ok,
        grad_smix,
    )
    grad_qkv = jnp.concatenate([grad_qs, grad_ks, grad_vs], -1)
    grad_sqkv = product_left_t(first_in, grad_qkv)
    grad_sqv = jnp.concatenate(
        [jnp.sum(grad_qs, 0, dtype=jnp.float32), jnp.sum(grad_vs, 0, dtype=jnp.float32)]
    )
    grad_in, grad_gain1, grad_shift1 = pull_one(product_right_t(grad_qkv, w_sqkv))
    grad_in = grad_in + grad_after
    input_grad = passed_along(
        grad_in.astype(jnp.bfloat16).reshape(1, batch_rows, length, width), "section", -1
    )
    grad_gain = jnp.stack([grad_gain1, grad_gain2, grad_gain3])
    grad_shift = jnp.stack([grad_shift1, grad_shift2, grad_shift3])
    grad_obias = jnp.stack([grad_bso, grad_bco, grad_b2])
    sums = (
        lax.psum_scatter(
            grad_gain.astype(jnp.bfloat16), "dp", scatter_dimension=1, tiled=True
        ).astype(jnp.float32),
        lax.psum_scatter(
            grad_shift.astype(jnp.bfloat16), "dp", scatter_dimension=1, tiled=True
        ).astype(jnp.float32),
        lax.psum_scatter(
            grad_sqkv.astype(jnp.bfloat16), "dp", scatter_dimension=0, tiled=True
        ).astype(jnp.float32),
        lax.psum_scatter(
            grad_sqv.astype(jnp.bfloat16), "dp", scatter_dimension=0, tiled=True
        ).astype(jnp.float32),
        lax.psum_scatter(
            grad_sout.astype(jnp.bfloat16), "dp", scatter_dimension=0, tiled=True
        ).astype(jnp.float32),
        lax.psum_scatter(
            grad_cq.astype(jnp.bfloat16), "dp", scatter_dimension=0, tiled=True
        ).astype(jnp.float32),
        lax.psum_scatter(
            grad_ckv.astype(jnp.bfloat16), "dp", scatter_dimension=0, tiled=True
        ).astype(jnp.float32),
        lax.psum_scatter(
            grad_cqv.astype(jnp.bfloat16), "dp", scatter_dimension=0, tiled=True
        ).astype(jnp.float32),
        lax.psum_scatter(
            grad_cout.astype(jnp.bfloat16), "dp", scatter_dimension=0, tiled=True
        ).astype(jnp.float32),
        lax.psum_scatter(
            grad_obias.astype(jnp.bfloat16), "dp", scatter_dimension=1, tiled=True
        ).astype(jnp.float32),
        lax.psum_scatter(
            grad_fc1.astype(jnp.bfloat16), "dp", scatter_dimension=0, tiled=True
        ).astype(jnp.float32),
        lax.psum_scatter(
            grad_b1.astype(jnp.bfloat16), "dp", scatter_dimension=0, tiled=True
        ).astype(jnp.float32),
        lax.psum_scatter(
            grad_fc2.astype(jnp.bfloat16), "dp", scatter_dimension=0, tiled=True
        ).astype(jnp.float32),
    )
    return (
        output,
        input_grad,
        memory_grad,
        sums[0][None],
        sums[1][None],
        sums[2][None],
        sums[3][None],
        sums[4][None],
        sums[5][None],
        sums[6][None],
        sums[7][None],
        sums[8][None],
        sums[9][None],
        sums[10][None],
        sums[11][None],
        sums[12][None],
    )


Z = 4
P_IN = 4
L = 192
D = 1024
T = P_IN * L
FL = 1024
TILE = 32
MESH = pl.DeviceIdType.MESH
F32 = jnp.float32
BF16 = jnp.bfloat16

WEIGHTS = dict(
    qkv=(256, 768, True),
    so=(64, 1024, False),
    ckv=(256, 512, True),
    cq=(256, 256, True),
    co=(64, 1024, False),
    f1=(256, 1024, True),
    f2=(256, 1024, False),
)
SEMS = 320


def run_if(cond, fn):
    if cond is None:
        fn()
    else:
        pl.when(cond)(fn)


def part(index, size, step=None):
    return pl.ds(pl.multiple_of(index * size, size), size if step is None else step)


def nn(left, right):
    return jnp.dot(left, right, preferred_element_type=F32)


def nt(left, right):
    return lax.dot_general(left, right, (((1,), (1,)), ((), ())), preferred_element_type=F32)


def tn(left, right):
    return lax.dot_general(left, right, (((0,), (0,)), ((), ())), preferred_element_type=F32)


def loop(count, body, unroll=1, first=0):
    def step(index, carry):
        body(index)
        return carry

    lax.fori_loop(first, first + count, step, 0, unroll=unroll)


HALF = L // 2
TILES = HALF // TILE


def gelu_pair(values):
    bell = jnp.exp(-0.5 * values * values)
    step = 1.0 / (1.0 + 0.3275911 * 0.7071067811865476 * jnp.abs(values))
    series = step * (
        0.254829592
        + step
        * (-0.284496736 + step * (1.421413741 + step * (-1.453152027 + step * 1.061405429)))
    )
    above = 0.5 * series * bell
    below = jnp.where(values < 0, above, 1.0 - above)
    return values * below, below + values * bell * 0.3989422804014327


def whiten(rows):
    center = rows - jnp.mean(rows, -1, keepdims=True)
    scale = lax.rsqrt(jnp.mean(center * center, -1, keepdims=True) + EPSILON)
    return center * scale, scale


def whole_kernel(n_sec, mem_cols, *refs):
    given = iter(refs)

    def take(names):
        return SimpleNamespace(**{name: next(given) for name in names})

    def take_weights(**fields):
        for name in WEIGHTS:
            for field in fields:
                setattr(getattr(wt, name), field, next(given))

    wt = SimpleNamespace(**{name: SimpleNamespace() for name in WEIGHTS})
    io = take(
        dict(
            prev=0, mem=0, cot=0, tgt=0, src=0, gain=0, shift=0, out_bias=0,
            self_bias=0, cross_bias=0, unit_bias=0,
        )
    )
    take_weights(source=0)
    vars(io).update(vars(take(dict(output=0, input_grad=0, memory_grad=0))))
    take_weights(result=0)
    vars(io).update(vars(take(dict(sums_out=0))))
    buf = take(buffer_shapes(n_sec, mem_cols))
    set_a, set_b, set_c = (take(REDUCE_SHAPES) for _ in range(3))
    take_weights(weight=0, grad=0, near=0, far=0)
    for weight in (wt.qkv, wt.so, wt.ckv, wt.cq, wt.co):
        weight.to_diag, weight.to_opp, weight.through = next(given), next(given), next(given)
    for weight in (wt.qkv, wt.ckv, wt.cq):
        weight.raw, weight.sorted = next(given), next(given)
    send_sems, recv_sems, local_sems = given

    s = lax.axis_index("section")
    d = lax.axis_index("dp")
    z, q = d // P_IN, d % P_IN
    x, c = q // 2, q % 2
    end = (z % 3) == 0
    mid = (z % 3) != 0
    q_core = q + 1 - 2 * c
    q_x = q + 2 - 4 * x
    q_xc = q_x + 1 - 2 * c
    z_adj = z + 1 - 2 * (z % 2)
    z_opp = 3 - z
    z_diag = (z + 2) % 4
    dev_core, dev_x, dev_xc = (s, z * P_IN + q_core), (s, z * P_IN + q_x), (s, z * P_IN + q_xc)
    dev_adj, dev_opp, dev_diag = (s, z_adj * P_IN + q), (s, z_opp * P_IN + q), (s, z_diag * P_IN + q)
    in_plane = ((q_core, dev_core), (q_x, dev_x), (q_xc, dev_xc))

    counter = [0]
    started = []
    local_counter = [0]

    def slot(count=1):
        counter[0] += count
        return counter[0] - count

    def remote(src, dst, k, device):
        return pltpu.make_async_remote_copy(
            src_ref=src, dst_ref=dst, send_sem=send_sems.at[k], recv_sem=recv_sems.at[k],
            device_id=device, device_id_type=MESH,
        )

    def send(src, dst, k, device, cond=None):
        copy = remote(src, dst, k, device)
        run_if(cond, copy.start)
        record = [copy, cond]
        started.append(record)
        return record

    def sent(record):
        run_if(record[1], record[0].wait_send)
        started[:] = [other for other in started if other is not record]

    def arrived(dst, k, cond=None):
        run_if(cond, remote(dst, dst, k, dev_core).wait_recv)

    def local(src, dst, cond=None):
        copy = pltpu.make_async_copy(src, dst, local_sems.at[local_counter[0]])
        local_counter[0] += 1
        run_if(cond, copy.start)
        return copy

    def keep(src, dst, cond=None):
        result_copies.append((local(src, dst, cond), cond))

    def rows(rows_of, index):
        return rows_of.at[part(index, L)]

    for name, (count, _, by_column) in WEIGHTS.items():
        weight = getattr(wt, name)
        weight.count, weight.by_column = count, by_column
        weight.pieces, weight.piece, weight.last_copies = 1, 0, []
        weight.to_use, weight.swap, weight.to_sum, weight.last = slot(5), slot(3), slot(6), slot(3)

    def block(name, index):
        return name.weight.at[part(index * name.pieces + name.piece, name.count)]

    first_weights = [
        SimpleNamespace(
            weight=wt.qkv.weight, count=wt.qkv.count // 2, pieces=2, piece=h, to_use=slot(5)
        )
        for h in range(2)
    ]

    def send_inward(name, src):
        send(src, block(name, z), name.to_use, dev_adj, end)

    def send_across(name, src):
        send(src, block(name, z), name.to_use + 1, dev_opp, mid)

    def weight_outward(name, src):
        send(src, block(name, z), name.to_use, dev_adj, mid)

    def relay_inward(name):
        k = name.to_use
        arrived(block(name, z_adj), k, mid)
        send(block(name, z_adj), block(name, z_adj), k + 2, dev_opp, mid)

    def relay_near(name):
        k = name.to_use
        arrived(block(name, z_opp), k + 1, mid)
        send(block(name, z_opp), block(name, z_opp), k + 3, dev_adj, mid)

    def relay_far(name):
        k = name.to_use
        arrived(block(name, z_diag), k + 2, mid)
        send(block(name, z_diag), block(name, z_diag), k + 4, dev_adj, mid)

    def weight_ready(name):
        k = name.to_use
        arrived(block(name, z_adj), k, end)
        arrived(block(name, z_diag), k + 3, end)
        arrived(block(name, z_opp), k + 4, end)

    def inner_ready(name):
        k = name.to_use
        arrived(block(name, z_opp), k + 1, mid)
        arrived(block(name, z_diag), k + 2, mid)


    def swap_start(name):
        size = name.count // P_IN
        place = name.weight.at[part(z * P_IN + q, size)]
        name.swapped = [
            send(name.sorted.at[q_to], place, name.swap + j, device)
            for j, (q_to, device) in enumerate(in_plane)
        ]
        name.own_copy = [local(name.sorted.at[q], place)]

    def swap_wait(name):
        size = name.count // P_IN
        for j, (q_from, _) in enumerate(in_plane):
            arrived(name.weight.at[part(z * P_IN + q_from, size)], name.swap + j)
        for copy in name.own_copy:
            copy.wait()
        for record in name.swapped:
            sent(record)

    def halves(first, second, odd):
        if odd:
            first = pltpu.roll(first, 64, 1)
        else:
            second = pltpu.roll(second, 64, 1)
        lane = lax.broadcasted_iota(jnp.int32, first.shape, 1)
        return jnp.where(lane < 64, first, second)

    def tile_of(index):
        return slice(index * 128, index * 128 + 128)

    def sort_columns(name):
        for q_to in range(P_IN):
            for tile in range(name.sorted.shape[2] // 128):
                at = 4 * tile + q_to // 2
                first = name.raw[:, tile_of(at)].astype(F32)
                second = name.raw[:, tile_of(at + 2)].astype(F32)
                name.sorted[q_to, :, tile_of(tile)] = halves(first, second, q_to % 2).astype(BF16)

    def unsort_columns(name):
        for tile in range(name.raw.shape[1] // 128):
            group, u = tile // 8, tile % 8
            at = 2 * group + u // 4
            first = name.sorted[2 * (u % 2), :, tile_of(at)].astype(F32)
            second = name.sorted[2 * (u % 2) + 1, :, tile_of(at)].astype(F32)
            name.raw[:, tile_of(tile)] = halves(first, second, (u // 2) % 2).astype(BF16)

    unit_swap, unit_last = slot(3 * Z), slot(3 * Z)

    def unit_columns(rows_of, tile, q_at):
        return rows_of.at[:, part(tile * P_IN + q_at, 256)]

    def unit_swap_start():
        size = wt.f1.count // P_IN
        place = wt.f1.weight.at[part(z * P_IN + q, size)]
        wt.f1.own_copy = []
        for tile in range(Z):
            at = place.at[:, part(tile, 256)]
            for j, (q_to, device) in enumerate(in_plane):
                send(unit_columns(wt.f1.source, tile, q_to), at, unit_swap + 3 * tile + j, device)
            wt.f1.own_copy.append(local(unit_columns(wt.f1.source, tile, q), at))

    def unit_swap_wait(cond):
        size = wt.f1.count // P_IN
        for tile in range(Z):
            for j, (q_from, _) in enumerate(in_plane):
                place = wt.f1.weight.at[part(z * P_IN + q_from, size)]
                arrived(place.at[:, part(tile, 256)], unit_swap + 3 * tile + j, cond)
        for copy in wt.f1.own_copy:
            run_if(cond, copy.wait)

    def grad_block(name, index):
        return name.grad.at[part(index, name.count)]

    def grad_send_far(name):
        return send(grad_block(name, z_opp), name.to_diag, name.to_sum, dev_adj, end)

    def grad_send_middle(name):
        return send(grad_block(name, z_diag), name.to_opp, name.to_sum + 1, dev_adj, end)

    def grad_send_near(name):
        return send(grad_block(name, z_adj), name.near, name.to_sum + 2, dev_adj, end)

    def grad_send(name):
        grad_send_far(name)
        grad_send_middle(name)

    def add_rows(count, body):
        size = min(count, 64)
        loop(count // size, lambda i: body(part(i, size)))

    def grad_add(name, landed, index):
        def one(place):
            own = grad_block(name, index)[place, :].astype(F32)
            landed[place, :] = (own + landed[place, :].astype(F32)).astype(BF16)

        add_rows(name.count, one)

    def grad_combine_far(name):
        k = name.to_sum
        arrived(name.to_diag, k, mid)
        run_if(mid, lambda: grad_add(name, name.to_diag, z_diag))
        send(name.to_diag, name.through, k + 3, dev_opp, mid)

    def grad_combine_middle(name):
        k = name.to_sum
        arrived(name.to_opp, k + 1, mid)
        run_if(mid, lambda: grad_add(name, name.to_opp, z_opp))
        send(name.to_opp, name.far, k + 4, dev_opp, mid)

    def grad_combine(name):
        grad_combine_far(name)
        grad_combine_middle(name)

    def grad_outward(name):
        k = name.to_sum
        arrived(name.through, k + 3, mid)
        run_if(mid, lambda: grad_add(name, name.through, z_adj))
        send(name.through, name.near, k + 5, dev_adj, mid)

    result_copies = []

    def inner_grad_far(name):
        send(grad_block(name, z_diag), name.far, name.to_sum, dev_opp, mid)

    def inner_grad_near(name):
        send(grad_block(name, z_opp), name.near, name.to_sum + 1, dev_opp, mid)

    def f2_half(rows_of, h):
        return rows_of.at[part(h, wt.f2.count // 2)]

    def f2_near(h):
        src = f2_half(grad_block(wt.f2, z_opp), h)
        send(src, f2_half(wt.f2.near, h), wt.f2.to_sum + 1 + 2 * h, dev_opp, mid)

    def inner_grad_combine(name):
        k = name.to_sum

        def add():
            arrived(name.far, k)

            def one(place):
                own = grad_block(name, z_adj)[place, :].astype(F32)
                name.far[place, :] = (own + name.far[place, :].astype(F32)).astype(BF16)

            add_rows(name.count, one)

        run_if(mid, add)
        send(name.far, name.near, k + 2, dev_adj, mid)

    def grad_total(name, cond):
        k = name.to_sum
        arrived(name.near, k + (5 if cond is end else 2), cond)
        if cond is mid:
            arrived(name.far, k + 4, mid)

        def add():
            def one(place):
                total = name.near[place, :].astype(F32)
                if cond is mid:
                    total = total + name.far[place, :].astype(F32)
                name.near[place, :] = (total + grad_block(name, z)[place, :].astype(F32)).astype(BF16)

            add_rows(name.count, one)

        run_if(cond, add)

    def grad_final(name, cond):
        grad_total(name, cond)
        if name.by_column:
            size = name.count // P_IN
            for j, (q_to, device) in enumerate(in_plane):
                src = name.near.at[part(q_to, size)]
                send(src, name.sorted.at[q], name.last + j, device, cond)
            src = name.near.at[part(q, size)]
            name.last_copies.append((local(src, name.sorted.at[q], cond), cond))
        else:
            keep(name.near, name.result, cond)

    def f2_final(cond):
        if cond is end:
            arrived(wt.f2.near, wt.f2.to_sum + 2, end)
        else:
            for h in range(2):
                arrived(f2_half(wt.f2.near, h), wt.f2.to_sum + 1 + 2 * h, mid)
            run_if(mid, lambda: grad_add(wt.f2, wt.f2.near, z))
        keep(wt.f2.near, wt.f2.result, cond)

    def f1_final(cond):
        if cond is end:
            arrived(wt.f1.near, wt.f1.to_sum + 2, end)
        else:
            arrived(wt.f1.near, wt.f1.to_sum + 1, mid)
            run_if(mid, lambda: grad_add(wt.f1, wt.f1.near, z))
        size = wt.f1.count // P_IN
        for tile in range(Z):
            dst = unit_columns(wt.f1.result, tile, q)
            for j, (q_to, device) in enumerate(in_plane):
                src = wt.f1.near.at[part(q_to, size), part(tile, 256)]
                send(src, dst, unit_last + 3 * tile + j, device, cond)
            keep(wt.f1.near.at[part(q, size), part(tile, 256)], dst, cond)

    def last_wait(name):
        for j, (q_from, _) in enumerate(in_plane):
            arrived(name.sorted.at[q_from], name.last + j)
        for copy, cond in name.last_copies:
            run_if(cond, copy.wait)
        unsort_columns(name)
        keep(name.raw, name.result)

    def unit_last_wait():
        for tile in range(Z):
            for j, (q_from, _) in enumerate(in_plane):
                place = unit_columns(wt.f1.result, tile, q_from)
                arrived(place, unit_last + 3 * tile + j)

    def piece(name, index, h, parts):
        size = L // parts
        return name.at[part(index * parts + h, size)]

    def half_major(name, index, h, parts=2):
        return name.at[part(h * P_IN + index, HALF)]

    def gather_open(name, cond=None, parts=1, lay=piece):
        return name, slot(3 * parts), [], cond, parts, lay

    def gather_part(ticket, h, cond=None):
        name, k, records, usual, parts, lay = ticket
        cond = usual if cond is None else cond
        own = lay(name, q, h, parts)
        records.append(send(own, own, k + 3 * h, dev_x, cond))
        records.append(send(own, own, k + 3 * h + 1, dev_core, cond))

    def gather_start(name, cond=None):
        ticket = gather_open(name, cond)
        gather_part(ticket, 0)
        return ticket

    def gather_relay_part(ticket, h):
        name, k, records, cond, parts, lay = ticket
        other = lay(name, q_x, h, parts)
        arrived(other, k + 3 * h, cond)
        records.append(send(other, other, k + 3 * h + 2, dev_core, cond))

    def gather_ready_part(ticket, h):
        name, k, _, cond, parts, lay = ticket
        arrived(lay(name, q_core, h, parts), k + 3 * h + 1, cond)
        arrived(lay(name, q_xc, h, parts), k + 3 * h + 2, cond)

    def gather_relay(ticket):
        for h in range(ticket[4]):
            gather_relay_part(ticket, h)

    def gather_ready(ticket):
        for h in range(ticket[4]):
            gather_ready_part(ticket, h)

    def gather_finish(ticket):
        gather_relay(ticket)
        gather_ready(ticket)

    def reduce_start(which, cond=None):
        k = slot(4)
        out = which.parts
        first = send(rows(out, q_xc), rows(which.core, 1), k, dev_core, cond)
        second = send(rows(out, q_core), rows(which.core, 0), k + 1, dev_core, cond)
        return which, k, [first, second], cond, piece

    def reduce_open(which, cond):
        return which, slot(6), [], cond, half_major

    def reduce_start_half(ticket, h):
        which, k, records, cond, lay = ticket
        for j, index in ((1, q_xc), (0, q_core)):
            src, dst = lay(which.parts, index, h), piece(which.core, j, h, 2)
            records.append(send(src, dst, k + 4 * h + 1 - j, dev_core, cond))

    def reduce_relay_half(ticket, h):
        which, k, records, cond, lay = ticket
        landed = piece(which.core, 1, h, 2)
        if lay is half_major:
            arrived(landed, k + 4 * h, cond)
        elif h == 0:
            arrived(rows(which.core, 1), k, cond)
        mine = lay(which.parts, q_x, h, 2)

        def add():
            def one(i):
                place = part(i, TILE)
                total = mine[place, :].astype(F32) + landed[place, :].astype(F32)
                mine[place, :] = total.astype(BF16)

            loop(TILES, one)

        run_if(cond, add)
        dst = which.across.at[part(h, HALF)]
        records.append(send(mine, dst, k + 2 + h, dev_x, cond))
        return records[-1]

    def reduce_relay(ticket):
        reduce_relay_half(ticket, 0)
        reduce_relay_half(ticket, 1)

    def reduce_ready_half(ticket, h):
        which, k, _, cond, lay = ticket
        if lay is half_major:
            arrived(piece(which.core, 0, h, 2), k + 4 * h + 1, cond)
        elif h == 0:
            arrived(rows(which.core, 0), k + 1, cond)
        arrived(which.across.at[part(h, HALF)], k + 2 + h, cond)

    def reduce_ready(ticket):
        reduce_ready_half(ticket, 0)
        reduce_ready_half(ticket, 1)

    def reduced(ticket, place):
        which = ticket[0]
        total = rows(which.parts, q)[place, :].astype(F32)
        total = total + rows(which.core, 0)[place, :].astype(F32)
        return total + which.across[place, :].astype(F32)

    def fold(ticket, dst, halves=(0, 1)):
        which, lay = ticket[0], ticket[4]
        for h in halves:
            mine, landed = lay(which.parts, q, h, 2), piece(which.core, 0, h, 2)

            def one(i, h=h, mine=mine, landed=landed):
                place, here = part(i, TILE), part(i + h * TILES, TILE)
                total = mine[place, :].astype(F32) + landed[place, :].astype(F32)
                dst[here, :] = (total + which.across[here, :].astype(F32)).astype(BF16)

            loop(TILES, one)

    def reduce_done(ticket):
        for record in ticket[2]:
            sent(record)

    def spread_start(place):
        k = slot(8)
        for j, device in enumerate((dev_diag, dev_opp, dev_adj)):
            send(place(z), place(z), k + j, device)
        return place, k

    def spread_wait(ticket):
        place, k = ticket
        for j, plane in enumerate((z_diag, z_opp, z_adj)):
            arrived(place(plane), k + j)

    def spread_plane(ticket, name):
        k = ticket[1]
        for j, (_, device) in enumerate(in_plane):
            send(name.at[q], name.at[q], k + 5 + j, device)

    def spread_ready(ticket, name):
        k = ticket[1]
        for j, (q_from, _) in enumerate(in_plane):
            arrived(name.at[q_from], k + 5 + j)

    def lanes(j, size=256):
        return part(j, size)

    def matmul(left, right, dst, bias=None, bias_row=0, bias_at=0):
        count = right.shape[1] // 256

        def one(j):
            tile = nn(left[...], right[:, lanes(j)])
            if bias is not None:
                tile = tile + bias[bias_row:bias_row + 1, part(j + bias_at, 256)]
            dst[:, lanes(j)] = tile.astype(BF16)

        loop(count, one)

    def matmul_back(left, right, dst, at=slice(0, T)):
        def one(j):
            dst[at, lanes(j)] = nt(left[at, :], right[lanes(j), :]).astype(BF16)

        loop(right.shape[0] // 256, one)

    def weight_grad(left, right, name, more=False):
        def one(j):
            total = tn(left[:, lanes(j)], right[...])
            if more:
                total = total + name.grad[lanes(j), :].astype(F32)
            name.grad[lanes(j), :] = total.astype(BF16)

        loop(left.shape[1] // 256, one)

    low_half = lax.broadcasted_iota(jnp.int32, (L, 128), 1) < 64
    keep_low = low_half.astype(F32).astype(BF16)
    keep_high = (1.0 - low_half.astype(F32)).astype(BF16)

    def both(pair):
        return jnp.concatenate([pair * keep_low, pair * keep_high], axis=0)

    def merge(stacked):
        return jnp.where(low_half, stacked[:L], stacked[L:])

    def attention(qref, q_at, kref, k_at, v_at, causal, length_row, probs, dst):
        def one(i):
            r, pair = i // 2, i % 2
            place = part(r, L)
            query = both(qref[place, part(pair + q_at, 128)])
            scores = nt(query, kref[place, part(pair + k_at, 128)]) * HD ** (-0.5)
            key = lax.broadcasted_iota(jnp.int32, scores.shape, 1)
            limit = buf.sva[r, z][length_row:length_row + 1, 0:1].astype(F32)
            allowed = key.astype(F32) < limit
            if causal:
                at = lax.broadcasted_iota(jnp.int32, scores.shape, 0)
                at = jnp.where(at < L, at, at - L)
                allowed = allowed & (key <= at)
            scores = jnp.where(allowed, scores, MASKED)
            raised = jnp.exp(scores - jnp.max(scores, -1, keepdims=True))
            weights = (raised * (1.0 / jnp.sum(raised, -1, keepdims=True))).astype(BF16)
            probs[i] = weights
            mixed = nn(weights, kref[place, part(pair + v_at, 128)])
            dst[place, part(pair, 128)] = merge(mixed).astype(BF16)

        loop(2 * P_IN, one, 2)

    def attention_back(qref, q_at, kref, k_at, v_at, probs, grad):
        def one(i):
            r, pair = i // 2, i % 2
            place = part(r, L)
            query = both(qref[place, part(pair + q_at, 128)])
            key = kref[place, part(pair + k_at, 128)]
            value = kref[place, part(pair + v_at, 128)]
            mixed_grad = both(grad[place, part(pair, 128)])
            weights = probs[i]
            soft = weights.astype(F32)
            grad_probs = nt(mixed_grad, value)
            delta = jnp.sum(soft * grad_probs, -1, keepdims=True)
            grad_scores = (soft * (grad_probs - delta)).astype(BF16)
            scale = HD ** (-0.5)
            grad_query = merge(nn(grad_scores, key)) * scale
            grad_key = tn(grad_scores, query) * scale
            grad_value = tn(weights, mixed_grad)
            qref[place, part(pair + q_at, 128)] = grad_query.astype(BF16)
            kref[place, part(pair + k_at, 128)] = grad_key.astype(BF16)
            kref[place, part(pair + v_at, 128)] = grad_value.astype(BF16)

        loop(2 * P_IN, one, 2)

    def column_sums(source, first, count, row, at):
        def one(j):
            values = source[:, part(j + first, 256)].astype(F32)
            buf.sg[row:row + 1, part(j + at, 256)] = jnp.sum(values, 0, keepdims=True)

        loop(count, one)

    def norm(load, index, dst, halves=(0, 1)):
        def one(i):
            place = part(i, TILE)
            normed, _ = whiten(load(place))
            gain, shift = buf.vec[index:index + 1, :], buf.vec[index + 3:index + 4, :]
            rows(dst, q)[place, :] = (normed * gain + shift).astype(BF16)

        loop(TILES * len(halves), one, first=TILES * halves[0])

    def norm_back(load, incoming, index, base, dst, low, out_row=None, halves=(0, 1)):
        zero = jnp.zeros((1, D), F32)

        def one(i, carry):
            gain_sum, shift_sum, out_sum = carry
            place = part(i, TILE)
            normed, scale = whiten(load(place))
            grad = incoming(place)
            gained = grad * buf.vec[index:index + 1, :]
            back = gained - jnp.mean(gained, -1, keepdims=True)
            back = back - normed * jnp.mean(gained * normed, -1, keepdims=True)
            total = base(place) + scale * back
            if dst is not None:
                dst[place, :] = total
            rounded = total.astype(BF16)
            low(place, rounded)
            return (
                gain_sum + jnp.sum(grad * normed, 0, keepdims=True),
                shift_sum + jnp.sum(grad, 0, keepdims=True),
                out_sum + jnp.sum(rounded.astype(F32), 0, keepdims=True),
            )

        first = TILES * halves[0]
        last = first + TILES * len(halves)
        gain_sum, shift_sum, out_sum = lax.fori_loop(first, last, one, (zero, zero, zero))
        buf.sg[index:index + 1, :] = buf.sg[index:index + 1, :] + gain_sum
        buf.sg[index + 3:index + 4, :] = buf.sg[index + 3:index + 4, :] + shift_sum
        if out_row is not None:
            buf.sg[out_row:out_row + 1, :] = buf.sg[out_row:out_row + 1, :] + out_sum

    gate = pltpu.get_barrier_semaphore()
    partners = [device for _, device in in_plane] + [dev_adj, dev_opp, dev_diag]
    partners += [((s + j) % n_sec, d) for j in range(1, n_sec)]
    for device in partners:
        pl.semaphore_signal(gate, inc=1, device_id=device, device_id_type=MESH)
    raw_copies = [local(weight.source, weight.raw) for weight in (wt.qkv, wt.ckv, wt.cq)]
    low_lanes = lax.broadcasted_iota(jnp.int32, (3, 128), 1) < 64
    even_lanes = (jnp.zeros((3, 128), jnp.int32) + c) == 0
    for row, pieces in ((0, io.gain), (3, io.shift), (6, io.out_bias)):
        value = pieces[...].astype(F32)
        twice = jnp.concatenate([value, value], 1)
        buf.sg[row:row + 3, 0:128] = jnp.where(low_lanes == even_lanes, twice, 0.0)
    buf.sg[9:10, 0:128] = io.self_bias[...].astype(F32)
    buf.sg[10:11, 0:128] = io.cross_bias[...].astype(F32)
    buf.sg[11:12, 0:128] = io.unit_bias[:, 0:128].astype(F32)
    buf.sg[12:13, 0:128] = io.unit_bias[:, 128:256].astype(F32)
    buf.sg[13:14, 0:128] = jnp.zeros((1, 128), F32) + io.tgt[0].astype(F32)
    buf.sg[14:15, 0:128] = jnp.zeros((1, 128), F32) + io.src[0].astype(F32)
    buf.sg[15:16, 0:128] = jnp.zeros((1, 128), F32)
    buf.sva[q, z] = buf.sg[:, 0:128].astype(BF16)

    raw_copies[0].wait()
    sort_columns(wt.qkv)
    pl.semaphore_wait(gate, len(partners))

    sv = spread_start(lambda plane: buf.sva.at[q, plane])
    swap_start(wt.qkv)
    k_prev, k_cot, k_mem = slot(), slot(), slot(n_sec)
    send(io.prev, buf.hb, k_prev, ((s + 1) % n_sec, d))
    mem_slot = rows(buf.m, q)
    for j in range(1, n_sec):
        send(io.mem, mem_slot.at[:, part(s, mem_cols)], k_mem + j, ((s + j) % n_sec, d))
    mem_copy = local(io.mem, mem_slot.at[:, part(s, mem_cols)])
    send(io.cot, rows(buf.e3, q), k_cot, ((s + n_sec - 1) % n_sec, d))
    for weight in (wt.so, wt.co, wt.f2):
        weight.own_copy = [local(weight.source, block(weight, z))]
    send_inward(wt.so, wt.so.source)
    send_across(wt.so, wt.so.source)
    weight_outward(wt.so, wt.so.source)
    swap_wait(wt.qkv)
    for weight in first_weights:
        send_inward(weight, block(weight, z))
        send_across(weight, block(weight, z))
        weight_outward(weight, block(weight, z))
    spread_wait(sv)
    spread_plane(sv, buf.sva)
    for weight, copy in ((wt.ckv, raw_copies[1]), (wt.cq, raw_copies[2])):
        copy.wait()
        sort_columns(weight)
        swap_start(weight)
    spread_ready(sv, buf.sva)

    for tile in range(D // 128):
        pair = buf.sva[2 * (tile % 2), tile // 2].astype(F32)
        pair = pair + buf.sva[2 * (tile % 2) + 1, tile // 2].astype(F32)
        buf.vec[:, tile * 128:(tile + 1) * 128] = pair
    half = lax.broadcasted_iota(jnp.int32, (16, 128), 1) < 64
    even = (jnp.zeros((16, 128), jnp.int32) + c) == 0
    buf.bias[...] = jnp.zeros((8, D), F32)
    for kind in range(2):
        for tile in range(2):
            first = buf.sva[x, tile + 2 * kind].astype(F32)
            second = buf.sva[2 + x, tile + 2 * kind].astype(F32)
            lower = jnp.where(even, first, pltpu.roll(first, 64, 1))
            upper = jnp.where(even, pltpu.roll(second, 64, 1), second)
            both_heads = jnp.where(half, lower, upper)
            for which in range(2):
                at = 512 * kind + 128 * tile
                buf.bias[which:which + 1, at:at + 128] = both_heads[9 + which:10 + which]
    for tile in range(Z):
        unit = buf.sva[q, tile].astype(F32)
        buf.bias[2:3, 256 * tile:256 * tile + 128] = unit[11:12]
        buf.bias[2:3, 256 * tile + 128:256 * tile + 256] = unit[12:13]
    buf.sg[...] = jnp.zeros((16, D), F32)

    relay_inward(first_weights[0])
    relay_near(first_weights[0])
    arrived(buf.hb, k_prev)

    def hidden(place):
        return buf.hb[place, :].astype(F32)

    norm(hidden, 0, buf.a1)
    a1 = gather_start(buf.a1)
    unit_swap_start()
    relay_inward(first_weights[1])
    relay_near(first_weights[1])
    relay_inward(wt.so)
    swap_wait(wt.ckv)
    send_inward(wt.ckv, block(wt.ckv, z))
    swap_wait(wt.cq)
    send_inward(wt.cq, block(wt.cq, z))
    send_inward(wt.co, wt.co.source)
    send_across(wt.ckv, block(wt.ckv, z))
    for j in range(1, n_sec):
        origin = (s + n_sec - j) % n_sec
        arrived(mem_slot.at[:, part(origin, mem_cols)], k_mem + j)
    mem_copy.wait()
    memory = gather_start(buf.m)
    arrived(rows(buf.e3, q), k_cot)
    k_units = slot(16)
    to_middle = [send(rows(buf.e3, q), rows(buf.e3, q), k_units + 9, dev_x, end)]

    def cot_inward(index, k):
        for h in range(2):
            src, dst = piece(buf.e3, index, h, 2), half_major(buf.e3b, index, h)
            to_middle.append(send(src, dst, k + h, dev_adj, end))

    cot_inward(q, k_units)
    relay_far(first_weights[0])
    gather_relay(a1)
    relay_far(first_weights[1])
    relay_near(wt.so)
    relay_inward(wt.ckv)
    gather_ready(a1)
    unit_swap_wait(end)
    send_inward(wt.f1, block(wt.f1, z))
    for weight in first_weights:
        weight_ready(weight)
    matmul(buf.a1, wt.qkv.weight, buf.qkv, buf.bias, 0)
    relay_far(wt.so)
    weight_outward(wt.ckv, block(wt.ckv, z))
    send_across(wt.cq, block(wt.cq, z))
    attention(buf.qkv, 0, buf.qkv, 2, 4, True, 13, buf.p1, buf.o1)
    relay_inward(wt.cq)
    send_across(wt.co, wt.co.source)
    wt.so.own_copy[0].wait()
    weight_ready(wt.so)
    matmul(buf.o1, wt.so.weight, set_a.parts)
    step = reduce_start(set_a)
    send_inward(wt.f2, wt.f2.source)
    relay_inward(wt.co)
    relay_near(wt.ckv)
    weight_outward(wt.cq, block(wt.cq, z))
    reduce_relay(step)
    arrived(rows(buf.e3, q_x), k_units + 9, end)
    cot_inward(q_x, k_units + 2)
    gather_finish(memory)
    relay_far(wt.ckv)
    unit_swap_wait(mid)
    send_across(wt.f1, block(wt.f1, z))

    def after_self(i):
        place = part(i, TILE)
        buf.h1[place, :] = hidden(place) + (reduced(step, place) + buf.vec[6:7, :])

    a2 = gather_open(buf.a2, None, 2)
    for h in range(2):
        reduce_ready_half(step, h)
        loop(TILES, after_self, first=h * TILES)
        norm(lambda place: buf.h1[place, :], 1, buf.a2, (h,))
        gather_part(a2, h)
    reduce_done(step)
    relay_near(wt.cq)
    weight_outward(wt.co, wt.co.source)
    relay_far(wt.cq)
    weight_ready(wt.ckv)
    matmul(buf.m, wt.ckv.weight, buf.kv, buf.bias, 1, 1)
    relay_near(wt.co)
    send_across(wt.f2, wt.f2.source)
    relay_far(wt.co)
    relay_inward(wt.f1)

    gather_finish(a2)
    e3 = gather_start(buf.e3, mid)
    weight_ready(wt.cq)
    matmul(buf.a2, wt.cq.weight, buf.q2, buf.bias, 1)
    attention(buf.q2, 0, buf.kv, 0, 2, False, 14, buf.p2, buf.o2)
    wt.co.own_copy[0].wait()
    weight_ready(wt.co)
    matmul(buf.o2, wt.co.weight, set_b.parts)
    step = reduce_start(set_b)
    relay_inward(wt.f2)
    gather_finish(e3)
    reduce_relay(step)

    def after_cross(i):
        place = part(i, TILE)
        buf.h2[place, :] = buf.h1[place, :] + (reduced(step, place) + buf.vec[7:8, :])

    a3 = gather_open(buf.a3, mid, 2)
    for h in range(2):
        reduce_ready_half(step, h)
        loop(TILES, after_cross, first=h * TILES)
        norm(lambda place: buf.h2[place, :], 2, buf.a3, (h,))
        send(piece(buf.a3, q, h, 2), half_major(buf.a3b, q, h), k_units + 10 + h, dev_adj, end)
        gather_part(a3, h)
    reduce_done(step)

    def units(normed, activs, slopes, at=slice(0, T)):
        def one(j):
            value = nn(normed[at, :], wt.f1.weight[:, lanes(j)]) + buf.bias[2:3, lanes(j)]
            activ, slope = gelu_pair(value)
            activs[at, lanes(j)] = activ.astype(BF16)
            slopes[at, lanes(j)] = slope.astype(BF16)

        loop(FL // 256, one, 2)

    def units_back(grad, slopes, at=slice(0, T)):
        def one(j):
            value = nt(grad[at, :], wt.f2.weight[lanes(j), :])
            low = (value * slopes[at, lanes(j)].astype(F32)).astype(BF16)
            slopes[at, lanes(j)] = low
            total = jnp.sum(low.astype(F32), 0, keepdims=True)
            buf.sg[10:11, lanes(j)] = buf.sg[10:11, lanes(j)] + total

        loop(FL // 256, one)

    def weight_grads(left, right, left_b, right_b, name, first, count):
        def one(j):
            total = tn(left[:, lanes(j)], right[...]) + tn(left_b[:, lanes(j)], right_b[...])
            name.grad[lanes(j), :] = total.astype(BF16)

        loop(count, one, first=first)

    def finish(incoming):
        def one(i):
            place = part(i, TILE)
            total = buf.h2[place, :] + (incoming(place) + buf.vec[8:9, :])
            buf.stage[place, :] = total.astype(BF16)

        loop(L // TILE, one)

    def on_mid(fn, *args):
        run_if(mid, lambda: fn(*args))

    def cot_sum(i, carry):
        return carry + jnp.sum(rows(buf.e3, q)[part(i, TILE), :].astype(F32), 0, keepdims=True)

    buf.sg[8:9, :] = lax.fori_loop(0, L // TILE, cot_sum, jnp.zeros((1, D), F32))

    for index, k in ((q, k_units), (q_x, k_units + 2)):
        for h in range(2):
            landed = half_major(buf.e3b, index, h)
            arrived(landed, k + h, mid)
            send(landed, landed, k + 4 + h, dev_core, mid)
    gather_relay(a3)
    a3b = gather_open(buf.a3b, mid, 2, half_major)
    arrived(half_major(buf.a3b, q, 0), k_units + 10, mid)
    gather_part(a3b, 0)
    gather_ready(a3)
    inner_ready(wt.f1)
    on_mid(units, buf.a3, buf.g, buf.gp)
    arrived(half_major(buf.a3b, q, 1), k_units + 11, mid)
    gather_part(a3b, 1)
    on_mid(weight_grad, buf.g, buf.e3, wt.f2)
    for index, k in ((q_core, k_units + 4), (q_xc, k_units + 6)):
        for h in range(2):
            arrived(half_major(buf.e3b, index, h), k + h, mid)
    gather_relay_part(a3b, 0)
    wt.f2.own_copy[0].wait()
    inner_ready(wt.f2)
    on_mid(matmul, buf.g, wt.f2.weight, set_c.parts)
    final = reduce_start(set_c, mid)
    gather_ready_part(a3b, 0)
    step_b = reduce_open(set_b, mid)
    for h in range(2):
        at = slice(h * T // 2, (h + 1) * T // 2)
        if h == 1:
            gather_ready_part(a3b, 1)
        on_mid(units, buf.a3b, buf.gb, buf.gpb, at)
        if h == 0:
            reduce_relay(final)
        else:
            reduce_relay_half(step_b, 0)
        on_mid(units_back, buf.e3b, buf.gpb, at)
        if h == 0:
            gather_relay_part(a3b, 1)
        on_mid(matmul_back, buf.gpb, wt.f1.weight, set_b.parts, at)
        reduce_start_half(step_b, h)

    def back_outward(h):
        reduce_ready_half(step_b, h)
        on_mid(fold, step_b, buf.back, (h,))
        ready = buf.back.at[part(h, HALF)]
        send(ready, ready, k_units + 12 + h, dev_adj, mid)

    on_mid(weight_grad, buf.gb, buf.e3b, wt.f2, True)
    inner_grad_far(wt.f2)
    f2_near(0)
    reduce_relay_half(step_b, 1)
    on_mid(units_back, buf.e3, buf.gp)
    back_outward(0)
    on_mid(matmul_back, buf.gp, wt.f1.weight, set_a.parts)
    reduce_ready(final)
    on_mid(finish, lambda place: reduced(final, place))
    reduce_done(final)
    step = reduce_start(set_a, mid)
    back_outward(1)
    reduce_relay(step)
    on_mid(weight_grads, buf.a3, buf.gp, buf.a3b, buf.gpb, wt.f1, 0, Z)
    inner_grad_far(wt.f1)
    inner_grad_near(wt.f1)
    on_mid(matmul, buf.gb, wt.f2.weight, set_c.parts)

    def store(name):
        def low(place, value):
            rows(name, q)[place, :] = value

        return low

    def units_norm_back(incoming, halves):
        norm_back(
            lambda place: buf.h2[place, :], incoming, 2,
            lambda place: rows(buf.e3, q)[place, :].astype(F32), buf.dh, store(buf.e2), 7, halves,
        )

    reduce_done(e3)
    for record in to_middle:
        sent(record)
    e2 = gather_open(buf.e2, None, 2)
    for h in range(2):
        reduce_ready_half(step, h)
        on_mid(units_norm_back, lambda place: reduced(step, place), (h,))
        gather_part(e2, h, mid)
    final_b = reduce_open(set_c, mid)
    reduce_start_half(final_b, 0)
    reduce_start_half(final_b, 1)
    inner_grad_combine(wt.f2)
    for h in range(2):
        arrived(buf.back.at[part(h, HALF)], k_units + 12 + h, end)
        run_if(
            end,
            lambda h=h: units_norm_back(lambda place: buf.back[place, :].astype(F32), (h,)),
        )
        gather_part(e2, h, end)
    reduce_done(step)
    reduce_done(step_b)
    gather_finish(e2)
    reduce_relay(final_b)

    weight_grad(buf.o2, buf.e2, wt.co)
    grad_send(wt.co)
    matmul_back(buf.e2, wt.co.weight, buf.do)
    attention_back(buf.q2, 0, buf.kv, 0, 2, buf.p2, buf.do)
    matmul_back(buf.q2, wt.cq.weight, set_b.parts)
    step = reduce_start(set_b)
    weight_grad(buf.a2, buf.q2, wt.cq)
    grad_send(wt.cq)
    reduce_relay(step)
    grad_combine(wt.co)
    grad_combine(wt.cq)
    weight_grad(buf.m, buf.kv, wt.ckv)
    grad_send(wt.ckv)
    grad_send_near(wt.ckv)
    matmul_back(buf.kv, wt.ckv.weight, set_a.parts)
    mem_step = reduce_start(set_a)
    column_sums(buf.q2, 0, 1, 9, 2)
    column_sums(buf.kv, 1, 1, 9, 3)
    reduce_ready(final_b)
    on_mid(fold, final_b, buf.tail)
    send(buf.tail, buf.tail, k_units + 14, dev_adj, mid)
    reduce_done(final_b)
    inner_grad_combine(wt.f1)
    e1 = gather_open(buf.e3, None, 2)
    for h in range(2):
        reduce_ready_half(step, h)
        norm_back(
            lambda place: buf.h1[place, :], lambda place: reduced(step, place), 1,
            lambda place: buf.dh[place, :], buf.dh, store(buf.e3), 6, (h,),
        )
        gather_part(e1, h)
    reduce_done(step)
    grad_combine(wt.ckv)
    gather_finish(e1)
    reduce_relay(mem_step)

    weight_grad(buf.o1, buf.e3, wt.so)
    grad_send(wt.so)
    matmul_back(buf.e3, wt.so.weight, buf.do)
    attention_back(buf.qkv, 0, buf.qkv, 2, 4, buf.p1, buf.do)
    grad_outward(wt.co)
    grad_combine(wt.so)
    run_if(end, lambda: weight_grad(buf.a1, buf.qkv, wt.qkv))
    grad_send(wt.qkv)
    matmul_back(buf.qkv, wt.qkv.weight, set_b.parts)
    step = reduce_start(set_b)
    on_mid(weight_grad, buf.a1, buf.qkv, wt.qkv)
    column_sums(buf.qkv, 0, 1, 9, 0)
    column_sums(buf.qkv, 2, 1, 9, 1)
    grad_outward(wt.cq)
    reduce_relay(step)
    f1_final(mid)
    grad_combine_far(wt.qkv)

    reduce_ready(mem_step)
    fold(mem_step, buf.mb)
    k_back = slot(n_sec)
    for j in range(1, n_sec):
        to = (s + j) % n_sec
        send(buf.mb.at[:, part(to, mem_cols)], buf.ml.at[j], k_back + j, (to, d))
    grad_outward(wt.ckv)
    grad_outward(wt.so)
    grad_combine_middle(wt.qkv)
    reduce_ready(step)

    def store_stage(place, value):
        buf.ig[place, :] = value

    norm_back(
        hidden, lambda place: reduced(step, place), 0,
        lambda place: buf.dh[place, :], None, store_stage,
    )
    k_in = slot()
    send(buf.ig, io.input_grad, k_in, ((s + n_sec - 1) % n_sec, d))
    buf.sga[z] = buf.sg[...].astype(BF16)
    sums = spread_start(lambda plane: buf.sga.at[plane])
    f2_near(1)
    for weight in (wt.qkv, wt.cq, wt.co, wt.so):
        grad_send_near(weight)
    f2_final(end)
    f1_final(end)
    for weight in (wt.co, wt.cq):
        grad_final(weight, end)
    grad_outward(wt.qkv)
    grad_final(wt.ckv, end)
    grad_final(wt.so, end)
    grad_final(wt.ckv, mid)
    grad_final(wt.qkv, mid)
    spread_wait(sums)
    planes = buf.sga[0].astype(F32)
    for plane in range(1, Z):
        planes = planes + buf.sga[plane].astype(F32)
    buf.sgp[q] = planes.astype(BF16)
    spread_plane(sums, buf.sgp)

    arrived(buf.tail, k_units + 14, end)
    run_if(end, lambda: finish(lambda place: buf.tail[place, :].astype(F32)))
    for j in range(1, n_sec):
        arrived(buf.ml.at[j], k_back + j)

    def memory_total(i):
        place = part(i, TILE)
        total = buf.mb[place, part(s, mem_cols)].astype(F32)
        for j in range(1, n_sec):
            total = total + buf.ml[j, place, :].astype(F32)
        buf.mo[place, :] = total.astype(BF16)

    loop(L // TILE, memory_total)
    keep(buf.mo, io.memory_grad)
    grad_final(wt.qkv, end)
    for weight in (wt.cq, wt.co, wt.so):
        grad_final(weight, mid)
    f2_final(mid)
    unit_last_wait()
    last_wait(wt.cq)
    last_wait(wt.ckv)
    keep(buf.stage, io.output)
    spread_ready(sums, buf.sgp)

    def per_unit(q_at, at):
        return buf.sgp[q_at, :, at].astype(F32)

    at = part(d // 2, 128)
    feature = per_unit(0, at)
    for q_at in range(1, P_IN):
        feature = feature + per_unit(q_at, at)
    swapped = pltpu.roll(feature, 64, 1)
    buf.sums[...] = jnp.where((jnp.zeros((16, 128), jnp.int32) + c) == 0, feature, swapped)
    head = d % 8
    at = part(2 * (d // 8) + head // 4, 128)
    low_head, high_head = per_unit(2 * c, at), per_unit(2 * c + 1, at)
    first_half = (jnp.zeros((16, 128), jnp.int32) + (head // 2) % 2) == 0
    low_head = jnp.where(first_half, low_head, pltpu.roll(low_head, 64, 1))
    high_head = jnp.where(first_half, pltpu.roll(high_head, 64, 1), high_head)
    buf.sums[9:10, :] = jnp.where(half, low_head, high_head)[9:10]
    at = part(2 * (d // 8) + 4 + head // 4, 128)
    low_head, high_head = per_unit(2 * c, at), per_unit(2 * c + 1, at)
    low_head = jnp.where(first_half, low_head, pltpu.roll(low_head, 64, 1))
    high_head = jnp.where(first_half, pltpu.roll(high_head, 64, 1), high_head)
    buf.sums[10:11, :] = jnp.where(half, low_head, high_head)[9:10]
    buf.sums[11:12, :] = per_unit(q, part(2 * z, 128))[10:11]
    buf.sums[12:13, :] = per_unit(q, part(2 * z + 1, 128))[10:11]
    keep(buf.sums, io.sums_out)
    last_wait(wt.qkv)
    arrived(io.input_grad, k_in)
    for copy, cond in result_copies:
        run_if(cond, copy.wait)
    for record in list(started):
        sent(record)
    assert counter[0] <= SEMS and local_counter[0] <= 64


def buffer_shapes(n_sec, mem_cols):
    tokens, row = (T, D), (L, D)
    shapes = dict(
        sva=(P_IN, Z, 16, 128),
        sga=(Z, 16, D),
        sgp=(P_IN, 16, D),
        hb=row, ig=row, stage=row, mb=row,
        ml=(n_sec, L, mem_cols),
        mo=(L, mem_cols),
        qkv=(T, 768), q2=(T, 256), kv=(T, 512), o1=(T, 256), o2=(T, 256), do=(T, 256),
        p1=(2 * P_IN, 2 * L, L), p2=(2 * P_IN, 2 * L, L),
        g=(T, FL), gp=(T, FL),
        a1=tokens, a2=tokens, a3=tokens, m=tokens, e3=tokens, e2=tokens,
        a3b=tokens, e3b=tokens, gb=(T, FL), gpb=(T, FL), back=row, tail=row,
    )
    exact = dict(vec=(16, D), bias=(8, D), sg=(16, D), sums=(16, 128), h1=row, h2=row, dh=row)
    kinds = {name: pltpu.VMEM(shape, BF16) for name, shape in shapes.items()}
    kinds.update({name: pltpu.VMEM(shape, F32) for name, shape in exact.items()})
    return kinds


REDUCE_SHAPES = dict(
    parts=pltpu.VMEM((T, D), BF16),
    core=pltpu.VMEM((2 * L, D), BF16),
    across=pltpu.VMEM((L, D), BF16),
)


def scratch_of(n_sec, mem_cols):
    scratch = list(buffer_shapes(n_sec, mem_cols).values())
    scratch += 3 * list(REDUCE_SHAPES.values())
    for count, columns, _ in WEIGHTS.values():
        scratch += 2 * [pltpu.VMEM((Z * count, columns), BF16)]
        scratch += 2 * [pltpu.VMEM((count, columns), BF16)]
    for count, columns, _ in list(WEIGHTS.values())[:5]:
        scratch += 3 * [pltpu.VMEM((count, columns), BF16)]
    for columns in (768, 512, 256):
        scratch.append(pltpu.VMEM((64, P_IN * columns), BF16))
        scratch.append(pltpu.VMEM((P_IN, 64, columns), BF16))
    return scratch + [
        pltpu.SemaphoreType.DMA((SEMS,)),
        pltpu.SemaphoreType.DMA((SEMS,)),
        pltpu.SemaphoreType.DMA((64,)),
    ]


def finish_kernel(*refs):
    moved, low, sums = refs[:3], refs[3:10], refs[10]
    moved_out, high, small = refs[11:14], refs[14:21], refs[21:27]
    low_buf, high_buf, moved_buf = refs[27:34], refs[34:41], refs[41:44]
    small_buf, sems = refs[44:50], refs[50]
    inward = [
        pltpu.make_async_copy(src, dst, sems.at[i])
        for i, (src, dst) in enumerate(zip(low + moved, low_buf + moved_buf))
    ]
    order = (7, 8, 5, 6, 0, 2, 9, 1, 4, 3)
    for i in order:
        inward[i].start()
    outward = []
    gain, shift, out_bias, self_bias, cross_bias, unit_bias = small_buf
    for row in range(3):
        gain[row] = sums[row:row + 1, 0:64]
        shift[row] = sums[row + 3:row + 4, 0:64]
        out_bias[row] = sums[row + 6:row + 7, 0:64]
    self_bias[...] = sums[9:10, :]
    cross_bias[...] = sums[10:11, :]
    unit_bias[:, 0:128] = sums[11:12, :]
    unit_bias[:, 128:256] = sums[12:13, :]
    for i, (src, dst) in enumerate(zip(small_buf, small)):
        back = pltpu.make_async_copy(src, dst, sems.at[20 + i])
        back.start()
        outward.append(back)
    for i in order:
        inward[i].wait()
        if i < 7:
            src, dst = high_buf[i], high[i]

            def one(j, i=i):
                place = part(j, 16)
                high_buf[i][place, :] = low_buf[i][place, :].astype(F32)

            loop(low_buf[i].shape[0] // 16, one)
        else:
            src, dst = moved_buf[i - 7], moved_out[i - 7]
        back = pltpu.make_async_copy(src, dst, sems.at[10 + i])
        back.start()
        outward.append(back)
    for copy in outward:
        copy.wait()


def on_device_planes(
    prev_act, memory, out_cot, tgt_len, src_len, norm_gain, norm_bias, self_qkv, self_qv_bias,
    self_out, cross_q, cross_kv, cross_qv_bias, cross_out, out_bias, fc1, fc1_bias, fc2,
):
    n_sec = lax.axis_size("section")
    mem_cols = memory.shape[2]
    operands = (
        prev_act[0, 0], memory[0], out_cot[0, 0], tgt_len, src_len,
        norm_gain[0], norm_bias[0], out_bias[0], self_qv_bias, cross_qv_bias, fc1_bias,
        self_qkv[0], self_out[0], cross_kv[0], cross_q[0], cross_out[0], fc1[0], fc2[0],
    )
    anywhere = pl.BlockSpec(memory_space=pl.ANY)
    in_specs = 3 * [anywhere] + 2 * [pl.BlockSpec(memory_space=pltpu.SMEM)]
    in_specs += 6 * [pl.BlockSpec(memory_space=pltpu.VMEM)] + 7 * [anywhere]
    out_shapes = [(L, D), (L, D), (L, mem_cols)]
    for count, columns, by_column in WEIGHTS.values():
        out_shapes.append((count // P_IN, P_IN * columns) if by_column else (count, columns))
    sums_shape = jax.ShapeDtypeStruct((16, 128), F32)
    results = pl.pallas_call(
        functools.partial(whole_kernel, n_sec, mem_cols),
        out_shape=[jax.ShapeDtypeStruct(shape, BF16) for shape in out_shapes] + [sums_shape],
        in_specs=in_specs,
        out_specs=[anywhere] * (len(out_shapes) + 1),
        scratch_shapes=scratch_of(n_sec, mem_cols),
        compiler_params=pltpu.CompilerParams(
            collective_id=0, has_side_effects=True, vmem_limit_bytes=64 * 2**20 - 2**16
        ),
        cost_estimate=pl.CostEstimate(
            flops=21 * 10**9, bytes_accessed=20 * 2**20, transcendentals=3 * 10**6
        ),
    )(*operands)
    shapes = [result.shape for result in results]
    small_shapes = [(3, 1, 64)] * 3 + [(1, 128), (1, 128), (1, 256)]
    vmem = pl.BlockSpec(memory_space=pltpu.VMEM)
    finished = pl.pallas_call(
        finish_kernel,
        out_shape=[jax.ShapeDtypeStruct(shape, BF16) for shape in shapes[:3]]
        + [jax.ShapeDtypeStruct(shape, F32) for shape in shapes[3:10]]
        + [jax.ShapeDtypeStruct(shape, F32) for shape in small_shapes],
        in_specs=10 * [anywhere] + [vmem],
        out_specs=16 * [anywhere],
        scratch_shapes=[pltpu.VMEM(shape, BF16) for shape in shapes[3:10]]
        + [pltpu.VMEM(shape, F32) for shape in shapes[3:10]]
        + [pltpu.VMEM(shape, BF16) for shape in shapes[:3]]
        + [pltpu.VMEM(shape, F32) for shape in small_shapes]
        + [pltpu.SemaphoreType.DMA((26,))],
        compiler_params=pltpu.CompilerParams(vmem_limit_bytes=63 * 2**20),
        cost_estimate=pl.CostEstimate(flops=0, bytes_accessed=9 * 2**20, transcendentals=0),
    )(*results)
    (
        output, input_grad, memory_grad, g_qkv, g_so, g_ckv, g_cq, g_co, g_f1, g_f2,
        gain, shift, biases, self_biases, cross_biases, units,
    ) = finished
    return (
        output[None, None],
        input_grad[None, None],
        memory_grad[None],
        gain.transpose(1, 0, 2),
        shift.transpose(1, 0, 2),
        g_qkv[None],
        self_biases,
        g_so[None],
        g_cq[None],
        g_ckv[None],
        cross_biases,
        g_co[None],
        biases.transpose(1, 0, 2),
        g_f1[None],
        units,
        g_f2[None],
    )


def solution(mesh):
    in_specs = (
        P("section", "dp", None, None),
        P("dp", None, "section"),
        P("section", "dp", None, None),
        P("dp"),
        P("dp"),
        P("section", None, "dp"),
        P("section", None, "dp"),
        P("section", "dp", None),
        P("section", "dp"),
        P("section", "dp", None),
        P("section", "dp", None),
        P("section", "dp", None),
        P("section", "dp"),
        P("section", "dp", None),
        P("section", None, "dp"),
        P("section", "dp", None),
        P("section", "dp"),
        P("section", "dp", None),
    )
    out_specs = (
        P("section", "dp", None, None),
        P("section", "dp", None, None),
        P("dp", None, "section"),
        P("section", None, "dp"),
        P("section", None, "dp"),
        P("section", "dp", None),
        P("section", "dp"),
        P("section", "dp", None),
        P("section", "dp", None),
        P("section", "dp", None),
        P("section", "dp"),
        P("section", "dp", None),
        P("section", None, "dp"),
        P("section", "dp", None),
        P("section", "dp"),
        P("section", "dp", None),
    )
    planes = Z * P_IN
    fits = mesh.shape["dp"] == planes
    return jax.shard_map(
        on_device_planes if fits else on_device, mesh=mesh, in_specs=in_specs, out_specs=out_specs, check_vma=False
    )
```

```python
import functools
from types import SimpleNamespace

import jax
import jax.numpy as jnp
from jax import lax
from jax.experimental import pallas as pl
from jax.experimental.pallas import tpu as pltpu
from jax.sharding import PartitionSpec as P

H = 16
HD = 64


EPSILON = 1e-05
MASKED = -1000000000.0


def passed_along(value, axis, by):
    length = lax.axis_size(axis)
    return lax.ppermute(value, axis, [(i, (i + by) % length) for i in range(length)])


def norm_fwd(rows, gain, shift_term):
    center = rows - jnp.mean(rows, -1, keepdims=True)
    scale = lax.rsqrt(jnp.mean(center * center, -1, keepdims=True) + EPSILON)
    return center * scale * gain + shift_term


def gelu_exact(values):
    return jax.nn.gelu(values, approximate=False)


def product(left, right):
    return jnp.dot(left, right, preferred_element_type=jnp.float32)


def product_right_t(left, right):
    return lax.dot_general(
        left, right, (((1,), (1,)), ((), ())), preferred_element_type=jnp.float32
    )


def product_left_t(left, right):
    return lax.dot_general(
        left, right, (((0,), (0,)), ((), ())), preferred_element_type=jnp.float32
    )


def split_heads(flat, batch_rows):
    return flat.reshape(batch_rows, -1, H, HD)


def softmax_probs(query, key_rows, allowed):
    scores = jnp.einsum(
        "rthd,rshd->rhts", query, key_rows, preferred_element_type=jnp.float32
    ) * HD ** (-0.5)
    scores = jnp.where(allowed[:, None], scores, MASKED)
    weights = jnp.exp(scores - jnp.max(scores, -1, keepdims=True))
    return weights / jnp.sum(weights, -1, keepdims=True)


def attend_fwd(query, key_rows, value_rows, allowed):
    probs = softmax_probs(query, key_rows, allowed)
    mixed = jnp.einsum(
        "rhts,rshd->rthd",
        probs.astype(jnp.bfloat16),
        value_rows,
        preferred_element_type=jnp.float32,
    )
    return mixed.reshape(mixed.shape[0] * mixed.shape[1], -1).astype(jnp.bfloat16)


def attend_back(query, key_rows, value_rows, allowed, grad_mixed):
    probs = softmax_probs(query, key_rows, allowed)
    grad_heads = grad_mixed.reshape(query.shape)
    grad_probs = jnp.einsum(
        "rthd,rshd->rhts", grad_heads, value_rows, preferred_element_type=jnp.float32
    )
    delta = jnp.sum(probs * grad_probs, -1, keepdims=True)
    grad_scores = (probs * (grad_probs - delta)).astype(jnp.bfloat16)
    scale = HD ** (-0.5)
    grad_query = (
        jnp.einsum("rhts,rshd->rthd", grad_scores, key_rows, preferred_element_type=jnp.float32)
        * scale
    )
    grad_keys = (
        jnp.einsum("rhts,rthd->rshd", grad_scores, query, preferred_element_type=jnp.float32)
        * scale
    )
    grad_values = jnp.einsum(
        "rhts,rthd->rshd",
        probs.astype(jnp.bfloat16),
        grad_heads,
        preferred_element_type=jnp.float32,
    )
    width = query.shape[2] * query.shape[3]
    return (
        grad_query.reshape(-1, width).astype(jnp.bfloat16),
        grad_keys.reshape(-1, width).astype(jnp.bfloat16),
        grad_values.reshape(-1, width).astype(jnp.bfloat16),
    )


def unpack(pieces):
    return tuple((piece[0] for piece in pieces))


def on_device(
    prev_act,
    memory,
    out_cot,
    tgt_len,
    src_len,
    norm_gain,
    norm_bias,
    self_qkv,
    self_qv_bias,
    self_out,
    cross_q,
    cross_kv,
    cross_qv_bias,
    cross_out,
    out_bias,
    fc1,
    fc1_bias,
    fc2,
):
    fetched = unpack(
        (
            lax.all_gather(norm_gain, "dp", axis=2, tiled=True),
            lax.all_gather(norm_bias, "dp", axis=2, tiled=True),
            lax.all_gather(self_qkv, "dp", axis=1, tiled=True),
            lax.all_gather(self_qv_bias, "dp", axis=1, tiled=True),
            lax.all_gather(self_out, "dp", axis=1, tiled=True),
            lax.all_gather(cross_q, "dp", axis=1, tiled=True),
            lax.all_gather(cross_kv, "dp", axis=1, tiled=True),
            lax.all_gather(cross_qv_bias, "dp", axis=1, tiled=True),
            lax.all_gather(cross_out, "dp", axis=1, tiled=True),
            lax.all_gather(out_bias, "dp", axis=2, tiled=True),
            lax.all_gather(fc1, "dp", axis=1, tiled=True),
            lax.all_gather(fc1_bias, "dp", axis=1, tiled=True),
            lax.all_gather(fc2, "dp", axis=1, tiled=True),
        )
    )
    gains, shifts, w_sqkv, b_sqv, w_sout, w_cq, w_ckv, b_cqv, w_cout, b_out, w_one, b_one, w_two = (
        fetched
    )
    gain_f = gains.astype(jnp.float32)
    shift_f = shifts.astype(jnp.float32)
    sqv_f = b_sqv.astype(jnp.float32)
    cqv_f = b_cqv.astype(jnp.float32)
    out_f = b_out.astype(jnp.float32)
    one_f = b_one.astype(jnp.float32)
    source = passed_along(prev_act, "section", 1)[0]
    batch_rows, length, width = source.shape
    encoded = lax.all_gather(memory, "section", axis=2, tiled=True)
    mem_flat = encoded.reshape(-1, width)
    places = jnp.arange(length)
    self_ok = (places[None, None, :] <= places[None, :, None]) & (
        places[None, None, :] < tgt_len[:, None, None]
    )
    cross_ok = jnp.arange(encoded.shape[1])[None, None, :] < src_len[:, None, None]
    resid = source.astype(jnp.float32).reshape(-1, width)
    normed_one, pull_one = jax.vjp(norm_fwd, resid, gain_f[0], shift_f[0])
    first_in = normed_one.astype(jnp.bfloat16)
    joint = product(first_in, w_sqkv)
    query_self = (joint[:, :width] + sqv_f[:width]).astype(jnp.bfloat16)
    keys_self = joint[:, width : 2 * width].astype(jnp.bfloat16)
    values_self = (joint[:, 2 * width :] + sqv_f[width:]).astype(jnp.bfloat16)
    self_mixed = attend_fwd(
        split_heads(query_self, batch_rows),
        split_heads(keys_self, batch_rows),
        split_heads(values_self, batch_rows),
        self_ok,
    )
    after_self = resid + (product(self_mixed, w_sout) + out_f[0])
    normed_two, pull_two = jax.vjp(norm_fwd, after_self, gain_f[1], shift_f[1])
    second_in = normed_two.astype(jnp.bfloat16)
    query_cross = (product(second_in, w_cq) + cqv_f[:width]).astype(jnp.bfloat16)
    memory_proj = product(mem_flat, w_ckv)
    keys_cross = memory_proj[:, :width].astype(jnp.bfloat16)
    values_cross = (memory_proj[:, width:] + cqv_f[width:]).astype(jnp.bfloat16)
    cross_mixed = attend_fwd(
        split_heads(query_cross, batch_rows),
        split_heads(keys_cross, batch_rows),
        split_heads(values_cross, batch_rows),
        cross_ok,
    )
    after_cross = after_self + (product(cross_mixed, w_cout) + out_f[1])
    normed_three, pull_three = jax.vjp(norm_fwd, after_cross, gain_f[2], shift_f[2])
    third_in = normed_three.astype(jnp.bfloat16)
    pre_act = product(third_in, w_one) + one_f
    activ, pull_gelu = jax.vjp(gelu_exact, pre_act)
    act_low = activ.astype(jnp.bfloat16)
    result = after_cross + (product(act_low, w_two) + out_f[2])
    output = result.astype(jnp.bfloat16).reshape(1, batch_rows, length, width)
    (
        unused_gains,
        unused_shifts,
        w_sqkv,
        unused_sqv,
        w_sout,
        w_cq,
        w_ckv,
        unused_cqv,
        w_cout,
        unused_out,
        w_one,
        unused_one,
        w_two,
    ) = fetched
    grad_out = passed_along(out_cot, "section", -1)[0].astype(jnp.float32).reshape(-1, width)
    ffn_grad = grad_out.astype(jnp.bfloat16)
    grad_fc2 = product_left_t(act_low, ffn_grad)
    grad_b2 = jnp.sum(ffn_grad, 0, dtype=jnp.float32)
    grad_act = product_right_t(ffn_grad, w_two)
    (grad_pre,) = pull_gelu(grad_act)
    pre_low = grad_pre.astype(jnp.bfloat16)
    grad_fc1 = product_left_t(third_in, pre_low)
    grad_b1 = jnp.sum(pre_low, 0, dtype=jnp.float32)
    grad_mid, grad_gain3, grad_shift3 = pull_three(product_right_t(pre_low, w_one))
    grad_mid = grad_mid + grad_out
    cross_grad = grad_mid.astype(jnp.bfloat16)
    grad_cout = product_left_t(cross_mixed, cross_grad)
    grad_bco = jnp.sum(cross_grad, 0, dtype=jnp.float32)
    grad_cmix = product_right_t(cross_grad, w_cout).astype(jnp.bfloat16)
    grad_qc, grad_kc, grad_vc = attend_back(
        split_heads(query_cross, batch_rows),
        split_heads(keys_cross, batch_rows),
        split_heads(values_cross, batch_rows),
        cross_ok,
        grad_cmix,
    )
    grad_cq = product_left_t(second_in, grad_qc)
    grad_kv = jnp.concatenate([grad_kc, grad_vc], -1)
    grad_ckv = product_left_t(mem_flat, grad_kv)
    grad_cqv = jnp.concatenate(
        [jnp.sum(grad_qc, 0, dtype=jnp.float32), jnp.sum(grad_vc, 0, dtype=jnp.float32)]
    )
    grad_memory = product_right_t(grad_kv, w_ckv).reshape(encoded.shape)
    memory_grad = lax.psum_scatter(
        grad_memory.astype(jnp.bfloat16), "section", scatter_dimension=2, tiled=True
    )
    grad_after, grad_gain2, grad_shift2 = pull_two(product_right_t(grad_qc, w_cq))
    grad_after = grad_after + grad_mid
    self_grad = grad_after.astype(jnp.bfloat16)
    grad_sout = product_left_t(self_mixed, self_grad)
    grad_bso = jnp.sum(self_grad, 0, dtype=jnp.float32)
    grad_smix = product_right_t(self_grad, w_sout).astype(jnp.bfloat16)
    grad_qs, grad_ks, grad_vs = attend_back(
        split_heads(query_self, batch_rows),
        split_heads(keys_self, batch_rows),
        split_heads(values_self, batch_rows),
        self_ok,
        grad_smix,
    )
    grad_qkv = jnp.concatenate([grad_qs, grad_ks, grad_vs], -1)
    grad_sqkv = product_left_t(first_in, grad_qkv)
    grad_sqv = jnp.concatenate(
        [jnp.sum(grad_qs, 0, dtype=jnp.float32), jnp.sum(grad_vs, 0, dtype=jnp.float32)]
    )
    grad_in, grad_gain1, grad_shift1 = pull_one(product_right_t(grad_qkv, w_sqkv))
    grad_in = grad_in + grad_after
    input_grad = passed_along(
        grad_in.astype(jnp.bfloat16).reshape(1, batch_rows, length, width), "section", -1
    )
    grad_gain = jnp.stack([grad_gain1, grad_gain2, grad_gain3])
    grad_shift = jnp.stack([grad_shift1, grad_shift2, grad_shift3])
    grad_obias = jnp.stack([grad_bso, grad_bco, grad_b2])
    sums = (
        lax.psum_scatter(
            grad_gain.astype(jnp.bfloat16), "dp", scatter_dimension=1, tiled=True
        ).astype(jnp.float32),
        lax.psum_scatter(
            grad_shift.astype(jnp.bfloat16), "dp", scatter_dimension=1, tiled=True
        ).astype(jnp.float32),
        lax.psum_scatter(
            grad_sqkv.astype(jnp.bfloat16), "dp", scatter_dimension=0, tiled=True
        ).astype(jnp.float32),
        lax.psum_scatter(
            grad_sqv.astype(jnp.bfloat16), "dp", scatter_dimension=0, tiled=True
        ).astype(jnp.float32),
        lax.psum_scatter(
            grad_sout.astype(jnp.bfloat16), "dp", scatter_dimension=0, tiled=True
        ).astype(jnp.float32),
        lax.psum_scatter(
            grad_cq.astype(jnp.bfloat16), "dp", scatter_dimension=0, tiled=True
        ).astype(jnp.float32),
        lax.psum_scatter(
            grad_ckv.astype(jnp.bfloat16), "dp", scatter_dimension=0, tiled=True
        ).astype(jnp.float32),
        lax.psum_scatter(
            grad_cqv.astype(jnp.bfloat16), "dp", scatter_dimension=0, tiled=True
        ).astype(jnp.float32),
        lax.psum_scatter(
            grad_cout.astype(jnp.bfloat16), "dp", scatter_dimension=0, tiled=True
        ).astype(jnp.float32),
        lax.psum_scatter(
            grad_obias.astype(jnp.bfloat16), "dp", scatter_dimension=1, tiled=True
        ).astype(jnp.float32),
        lax.psum_scatter(
            grad_fc1.astype(jnp.bfloat16), "dp", scatter_dimension=0, tiled=True
        ).astype(jnp.float32),
        lax.psum_scatter(
            grad_b1.astype(jnp.bfloat16), "dp", scatter_dimension=0, tiled=True
        ).astype(jnp.float32),
        lax.psum_scatter(
            grad_fc2.astype(jnp.bfloat16), "dp", scatter_dimension=0, tiled=True
        ).astype(jnp.float32),
    )
    return (
        output,
        input_grad,
        memory_grad,
        sums[0][None],
        sums[1][None],
        sums[2][None],
        sums[3][None],
        sums[4][None],
        sums[5][None],
        sums[6][None],
        sums[7][None],
        sums[8][None],
        sums[9][None],
        sums[10][None],
        sums[11][None],
        sums[12][None],
    )


Z = 4
P_IN = 4
L = 192
D = 1024
T = P_IN * L
FL = 1024
TILE = 32
MESH = pl.DeviceIdType.MESH
F32 = jnp.float32
BF16 = jnp.bfloat16

WEIGHTS = dict(
    qkv=(256, 768, True),
    so=(64, 1024, False),
    ckv=(256, 512, True),
    cq=(256, 256, True),
    co=(64, 1024, False),
    f1=(256, 1024, True),
    f2=(256, 1024, False),
)
SEMS = 320


def run_if(cond, fn):
    if cond is None:
        fn()
    else:
        pl.when(cond)(fn)


def part(index, size, step=None):
    return pl.ds(pl.multiple_of(index * size, size), size if step is None else step)


def nn(left, right):
    return jnp.dot(left, right, preferred_element_type=F32)


def nt(left, right):
    return lax.dot_general(left, right, (((1,), (1,)), ((), ())), preferred_element_type=F32)


def tn(left, right):
    return lax.dot_general(left, right, (((0,), (0,)), ((), ())), preferred_element_type=F32)


def loop(count, body, unroll=1, first=0):
    def step(index, carry):
        body(index)
        return carry

    lax.fori_loop(first, first + count, step, 0, unroll=unroll)


HALF = L // 2
TILES = HALF // TILE


def gelu_pair(values):
    bell = jnp.exp(-0.5 * values * values)
    step = 1.0 / (1.0 + 0.3275911 * 0.7071067811865476 * jnp.abs(values))
    series = step * (
        0.254829592
        + step
        * (-0.284496736 + step * (1.421413741 + step * (-1.453152027 + step * 1.061405429)))
    )
    above = 0.5 * series * bell
    below = jnp.where(values < 0, above, 1.0 - above)
    return values * below, below + values * bell * 0.3989422804014327


def whiten(rows):
    center = rows - jnp.mean(rows, -1, keepdims=True)
    scale = lax.rsqrt(jnp.mean(center * center, -1, keepdims=True) + EPSILON)
    return center * scale, scale


def whole_kernel(n_sec, mem_cols, *refs):
    given = iter(refs)

    def take(names):
        return SimpleNamespace(**{name: next(given) for name in names})

    def take_weights(**fields):
        for name in WEIGHTS:
            for field in fields:
                setattr(getattr(wt, name), field, next(given))

    wt = SimpleNamespace(**{name: SimpleNamespace() for name in WEIGHTS})
    io = take(
        dict(
            prev=0, mem=0, cot=0, tgt=0, src=0, gain=0, shift=0, out_bias=0,
            self_bias=0, cross_bias=0, unit_bias=0,
        )
    )
    take_weights(source=0)
    vars(io).update(vars(take(dict(output=0, input_grad=0, memory_grad=0))))
    take_weights(result=0)
    vars(io).update(vars(take(dict(sums_out=0))))
    buf = take(buffer_shapes(n_sec, mem_cols))
    set_a, set_b, set_c = (take(REDUCE_SHAPES) for _ in range(3))
    take_weights(weight=0, grad=0, near=0, far=0)
    for weight in (wt.qkv, wt.so, wt.ckv, wt.cq, wt.co):
        weight.to_diag, weight.to_opp, weight.through = next(given), next(given), next(given)
    for weight in (wt.qkv, wt.ckv, wt.cq):
        weight.raw, weight.sorted = next(given), next(given)
    send_sems, recv_sems, local_sems = given

    s = lax.axis_index("section")
    d = lax.axis_index("dp")
    z, q = d // P_IN, d % P_IN
    x, c = q // 2, q % 2
    end = (z % 3) == 0
    mid = (z % 3) != 0
    q_core = q + 1 - 2 * c
    q_x = q + 2 - 4 * x
    q_xc = q_x + 1 - 2 * c
    z_adj = z + 1 - 2 * (z % 2)
    z_opp = 3 - z
    z_diag = (z + 2) % 4
    dev_core, dev_x, dev_xc = (s, z * P_IN + q_core), (s, z * P_IN + q_x), (s, z * P_IN + q_xc)
    dev_adj, dev_opp, dev_diag = (s, z_adj * P_IN + q), (s, z_opp * P_IN + q), (s, z_diag * P_IN + q)
    in_plane = ((q_core, dev_core), (q_x, dev_x), (q_xc, dev_xc))

    counter = [0]
    started = []
    local_counter = [0]

    def slot(count=1):
        counter[0] += count
        return counter[0] - count

    def remote(src, dst, k, device):
        return pltpu.make_async_remote_copy(
            src_ref=src, dst_ref=dst, send_sem=send_sems.at[k], recv_sem=recv_sems.at[k],
            device_id=device, device_id_type=MESH,
        )

    def send(src, dst, k, device, cond=None):
        copy = remote(src, dst, k, device)
        run_if(cond, copy.start)
        record = [copy, cond]
        started.append(record)
        return record

    def sent(record):
        run_if(record[1], record[0].wait_send)
        started[:] = [other for other in started if other is not record]

    def arrived(dst, k, cond=None):
        run_if(cond, remote(dst, dst, k, dev_core).wait_recv)

    def local(src, dst, cond=None):
        copy = pltpu.make_async_copy(src, dst, local_sems.at[local_counter[0]])
        local_counter[0] += 1
        run_if(cond, copy.start)
        return copy

    def keep(src, dst, cond=None):
        result_copies.append((local(src, dst, cond), cond))

    def rows(rows_of, index):
        return rows_of.at[part(index, L)]

    for name, (count, _, by_column) in WEIGHTS.items():
        weight = getattr(wt, name)
        weight.count, weight.by_column = count, by_column
        weight.pieces, weight.piece, weight.last_copies = 1, 0, []
        weight.to_use, weight.swap, weight.to_sum, weight.last = slot(5), slot(3), slot(6), slot(3)

    def block(name, index):
        return name.weight.at[part(index * name.pieces + name.piece, name.count)]

    first_weights = [
        SimpleNamespace(
            weight=wt.qkv.weight, count=wt.qkv.count // 2, pieces=2, piece=h, to_use=slot(5)
        )
        for h in range(2)
    ]

    def send_inward(name, src):
        send(src, block(name, z), name.to_use, dev_adj, end)

    def send_across(name, src):
        send(src, block(name, z), name.to_use + 1, dev_opp, mid)

    def weight_outward(name, src):
        send(src, block(name, z), name.to_use, dev_adj, mid)

    def relay_inward(name):
        k = name.to_use
        arrived(block(name, z_adj), k, mid)
        send(block(name, z_adj), block(name, z_adj), k + 2, dev_opp, mid)

    def relay_near(name):
        k = name.to_use
        arrived(block(name, z_opp), k + 1, mid)
        send(block(name, z_opp), block(name, z_opp), k + 3, dev_adj, mid)

    def relay_far(name):
        k = name.to_use
        arrived(block(name, z_diag), k + 2, mid)
        send(block(name, z_diag), block(name, z_diag), k + 4, dev_adj, mid)

    def weight_ready(name):
        k = name.to_use
        arrived(block(name, z_adj), k, end)
        arrived(block(name, z_diag), k + 3, end)
        arrived(block(name, z_opp), k + 4, end)

    def inner_ready(name):
        k = name.to_use
        arrived(block(name, z_opp), k + 1, mid)
        arrived(block(name, z_diag), k + 2, mid)


    def swap_start(name):
        size = name.count // P_IN
        place = name.weight.at[part(z * P_IN + q, size)]
        name.swapped = [
            send(name.sorted.at[q_to], place, name.swap + j, device)
            for j, (q_to, device) in enumerate(in_plane)
        ]
        name.own_copy = [local(name.sorted.at[q], place)]

    def swap_wait(name):
        size = name.count // P_IN
        for j, (q_from, _) in enumerate(in_plane):
            arrived(name.weight.at[part(z * P_IN + q_from, size)], name.swap + j)
        for copy in name.own_copy:
            copy.wait()
        for record in name.swapped:
            sent(record)

    def halves(first, second, odd):
        if odd:
            first = pltpu.roll(first, 64, 1)
        else:
            second = pltpu.roll(second, 64, 1)
        lane = lax.broadcasted_iota(jnp.int32, first.shape, 1)
        return jnp.where(lane < 64, first, second)

    def tile_of(index):
        return slice(index * 128, index * 128 + 128)

    def sort_columns(name):
        for q_to in range(P_IN):
            for tile in range(name.sorted.shape[2] // 128):
                at = 4 * tile + q_to // 2
                first = name.raw[:, tile_of(at)].astype(F32)
                second = name.raw[:, tile_of(at + 2)].astype(F32)
                name.sorted[q_to, :, tile_of(tile)] = halves(first, second, q_to % 2).astype(BF16)

    def unsort_columns(name):
        for tile in range(name.raw.shape[1] // 128):
            group, u = tile // 8, tile % 8
            at = 2 * group + u // 4
            first = name.sorted[2 * (u % 2), :, tile_of(at)].astype(F32)
            second = name.sorted[2 * (u % 2) + 1, :, tile_of(at)].astype(F32)
            name.raw[:, tile_of(tile)] = halves(first, second, (u // 2) % 2).astype(BF16)

    unit_swap, unit_last = slot(3 * Z), slot(3 * Z)

    def unit_columns(rows_of, tile, q_at):
        return rows_of.at[:, part(tile * P_IN + q_at, 256)]

    def unit_swap_start():
        size = wt.f1.count // P_IN
        place = wt.f1.weight.at[part(z * P_IN + q, size)]
        wt.f1.own_copy = []
        for tile in range(Z):
            at = place.at[:, part(tile, 256)]
            for j, (q_to, device) in enumerate(in_plane):
                send(unit_columns(wt.f1.source, tile, q_to), at, unit_swap + 3 * tile + j, device)
            wt.f1.own_copy.append(local(unit_columns(wt.f1.source, tile, q), at))

    def unit_swap_wait(cond):
        size = wt.f1.count // P_IN
        for tile in range(Z):
            for j, (q_from, _) in enumerate(in_plane):
                place = wt.f1.weight.at[part(z * P_IN + q_from, size)]
                arrived(place.at[:, part(tile, 256)], unit_swap + 3 * tile + j, cond)
        for copy in wt.f1.own_copy:
            run_if(cond, copy.wait)

    def grad_block(name, index):
        return name.grad.at[part(index, name.count)]

    def grad_send_far(name):
        return send(grad_block(name, z_opp), name.to_diag, name.to_sum, dev_adj, end)

    def grad_send_middle(name):
        return send(grad_block(name, z_diag), name.to_opp, name.to_sum + 1, dev_adj, end)

    def grad_send_near(name):
        return send(grad_block(name, z_adj), name.near, name.to_sum + 2, dev_adj, end)

    def grad_send(name):
        grad_send_far(name)
        grad_send_middle(name)

    def add_rows(count, body):
        size = min(count, 64)
        loop(count // size, lambda i: body(part(i, size)))

    def grad_add(name, landed, index):
        def one(place):
            own = grad_block(name, index)[place, :].astype(F32)
            landed[place, :] = (own + landed[place, :].astype(F32)).astype(BF16)

        add_rows(name.count, one)

    def grad_combine_far(name):
        k = name.to_sum
        arrived(name.to_diag, k, mid)
        run_if(mid, lambda: grad_add(name, name.to_diag, z_diag))
        send(name.to_diag, name.through, k + 3, dev_opp, mid)

    def grad_combine_middle(name):
        k = name.to_sum
        arrived(name.to_opp, k + 1, mid)
        run_if(mid, lambda: grad_add(name, name.to_opp, z_opp))
        send(name.to_opp, name.far, k + 4, dev_opp, mid)

    def grad_combine(name):
        grad_combine_far(name)
        grad_combine_middle(name)

    def grad_outward(name):
        k = name.to_sum
        arrived(name.through, k + 3, mid)
        run_if(mid, lambda: grad_add(name, name.through, z_adj))
        send(name.through, name.near, k + 5, dev_adj, mid)

    result_copies = []

    def inner_grad_far(name):
        send(grad_block(name, z_diag), name.far, name.to_sum, dev_opp, mid)

    def inner_grad_near(name):
        send(grad_block(name, z_opp), name.near, name.to_sum + 1, dev_opp, mid)

    def f2_half(rows_of, h):
        return rows_of.at[part(h, wt.f2.count // 2)]

    def f2_near(h):
        src = f2_half(grad_block(wt.f2, z_opp), h)
        send(src, f2_half(wt.f2.near, h), wt.f2.to_sum + 1 + 2 * h, dev_opp, mid)

    def inner_grad_combine(name):
        k = name.to_sum

        def add():
            arrived(name.far, k)

            def one(place):
                own = grad_block(name, z_adj)[place, :].astype(F32)
                name.far[place, :] = (own + name.far[place, :].astype(F32)).astype(BF16)

            add_rows(name.count, one)

        run_if(mid, add)
        send(name.far, name.near, k + 2, dev_adj, mid)

    def grad_total(name, cond):
        k = name.to_sum
        arrived(name.near, k + (5 if cond is end else 2), cond)
        if cond is mid:
            arrived(name.far, k + 4, mid)

        def add():
            def one(place):
                total = name.near[place, :].astype(F32)
                if cond is mid:
                    total = total + name.far[place, :].astype(F32)
                name.near[place, :] = (total + grad_block(name, z)[place, :].astype(F32)).astype(BF16)

            add_rows(name.count, one)

        run_if(cond, add)

    def grad_final(name, cond):
        grad_total(name, cond)
        if name.by_column:
            size = name.count // P_IN
            for j, (q_to, device) in enumerate(in_plane):
                src = name.near.at[part(q_to, size)]
                send(src, name.sorted.at[q], name.last + j, device, cond)
            src = name.near.at[part(q, size)]
            name.last_copies.append((local(src, name.sorted.at[q], cond), cond))
        else:
            keep(name.near, name.result, cond)

    def f2_final(cond):
        if cond is end:
            arrived(wt.f2.near, wt.f2.to_sum + 2, end)
        else:
            for h in range(2):
                arrived(f2_half(wt.f2.near, h), wt.f2.to_sum + 1 + 2 * h, mid)
            run_if(mid, lambda: grad_add(wt.f2, wt.f2.near, z))
        keep(wt.f2.near, wt.f2.result, cond)

    def f1_final(cond):
        if cond is end:
            arrived(wt.f1.near, wt.f1.to_sum + 2, end)
        else:
            arrived(wt.f1.near, wt.f1.to_sum + 1, mid)
            run_if(mid, lambda: grad_add(wt.f1, wt.f1.near, z))
        size = wt.f1.count // P_IN
        for tile in range(Z):
            dst = unit_columns(wt.f1.result, tile, q)
            for j, (q_to, device) in enumerate(in_plane):
                src = wt.f1.near.at[part(q_to, size), part(tile, 256)]
                send(src, dst, unit_last + 3 * tile + j, device, cond)
            keep(wt.f1.near.at[part(q, size), part(tile, 256)], dst, cond)

    def last_wait(name):
        for j, (q_from, _) in enumerate(in_plane):
            arrived(name.sorted.at[q_from], name.last + j)
        for copy, cond in name.last_copies:
            run_if(cond, copy.wait)
        unsort_columns(name)
        keep(name.raw, name.result)

    def unit_last_wait():
        for tile in range(Z):
            for j, (q_from, _) in enumerate(in_plane):
                place = unit_columns(wt.f1.result, tile, q_from)
                arrived(place, unit_last + 3 * tile + j)

    def piece(name, index, h, parts):
        size = L // parts
        return name.at[part(index * parts + h, size)]

    def half_major(name, index, h, parts=2):
        return name.at[part(h * P_IN + index, HALF)]

    def gather_open(name, cond=None, parts=1, lay=piece):
        return name, slot(3 * parts), [], cond, parts, lay

    def gather_part(ticket, h, cond=None):
        name, k, records, usual, parts, lay = ticket
        cond = usual if cond is None else cond
        own = lay(name, q, h, parts)
        records.append(send(own, own, k + 3 * h, dev_x, cond))
        records.append(send(own, own, k + 3 * h + 1, dev_core, cond))

    def gather_start(name, cond=None):
        ticket = gather_open(name, cond)
        gather_part(ticket, 0)
        return ticket

    def gather_relay_part(ticket, h):
        name, k, records, cond, parts, lay = ticket
        other = lay(name, q_x, h, parts)
        arrived(other, k + 3 * h, cond)
        records.append(send(other, other, k + 3 * h + 2, dev_core, cond))

    def gather_ready_part(ticket, h):
        name, k, _, cond, parts, lay = ticket
        arrived(lay(name, q_core, h, parts), k + 3 * h + 1, cond)
        arrived(lay(name, q_xc, h, parts), k + 3 * h + 2, cond)

    def gather_relay(ticket):
        for h in range(ticket[4]):
            gather_relay_part(ticket, h)

    def gather_ready(ticket):
        for h in range(ticket[4]):
            gather_ready_part(ticket, h)

    def gather_finish(ticket):
        gather_relay(ticket)
        gather_ready(ticket)

    def reduce_start(which, cond=None):
        k = slot(4)
        out = which.parts
        first = send(rows(out, q_xc), rows(which.core, 1), k, dev_core, cond)
        second = send(rows(out, q_core), rows(which.core, 0), k + 1, dev_core, cond)
        return which, k, [first, second], cond, piece

    def reduce_open(which, cond):
        return which, slot(6), [], cond, half_major

    def reduce_start_half(ticket, h):
        which, k, records, cond, lay = ticket
        for j, index in ((1, q_xc), (0, q_core)):
            src, dst = lay(which.parts, index, h), piece(which.core, j, h, 2)
            records.append(send(src, dst, k + 4 * h + 1 - j, dev_core, cond))

    def reduce_relay_half(ticket, h):
        which, k, records, cond, lay = ticket
        landed = piece(which.core, 1, h, 2)
        if lay is half_major:
            arrived(landed, k + 4 * h, cond)
        elif h == 0:
            arrived(rows(which.core, 1), k, cond)
        mine = lay(which.parts, q_x, h, 2)

        def add():
            def one(i):
                place = part(i, TILE)
                total = mine[place, :].astype(F32) + landed[place, :].astype(F32)
                mine[place, :] = total.astype(BF16)

            loop(TILES, one)

        run_if(cond, add)
        dst = which.across.at[part(h, HALF)]
        records.append(send(mine, dst, k + 2 + h, dev_x, cond))
        return records[-1]

    def reduce_relay(ticket):
        reduce_relay_half(ticket, 0)
        reduce_relay_half(ticket, 1)

    def reduce_ready_half(ticket, h):
        which, k, _, cond, lay = ticket
        if lay is half_major:
            arrived(piece(which.core, 0, h, 2), k + 4 * h + 1, cond)
        elif h == 0:
            arrived(rows(which.core, 0), k + 1, cond)
        arrived(which.across.at[part(h, HALF)], k + 2 + h, cond)

    def reduce_ready(ticket):
        reduce_ready_half(ticket, 0)
        reduce_ready_half(ticket, 1)

    def reduced(ticket, place):
        which = ticket[0]
        total = rows(which.parts, q)[place, :].astype(F32)
        total = total + rows(which.core, 0)[place, :].astype(F32)
        return total + which.across[place, :].astype(F32)

    def fold(ticket, dst, halves=(0, 1)):
        which, lay = ticket[0], ticket[4]
        for h in halves:
            mine, landed = lay(which.parts, q, h, 2), piece(which.core, 0, h, 2)

            def one(i, h=h, mine=mine, landed=landed):
                place, here = part(i, TILE), part(i + h * TILES, TILE)
                total = mine[place, :].astype(F32) + landed[place, :].astype(F32)
                dst[here, :] = (total + which.across[here, :].astype(F32)).astype(BF16)

            loop(TILES, one)

    def reduce_done(ticket):
        for record in ticket[2]:
            sent(record)

    def spread_start(place):
        k = slot(8)
        for j, device in enumerate((dev_diag, dev_opp, dev_adj)):
            send(place(z), place(z), k + j, device)
        return place, k

    def spread_wait(ticket):
        place, k = ticket
        for j, plane in enumerate((z_diag, z_opp, z_adj)):
            arrived(place(plane), k + j)

    def spread_plane(ticket, name):
        k = ticket[1]
        for j, (_, device) in enumerate(in_plane):
            send(name.at[q], name.at[q], k + 5 + j, device)

    def spread_ready(ticket, name):
        k = ticket[1]
        for j, (q_from, _) in enumerate(in_plane):
            arrived(name.at[q_from], k + 5 + j)

    def lanes(j, size=256):
        return part(j, size)

    def matmul(left, right, dst, bias=None, bias_row=0, bias_at=0):
        count = right.shape[1] // 256

        def one(j):
            tile = nn(left[...], right[:, lanes(j)])
            if bias is not None:
                tile = tile + bias[bias_row:bias_row + 1, part(j + bias_at, 256)]
            dst[:, lanes(j)] = tile.astype(BF16)

        loop(count, one)

    def matmul_back(left, right, dst, at=slice(0, T)):
        def one(j):
            dst[at, lanes(j)] = nt(left[at, :], right[lanes(j), :]).astype(BF16)

        loop(right.shape[0] // 256, one)

    def weight_grad(left, right, name, more=False):
        def one(j):
            total = tn(left[:, lanes(j)], right[...])
            if more:
                total = total + name.grad[lanes(j), :].astype(F32)
            name.grad[lanes(j), :] = total.astype(BF16)

        loop(left.shape[1] // 256, one)

    low_half = lax.broadcasted_iota(jnp.int32, (L, 128), 1) < 64
    keep_low = low_half.astype(F32).astype(BF16)
    keep_high = (1.0 - low_half.astype(F32)).astype(BF16)

    def both(pair):
        return jnp.concatenate([pair * keep_low, pair * keep_high], axis=0)

    def merge(stacked):
        return jnp.where(low_half, stacked[:L], stacked[L:])

    def attention(qref, q_at, kref, k_at, v_at, causal, length_row, probs, dst):
        def one(i):
            r, pair = i // 2, i % 2
            place = part(r, L)
            query = both(qref[place, part(pair + q_at, 128)])
            scores = nt(query, kref[place, part(pair + k_at, 128)]) * HD ** (-0.5)
            key = lax.broadcasted_iota(jnp.int32, scores.shape, 1)
            limit = buf.sva[r, z][length_row:length_row + 1, 0:1].astype(F32)
            allowed = key.astype(F32) < limit
            if causal:
                at = lax.broadcasted_iota(jnp.int32, scores.shape, 0)
                at = jnp.where(at < L, at, at - L)
                allowed = allowed & (key <= at)
            scores = jnp.where(allowed, scores, MASKED)
            raised = jnp.exp(scores - jnp.max(scores, -1, keepdims=True))
            weights = (raised * (1.0 / jnp.sum(raised, -1, keepdims=True))).astype(BF16)
            probs[i] = weights
            mixed = nn(weights, kref[place, part(pair + v_at, 128)])
            dst[place, part(pair, 128)] = merge(mixed).astype(BF16)

        loop(2 * P_IN, one, 2)

    def attention_back(qref, q_at, kref, k_at, v_at, probs, grad):
        def one(i):
            r, pair = i // 2, i % 2
            place = part(r, L)
            query = both(qref[place, part(pair + q_at, 128)])
            key = kref[place, part(pair + k_at, 128)]
            value = kref[place, part(pair + v_at, 128)]
            mixed_grad = both(grad[place, part(pair, 128)])
            weights = probs[i]
            soft = weights.astype(F32)
            grad_probs = nt(mixed_grad, value)
            delta = jnp.sum(soft * grad_probs, -1, keepdims=True)
            grad_scores = (soft * (grad_probs - delta)).astype(BF16)
            scale = HD ** (-0.5)
            grad_query = merge(nn(grad_scores, key)) * scale
            grad_key = tn(grad_scores, query) * scale
            grad_value = tn(weights, mixed_grad)
            qref[place, part(pair + q_at, 128)] = grad_query.astype(BF16)
            kref[place, part(pair + k_at, 128)] = grad_key.astype(BF16)
            kref[place, part(pair + v_at, 128)] = grad_value.astype(BF16)

        loop(2 * P_IN, one, 2)

    def column_sums(source, first, count, row, at):
        def one(j):
            values = source[:, part(j + first, 256)].astype(F32)
            buf.sg[row:row + 1, part(j + at, 256)] = jnp.sum(values, 0, keepdims=True)

        loop(count, one)

    def norm(load, index, dst, halves=(0, 1)):
        def one(i):
            place = part(i, TILE)
            normed, _ = whiten(load(place))
            gain, shift = buf.vec[index:index + 1, :], buf.vec[index + 3:index + 4, :]
            rows(dst, q)[place, :] = (normed * gain + shift).astype(BF16)

        loop(TILES * len(halves), one, first=TILES * halves[0])

    def norm_back(load, incoming, index, base, dst, low, out_row=None, halves=(0, 1)):
        zero = jnp.zeros((1, D), F32)

        def one(i, carry):
            gain_sum, shift_sum, out_sum = carry
            place = part(i, TILE)
            normed, scale = whiten(load(place))
            grad = incoming(place)
            gained = grad * buf.vec[index:index + 1, :]
            back = gained - jnp.mean(gained, -1, keepdims=True)
            back = back - normed * jnp.mean(gained * normed, -1, keepdims=True)
            total = base(place) + scale * back
            if dst is not None:
                dst[place, :] = total
            rounded = total.astype(BF16)
            low(place, rounded)
            return (
                gain_sum + jnp.sum(grad * normed, 0, keepdims=True),
                shift_sum + jnp.sum(grad, 0, keepdims=True),
                out_sum + jnp.sum(rounded.astype(F32), 0, keepdims=True),
            )

        first = TILES * halves[0]
        last = first + TILES * len(halves)
        gain_sum, shift_sum, out_sum = lax.fori_loop(first, last, one, (zero, zero, zero))
        buf.sg[index:index + 1, :] = buf.sg[index:index + 1, :] + gain_sum
        buf.sg[index + 3:index + 4, :] = buf.sg[index + 3:index + 4, :] + shift_sum
        if out_row is not None:
            buf.sg[out_row:out_row + 1, :] = buf.sg[out_row:out_row + 1, :] + out_sum

    gate = pltpu.get_barrier_semaphore()
    partners = [device for _, device in in_plane] + [dev_adj, dev_opp, dev_diag]
    partners += [((s + j) % n_sec, d) for j in range(1, n_sec)]
    for device in partners:
        pl.semaphore_signal(gate, inc=1, device_id=device, device_id_type=MESH)
    raw_copies = [local(weight.source, weight.raw) for weight in (wt.qkv, wt.ckv, wt.cq)]
    low_lanes = lax.broadcasted_iota(jnp.int32, (3, 128), 1) < 64
    even_lanes = (jnp.zeros((3, 128), jnp.int32) + c) == 0
    for row, pieces in ((0, io.gain), (3, io.shift), (6, io.out_bias)):
        value = pieces[...].astype(F32)
        twice = jnp.concatenate([value, value], 1)
        buf.sg[row:row + 3, 0:128] = jnp.where(low_lanes == even_lanes, twice, 0.0)
    buf.sg[9:10, 0:128] = io.self_bias[...].astype(F32)
    buf.sg[10:11, 0:128] = io.cross_bias[...].astype(F32)
    buf.sg[11:12, 0:128] = io.unit_bias[:, 0:128].astype(F32)
    buf.sg[12:13, 0:128] = io.unit_bias[:, 128:256].astype(F32)
    buf.sg[13:14, 0:128] = jnp.zeros((1, 128), F32) + io.tgt[0].astype(F32)
    buf.sg[14:15, 0:128] = jnp.zeros((1, 128), F32) + io.src[0].astype(F32)
    buf.sg[15:16, 0:128] = jnp.zeros((1, 128), F32)
    buf.sva[q, z] = buf.sg[:, 0:128].astype(BF16)

    raw_copies[0].wait()
    sort_columns(wt.qkv)
    pl.semaphore_wait(gate, len(partners))

    sv = spread_start(lambda plane: buf.sva.at[q, plane])
    swap_start(wt.qkv)
    k_prev, k_cot, k_mem = slot(), slot(), slot(n_sec)
    send(io.prev, buf.hb, k_prev, ((s + 1) % n_sec, d))
    mem_slot = rows(buf.m, q)
    for j in range(1, n_sec):
        send(io.mem, mem_slot.at[:, part(s, mem_cols)], k_mem + j, ((s + j) % n_sec, d))
    mem_copy = local(io.mem, mem_slot.at[:, part(s, mem_cols)])
    send(io.cot, rows(buf.e3, q), k_cot, ((s + n_sec - 1) % n_sec, d))
    for weight in (wt.so, wt.co, wt.f2):
        weight.own_copy = [local(weight.source, block(weight, z))]
    send_inward(wt.so, wt.so.source)
    send_across(wt.so, wt.so.source)
    weight_outward(wt.so, wt.so.source)
    swap_wait(wt.qkv)
    for weight in first_weights:
        send_inward(weight, block(weight, z))
        send_across(weight, block(weight, z))
        weight_outward(weight, block(weight, z))
    spread_wait(sv)
    spread_plane(sv, buf.sva)
    for weight, copy in ((wt.ckv, raw_copies[1]), (wt.cq, raw_copies[2])):
        copy.wait()
        sort_columns(weight)
        swap_start(weight)
    spread_ready(sv, buf.sva)

    for tile in range(D // 128):
        pair = buf.sva[2 * (tile % 2), tile // 2].astype(F32)
        pair = pair + buf.sva[2 * (tile % 2) + 1, tile // 2].astype(F32)
        buf.vec[:, tile * 128:(tile + 1) * 128] = pair
    half = lax.broadcasted_iota(jnp.int32, (16, 128), 1) < 64
    even = (jnp.zeros((16, 128), jnp.int32) + c) == 0
    buf.bias[...] = jnp.zeros((8, D), F32)
    for kind in range(2):
        for tile in range(2):
            first = buf.sva[x, tile + 2 * kind].astype(F32)
            second = buf.sva[2 + x, tile + 2 * kind].astype(F32)
            lower = jnp.where(even, first, pltpu.roll(first, 64, 1))
            upper = jnp.where(even, pltpu.roll(second, 64, 1), second)
            both_heads = jnp.where(half, lower, upper)
            for which in range(2):
                at = 512 * kind + 128 * tile
                buf.bias[which:which + 1, at:at + 128] = both_heads[9 + which:10 + which]
    for tile in range(Z):
        unit = buf.sva[q, tile].astype(F32)
        buf.bias[2:3, 256 * tile:256 * tile + 128] = unit[11:12]
        buf.bias[2:3, 256 * tile + 128:256 * tile + 256] = unit[12:13]
    buf.sg[...] = jnp.zeros((16, D), F32)

    relay_inward(first_weights[0])
    relay_near(first_weights[0])
    arrived(buf.hb, k_prev)

    def hidden(place):
        return buf.hb[place, :].astype(F32)

    norm(hidden, 0, buf.a1)
    a1 = gather_start(buf.a1)
    unit_swap_start()
    relay_inward(first_weights[1])
    relay_near(first_weights[1])
    relay_inward(wt.so)
    swap_wait(wt.ckv)
    send_inward(wt.ckv, block(wt.ckv, z))
    swap_wait(wt.cq)
    send_inward(wt.cq, block(wt.cq, z))
    send_inward(wt.co, wt.co.source)
    send_across(wt.ckv, block(wt.ckv, z))
    for j in range(1, n_sec):
        origin = (s + n_sec - j) % n_sec
        arrived(mem_slot.at[:, part(origin, mem_cols)], k_mem + j)
    mem_copy.wait()
    memory = gather_start(buf.m)
    arrived(rows(buf.e3, q), k_cot)
    k_units = slot(16)
    to_middle = [send(rows(buf.e3, q), rows(buf.e3, q), k_units + 9, dev_x, end)]

    def cot_inward(index, k):
        for h in range(2):
            src, dst = piece(buf.e3, index, h, 2), half_major(buf.e3b, index, h)
            to_middle.append(send(src, dst, k + h, dev_adj, end))

    cot_inward(q, k_units)
    relay_far(first_weights[0])
    gather_relay(a1)
    relay_far(first_weights[1])
    relay_near(wt.so)
    relay_inward(wt.ckv)
    gather_ready(a1)
    unit_swap_wait(end)
    send_inward(wt.f1, block(wt.f1, z))
    for weight in first_weights:
        weight_ready(weight)
    matmul(buf.a1, wt.qkv.weight, buf.qkv, buf.bias, 0)
    relay_far(wt.so)
    weight_outward(wt.ckv, block(wt.ckv, z))
    send_across(wt.cq, block(wt.cq, z))
    attention(buf.qkv, 0, buf.qkv, 2, 4, True, 13, buf.p1, buf.o1)
    relay_inward(wt.cq)
    send_across(wt.co, wt.co.source)
    wt.so.own_copy[0].wait()
    weight_ready(wt.so)
    matmul(buf.o1, wt.so.weight, set_a.parts)
    step = reduce_start(set_a)
    send_inward(wt.f2, wt.f2.source)
    relay_inward(wt.co)
    relay_near(wt.ckv)
    weight_outward(wt.cq, block(wt.cq, z))
    reduce_relay(step)
    arrived(rows(buf.e3, q_x), k_units + 9, end)
    cot_inward(q_x, k_units + 2)
    gather_finish(memory)
    relay_far(wt.ckv)
    unit_swap_wait(mid)
    send_across(wt.f1, block(wt.f1, z))

    def after_self(i):
        place = part(i, TILE)
        buf.h1[place, :] = hidden(place) + (reduced(step, place) + buf.vec[6:7, :])

    a2 = gather_open(buf.a2, None, 2)
    for h in range(2):
        reduce_ready_half(step, h)
        loop(TILES, after_self, first=h * TILES)
        norm(lambda place: buf.h1[place, :], 1, buf.a2, (h,))
        gather_part(a2, h)
    reduce_done(step)
    relay_near(wt.cq)
    relay_far(wt.cq)
    weight_outward(wt.co, wt.co.source)
    weight_ready(wt.ckv)
    matmul(buf.m, wt.ckv.weight, buf.kv, buf.bias, 1, 1)
    relay_near(wt.co)
    send_across(wt.f2, wt.f2.source)
    relay_far(wt.co)
    relay_inward(wt.f1)

    gather_finish(a2)
    e3 = gather_start(buf.e3, mid)
    weight_ready(wt.cq)
    matmul(buf.a2, wt.cq.weight, buf.q2, buf.bias, 1)
    attention(buf.q2, 0, buf.kv, 0, 2, False, 14, buf.p2, buf.o2)
    wt.co.own_copy[0].wait()
    weight_ready(wt.co)
    matmul(buf.o2, wt.co.weight, set_b.parts)
    step = reduce_start(set_b)
    relay_inward(wt.f2)
    gather_finish(e3)
    reduce_relay(step)

    def after_cross(i):
        place = part(i, TILE)
        buf.h2[place, :] = buf.h1[place, :] + (reduced(step, place) + buf.vec[7:8, :])

    a3 = gather_open(buf.a3, mid, 2)
    for h in range(2):
        reduce_ready_half(step, h)
        loop(TILES, after_cross, first=h * TILES)
        norm(lambda place: buf.h2[place, :], 2, buf.a3, (h,))
        send(piece(buf.a3, q, h, 2), half_major(buf.a3b, q, h), k_units + 10 + h, dev_adj, end)
        gather_part(a3, h)
    reduce_done(step)

    def units(normed, activs, slopes, at=slice(0, T)):
        def one(j):
            value = nn(normed[at, :], wt.f1.weight[:, lanes(j)]) + buf.bias[2:3, lanes(j)]
            activ, slope = gelu_pair(value)
            activs[at, lanes(j)] = activ.astype(BF16)
            slopes[at, lanes(j)] = slope.astype(BF16)

        loop(FL // 256, one, 2)

    def units_back(grad, slopes, at=slice(0, T)):
        def one(j):
            value = nt(grad[at, :], wt.f2.weight[lanes(j), :])
            low = (value * slopes[at, lanes(j)].astype(F32)).astype(BF16)
            slopes[at, lanes(j)] = low
            total = jnp.sum(low.astype(F32), 0, keepdims=True)
            buf.sg[10:11, lanes(j)] = buf.sg[10:11, lanes(j)] + total

        loop(FL // 256, one)

    def weight_grads(left, right, left_b, right_b, name, first, count):
        def one(j):
            total = tn(left[:, lanes(j)], right[...]) + tn(left_b[:, lanes(j)], right_b[...])
            name.grad[lanes(j), :] = total.astype(BF16)

        loop(count, one, first=first)

    def finish(incoming):
        def one(i):
            place = part(i, TILE)
            total = buf.h2[place, :] + (incoming(place) + buf.vec[8:9, :])
            buf.stage[place, :] = total.astype(BF16)

        loop(L // TILE, one)

    def on_mid(fn, *args):
        run_if(mid, lambda: fn(*args))

    def cot_sum(i, carry):
        return carry + jnp.sum(rows(buf.e3, q)[part(i, TILE), :].astype(F32), 0, keepdims=True)

    buf.sg[8:9, :] = lax.fori_loop(0, L // TILE, cot_sum, jnp.zeros((1, D), F32))

    for index, k in ((q, k_units), (q_x, k_units + 2)):
        for h in range(2):
            landed = half_major(buf.e3b, index, h)
            arrived(landed, k + h, mid)
            send(landed, landed, k + 4 + h, dev_core, mid)
    gather_relay(a3)
    a3b = gather_open(buf.a3b, mid, 2, half_major)
    arrived(half_major(buf.a3b, q, 0), k_units + 10, mid)
    gather_part(a3b, 0)
    gather_ready(a3)
    inner_ready(wt.f1)
    on_mid(units, buf.a3, buf.g, buf.gp)
    arrived(half_major(buf.a3b, q, 1), k_units + 11, mid)
    gather_part(a3b, 1)
    on_mid(weight_grad, buf.g, buf.e3, wt.f2)
    for index, k in ((q_core, k_units + 4), (q_xc, k_units + 6)):
        for h in range(2):
            arrived(half_major(buf.e3b, index, h), k + h, mid)
    gather_relay_part(a3b, 0)
    wt.f2.own_copy[0].wait()
    inner_ready(wt.f2)
    on_mid(matmul, buf.g, wt.f2.weight, set_c.parts)
    final = reduce_start(set_c, mid)
    gather_ready_part(a3b, 0)
    step_b = reduce_open(set_b, mid)
    for h in range(2):
        at = slice(h * T // 2, (h + 1) * T // 2)
        if h == 1:
            gather_ready_part(a3b, 1)
        on_mid(units, buf.a3b, buf.gb, buf.gpb, at)
        if h == 0:
            reduce_relay(final)
        else:
            reduce_relay_half(step_b, 0)
        on_mid(units_back, buf.e3b, buf.gpb, at)
        if h == 0:
            gather_relay_part(a3b, 1)
        on_mid(matmul_back, buf.gpb, wt.f1.weight, set_b.parts, at)
        reduce_start_half(step_b, h)

    def back_outward(h):
        reduce_ready_half(step_b, h)
        on_mid(fold, step_b, buf.back, (h,))
        ready = buf.back.at[part(h, HALF)]
        send(ready, ready, k_units + 12 + h, dev_adj, mid)

    on_mid(weight_grad, buf.gb, buf.e3b, wt.f2, True)
    inner_grad_far(wt.f2)
    f2_near(0)
    reduce_relay_half(step_b, 1)
    on_mid(units_back, buf.e3, buf.gp)
    back_outward(0)
    on_mid(matmul_back, buf.gp, wt.f1.weight, set_a.parts)
    reduce_ready(final)
    on_mid(finish, lambda place: reduced(final, place))
    reduce_done(final)
    step = reduce_start(set_a, mid)
    back_outward(1)
    reduce_relay(step)
    on_mid(weight_grads, buf.a3, buf.gp, buf.a3b, buf.gpb, wt.f1, 0, Z)
    inner_grad_far(wt.f1)
    inner_grad_near(wt.f1)
    on_mid(matmul, buf.gb, wt.f2.weight, set_c.parts)

    def store(name):
        def low(place, value):
            rows(name, q)[place, :] = value

        return low

    def units_norm_back(incoming, halves):
        norm_back(
            lambda place: buf.h2[place, :], incoming, 2,
            lambda place: rows(buf.e3, q)[place, :].astype(F32), buf.dh, store(buf.e2), 7, halves,
        )

    reduce_done(e3)
    for record in to_middle:
        sent(record)
    e2 = gather_open(buf.e2, None, 2)
    for h in range(2):
        reduce_ready_half(step, h)
        on_mid(units_norm_back, lambda place: reduced(step, place), (h,))
        gather_part(e2, h, mid)
    final_b = reduce_open(set_c, mid)
    reduce_start_half(final_b, 0)
    reduce_start_half(final_b, 1)
    inner_grad_combine(wt.f2)
    for h in range(2):
        arrived(buf.back.at[part(h, HALF)], k_units + 12 + h, end)
        run_if(
            end,
            lambda h=h: units_norm_back(lambda place: buf.back[place, :].astype(F32), (h,)),
        )
        gather_part(e2, h, end)
    reduce_done(step)
    reduce_done(step_b)
    gather_finish(e2)
    reduce_relay(final_b)

    weight_grad(buf.o2, buf.e2, wt.co)
    grad_send(wt.co)
    matmul_back(buf.e2, wt.co.weight, buf.do)
    attention_back(buf.q2, 0, buf.kv, 0, 2, buf.p2, buf.do)
    matmul_back(buf.q2, wt.cq.weight, set_b.parts)
    step = reduce_start(set_b)
    weight_grad(buf.a2, buf.q2, wt.cq)
    grad_send(wt.cq)
    reduce_relay(step)
    grad_combine(wt.co)
    grad_combine(wt.cq)
    weight_grad(buf.m, buf.kv, wt.ckv)
    grad_send(wt.ckv)
    grad_send_near(wt.ckv)
    matmul_back(buf.kv, wt.ckv.weight, set_a.parts)
    mem_step = reduce_start(set_a)
    column_sums(buf.q2, 0, 1, 9, 2)
    column_sums(buf.kv, 1, 1, 9, 3)
    reduce_ready(final_b)
    on_mid(fold, final_b, buf.tail)
    send(buf.tail, buf.tail, k_units + 14, dev_adj, mid)
    reduce_done(final_b)
    inner_grad_combine(wt.f1)
    e1 = gather_open(buf.e3, None, 2)
    for h in range(2):
        reduce_ready_half(step, h)
        norm_back(
            lambda place: buf.h1[place, :], lambda place: reduced(step, place), 1,
            lambda place: buf.dh[place, :], buf.dh, store(buf.e3), 6, (h,),
        )
        gather_part(e1, h)
    reduce_done(step)
    grad_combine(wt.ckv)
    gather_finish(e1)
    reduce_relay(mem_step)

    weight_grad(buf.o1, buf.e3, wt.so)
    grad_send(wt.so)
    matmul_back(buf.e3, wt.so.weight, buf.do)
    attention_back(buf.qkv, 0, buf.qkv, 2, 4, buf.p1, buf.do)
    grad_outward(wt.co)
    grad_combine(wt.so)
    run_if(end, lambda: weight_grad(buf.a1, buf.qkv, wt.qkv))
    grad_send(wt.qkv)
    matmul_back(buf.qkv, wt.qkv.weight, set_b.parts)
    step = reduce_start(set_b)
    on_mid(weight_grad, buf.a1, buf.qkv, wt.qkv)
    column_sums(buf.qkv, 0, 1, 9, 0)
    column_sums(buf.qkv, 2, 1, 9, 1)
    grad_outward(wt.cq)
    reduce_relay(step)
    f1_final(mid)
    grad_combine_far(wt.qkv)

    reduce_ready(mem_step)
    fold(mem_step, buf.mb)
    k_back = slot(n_sec)
    for j in range(1, n_sec):
        to = (s + j) % n_sec
        send(buf.mb.at[:, part(to, mem_cols)], buf.ml.at[j], k_back + j, (to, d))
    grad_outward(wt.ckv)
    grad_outward(wt.so)
    grad_combine_middle(wt.qkv)
    reduce_ready(step)

    def store_stage(place, value):
        buf.ig[place, :] = value

    norm_back(
        hidden, lambda place: reduced(step, place), 0,
        lambda place: buf.dh[place, :], None, store_stage,
    )
    k_in = slot()
    send(buf.ig, io.input_grad, k_in, ((s + n_sec - 1) % n_sec, d))
    buf.sga[z] = buf.sg[...].astype(BF16)
    sums = spread_start(lambda plane: buf.sga.at[plane])
    f2_near(1)
    for weight in (wt.qkv, wt.cq, wt.co, wt.so):
        grad_send_near(weight)
    f2_final(end)
    f1_final(end)
    for weight in (wt.co, wt.cq):
        grad_final(weight, end)
    grad_outward(wt.qkv)
    grad_final(wt.ckv, end)
    grad_final(wt.so, end)
    grad_final(wt.ckv, mid)
    grad_final(wt.qkv, mid)
    spread_wait(sums)
    planes = buf.sga[0].astype(F32)
    for plane in range(1, Z):
        planes = planes + buf.sga[plane].astype(F32)
    buf.sgp[q] = planes.astype(BF16)
    spread_plane(sums, buf.sgp)

    arrived(buf.tail, k_units + 14, end)
    run_if(end, lambda: finish(lambda place: buf.tail[place, :].astype(F32)))
    for j in range(1, n_sec):
        arrived(buf.ml.at[j], k_back + j)

    def memory_total(i):
        place = part(i, TILE)
        total = buf.mb[place, part(s, mem_cols)].astype(F32)
        for j in range(1, n_sec):
            total = total + buf.ml[j, place, :].astype(F32)
        buf.mo[place, :] = total.astype(BF16)

    loop(L // TILE, memory_total)
    keep(buf.mo, io.memory_grad)
    grad_final(wt.qkv, end)
    for weight in (wt.cq, wt.co, wt.so):
        grad_final(weight, mid)
    f2_final(mid)
    unit_last_wait()
    last_wait(wt.cq)
    last_wait(wt.ckv)
    keep(buf.stage, io.output)
    spread_ready(sums, buf.sgp)

    def per_unit(q_at, at):
        return buf.sgp[q_at, :, at].astype(F32)

    at = part(d // 2, 128)
    feature = per_unit(0, at)
    for q_at in range(1, P_IN):
        feature = feature + per_unit(q_at, at)
    swapped = pltpu.roll(feature, 64, 1)
    buf.sums[...] = jnp.where((jnp.zeros((16, 128), jnp.int32) + c) == 0, feature, swapped)
    head = d % 8
    at = part(2 * (d // 8) + head // 4, 128)
    low_head, high_head = per_unit(2 * c, at), per_unit(2 * c + 1, at)
    first_half = (jnp.zeros((16, 128), jnp.int32) + (head // 2) % 2) == 0
    low_head = jnp.where(first_half, low_head, pltpu.roll(low_head, 64, 1))
    high_head = jnp.where(first_half, pltpu.roll(high_head, 64, 1), high_head)
    buf.sums[9:10, :] = jnp.where(half, low_head, high_head)[9:10]
    at = part(2 * (d // 8) + 4 + head // 4, 128)
    low_head, high_head = per_unit(2 * c, at), per_unit(2 * c + 1, at)
    low_head = jnp.where(first_half, low_head, pltpu.roll(low_head, 64, 1))
    high_head = jnp.where(first_half, pltpu.roll(high_head, 64, 1), high_head)
    buf.sums[10:11, :] = jnp.where(half, low_head, high_head)[9:10]
    buf.sums[11:12, :] = per_unit(q, part(2 * z, 128))[10:11]
    buf.sums[12:13, :] = per_unit(q, part(2 * z + 1, 128))[10:11]
    keep(buf.sums, io.sums_out)
    last_wait(wt.qkv)
    arrived(io.input_grad, k_in)
    for copy, cond in result_copies:
        run_if(cond, copy.wait)
    for record in list(started):
        sent(record)
    assert counter[0] <= SEMS and local_counter[0] <= 64


def buffer_shapes(n_sec, mem_cols):
    tokens, row = (T, D), (L, D)
    shapes = dict(
        sva=(P_IN, Z, 16, 128),
        sga=(Z, 16, D),
        sgp=(P_IN, 16, D),
        hb=row, ig=row, stage=row, mb=row,
        ml=(n_sec, L, mem_cols),
        mo=(L, mem_cols),
        qkv=(T, 768), q2=(T, 256), kv=(T, 512), o1=(T, 256), o2=(T, 256), do=(T, 256),
        p1=(2 * P_IN, 2 * L, L), p2=(2 * P_IN, 2 * L, L),
        g=(T, FL), gp=(T, FL),
        a1=tokens, a2=tokens, a3=tokens, m=tokens, e3=tokens, e2=tokens,
        a3b=tokens, e3b=tokens, gb=(T, FL), gpb=(T, FL), back=row, tail=row,
    )
    exact = dict(vec=(16, D), bias=(8, D), sg=(16, D), sums=(16, 128), h1=row, h2=row, dh=row)
    kinds = {name: pltpu.VMEM(shape, BF16) for name, shape in shapes.items()}
    kinds.update({name: pltpu.VMEM(shape, F32) for name, shape in exact.items()})
    return kinds


REDUCE_SHAPES = dict(
    parts=pltpu.VMEM((T, D), BF16),
    core=pltpu.VMEM((2 * L, D), BF16),
    across=pltpu.VMEM((L, D), BF16),
)


def scratch_of(n_sec, mem_cols):
    scratch = list(buffer_shapes(n_sec, mem_cols).values())
    scratch += 3 * list(REDUCE_SHAPES.values())
    for count, columns, _ in WEIGHTS.values():
        scratch += 2 * [pltpu.VMEM((Z * count, columns), BF16)]
        scratch += 2 * [pltpu.VMEM((count, columns), BF16)]
    for count, columns, _ in list(WEIGHTS.values())[:5]:
        scratch += 3 * [pltpu.VMEM((count, columns), BF16)]
    for columns in (768, 512, 256):
        scratch.append(pltpu.VMEM((64, P_IN * columns), BF16))
        scratch.append(pltpu.VMEM((P_IN, 64, columns), BF16))
    return scratch + [
        pltpu.SemaphoreType.DMA((SEMS,)),
        pltpu.SemaphoreType.DMA((SEMS,)),
        pltpu.SemaphoreType.DMA((64,)),
    ]


def finish_kernel(*refs):
    moved, low, sums = refs[:3], refs[3:10], refs[10]
    moved_out, high, small = refs[11:14], refs[14:21], refs[21:27]
    low_buf, high_buf, moved_buf = refs[27:34], refs[34:41], refs[41:44]
    small_buf, sems = refs[44:50], refs[50]
    inward = [
        pltpu.make_async_copy(src, dst, sems.at[i])
        for i, (src, dst) in enumerate(zip(low + moved, low_buf + moved_buf))
    ]
    order = (7, 8, 5, 6, 0, 2, 9, 1, 4, 3)
    for i in order:
        inward[i].start()
    outward = []
    gain, shift, out_bias, self_bias, cross_bias, unit_bias = small_buf
    for row in range(3):
        gain[row] = sums[row:row + 1, 0:64]
        shift[row] = sums[row + 3:row + 4, 0:64]
        out_bias[row] = sums[row + 6:row + 7, 0:64]
    self_bias[...] = sums[9:10, :]
    cross_bias[...] = sums[10:11, :]
    unit_bias[:, 0:128] = sums[11:12, :]
    unit_bias[:, 128:256] = sums[12:13, :]
    for i, (src, dst) in enumerate(zip(small_buf, small)):
        back = pltpu.make_async_copy(src, dst, sems.at[20 + i])
        back.start()
        outward.append(back)
    for i in order:
        inward[i].wait()
        if i < 7:
            src, dst = high_buf[i], high[i]

            def one(j, i=i):
                place = part(j, 16)
                high_buf[i][place, :] = low_buf[i][place, :].astype(F32)

            loop(low_buf[i].shape[0] // 16, one)
        else:
            src, dst = moved_buf[i - 7], moved_out[i - 7]
        back = pltpu.make_async_copy(src, dst, sems.at[10 + i])
        back.start()
        outward.append(back)
    for copy in outward:
        copy.wait()


def on_device_planes(
    prev_act, memory, out_cot, tgt_len, src_len, norm_gain, norm_bias, self_qkv, self_qv_bias,
    self_out, cross_q, cross_kv, cross_qv_bias, cross_out, out_bias, fc1, fc1_bias, fc2,
):
    n_sec = lax.axis_size("section")
    mem_cols = memory.shape[2]
    operands = (
        prev_act[0, 0], memory[0], out_cot[0, 0], tgt_len, src_len,
        norm_gain[0], norm_bias[0], out_bias[0], self_qv_bias, cross_qv_bias, fc1_bias,
        self_qkv[0], self_out[0], cross_kv[0], cross_q[0], cross_out[0], fc1[0], fc2[0],
    )
    anywhere = pl.BlockSpec(memory_space=pl.ANY)
    in_specs = 3 * [anywhere] + 2 * [pl.BlockSpec(memory_space=pltpu.SMEM)]
    in_specs += 6 * [pl.BlockSpec(memory_space=pltpu.VMEM)] + 7 * [anywhere]
    out_shapes = [(L, D), (L, D), (L, mem_cols)]
    for count, columns, by_column in WEIGHTS.values():
        out_shapes.append((count // P_IN, P_IN * columns) if by_column else (count, columns))
    sums_shape = jax.ShapeDtypeStruct((16, 128), F32)
    results = pl.pallas_call(
        functools.partial(whole_kernel, n_sec, mem_cols),
        out_shape=[jax.ShapeDtypeStruct(shape, BF16) for shape in out_shapes] + [sums_shape],
        in_specs=in_specs,
        out_specs=[anywhere] * (len(out_shapes) + 1),
        scratch_shapes=scratch_of(n_sec, mem_cols),
        compiler_params=pltpu.CompilerParams(
            collective_id=0, has_side_effects=True, vmem_limit_bytes=64 * 2**20 - 2**16
        ),
        cost_estimate=pl.CostEstimate(
            flops=21 * 10**9, bytes_accessed=20 * 2**20, transcendentals=3 * 10**6
        ),
    )(*operands)
    shapes = [result.shape for result in results]
    small_shapes = [(3, 1, 64)] * 3 + [(1, 128), (1, 128), (1, 256)]
    vmem = pl.BlockSpec(memory_space=pltpu.VMEM)
    finished = pl.pallas_call(
        finish_kernel,
        out_shape=[jax.ShapeDtypeStruct(shape, BF16) for shape in shapes[:3]]
        + [jax.ShapeDtypeStruct(shape, F32) for shape in shapes[3:10]]
        + [jax.ShapeDtypeStruct(shape, F32) for shape in small_shapes],
        in_specs=10 * [anywhere] + [vmem],
        out_specs=16 * [anywhere],
        scratch_shapes=[pltpu.VMEM(shape, BF16) for shape in shapes[3:10]]
        + [pltpu.VMEM(shape, F32) for shape in shapes[3:10]]
        + [pltpu.VMEM(shape, BF16) for shape in shapes[:3]]
        + [pltpu.VMEM(shape, F32) for shape in small_shapes]
        + [pltpu.SemaphoreType.DMA((26,))],
        compiler_params=pltpu.CompilerParams(vmem_limit_bytes=63 * 2**20),
        cost_estimate=pl.CostEstimate(flops=0, bytes_accessed=9 * 2**20, transcendentals=0),
    )(*results)
    (
        output, input_grad, memory_grad, g_qkv, g_so, g_ckv, g_cq, g_co, g_f1, g_f2,
        gain, shift, biases, self_biases, cross_biases, units,
    ) = finished
    return (
        output[None, None],
        input_grad[None, None],
        memory_grad[None],
        gain.transpose(1, 0, 2),
        shift.transpose(1, 0, 2),
        g_qkv[None],
        self_biases,
        g_so[None],
        g_cq[None],
        g_ckv[None],
        cross_biases,
        g_co[None],
        biases.transpose(1, 0, 2),
        g_f1[None],
        units,
        g_f2[None],
    )


def solution(mesh):
    in_specs = (
        P("section", "dp", None, None),
        P("dp", None, "section"),
        P("section", "dp", None, None),
        P("dp"),
        P("dp"),
        P("section", None, "dp"),
        P("section", None, "dp"),
        P("section", "dp", None),
        P("section", "dp"),
        P("section", "dp", None),
        P("section", "dp", None),
        P("section", "dp", None),
        P("section", "dp"),
        P("section", "dp", None),
        P("section", None, "dp"),
        P("section", "dp", None),
        P("section", "dp"),
        P("section", "dp", None),
    )
    out_specs = (
        P("section", "dp", None, None),
        P("section", "dp", None, None),
        P("dp", None, "section"),
        P("section", None, "dp"),
        P("section", None, "dp"),
        P("section", "dp", None),
        P("section", "dp"),
        P("section", "dp", None),
        P("section", "dp", None),
        P("section", "dp", None),
        P("section", "dp"),
        P("section", "dp", None),
        P("section", None, "dp"),
        P("section", "dp", None),
        P("section", "dp"),
        P("section", "dp", None),
    )
    planes = Z * P_IN
    fits = mesh.shape["dp"] == planes
    return jax.shard_map(
        on_device_planes if fits else on_device, mesh=mesh, in_specs=in_specs, out_specs=out_specs, check_vma=False
    )
```
